32 devices in a mesh: fsdp: 32 (over z, y, x, core).
Axes of the slice: x: 2, y: 2, z: 4, core: 2. Of those that a mesh axis runs over, the one named last changes fastest.
Arguments:
- tokens: bfloat16 [4096, 1600], P('fsdp'), may hold values from -6 to 6
- cotangent: bfloat16 [4096, 1600], P('fsdp'), may hold values from -6 to 6
- seq_lengths: int32 [128], P('fsdp'), may hold values from 0 to 128, as said below
- qkv_proj: bfloat16 [3584000], P('fsdp'), may hold values from -0.15625 to 0.15625
- mamba_in: bfloat16 [10240000], P('fsdp'), may hold values from -0.15625 to 0.15625
- select_proj: bfloat16 [422400], P('fsdp'), may hold values from -0.21875 to 0.21875
- step_proj: bfloat16 [320000], P('fsdp'), may hold values from -0.625 to 0.625
- mamba_out: bfloat16 [5120000], P('fsdp'), may hold values from -0.109375 to 0.109375
- join_out: bfloat16 [2560000], P('fsdp'), may hold values from -0.15625 to 0.15625
- conv_taps: bfloat16 [12800], P('fsdp'), may hold values from -3 to 3
- conv_bias: bfloat16 [3200], P('fsdp'), may hold values from -3 to 3
- step_bias: bfloat16 [3200], P('fsdp'), may hold values from -4.5 to -1.5
- decay_rates: bfloat16 [51200], P('fsdp'), may hold values from 1 to 16
- skip_gain: bfloat16 [3200], P('fsdp'), may hold values from 0.5 to 1.5
- norm_gains: bfloat16 [6400], P('fsdp'), may hold values from 0.5 to 1.5
- ffn_gate: bfloat16 [8806400], P('fsdp'), may hold values from -0.15625 to 0.15625
- ffn_up: bfloat16 [8806400], P('fsdp'), may hold values from -0.15625 to 0.15625
- ffn_down: bfloat16 [8806400], P('fsdp'), may hold values from -0.078125 to 0.078125
Outputs:
- block_out: bfloat16 [4096, 1600], P('fsdp')
- input_grad: float32 [4096, 1600], P('fsdp')
- qkv_proj_grad: float32 [3584000], P('fsdp')
- mamba_in_grad: float32 [10240000], P('fsdp')
- select_proj_grad: float32 [422400], P('fsdp')
- step_proj_grad: float32 [320000], P('fsdp')
- mamba_out_grad: float32 [5120000], P('fsdp')
- join_out_grad: float32 [2560000], P('fsdp')
- conv_taps_grad: float32 [12800], P('fsdp')
- conv_bias_grad: float32 [3200], P('fsdp')
- step_bias_grad: float32 [3200], P('fsdp')
- decay_rates_grad: float32 [51200], P('fsdp')
- skip_gain_grad: float32 [3200], P('fsdp')
- norm_gains_grad: float32 [6400], P('fsdp')
- ffn_gate_grad: float32 [8806400], P('fsdp')
- ffn_up_grad: float32 [8806400], P('fsdp')
- ffn_down_grad: float32 [8806400], P('fsdp')
The draws below stay inside these ranges and needn't reach their ends.
Inputs may be any that keep to these rules, and one draw needn't show every extreme that they name: `seq_lengths`: each aligned group of 4 entries holds the lengths of the sequences packed, in order, into one device's 128 rows; they sum to at most 128, the remaining rows being padding; in every draw some device holds a single sequence of 128 tokens.
All inputs are finite; a program needn't handle non-finite values.
Results may differ from the reference program's by a relative error of at most 0.015.
The reference program's roundings to bfloat16 on the way count: a program that leaves them out, or rounds other values in their place, can miss the bound.
Values may be sent and summed in bfloat16 or wider, within the bound.
A program may use at most 640 MiB of HBM per device.

```python
import math
import jax
import jax.numpy as jnp
from jax import lax

D = 1600
HEADS = 25
KV_HEADS = 5
HEAD = 64
INNER = 3200
STATE = 16
CONV = 4
RANK = 100
FF = 5504
TOK_DEV = 128
SEQ_DEV = 4
TOKENS = 4096
SEQS = 128
QKV = 2240
XPROJ = 132
N_FSDP = 32


def draw_seq_lengths(key, part):
    key = jax.random.fold_in(key, 7)
    device_count = SEQS // SEQ_DEV
    total_key, full_key, cut_key = jax.random.split(key, 3)
    device_totals = jax.random.randint(total_key, (device_count,), TOK_DEV // 4, TOK_DEV + 1)
    full_device = jax.random.randint(full_key, (), 0, device_count)
    device_rows = jnp.arange(device_count)
    device_totals = jnp.where(device_rows == full_device, TOK_DEV, device_totals)
    cut_points = jax.random.randint(cut_key, (device_count, SEQ_DEV - 1), 0, TOK_DEV + 1)
    cut_points = jnp.sort(cut_points * device_totals[:, None] // TOK_DEV, axis=1)
    edge_points = jnp.concatenate([jnp.zeros((device_count, 1), jnp.int32), cut_points.astype(jnp.int32), device_totals[:, None].astype(jnp.int32)], axis=1)
    lengths = edge_points[:, 1:] - edge_points[:, :-1]
    one_long = jnp.zeros((SEQ_DEV,), jnp.int32).at[0].set(TOK_DEV)
    lengths = jnp.where((device_rows == full_device)[:, None], one_long[None, :], lengths)
    return lengths.reshape(-1).astype(jnp.int32)


def shard_levels(own_key, extent, cuts, smallest, top_value):
    loudness, own = 1.0, jax.random.fold_in(own_key, 6)
    for dim, parts in cuts:
        heights = jnp.exp(jax.random.uniform(jax.random.fold_in(own, dim), (parts,), jnp.float32, smallest / len(cuts), top_value / len(cuts)))
        loudness = loudness * jnp.repeat(heights, extent[dim] // parts).reshape([-1 if axis == dim else 1 for axis in range(len(extent))])
    return loudness


def bell_draw(stream_key, shape, deviation, limit, shards=(), kind=jnp.bfloat16):
    values = deviation * jax.random.normal(stream_key, shape, jnp.float32)
    if shards:
        values = values * shard_levels(stream_key, shape, shards, -0.22, 0.18)
    return jnp.clip(values, -limit, limit).astype(kind)


def setup_inputs(seed: int = 0) -> dict:
    key_list = jax.random.split(jax.random.key(seed), 19)
    tokens = bell_draw(key_list[0], (TOKENS, D), 1.0, 6.0, ((0, 32),))
    cotangent = bell_draw(key_list[1], (TOKENS, D), 1.0, 6.0, ((0, 32),))
    seq_lengths = draw_seq_lengths(jax.random.fold_in(key_list[18], 71), 0)
    qkv_proj = bell_draw(key_list[3], (D * QKV,), D ** -0.5, 0.15625, ((0, 32),))
    mamba_in = bell_draw(key_list[4], (2 * D * INNER,), D ** -0.5, 0.15625, ((0, 32),))
    select_proj = bell_draw(key_list[5], (INNER * XPROJ,), (INNER // 4) ** -0.5, 0.21875, ((0, 32),))
    step_proj = bell_draw(key_list[6], (RANK * INNER,), RANK ** -0.5, 0.625, ((0, 32),))
    mamba_out = bell_draw(key_list[7], (INNER * D,), INNER ** -0.5, 0.109375, ((0, 32),))
    join_out = bell_draw(key_list[8], (D * D,), D ** -0.5, 0.15625, ((0, 32),))
    conv_taps = bell_draw(key_list[9], (CONV * INNER,), CONV ** -0.5, 3.0, ((0, 32),))
    conv_bias = bell_draw(key_list[10], (INNER,), 0.5, 3.0, ((0, 32),))
    step_bias = jnp.clip(-4.5 + 3.0 * jax.random.uniform(key_list[11], (INNER,), jnp.float32) ** shard_levels(key_list[11], (INNER,), ((0, 32),), -0.2, 0.2), -4.5, -1.5).astype(jnp.bfloat16)
    decay_rates = jnp.clip(jnp.exp(math.log(16.0) - 2.7725887 * jax.random.uniform(key_list[12], (STATE * INNER,), jnp.float32) ** shard_levels(key_list[12], (STATE * INNER,), ((0, 32),), -0.2, 0.2)), 1.0, 16.0).astype(jnp.bfloat16)
    skip_gain = jnp.clip(0.5 + 1.0 * jax.random.uniform(key_list[13], (INNER,), jnp.float32) ** shard_levels(key_list[13], (INNER,), ((0, 32),), -0.2, 0.2), 0.5, 1.5).astype(jnp.bfloat16)
    norm_gains = jnp.clip(0.5 + 1.0 * jax.random.uniform(key_list[14], (4 * D,), jnp.float32) ** shard_levels(key_list[14], (4 * D,), ((0, 32),), -0.2, 0.2), 0.5, 1.5).astype(jnp.bfloat16)
    ffn_gate = bell_draw(key_list[15], (D * FF,), D ** -0.5, 0.15625, ((0, 32),))
    ffn_up = bell_draw(key_list[16], (D * FF,), D ** -0.5, 0.15625, ((0, 32),))
    ffn_down = bell_draw(key_list[17], (FF * D,), FF ** -0.5, 0.078125, ((0, 32),))
    return {"tokens": tokens, "cotangent": cotangent, "seq_lengths": seq_lengths, "qkv_proj": qkv_proj, "mamba_in": mamba_in, "select_proj": select_proj, "step_proj": step_proj, "mamba_out": mamba_out, "join_out": join_out, "conv_taps": conv_taps, "conv_bias": conv_bias, "step_bias": step_bias, "decay_rates": decay_rates, "skip_gain": skip_gain, "norm_gains": norm_gains, "ffn_gate": ffn_gate, "ffn_up": ffn_up, "ffn_down": ffn_down}


epsilon = 1e-06
highest = lax.Precision.HIGHEST

@jax.custom_vjp
def low(v):
    return lax.optimization_barrier(v.astype(jnp.bfloat16)).astype(jnp.float32)

@jax.custom_vjp
def low_back(v):
    return v

def low_keep(v):
    return (low(v), None)

def low_pass(kept, grad):
    return (grad,)

def back_keep(v):
    return (v, None)

def back_low(kept, grad):
    return (low(grad),)
low.defvjp(low_keep, low_pass)
low_back.defvjp(back_keep, back_low)

def product(left, right):
    return jnp.dot(left, right, precision=highest, preferred_element_type=jnp.float32)

def rms_scale(values, scale_row):
    return values * lax.rsqrt(lax.optimization_barrier(jnp.mean(values * values, axis=-1, keepdims=True)) + epsilon) * scale_row

def segment_ids(lengths, row_count):
    seq_ends = jnp.cumsum(lengths).astype(jnp.int32)
    places = jnp.arange(row_count, dtype=jnp.int32)
    return lax.optimization_barrier(jnp.sum((places[:, None] >= seq_ends[None, :]).astype(jnp.int32), axis=1))

def keep_flags(segments):
    same_seq = (segments[1:] == segments[:-1]).astype(jnp.float32)
    return jnp.concatenate([jnp.zeros((1,), jnp.float32), same_seq])

def conv_silu(inner_rows, tap_matrix, conv_shift, segments):
    tap_count = tap_matrix.shape[0]
    summed = conv_shift[None, :] + tap_matrix[tap_count - 1][None, :] * inner_rows
    for offset in range(1, tap_count):
        shifted = jnp.concatenate([jnp.zeros((offset, inner_rows.shape[1]), jnp.float32), inner_rows[:-offset]], axis=0)
        earlier = jnp.concatenate([jnp.full((offset,), -1, jnp.int32), segments[:-offset]])
        same_seq = (earlier == segments).astype(jnp.float32)
        summed = summed + tap_matrix[tap_count - 1 - offset][None, :] * shifted * same_seq[:, None]
    return jax.nn.silu(summed)

def scan_block(state_now, decay_matrix, block_data):
    step_sizes, step_inputs, step_b, step_c, step_keep = block_data
    outputs = []
    for step_index in range(step_sizes.shape[0]):
        decay_now = jnp.exp(-step_sizes[step_index][None, :] * decay_matrix)
        state_now = step_keep[step_index] * decay_now * state_now + step_b[step_index][:, None] * (step_sizes[step_index] * step_inputs[step_index])[None, :]
        outputs.append(lax.optimization_barrier(jnp.sum(step_c[step_index][:, None] * state_now, axis=0)))
    return (state_now, jnp.stack(outputs))

def selective_scan(step_sizes, step_inputs, b_rows, c_rows, keep_rows, decay_matrix):
    block_len = 16

    def advance(state_now, block_data):
        return jax.checkpoint(scan_block)(state_now, decay_matrix, block_data)
    blocks = tuple((piece_array.reshape((-1, block_len) + piece_array.shape[1:]) for piece_array in (step_sizes, step_inputs, b_rows, c_rows, keep_rows)))
    start_state = jnp.zeros((b_rows.shape[1], step_inputs.shape[1]), jnp.float32)
    final_state, outputs = lax.scan(advance, start_state, blocks)
    return outputs.reshape(step_inputs.shape)

def mamba_core(conv_act, select_rows, step_pre, gate_in, step_shift, decay_matrix, skip_row, keep_rows):
    step_sizes = jax.nn.softplus(step_pre + step_shift)
    scanned = selective_scan(step_sizes, conv_act, select_rows[:, :STATE], select_rows[:, STATE:], keep_rows, decay_matrix)
    return (scanned + skip_row * conv_act) * jax.nn.silu(gate_in)

def join_branches(attn_rows, mamba_rows, attn_gain, mamba_gain):
    return 0.5 * (rms_scale(attn_rows, attn_gain) + rms_scale(mamba_rows, mamba_gain))

def swiglu(gate_rows, up_rows):
    return jax.nn.silu(gate_rows) * up_rows

def attend(queries, key_rows, value_rows, segments):
    row_count = queries.shape[0]
    block_rows = min(row_count, 512)
    places = jnp.arange(row_count, dtype=jnp.int32)

    def one_block(query_block, start):
        query_places = start + jnp.arange(block_rows, dtype=jnp.int32)
        query_segs = lax.dynamic_slice_in_dim(segments, start, block_rows)
        allowed = (query_segs[:, None] == segments[None, :]) & (places[None, :] <= query_places[:, None])
        scores = low_back(jnp.einsum('tgrd,ugd->grtu', query_block, key_rows, precision=highest) * HEAD ** (-0.5))
        scores = jnp.where(allowed[None, None], scores, -1e+30)
        weights = low(jax.nn.softmax(scores, axis=-1))
        return jnp.einsum('grtu,ugd->tgrd', weights, value_rows, precision=highest)
    query_blocks = queries.reshape((row_count // block_rows, block_rows) + queries.shape[1:])
    starts = jnp.arange(row_count // block_rows, dtype=jnp.int32) * block_rows
    outputs = lax.map(lambda block_item: jax.checkpoint(one_block)(block_item[0], block_item[1]), (query_blocks, starts))
    return outputs.reshape(row_count, -1)

def shaped(flat_list):
    return (flat_list[0].reshape(D, QKV), flat_list[1].reshape(D, 2 * INNER), flat_list[2].reshape(INNER, XPROJ), flat_list[3].reshape(RANK, INNER), flat_list[4].reshape(INNER, D), flat_list[5].reshape(D, D), flat_list[6].reshape(CONV, INNER), flat_list[7], flat_list[8], flat_list[9].reshape(STATE, INNER), flat_list[10], flat_list[11].reshape(4, D), flat_list[12].reshape(D, FF), flat_list[13].reshape(D, FF), flat_list[14].reshape(FF, D))

def layer(inputs, params, segments, live_rows, keep_rows):
    qkv_matrix, mamba_in_matrix, select_matrix, step_matrix, mamba_out_matrix, join_matrix, tap_matrix, conv_shift, step_shift, decay_matrix, skip_row, gain_rows, gate_matrix, up_matrix, down_matrix = params
    row_count = inputs.shape[0]
    normed = low(rms_scale(inputs, gain_rows[0]))
    qkv_rows = low(low_back(product(normed, qkv_matrix)))
    queries = qkv_rows[:, :D].reshape(row_count, KV_HEADS, HEADS // KV_HEADS, HEAD)
    key_rows = qkv_rows[:, D:D + KV_HEADS * HEAD].reshape(row_count, KV_HEADS, HEAD)
    value_rows = qkv_rows[:, D + KV_HEADS * HEAD:].reshape(row_count, KV_HEADS, HEAD)
    attn_rows = low_back(attend(queries, key_rows, value_rows, segments))
    mixed_in = low_back(product(normed, mamba_in_matrix))
    conv_act = conv_silu(mixed_in[:, :INNER], tap_matrix, conv_shift, segments)
    selected = low_back(product(low(conv_act), select_matrix))
    step_low = low(selected[:, :RANK])
    step_pre = low_back(product(step_low, step_matrix))
    gated = low(mamba_core(conv_act, selected[:, RANK:], step_pre, mixed_in[:, INNER:], step_shift, decay_matrix, skip_row, keep_rows))
    mamba_rows = low_back(product(gated, mamba_out_matrix))
    joined = low(join_branches(attn_rows, mamba_rows, gain_rows[1], gain_rows[2]))
    middle = inputs + low_back(product(joined, join_matrix))
    normed_two = low(rms_scale(middle, gain_rows[3]))
    gate_rows = low_back(product(normed_two, gate_matrix))
    up_rows = low_back(product(normed_two, up_matrix))
    activated = low(swiglu(gate_rows, up_rows))
    return (middle + low_back(product(activated, down_matrix))) * live_rows[:, None]

def reference(tokens, cotangent, seq_lengths, qkv_proj, mamba_in, select_proj, step_proj, mamba_out, join_out, conv_taps, conv_bias, step_bias, decay_rates, skip_gain, norm_gains, ffn_gate, ffn_up, ffn_down):
    flats = tuple((weight.astype(jnp.float32) for weight in (qkv_proj, mamba_in, select_proj, step_proj, mamba_out, join_out, conv_taps, conv_bias, step_bias, decay_rates, skip_gain, norm_gains, ffn_gate, ffn_up, ffn_down)))
    token_packs = tokens.astype(jnp.float32).reshape(N_FSDP, TOK_DEV, D)
    grad_packs = cotangent.astype(jnp.float32).reshape(N_FSDP, TOK_DEV, D)
    length_packs = seq_lengths.reshape(N_FSDP, SEQ_DEV)

    def one_pack(sums_so_far, pack):
        pack_tokens, pack_grad, pack_lengths = pack
        segments = segment_ids(pack_lengths, TOK_DEV)
        live_rows = (segments < SEQ_DEV).astype(jnp.float32)
        keep_rows = keep_flags(segments)

        def forward(inputs, weights):
            return layer(inputs, shaped(weights), segments, live_rows, keep_rows)
        outputs, pullback = jax.vjp(forward, pack_tokens, flats)
        input_grad, weight_grads = pullback(pack_grad)
        sums_so_far = tuple((running + grad_piece for running, grad_piece in zip(sums_so_far, weight_grads)))
        return (sums_so_far, (outputs.astype(jnp.bfloat16), input_grad))
    start_sums = tuple((jnp.zeros(weight.shape, jnp.float32) for weight in flats))
    weight_sums, (out_packs, input_packs) = lax.scan(one_pack, start_sums, (token_packs, grad_packs, length_packs))
    return (out_packs.reshape(TOKENS, D), input_packs.reshape(TOKENS, D), weight_sums[0], weight_sums[1], weight_sums[2], weight_sums[3], weight_sums[4], weight_sums[5], weight_sums[6], weight_sums[7], weight_sums[8], weight_sums[9], weight_sums[10], weight_sums[11], weight_sums[12], weight_sums[13], weight_sums[14])
```

```python
import functools

import jax
import jax.numpy as jnp
import numpy as np
from jax import lax
from jax.experimental import pallas as pl
from jax.experimental.pallas import tpu as pltpu
from jax.sharding import PartitionSpec as P

D = 1600
HEADS = 25
KV_HEADS = 5
HEAD = 64
INNER = 3200
STATE = 16
CONV = 4
RANK = 100
FF = 5504
QKV = 2240
XPROJ = 132


epsilon = 1e-06


def flat_product(left, right):
    return jnp.dot(left, right, preferred_element_type=jnp.float32)


def outer_sum(left, right):
    return lax.dot_general(
        left, right, (((0,), (0,)), ((), ())), preferred_element_type=jnp.float32
    )


def back_product(grad_rows, matrix):
    return lax.dot_general(
        grad_rows, matrix, (((1,), (1,)), ((), ())), preferred_element_type=jnp.float32
    )


def rms_scale(values, scale_row):
    return (
        values * lax.rsqrt(jnp.mean(values * values, axis=-1, keepdims=True) + epsilon) * scale_row
    )


def segment_ids(lengths, row_count):
    seq_ends = jnp.cumsum(lengths)
    places = jnp.arange(row_count, dtype=jnp.int32)
    return jnp.sum((places[:, None] >= seq_ends[None, :]).astype(jnp.int32), axis=1)


def keep_flags(segments):
    same_seq = (segments[1:] == segments[:-1]).astype(jnp.float32)
    return jnp.concatenate([jnp.zeros((1,), jnp.float32), same_seq])


def conv_silu(inner_rows, tap_matrix, conv_shift, segments):
    tap_count = tap_matrix.shape[0]
    summed = conv_shift[None, :] + tap_matrix[tap_count - 1][None, :] * inner_rows
    for offset in range(1, tap_count):
        shifted = jnp.concatenate(
            [jnp.zeros((offset, inner_rows.shape[1]), jnp.float32), inner_rows[:-offset]], axis=0
        )
        earlier = jnp.concatenate([jnp.full((offset,), -1, jnp.int32), segments[:-offset]])
        same_seq = (earlier == segments).astype(jnp.float32)
        summed = summed + tap_matrix[tap_count - 1 - offset][None, :] * shifted * same_seq[:, None]
    return jax.nn.silu(summed)


def scan_block(state_now, decay_matrix, block_data):
    step_sizes, step_inputs, step_b, step_c, step_keep = block_data
    outputs = []
    for step_index in range(step_sizes.shape[0]):
        decay_now = jnp.exp(-step_sizes[step_index][None, :] * decay_matrix)
        state_now = (
            step_keep[step_index] * decay_now * state_now
            + step_b[step_index][:, None]
            * (step_sizes[step_index] * step_inputs[step_index])[None, :]
        )
        outputs.append(jnp.sum(step_c[step_index][:, None] * state_now, axis=0))
    return (state_now, jnp.stack(outputs))


def selective_scan(step_sizes, step_inputs, b_rows, c_rows, keep_rows, decay_matrix):
    block_len = 16

    def advance(state_now, block_data):
        return jax.checkpoint(scan_block)(state_now, decay_matrix, block_data)

    blocks = tuple(
        (
            piece_array.reshape((-1, block_len) + piece_array.shape[1:])
            for piece_array in (step_sizes, step_inputs, b_rows, c_rows, keep_rows)
        )
    )
    start_state = jnp.zeros((b_rows.shape[1], step_inputs.shape[1]), jnp.float32)
    final_state, outputs = lax.scan(advance, start_state, blocks)
    return outputs.reshape(step_inputs.shape)


def mamba_core(
    conv_act, select_rows, step_pre, gate_in, step_shift, decay_matrix, skip_row, keep_rows
):
    step_sizes = jax.nn.softplus(step_pre + step_shift)
    scanned = selective_scan(
        step_sizes,
        conv_act,
        select_rows[:, :STATE],
        select_rows[:, STATE:],
        keep_rows,
        decay_matrix,
    )
    return (scanned + skip_row * conv_act) * jax.nn.silu(gate_in)


def join_branches(attn_rows, mamba_rows, attn_gain, mamba_gain):
    return 0.5 * (rms_scale(attn_rows, attn_gain) + rms_scale(mamba_rows, mamba_gain))


def swiglu(gate_rows, up_rows):
    return jax.nn.silu(gate_rows) * up_rows


def block_scores(query_block, start, key_rows, segments):
    block_rows = query_block.shape[0]
    places = jnp.arange(segments.shape[0], dtype=jnp.int32)
    query_places = start + jnp.arange(block_rows, dtype=jnp.int32)
    allowed = (segments[:, None] == segments[None, :]) & (places[None, :] <= query_places[:, None])
    scores = jnp.einsum(
        "tgrd,ugd->grtu", query_block, key_rows, preferred_element_type=jnp.float32
    ) * HEAD ** (-0.5)
    return jnp.where(allowed[None, None], scores, -1e30)


def attention_forward(queries, key_rows, value_rows, segments):
    row_count = queries.shape[0]
    block_rows = min(row_count, 512)
    query_blocks = queries.reshape((row_count // block_rows, block_rows) + queries.shape[1:])
    starts = jnp.arange(row_count // block_rows, dtype=jnp.int32) * block_rows

    def one_block(block_item):
        scores = block_scores(block_item[0], block_item[1], key_rows, segments)
        top_score = jnp.max(scores, axis=-1, keepdims=True)
        raised = jnp.exp(scores - top_score)
        exp_sum = jnp.sum(raised, axis=-1, keepdims=True)
        weights = (raised / exp_sum).astype(jnp.bfloat16)
        outputs = jnp.einsum(
            "grtu,ugd->tgrd", weights, value_rows, preferred_element_type=jnp.float32
        )
        return (outputs, top_score, exp_sum)

    outputs, top_scores, exp_sums = lax.map(one_block, (query_blocks, starts))
    return (outputs.reshape(row_count, -1), top_scores, exp_sums, query_blocks, starts)


def attention_backward(
    query_blocks, starts, key_rows, value_rows, segments, top_scores, exp_sums, out_grad
):
    row_count = key_rows.shape[0]
    grad_blocks = out_grad.reshape(query_blocks.shape)

    def one_block(carry_sums, block_item):
        key_acc, value_acc = carry_sums
        query_block, start, top_score, exp_sum, grad_block = block_item
        scores = block_scores(query_block, start, key_rows, segments)
        weights = jnp.exp(scores - top_score) / exp_sum
        weight_grad = jnp.einsum(
            "tgrd,ugd->grtu", grad_block, value_rows, preferred_element_type=jnp.float32
        )
        score_grad = (
            weights * (weight_grad - jnp.sum(weights * weight_grad, axis=-1, keepdims=True))
        ).astype(jnp.bfloat16)
        query_grad = jnp.einsum(
            "grtu,ugd->tgrd", score_grad, key_rows, preferred_element_type=jnp.float32
        ) * HEAD ** (-0.5)
        key_acc = key_acc + jnp.einsum(
            "grtu,tgrd->ugd", score_grad, query_block, preferred_element_type=jnp.float32
        ) * HEAD ** (-0.5)
        value_acc = value_acc + jnp.einsum(
            "grtu,tgrd->ugd",
            weights.astype(jnp.bfloat16),
            grad_block,
            preferred_element_type=jnp.float32,
        )
        return ((key_acc, value_acc), query_grad)

    zero_rows = jnp.zeros(key_rows.shape, jnp.float32)
    (key_grad, value_grad), query_grads = lax.scan(
        one_block, (zero_rows, zero_rows), (query_blocks, starts, top_scores, exp_sums, grad_blocks)
    )
    return (
        query_grads.reshape(row_count, -1),
        key_grad.reshape(row_count, -1),
        value_grad.reshape(row_count, -1),
    )


def shape_mixer(flat_list):
    return (
        flat_list[0].reshape(D, QKV),
        flat_list[1].reshape(D, 2 * INNER),
        flat_list[2].reshape(INNER, XPROJ),
        flat_list[3].reshape(RANK, INNER),
        flat_list[4].reshape(INNER, D),
        flat_list[5].reshape(D, D),
    )


def small_mixer(flat_list):
    return (
        flat_list[6].astype(jnp.float32).reshape(CONV, INNER),
        flat_list[7].astype(jnp.float32),
        flat_list[8].astype(jnp.float32),
        flat_list[9].astype(jnp.float32).reshape(STATE, INNER),
        flat_list[10].astype(jnp.float32),
        flat_list[11].astype(jnp.float32).reshape(4, D),
    )


def shape_ffn(flat_list):
    return (flat_list[0].reshape(D, FF), flat_list[1].reshape(D, FF), flat_list[2].reshape(FF, D))


def on_device(
    tokens,
    cotangent,
    seq_lengths,
    qkv_proj,
    mamba_in,
    select_proj,
    step_proj,
    mamba_out,
    join_out,
    conv_taps,
    conv_bias,
    step_bias,
    decay_rates,
    skip_gain,
    norm_gains,
    ffn_gate,
    ffn_up,
    ffn_down,
):
    mixer_flat = (
        lax.all_gather(qkv_proj, "fsdp", axis=0, tiled=True),
        lax.all_gather(mamba_in, "fsdp", axis=0, tiled=True),
        lax.all_gather(select_proj, "fsdp", axis=0, tiled=True),
        lax.all_gather(step_proj, "fsdp", axis=0, tiled=True),
        lax.all_gather(mamba_out, "fsdp", axis=0, tiled=True),
        lax.all_gather(join_out, "fsdp", axis=0, tiled=True),
        lax.all_gather(conv_taps, "fsdp", axis=0, tiled=True),
        lax.all_gather(conv_bias, "fsdp", axis=0, tiled=True),
        lax.all_gather(step_bias, "fsdp", axis=0, tiled=True),
        lax.all_gather(decay_rates, "fsdp", axis=0, tiled=True),
        lax.all_gather(skip_gain, "fsdp", axis=0, tiled=True),
        lax.all_gather(norm_gains, "fsdp", axis=0, tiled=True),
    )
    ffn_flat = (
        lax.all_gather(ffn_gate, "fsdp", axis=0, tiled=True),
        lax.all_gather(ffn_up, "fsdp", axis=0, tiled=True),
        lax.all_gather(ffn_down, "fsdp", axis=0, tiled=True),
    )
    qkv_matrix, mamba_in_matrix, select_matrix, step_matrix, mamba_out_matrix, join_matrix = (
        shape_mixer(mixer_flat)
    )
    tap_matrix, conv_shift, step_shift, decay_matrix, skip_row, gain_rows = small_mixer(mixer_flat)
    gate_matrix, up_matrix, down_matrix = shape_ffn(ffn_flat)
    row_count = tokens.shape[0]
    segments = segment_ids(seq_lengths, row_count)
    live_rows = (segments < seq_lengths.shape[0]).astype(jnp.float32)
    keep_rows = keep_flags(segments)
    inputs = tokens.astype(jnp.float32)
    normed_full, norm_pull = jax.vjp(rms_scale, inputs, gain_rows[0])
    normed = normed_full.astype(jnp.bfloat16)
    qkv_rows = flat_product(normed, qkv_matrix).astype(jnp.bfloat16)
    queries = qkv_rows[:, :D].reshape(row_count, KV_HEADS, HEADS // KV_HEADS, HEAD)
    key_rows = qkv_rows[:, D : D + KV_HEADS * HEAD].reshape(row_count, KV_HEADS, HEAD)
    value_rows = qkv_rows[:, D + KV_HEADS * HEAD :].reshape(row_count, KV_HEADS, HEAD)
    attn_rows, top_scores, exp_sums, query_blocks, starts = attention_forward(
        queries, key_rows, value_rows, segments
    )
    mixed_in = flat_product(normed, mamba_in_matrix)

    def conv_piece(inner_rows, tap_values, shift_values):
        return conv_silu(inner_rows, tap_values, shift_values, segments)

    conv_act, conv_pull = jax.vjp(conv_piece, mixed_in[:, :INNER], tap_matrix, conv_shift)
    conv_low = conv_act.astype(jnp.bfloat16)
    selected = flat_product(conv_low, select_matrix)
    step_low = selected[:, :RANK].astype(jnp.bfloat16)
    step_pre = flat_product(step_low, step_matrix)

    def core_piece(
        conv_values,
        select_values,
        step_values,
        gate_values,
        shift_values,
        decay_values,
        skip_values,
    ):
        return mamba_core(
            conv_values,
            select_values,
            step_values,
            gate_values,
            shift_values,
            decay_values,
            skip_values,
            keep_rows,
        )

    gated_full, core_pull = jax.vjp(
        core_piece,
        conv_act,
        selected[:, RANK:],
        step_pre,
        mixed_in[:, INNER:],
        step_shift,
        decay_matrix,
        skip_row,
    )
    gated = gated_full.astype(jnp.bfloat16)
    mamba_rows = flat_product(gated, mamba_out_matrix)
    joined_full, join_pull = jax.vjp(
        join_branches, attn_rows, mamba_rows, gain_rows[1], gain_rows[2]
    )
    joined = joined_full.astype(jnp.bfloat16)
    middle = inputs + flat_product(joined, join_matrix)
    normed_two_full, norm_two_pull = jax.vjp(rms_scale, middle, gain_rows[3])
    normed_two = normed_two_full.astype(jnp.bfloat16)
    gate_rows = flat_product(normed_two, gate_matrix)
    up_rows = flat_product(normed_two, up_matrix)
    act_full, act_pull = jax.vjp(swiglu, gate_rows, up_rows)
    activated = act_full.astype(jnp.bfloat16)
    result_rows = middle + flat_product(activated, down_matrix)
    block_out = (result_rows * live_rows[:, None]).astype(jnp.bfloat16)
    ffn_flat = (
        lax.all_gather(ffn_gate, "fsdp", axis=0, tiled=True),
        lax.all_gather(ffn_up, "fsdp", axis=0, tiled=True),
        lax.all_gather(ffn_down, "fsdp", axis=0, tiled=True),
    )
    gate_matrix, up_matrix, down_matrix = shape_ffn(ffn_flat)
    out_grad = cotangent.astype(jnp.float32) * live_rows[:, None]
    down_low = out_grad.astype(jnp.bfloat16)
    down_weight_grad = outer_sum(activated, down_low)
    gate_grad, up_grad = act_pull(back_product(down_low, down_matrix))
    gate_low = gate_grad.astype(jnp.bfloat16)
    up_low = up_grad.astype(jnp.bfloat16)
    gate_weight_grad = outer_sum(normed_two, gate_low)
    up_weight_grad = outer_sum(normed_two, up_low)
    middle_norm_grad, ffn_gain_grad = norm_two_pull(
        back_product(gate_low, gate_matrix) + back_product(up_low, up_matrix)
    )
    middle_grad = out_grad + middle_norm_grad
    ffn_sums = (
        lax.psum_scatter(gate_weight_grad.reshape(-1), "fsdp", scatter_dimension=0, tiled=True),
        lax.psum_scatter(up_weight_grad.reshape(-1), "fsdp", scatter_dimension=0, tiled=True),
        lax.psum_scatter(down_weight_grad.reshape(-1), "fsdp", scatter_dimension=0, tiled=True),
    )
    mixer_flat = (
        lax.all_gather(qkv_proj, "fsdp", axis=0, tiled=True),
        lax.all_gather(mamba_in, "fsdp", axis=0, tiled=True),
        lax.all_gather(select_proj, "fsdp", axis=0, tiled=True),
        lax.all_gather(step_proj, "fsdp", axis=0, tiled=True),
        lax.all_gather(mamba_out, "fsdp", axis=0, tiled=True),
        lax.all_gather(join_out, "fsdp", axis=0, tiled=True),
        lax.all_gather(conv_taps, "fsdp", axis=0, tiled=True),
        lax.all_gather(conv_bias, "fsdp", axis=0, tiled=True),
        lax.all_gather(step_bias, "fsdp", axis=0, tiled=True),
        lax.all_gather(decay_rates, "fsdp", axis=0, tiled=True),
        lax.all_gather(skip_gain, "fsdp", axis=0, tiled=True),
        lax.all_gather(norm_gains, "fsdp", axis=0, tiled=True),
    )
    qkv_matrix, mamba_in_matrix, select_matrix, step_matrix, mamba_out_matrix, join_matrix = (
        shape_mixer(mixer_flat)
    )
    join_low = middle_grad.astype(jnp.bfloat16)
    join_weight_grad = outer_sum(joined, join_low)
    attn_grad, mamba_grad, attn_gain_grad, mamba_gain_grad = join_pull(
        back_product(join_low, join_matrix)
    )
    mamba_low = mamba_grad.astype(jnp.bfloat16)
    mamba_out_weight_grad = outer_sum(gated, mamba_low)
    (
        conv_core_grad,
        select_part_grad,
        step_pre_grad,
        gate_in_grad,
        step_shift_grad,
        decay_grad,
        skip_grad,
    ) = core_pull(back_product(mamba_low, mamba_out_matrix))
    step_low_grad = step_pre_grad.astype(jnp.bfloat16)
    step_weight_grad = outer_sum(step_low, step_low_grad)
    select_low = jnp.concatenate(
        [back_product(step_low_grad, step_matrix), select_part_grad], axis=1
    ).astype(jnp.bfloat16)
    select_weight_grad = outer_sum(conv_low, select_low)
    conv_grad = conv_core_grad + back_product(select_low, select_matrix)
    conv_in_grad, taps_grad, conv_shift_grad = conv_pull(conv_grad)
    mixed_low = jnp.concatenate([conv_in_grad, gate_in_grad], axis=1).astype(jnp.bfloat16)
    mamba_in_weight_grad = outer_sum(normed, mixed_low)
    query_grad, key_grad, value_grad = attention_backward(
        query_blocks,
        starts,
        key_rows,
        value_rows,
        segments,
        top_scores,
        exp_sums,
        attn_grad.astype(jnp.bfloat16),
    )
    qkv_low = jnp.concatenate([query_grad, key_grad, value_grad], axis=1).astype(jnp.bfloat16)
    qkv_weight_grad = outer_sum(normed, qkv_low)
    normed_grad = back_product(qkv_low, qkv_matrix) + back_product(mixed_low, mamba_in_matrix)
    input_norm_grad, input_gain_grad = norm_pull(normed_grad)
    input_grad = middle_grad + input_norm_grad
    gain_grads = jnp.stack(
        [input_gain_grad, attn_gain_grad, mamba_gain_grad, ffn_gain_grad]
    ).reshape(-1)
    mixer_sums = (
        lax.psum_scatter(qkv_weight_grad.reshape(-1), "fsdp", scatter_dimension=0, tiled=True),
        lax.psum_scatter(mamba_in_weight_grad.reshape(-1), "fsdp", scatter_dimension=0, tiled=True),
        lax.psum_scatter(select_weight_grad.reshape(-1), "fsdp", scatter_dimension=0, tiled=True),
        lax.psum_scatter(step_weight_grad.reshape(-1), "fsdp", scatter_dimension=0, tiled=True),
        lax.psum_scatter(
            mamba_out_weight_grad.reshape(-1), "fsdp", scatter_dimension=0, tiled=True
        ),
        lax.psum_scatter(join_weight_grad.reshape(-1), "fsdp", scatter_dimension=0, tiled=True),
        lax.psum_scatter(taps_grad.reshape(-1), "fsdp", scatter_dimension=0, tiled=True),
        lax.psum_scatter(conv_shift_grad, "fsdp", scatter_dimension=0, tiled=True),
        lax.psum_scatter(step_shift_grad, "fsdp", scatter_dimension=0, tiled=True),
        lax.psum_scatter(decay_grad.reshape(-1), "fsdp", scatter_dimension=0, tiled=True),
        lax.psum_scatter(skip_grad, "fsdp", scatter_dimension=0, tiled=True),
        lax.psum_scatter(gain_grads, "fsdp", scatter_dimension=0, tiled=True),
    )
    return (block_out, input_grad) + tuple(mixer_sums) + tuple(ffn_sums)


PLANES = 4
CHIPS = 4
CORES = 2
PLANE_DEV = CHIPS * CORES
FAST_DEV = PLANES * PLANE_DEV
RING = (0, 1, 3, 2)
MAIN_D = 48
MAIN_I = 96
SLICE_FF = FF // FAST_DEV
PAD_FF = 176
WIDE = 2 * INNER + QKV
GU = 2 * PLANES * PAD_FF
MISC_ROWS = 416
GU_REST_ROWS = 32
LANES = 640
BIG = 1e30
LOG2E = 1.4426950408889634


def ring_place(k):
    return k + k // 2 - 2 * (k // 3)


def chip_pairs(step):
    pairs = []
    for d in range(FAST_DEV):
        z, v, c = d // PLANE_DEV, (d // CORES) % CHIPS, d % CORES
        w = RING[(RING.index(v) + step) % CHIPS]
        pairs.append((d, z * PLANE_DEV + w * CORES + c))
    return pairs


def plane_pairs(step):
    return [
        (d, RING[(RING.index(d // PLANE_DEV) + step) % PLANES] * PLANE_DEV + d % PLANE_DEV)
        for d in range(FAST_DEV)
    ]


CORE_PAIRS = [(d, d ^ 1) for d in range(FAST_DEV)]


def gather_kernel(names, *refs):
    count = len(names)
    ins, outs = refs[:count], refs[count : 2 * count]
    own_sem, z_send, z_recv, p_send, p_recv, c_send, c_recv, a_send, a_recv = refs[2 * count :]
    me = lax.axis_index("fsdp")
    z, v, c = me // PLANE_DEV, (me // CORES) % CHIPS, me % CORES
    zp, vp = ring_place(z), ring_place(v)
    mesh_id = pl.DeviceIdType.MESH

    def device(zz, vv, cc):
        return zz * PLANE_DEV + vv * CORES + cc

    def z_at(k):
        return ring_place((zp + k) % PLANES)

    def v_at(k):
        return ring_place((vp + k) % CHIPS)

    z_next, z_prev = device(z_at(1), v, c), device(z_at(3), v, c)
    right, left = device(z, v_at(1), c), device(z, v_at(3), c)
    partner = device(z, v, 1 - c)
    others = [(me // PLANE_DEV) * PLANE_DEV + (me % PLANE_DEV + k) % PLANE_DEV for k in range(1, PLANE_DEV)]

    barrier = pltpu.get_barrier_semaphore()
    greeted = others + [z_next, z_prev]
    for d in greeted:
        pl.semaphore_signal(barrier, inc=1, device_id=(d,), device_id_type=mesh_id)
    pl.semaphore_wait(barrier, len(greeted))

    def slot(name, zz, vv, cc):
        if name == "mamba_out":
            return (zz // 2) * 16 + cc * 8 + (zz % 2) * 4 + vv
        if name == "misc":
            return device(zz, vv, cc)
        return cc * 16 + zz * 4 + vv

    started = []

    def send(src, dst, ss, rs, target):
        copy = pltpu.make_async_remote_copy(
            src_ref=src, dst_ref=dst, send_sem=ss, recv_sem=rs, device_id=(target,), device_id_type=mesh_id
        )
        copy.start()
        started.append(copy)
        return copy

    full = [k for k, name in enumerate(names) if name in ("wide", "mamba_out", "join", "misc")]
    exchanged = [k for k, name in enumerate(names) if name in ("gu", "gu_rest")]
    down = names.index("down")

    own = []
    for k in full:
        own.append(pltpu.make_async_copy(ins[k], outs[k].at[slot(names[k], z, v, c)], own_sem.at[k]))
    for k in exchanged:
        own.append(pltpu.make_async_copy(ins[k].at[me % PLANE_DEV], outs[k].at[slot(names[k], z, v, c)], own_sem.at[k]))
    own.append(pltpu.make_async_copy(ins[down], outs[down].at[z], own_sem.at[down]))
    for copy in own:
        copy.start()

    z_copies, p_copies, c_copies, a_copies = {}, {}, {}, {}

    def core_send(k, event, src, zz, vv):
        c_copies[k, event] = send(
            src, outs[k].at[slot(names[k], zz, vv, c)], c_send.at[k, event], c_recv.at[k, event], partner
        )

    def hop(k, s):
        zz = z_at(4 - s) if s else z
        here = outs[k].at[slot(names[k], zz, v, c)]
        src = ins[k] if s == 0 else here
        if s < PLANES - 1:
            z_copies[k, s] = send(src, here, z_send.at[k, s], z_recv.at[k, s], z_next)
        p_copies[k, s] = send(src, here, p_send.at[k, s], p_recv.at[k, s], right)
        p_copies[k, 4 + s] = send(src, here, p_send.at[k, 4 + s], p_recv.at[k, 4 + s], left)
        core_send(k, s, src, zz, v)

    def near(k, s):
        zz = z_at(4 - s) if s else z
        for from_left, event in ((True, s), (False, 4 + s)):
            origin = v_at(3) if from_left else v_at(1)
            p_copies[k, event].wait_recv()
            block = outs[k].at[slot(names[k], zz, origin, c)]
            if from_left == (s < 2):
                p_copies[k, 8 + s] = send(
                    block, block, p_send.at[k, 8 + s], p_recv.at[k, 8 + s], right if from_left else left
                )
            core_send(k, 4 + event, block, zz, origin)

    def far(k, s):
        zz = z_at(4 - s) if s else z
        p_copies[k, 8 + s].wait_recv()
        core_send(k, 12 + s, outs[k].at[slot(names[k], zz, v_at(2), c)], zz, v_at(2))

    for k in full:
        hop(k, 0)
    for k in exchanged:
        for i, d in enumerate(others):
            a_copies[k, i] = send(
                ins[k].at[d % PLANE_DEV],
                outs[k].at[slot(names[k], z, v, c)],
                a_send.at[k, i],
                a_recv.at[k, i],
                d,
            )
    z_copies[down, 0] = send(ins[down], outs[down].at[z], z_send.at[down, 0], z_recv.at[down, 0], z_next)

    def plane_blocks(k, s):
        zz = z_at(4 - s) if s else z
        for half in range(CORES):
            group = outs[k].at[pl.ds(half * 16 + zz * 4, 4)]
            z_copies[k, 4 * half + s] = send(
                group, group, z_send.at[k, 4 * half + s], z_recv.at[k, 4 * half + s], z_next
            )

    for s in range(1, PLANES):
        for k in full:
            z_copies[k, s - 1].wait_recv()
            hop(k, s)
        if s == 1:
            for k in exchanged:
                own[names.index(names[k])].wait()
                for i in range(PLANE_DEV - 1):
                    a_copies[k, i].wait_recv()
                plane_blocks(k, 0)
        else:
            for k in exchanged:
                for half in range(CORES):
                    z_copies[k, 4 * half + s - 2].wait_recv()
                plane_blocks(k, s - 1)
        z_copies[down, s - 1].wait_recv()
        if s < PLANES - 1:
            zz = z_at(4 - s)
            z_copies[down, s] = send(
                outs[down].at[zz], outs[down].at[zz], z_send.at[down, s], z_recv.at[down, s], z_next
            )
        for k in full:
            near(k, s - 1)
            if s > 1:
                far(k, s - 2)
    for k in full:
        near(k, 3)
    for k in full:
        far(k, 2)
        far(k, 3)
    for k in exchanged:
        for half in range(CORES):
            z_copies[k, 4 * half + 2].wait_recv()
    for (k, event), copy in c_copies.items():
        copy.wait_recv()
    for copy in started:
        copy.wait_send()
    for i, copy in enumerate(own):
        if i < len(full) or i == len(own) - 1:
            copy.wait()


GATHERED = ("wide", "mamba_out", "join", "misc", "gu", "gu_rest", "down")


def gather_weights(blocks):
    count = len(GATHERED)
    shapes = []
    for name, block in zip(GATHERED, blocks):
        if name == "down":
            shapes.append((PLANES,) + block.shape)
        elif name in ("gu", "gu_rest"):
            shapes.append((FAST_DEV,) + block.shape[1:])
        else:
            shapes.append((FAST_DEV,) + block.shape)
    sem = pltpu.SemaphoreType.DMA
    return pl.pallas_call(
        functools.partial(gather_kernel, GATHERED),
        out_shape=[jax.ShapeDtypeStruct(shape, jnp.bfloat16) for shape in shapes],
        in_specs=[pl.BlockSpec(memory_space=pl.ANY)] * count,
        out_specs=[pl.BlockSpec(memory_space=pl.ANY)] * count,
        scratch_shapes=[
            sem((count,)),
            sem((count, 8)),
            sem((count, 8)),
            sem((count, 12)),
            sem((count, 12)),
            sem((count, 16)),
            sem((count, 16)),
            sem((count, 7)),
            sem((count, 7)),
        ],
        compiler_params=pltpu.CompilerParams(collective_id=0, has_side_effects=True),
        name="gather_weights",
    )(*blocks)


def scan_setup(pre, shift, conv, hold):
    step = jax.nn.softplus(pre + shift)
    return step, step + hold, step * conv


def tiled(block):
    return jnp.concatenate([block] * (LANES // 128), axis=1)


def folded(block):
    total = block[:, :128]
    for k in range(1, LANES // 128):
        total = total + block[:, 128 * k : 128 * (k + 1)]
    return total


def scan_forward_kernel(
    pre_ref, shift_ref, conv_ref, gate_ref, decay_ref, skip_ref, hold_ref, b_ref, c_ref,
    gated_ref, y_ref, decay_step, step_input,
):
    conv = conv_ref[...]
    _, decay_step[...], step_input[...] = scan_setup(pre_ref[...], shift_ref[...], conv, hold_ref[...])
    rates = decay_ref[...] * (-LOG2E)

    def eight(k, state):
        base = pl.multiple_of(k * 8, 8)
        steps = decay_step[pl.ds(base, 8), :]
        inputs = step_input[pl.ds(base, 8), :]
        rows = []
        for i in range(8):
            decay = jnp.exp2(steps[i : i + 1] * rates)
            state = decay * state + tiled(b_ref[base + i]) * inputs[i : i + 1]
            rows.append(jnp.sum(tiled(c_ref[base + i]) * state, axis=0, keepdims=True))
        y_ref[pl.ds(base, 8), :] = jnp.concatenate(rows, axis=0)
        return state

    lax.fori_loop(0, pre_ref.shape[0] // 8, eight, jnp.zeros((STATE, LANES), jnp.float32))
    gated_ref[...] = (
        (y_ref[...] + skip_ref[...] * conv) * jax.nn.silu(gate_ref[...])
    ).astype(jnp.bfloat16)


def scan_backward_kernel(
    pre_ref, shift_ref, conv_ref, gate_ref, decay_ref, skip_ref, hold_ref, b_ref, c_ref, y_ref, grad_ref,
    conv_grad_ref, pre_grad_ref, gate_grad_ref, b_grad_ref, c_grad_ref, decay_grad_ref, skip_grad_ref, shift_grad_ref,
    step_size, decay_step, step_input, y_grad, input_grad, step_grad, states, decays,
):
    rows_all = pre_ref.shape[0]
    conv = conv_ref[...]
    step_size[...], decay_step[...], step_input[...] = scan_setup(
        pre_ref[...], shift_ref[...], conv, hold_ref[...]
    )
    gate = gate_ref[...]
    grad = grad_ref[...]
    open_gate = 1.0 / (1.0 + jnp.exp(-gate))
    gate_grad_ref[...] = (
        grad * (y_ref[...] + skip_ref[...] * conv) * open_gate * (1.0 + gate * (1.0 - open_gate))
    )
    y_grad[...] = grad * gate * open_gate
    skip_grad_ref[...] = jnp.sum(y_grad[...] * conv, axis=0, keepdims=True)
    rates = decay_ref[...] * (-LOG2E)
    minus_decay = -decay_ref[...]
    states[0] = jnp.zeros((STATE, LANES), jnp.float32)

    def forward(k, state):
        base = pl.multiple_of(k * 8, 8)
        steps = decay_step[pl.ds(base, 8), :]
        inputs = step_input[pl.ds(base, 8), :]
        for i in range(8):
            decay = jnp.exp2(steps[i : i + 1] * rates)
            decays[base + i] = decay
            state = decay * state + tiled(b_ref[base + i]) * inputs[i : i + 1]
            states[base + i + 1] = state
        return state

    zeros = jnp.zeros((STATE, LANES), jnp.float32)
    lax.fori_loop(0, rows_all // 8, forward, zeros)
    first = pl.program_id(0) == 0

    @pl.when(first)
    def _():
        b_grad_ref[...] = jnp.zeros_like(b_grad_ref)
        c_grad_ref[...] = jnp.zeros_like(c_grad_ref)

    def backward(k, carry):
        state_grad, decay_grad = carry
        base = pl.multiple_of(rows_all - 8 - k * 8, 8)
        inputs = step_input[pl.ds(base, 8), :]
        sizes = step_size[pl.ds(base, 8), :]
        y_rows = y_grad[pl.ds(base, 8), :]
        input_rows, step_rows = [None] * 8, [None] * 8
        for i in range(7, -1, -1):
            t = base + i
            y_row = y_rows[i : i + 1]
            full = state_grad + tiled(c_ref[t]) * y_row
            c_grad_ref[t] += folded(states[t + 1] * y_row)
            b_grad_ref[t] += folded(full * inputs[i : i + 1])
            input_rows[i] = jnp.sum(tiled(b_ref[t]) * full, axis=0, keepdims=True)
            state_grad = decays[t] * full
            through = state_grad * states[t]
            step_rows[i] = jnp.sum(minus_decay * through, axis=0, keepdims=True)
            decay_grad = decay_grad - sizes[i : i + 1] * through
        input_grad[pl.ds(base, 8), :] = jnp.concatenate(input_rows, axis=0)
        step_grad[pl.ds(base, 8), :] = jnp.concatenate(step_rows, axis=0)
        return state_grad, decay_grad

    _, decay_grad = lax.fori_loop(0, rows_all // 8, backward, (zeros, zeros))
    decay_grad_ref[...] = decay_grad
    conv_grad_ref[...] = input_grad[...] * step_size[...] + skip_ref[...] * y_grad[...]
    shifted = pre_ref[...] + shift_ref[...]
    pre_grad = (step_grad[...] + input_grad[...] * conv) / (1.0 + jnp.exp(-shifted))
    pre_grad_ref[...] = pre_grad
    shift_grad_ref[...] = jnp.sum(pre_grad, axis=0, keepdims=True)


def scan_specs(rows):
    by_lane = pl.BlockSpec((rows, LANES), lambda k: (0, k))
    row = pl.BlockSpec((1, LANES), lambda k: (0, k))
    state = pl.BlockSpec((STATE, LANES), lambda k: (0, k))
    hold = pl.BlockSpec((rows, 1), lambda k: (0, 0))
    spread = pl.BlockSpec((rows, STATE, 128), lambda k: (0, 0, 0))
    return by_lane, row, state, hold, spread


def scan_forward(pre, shift, conv, mixed, decay, skip, hold, b_wide, c_wide):
    rows = pre.shape[0]
    by_lane, row, state, hold_spec, spread = scan_specs(rows)
    gate_spec = pl.BlockSpec((rows, LANES), lambda k: (0, k + INNER // LANES))
    return pl.pallas_call(
        scan_forward_kernel,
        grid=(INNER // LANES,),
        out_shape=[
            jax.ShapeDtypeStruct((rows, INNER), jnp.bfloat16),
            jax.ShapeDtypeStruct((rows, INNER), jnp.float32),
        ],
        in_specs=[by_lane, row, by_lane, gate_spec, state, row, hold_spec, spread, spread],
        out_specs=[by_lane, by_lane],
        scratch_shapes=[pltpu.VMEM((rows, LANES), jnp.float32)] * 2,
        compiler_params=pltpu.CompilerParams(vmem_limit_bytes=40 * 1024 * 1024),
        cost_estimate=pl.CostEstimate(flops=60_000_000, bytes_accessed=9_000_000, transcendentals=7_000_000),
        name="scan_forward",
    )(pre, shift, conv, mixed, decay, skip, hold, b_wide, c_wide)


def scan_backward(pre, shift, conv, mixed, decay, skip, hold, b_wide, c_wide, y, grad):
    rows = pre.shape[0]
    by_lane, row, state, hold_spec, spread = scan_specs(rows)
    gate_spec = pl.BlockSpec((rows, LANES), lambda k: (0, k + INNER // LANES))
    f32 = jnp.float32
    lane_scratch = pltpu.VMEM((rows, LANES), f32)
    return pl.pallas_call(
        scan_backward_kernel,
        grid=(INNER // LANES,),
        out_shape=[
            jax.ShapeDtypeStruct((rows, INNER), f32),
            jax.ShapeDtypeStruct((rows, INNER), f32),
            jax.ShapeDtypeStruct((rows, INNER), f32),
            jax.ShapeDtypeStruct((rows, STATE, 128), f32),
            jax.ShapeDtypeStruct((rows, STATE, 128), f32),
            jax.ShapeDtypeStruct((STATE, INNER), f32),
            jax.ShapeDtypeStruct((1, INNER), f32),
            jax.ShapeDtypeStruct((1, INNER), f32),
        ],
        in_specs=[by_lane, row, by_lane, gate_spec, state, row, hold_spec, spread, spread, by_lane, by_lane],
        out_specs=[by_lane, by_lane, by_lane, spread, spread, state, row, row],
        scratch_shapes=[lane_scratch] * 6
        + [pltpu.VMEM((rows + 1, STATE, LANES), f32), pltpu.VMEM((rows, STATE, LANES), f32)],
        compiler_params=pltpu.CompilerParams(vmem_limit_bytes=48 * 1024 * 1024),
        cost_estimate=pl.CostEstimate(flops=200_000_000, bytes_accessed=16_000_000, transcendentals=7_000_000),
        name="scan_backward",
    )(pre, shift, conv, mixed, decay, skip, hold, b_wide, c_wide, y, grad)


GROUP = HEADS // KV_HEADS


def group_scores(qkv_ref, seg_col_ref, seg_row_ref, g):
    rows = qkv_ref.shape[0]
    queries = jnp.concatenate(
        [qkv_ref[:, (g * GROUP + r) * HEAD : (g * GROUP + r + 1) * HEAD] for r in range(GROUP)], axis=0
    )
    keys = qkv_ref[:, D + g * HEAD : D + (g + 1) * HEAD]
    values = qkv_ref[:, D + (KV_HEADS + g) * HEAD : D + (KV_HEADS + g + 1) * HEAD]
    scores = back_product(queries, keys) * HEAD ** (-0.5)
    t = lax.broadcasted_iota(jnp.int32, (rows, rows), 0)
    u = lax.broadcasted_iota(jnp.int32, (rows, rows), 1)
    allowed = (seg_col_ref[...] == seg_row_ref[...]) & (u <= t)
    scores = jnp.where(jnp.concatenate([allowed] * GROUP, axis=0), scores, -1e30)
    raised = jnp.exp(scores - jnp.max(scores, axis=-1, keepdims=True))
    probs = raised / jnp.sum(raised, axis=-1, keepdims=True)
    return queries, keys, values, probs


def attention_forward_kernel(qkv_ref, seg_col_ref, seg_row_ref, out_ref):
    rows = qkv_ref.shape[0]
    for g in range(KV_HEADS):
        _, _, values, probs = group_scores(qkv_ref, seg_col_ref, seg_row_ref, g)
        mixed = flat_product(probs.astype(jnp.bfloat16), values)
        for r in range(GROUP):
            head = g * GROUP + r
            out_ref[:, head * HEAD : (head + 1) * HEAD] = mixed[r * rows : (r + 1) * rows]


def attention_backward_kernel(qkv_ref, seg_col_ref, seg_row_ref, grad_ref, low_ref):
    rows = qkv_ref.shape[0]
    bf16 = jnp.bfloat16
    for g in range(KV_HEADS):
        queries, keys, values, probs = group_scores(qkv_ref, seg_col_ref, seg_row_ref, g)
        grads = jnp.concatenate(
            [grad_ref[:, (g * GROUP + r) * HEAD : (g * GROUP + r + 1) * HEAD] for r in range(GROUP)], axis=0
        )
        prob_grad = back_product(grads, values)
        score_low = (
            probs * (prob_grad - jnp.sum(probs * prob_grad, axis=-1, keepdims=True))
        ).astype(bf16)
        query_grad = (flat_product(score_low, keys) * HEAD ** (-0.5)).astype(bf16)
        for r in range(GROUP):
            head = g * GROUP + r
            low_ref[:, head * HEAD : (head + 1) * HEAD] = query_grad[r * rows : (r + 1) * rows]
        key_grad = outer_sum(score_low, queries) * HEAD ** (-0.5)
        low_ref[:, D + g * HEAD : D + (g + 1) * HEAD] = key_grad.astype(bf16)
        value_grad = outer_sum(probs.astype(bf16), grads)
        low_ref[:, D + (KV_HEADS + g) * HEAD : D + (KV_HEADS + g + 1) * HEAD] = value_grad.astype(bf16)


def attention_call(kernel, out_shape, name, *operands):
    return pl.pallas_call(
        kernel,
        out_shape=out_shape,
        in_specs=[pl.BlockSpec(memory_space=pltpu.VMEM)] * len(operands),
        out_specs=pl.BlockSpec(memory_space=pltpu.VMEM),
        compiler_params=pltpu.CompilerParams(vmem_limit_bytes=32 * 1024 * 1024),
        cost_estimate=pl.CostEstimate(flops=200_000_000, bytes_accessed=3_000_000, transcendentals=400_000),
        name=name,
    )(*operands)


def spread_table(shard_rows, main_rows, shards):
    half = shards // CORES
    order = [k * CORES + c for c in range(CORES) for k in range(half)]
    main = [d * shard_rows + r for d in order for r in range(main_rows)]
    rest = [d * shard_rows + r for d in range(shards) for r in range(main_rows, shard_rows)]
    return np.asarray(main + rest, np.int32)


def spread_matrix(table):
    places = lax.broadcasted_iota(jnp.int32, (table.size, table.size), 0)
    return (places == jnp.asarray(table)[None, :]).astype(jnp.bfloat16)


def into_order(rows_low, matrix):
    return flat_product(rows_low, matrix).astype(jnp.bfloat16)


def out_of_order(rows_wide, matrix):
    high = rows_wide.astype(jnp.bfloat16)
    rest = (rows_wide - high.astype(jnp.float32)).astype(jnp.bfloat16)
    return back_product(high, matrix) + back_product(rest, matrix)


def pick(array, index, axis):
    return lax.dynamic_index_in_dim(array, index, axis, keepdims=False)


def plus(left, right):
    return (left.astype(jnp.float32) + right.astype(jnp.float32)).astype(jnp.bfloat16)


def shift_chip(rows, step):
    return lax.ppermute(rows, "fsdp", chip_pairs(step))


def shift_plane(rows, step):
    return lax.ppermute(rows, "fsdp", plane_pairs(step))


def swap_core(rows):
    return lax.ppermute(rows, "fsdp", CORE_PAIRS)


def plane_sum(parts, place):
    moving = pick(parts, ring_place((place + 3) % PLANES), 0)
    for k in (2, 1, 0):
        here = pick(parts, ring_place((place + k) % PLANES), 0)
        came = shift_plane(moving, 1)
        if k:
            moving = plus(here, came)
    return here.astype(jnp.float32) + came.astype(jnp.float32)


def chip_sum(parts, zp, vp):
    right, far, left, own = [pick(parts, ring_place((vp + k) % CHIPS), 1) for k in (1, 2, 3, 0)]
    from_left = shift_chip(far[:2], 1)
    from_right = shift_chip(far[2:], 3)
    low_left, high_right = shift_chip(right[2:], 1), shift_chip(left[:2], 3)
    high_left = shift_chip(plus(right[:2], from_left), 1)
    low_right = shift_chip(plus(left[2:], from_right), 3)
    f32 = jnp.float32
    first = own[:2].astype(f32) + high_left.astype(f32) + high_right.astype(f32)
    second = own[2:].astype(f32) + low_left.astype(f32) + low_right.astype(f32)
    total = jnp.concatenate([first, second], axis=0).astype(jnp.bfloat16)
    return plane_sum(total, zp)


def gather_plane(rows):
    half = rows.shape[0] // 2
    right, left = shift_chip(rows, 3), shift_chip(rows, 1)
    far = [shift_chip(right[:half], 3), shift_chip(left[half:], 1)]
    chips = jnp.concatenate([rows, right] + far + [left], axis=0)
    return jnp.concatenate([chips, swap_core(chips)], axis=0)


def scatter_plane(parts):
    rows = parts.shape[0] // PLANE_DEV
    half = rows // 2
    chips = plus(parts[: CHIPS * rows], swap_core(parts[CHIPS * rows :]))
    own, right, far, left = [chips[k * rows : (k + 1) * rows] for k in range(CHIPS)]
    from_left = shift_chip(far[:half], 1)
    from_right = shift_chip(far[half:], 3)
    right = jnp.concatenate([plus(right[:half], from_left), right[half:]], axis=0)
    left = jnp.concatenate([left[:half], plus(left[half:], from_right)], axis=0)
    came_left, came_right = shift_chip(right, 1), shift_chip(left, 3)
    return own.astype(jnp.float32) + came_left.astype(jnp.float32) + came_right.astype(jnp.float32)


def pair_rows(rows):
    return jnp.concatenate([rows, swap_core(rows)], axis=0)


def by_core(columns, core):
    half = columns.shape[1] // CORES
    low, high = columns[:, :half], columns[:, half:]
    keep = jnp.where(core == 0, low, high)
    give = jnp.where(core == 0, high, low)
    return jnp.concatenate([keep, swap_core(give)], axis=0)


def split_flat(block, sizes):
    pieces, at = [], 0
    for size in sizes:
        pieces.append(block[..., at : at + size])
        at += size
    return pieces


def on_fast_device(
    tokens, cotangent, seq_lengths, qkv_proj, mamba_in, select_proj, step_proj, mamba_out, join_out,
    conv_taps, conv_bias, step_bias, decay_rates, skip_gain, norm_gains, ffn_gate, ffn_up, ffn_down,
):
    bf16, f32 = jnp.bfloat16, jnp.float32
    n = FAST_DEV
    me = lax.axis_index("fsdp")
    zp, vp, core = ring_place(me // PLANE_DEV), ring_place((me // CORES) % CHIPS), me % CORES
    row_count = tokens.shape[0]
    d_rows, i_rows = D // n, INNER // n
    d_rest, i_rest = d_rows - MAIN_D, i_rows - MAIN_I

    wide = jnp.concatenate([mamba_in.reshape(d_rows, 2 * INNER), qkv_proj.reshape(d_rows, QKV)], axis=1)
    out_block = mamba_out.reshape(i_rows, D)
    join_block = join_out.reshape(d_rows, D)
    smalls = (select_proj, step_proj, conv_taps, conv_bias, step_bias, decay_rates, skip_gain, norm_gains)
    misc_sizes = [d_rest * WIDE, d_rest * D, i_rest * D] + [s.size for s in smalls]
    misc = jnp.concatenate(
        [wide[MAIN_D:].reshape(-1), join_block[MAIN_D:].reshape(-1), out_block[MAIN_I:].reshape(-1)] + list(smalls)
    )
    misc = jnp.pad(misc, (0, MISC_ROWS * 128 - misc.size)).reshape(MISC_ROWS, 128)

    def ff_columns(flat):
        block = flat.reshape(d_rows, PLANES, PLANE_DEV, SLICE_FF)
        block = jnp.pad(block, ((0, 0), (0, 0), (0, 0), (0, PAD_FF - SLICE_FF)))
        return block.transpose(2, 0, 1, 3).reshape(PLANE_DEV, d_rows, PLANES * PAD_FF)

    gu = jnp.concatenate([ff_columns(ffn_gate), ff_columns(ffn_up)], axis=2)
    gu_rest = gu[:, MAIN_D:].reshape(PLANE_DEV, d_rest * GU)
    gu_rest = jnp.pad(gu_rest, ((0, 0), (0, GU_REST_ROWS * 128 - d_rest * GU))).reshape(
        PLANE_DEV, GU_REST_ROWS, 128
    )
    down = jnp.pad(ffn_down.reshape(SLICE_FF, D), ((0, PAD_FF - SLICE_FF), (0, 0)))
    wide_all, out_all, join_all, misc_all, gu_all, gu_rest_all, down_all = gather_weights(
        (wide[:MAIN_D], out_block[:MAIN_I], join_block[:MAIN_D], misc, gu[:, :MAIN_D], gu_rest, down)
    )
    main_d, main_i = n * MAIN_D, n * MAIN_I // 2
    wide_main = wide_all.reshape(main_d, WIDE)
    join_main = join_all.reshape(main_d, D)
    out_main = out_all.reshape(2, main_i, D)
    pieces = split_flat(misc_all.reshape(n, MISC_ROWS * 128), misc_sizes)
    wide_rest = pieces[0].reshape(n * d_rest, WIDE)
    join_rest = pieces[1].reshape(n * d_rest, D)
    out_rest = pieces[2].reshape(2, n * i_rest // 2, D)
    select_matrix = pieces[3].reshape(INNER, XPROJ)
    step_matrix = pieces[4].reshape(RANK, INNER)
    tap_matrix = pieces[5].reshape(CONV, INNER).astype(f32)
    conv_shift = pieces[6].reshape(INNER).astype(f32)
    step_shift = pieces[7].reshape(1, INNER).astype(f32)
    decay_matrix = pieces[8].reshape(STATE, INNER).astype(f32)
    skip_row = pieces[9].reshape(1, INNER).astype(f32)
    gain_rows = pieces[10].reshape(4, D).astype(f32)
    gu_main = gu_all.reshape(main_d, GU)
    gu_rest_rows = gu_rest_all.reshape(CORES, n // CORES, GU_REST_ROWS * 128)[:, :, : d_rest * GU]
    gu_rest_rows = gu_rest_rows.transpose(1, 0, 2).reshape(n * d_rest, GU)
    down_matrix = down_all.reshape(PLANES * PAD_FF, D)

    order_d = spread_matrix(spread_table(d_rows, MAIN_D, n))
    order_i = spread_matrix(spread_table(i_rows, MAIN_I, n // 2))

    segments = segment_ids(seq_lengths, row_count)
    live_rows = (segments < seq_lengths.shape[0]).astype(f32)
    hold = ((1.0 - keep_flags(segments)) * BIG)[:, None]
    seg_col, seg_row = segments[:, None], segments[None, :]
    inputs = tokens.astype(f32)
    normed_full, norm_pull = jax.vjp(rms_scale, inputs, gain_rows[0])
    normed = into_order(normed_full.astype(bf16), order_d)
    mixed = flat_product(normed[:, :main_d], wide_main) + flat_product(normed[:, main_d:], wide_rest)
    qkv_rows = mixed[:, 2 * INNER :].astype(bf16)

    def conv_piece(inner_rows, tap_values, shift_values):
        return conv_silu(inner_rows, tap_values, shift_values, segments)

    conv_act, conv_pull = jax.vjp(conv_piece, mixed[:, :INNER], tap_matrix, conv_shift)
    conv_low = conv_act.astype(bf16)
    selected = flat_product(conv_low, select_matrix)
    step_low = selected[:, :RANK].astype(bf16)
    step_pre = flat_product(step_low, step_matrix)
    b_wide = jnp.broadcast_to(selected[:, RANK : RANK + STATE, None], (row_count, STATE, 128))
    c_wide = jnp.broadcast_to(selected[:, RANK + STATE :, None], (row_count, STATE, 128))
    scan_args = (step_pre, step_shift, conv_act, mixed, decay_matrix, skip_row, hold, b_wide, c_wide)
    gated, scanned = scan_forward(*scan_args)
    attn_rows = attention_call(
        attention_forward_kernel,
        jax.ShapeDtypeStruct((row_count, D), f32),
        "attention_forward",
        qkv_rows,
        seg_col,
        seg_row,
    )
    half_i = INNER // 2
    gated_halves = [into_order(gated[:, k * half_i : (k + 1) * half_i], order_i) for k in range(2)]
    mamba_rows = sum(
        flat_product(gated_halves[k][:, :main_i], out_main[k])
        + flat_product(gated_halves[k][:, main_i:], out_rest[k])
        for k in range(2)
    )
    joined_full, join_pull = jax.vjp(join_branches, attn_rows, mamba_rows, gain_rows[1], gain_rows[2])
    joined = into_order(joined_full.astype(bf16), order_d)
    middle = inputs + flat_product(joined[:, :main_d], join_main) + flat_product(joined[:, main_d:], join_rest)

    normed_two_full, norm_two_pull = jax.vjp(rms_scale, middle, gain_rows[3])
    out_grad = cotangent.astype(f32) * live_rows[:, None]
    out_low = gather_plane(out_grad.astype(bf16))
    normed_two = gather_plane(into_order(normed_two_full.astype(bf16), order_d))
    gu_rows = flat_product(normed_two[:, :main_d], gu_main) + flat_product(normed_two[:, main_d:], gu_rest_rows)
    act_full, act_pull = jax.vjp(swiglu, gu_rows[:, : GU // 2], gu_rows[:, GU // 2 :])
    activated = act_full.astype(bf16)
    ffn_part = flat_product(activated, down_matrix).astype(bf16)
    act_grad = back_product(out_low, down_matrix)
    gu_low = jnp.concatenate(act_pull(act_grad), axis=1).astype(bf16)
    normed_two_part = jnp.concatenate(
        [back_product(gu_low, gu_main), back_product(gu_low, gu_rest_rows)], axis=1
    ).astype(bf16)
    middle_norm_grad, ffn_gain_grad = norm_two_pull(out_of_order(scatter_plane(normed_two_part), order_d))
    block_out = ((middle + scatter_plane(ffn_part)) * live_rows[:, None]).astype(bf16)
    middle_grad = out_grad + middle_norm_grad

    down_grad = outer_sum(activated, out_low).astype(bf16).reshape(PLANES, PAD_FF, D)
    down_sum = plane_sum(down_grad, zp)[:SLICE_FF].reshape(-1)
    gu_grad = outer_sum(normed_two[:, :main_d], gu_low).astype(bf16).reshape(CORES, PLANES, CHIPS, MAIN_D, GU)
    gu_rest_grad = outer_sum(normed_two[:, main_d:], gu_low).astype(bf16).reshape(
        PLANES, PLANE_DEV, d_rest, GU
    )
    gu_sum = plane_sum(gu_grad.transpose(1, 2, 0, 3, 4).reshape(PLANES, PLANE_DEV, MAIN_D, GU), zp)
    gu_sum = jnp.concatenate([gu_sum, plane_sum(gu_rest_grad, zp)], axis=1).astype(bf16)
    planes = [[z * PLANE_DEV + p for p in range(PLANE_DEV)] for z in range(PLANES)]
    gu_sum = lax.all_to_all(gu_sum, "fsdp", 0, 0, axis_index_groups=planes, tiled=True)
    gu_sum = gu_sum.reshape(PLANE_DEV, d_rows, 2, PLANES, PAD_FF)[..., :SLICE_FF].transpose(2, 1, 3, 0, 4)
    gu_sum = gu_sum.astype(f32).reshape(2, -1)

    join_low = middle_grad.astype(bf16)
    joined_grad = jnp.concatenate([back_product(join_low, join_main), back_product(join_low, join_rest)], axis=1)
    attn_grad, mamba_grad, attn_gain_grad, mamba_gain_grad = join_pull(out_of_order(joined_grad, order_d))
    mamba_low = mamba_grad.astype(bf16)
    join_pair = pair_rows(join_low)
    join_weight = outer_sum(by_core(joined[:, :main_d], core), join_pair).astype(bf16)
    join_sum = chip_sum(join_weight.reshape(PLANES, CHIPS, MAIN_D, D), zp, vp)
    join_rest_grad = outer_sum(joined[:, main_d:], join_low)
    mamba_pair = pair_rows(mamba_low)
    out_weight = jnp.concatenate(
        [outer_sum(by_core(half[:, :main_i], core), mamba_pair).astype(bf16) for half in gated_halves], axis=0
    )
    out_sum = chip_sum(out_weight.reshape(PLANES, CHIPS, MAIN_I, D), zp, vp)
    out_rest_grad = jnp.concatenate([outer_sum(half[:, main_i:], mamba_low) for half in gated_halves], axis=0)

    gated_grad = jnp.concatenate(
        [
            out_of_order(
                jnp.concatenate([back_product(mamba_low, out_main[k]), back_product(mamba_low, out_rest[k])], axis=1),
                order_i,
            )
            for k in range(2)
        ],
        axis=1,
    )
    (
        conv_core_grad, step_pre_grad, gate_in_grad, b_grad, c_grad, decay_grad, skip_grad, step_shift_grad,
    ) = scan_backward(*scan_args, scanned, gated_grad)
    step_low_grad = step_pre_grad.astype(bf16)
    step_weight_grad = outer_sum(step_low, step_low_grad)
    select_low = jnp.concatenate(
        [back_product(step_low_grad, step_matrix), jnp.sum(b_grad, axis=2), jnp.sum(c_grad, axis=2)], axis=1
    ).astype(bf16)
    select_weight_grad = outer_sum(conv_low, select_low)
    conv_grad = conv_core_grad + back_product(select_low, select_matrix)
    conv_in_grad, taps_grad, conv_shift_grad = conv_pull(conv_grad)
    qkv_low = attention_call(
        attention_backward_kernel,
        jax.ShapeDtypeStruct((row_count, QKV), bf16),
        "attention_backward",
        qkv_rows,
        seg_col,
        seg_row,
        attn_grad.astype(bf16),
    )
    wide_low = jnp.concatenate([conv_in_grad.astype(bf16), gate_in_grad.astype(bf16), qkv_low], axis=1)
    wide_x, wide_pair = by_core(normed[:, :main_d], core), pair_rows(wide_low)
    wide_sums = []
    edges = (0, 2176, 4352, 6528, WIDE)
    for low, high in zip(edges[:-1], edges[1:]):
        part = outer_sum(wide_x, wide_pair[:, low:high]).astype(bf16)
        wide_sums.append(chip_sum(part.reshape(PLANES, CHIPS, MAIN_D, high - low), zp, vp))
    wide_sum = jnp.concatenate(wide_sums, axis=1)
    wide_rest_grad = outer_sum(normed[:, main_d:], wide_low)
    normed_grad = jnp.concatenate([back_product(wide_low, wide_main), back_product(wide_low, wide_rest)], axis=1)
    input_norm_grad, input_gain_grad = norm_pull(out_of_order(normed_grad, order_d))
    input_grad = middle_grad + input_norm_grad
    gain_grads = jnp.stack([input_gain_grad, attn_gain_grad, mamba_gain_grad, ffn_gain_grad])

    misc_grads = [
        wide_rest_grad, join_rest_grad, out_rest_grad, select_weight_grad, step_weight_grad, taps_grad,
        conv_shift_grad, step_shift_grad, decay_grad, skip_grad, gain_grads,
    ]
    misc_grad = jnp.concatenate([g.astype(bf16).reshape(n, -1) for g in misc_grads], axis=1)
    misc_grad = misc_grad.reshape(n // CORES, CORES, -1)
    misc_chip = plus(pick(misc_grad, core, 1), swap_core(pick(misc_grad, 1 - core, 1)))
    misc_sum = chip_sum(misc_chip.reshape(PLANES, CHIPS, -1), zp, vp)
    sums = split_flat(misc_sum, misc_sizes)
    wide_sum = jnp.concatenate([wide_sum, sums[0].reshape(d_rest, WIDE)], axis=0)
    join_sum = jnp.concatenate([join_sum, sums[1].reshape(d_rest, D)], axis=0)
    out_sum = jnp.concatenate([out_sum, sums[2].reshape(i_rest, D)], axis=0)
    return (
        block_out,
        input_grad,
        wide_sum[:, 2 * INNER :].reshape(-1),
        wide_sum[:, : 2 * INNER].reshape(-1),
        sums[3],
        sums[4],
        out_sum.reshape(-1),
        join_sum.reshape(-1),
    ) + tuple(sums[5:]) + (gu_sum[0], gu_sum[1], down_sum)


def fits_fast_plan(mesh):
    return mesh.shape["fsdp"] == FAST_DEV


def solution(mesh):
    rows, flat = P("fsdp", None), P("fsdp")
    return jax.shard_map(
        on_fast_device if fits_fast_plan(mesh) else on_device,
        mesh=mesh,
        in_specs=(rows, rows) + (flat,) * 16,
        out_specs=(rows, rows) + (flat,) * 15,
        check_vma=False,
    )
```

```python
import functools

import jax
import jax.numpy as jnp
import numpy as np
from jax import lax
from jax.experimental import pallas as pl
from jax.experimental.pallas import tpu as pltpu
from jax.sharding import PartitionSpec as P

D = 1600
HEADS = 25
KV_HEADS = 5
HEAD = 64
INNER = 3200
STATE = 16
CONV = 4
RANK = 100
FF = 5504
QKV = 2240
XPROJ = 132


epsilon = 1e-06


def flat_product(left, right):
    return jnp.dot(left, right, preferred_element_type=jnp.float32)


def outer_sum(left, right):
    return lax.dot_general(
        left, right, (((0,), (0,)), ((), ())), preferred_element_type=jnp.float32
    )


def back_product(grad_rows, matrix):
    return lax.dot_general(
        grad_rows, matrix, (((1,), (1,)), ((), ())), preferred_element_type=jnp.float32
    )


def rms_scale(values, scale_row):
    return (
        values * lax.rsqrt(jnp.mean(values * values, axis=-1, keepdims=True) + epsilon) * scale_row
    )


def segment_ids(lengths, row_count):
    seq_ends = jnp.cumsum(lengths)
    places = jnp.arange(row_count, dtype=jnp.int32)
    return jnp.sum((places[:, None] >= seq_ends[None, :]).astype(jnp.int32), axis=1)


def keep_flags(segments):
    same_seq = (segments[1:] == segments[:-1]).astype(jnp.float32)
    return jnp.concatenate([jnp.zeros((1,), jnp.float32), same_seq])


def conv_silu(inner_rows, tap_matrix, conv_shift, segments):
    tap_count = tap_matrix.shape[0]
    summed = conv_shift[None, :] + tap_matrix[tap_count - 1][None, :] * inner_rows
    for offset in range(1, tap_count):
        shifted = jnp.concatenate(
            [jnp.zeros((offset, inner_rows.shape[1]), jnp.float32), inner_rows[:-offset]], axis=0
        )
        earlier = jnp.concatenate([jnp.full((offset,), -1, jnp.int32), segments[:-offset]])
        same_seq = (earlier == segments).astype(jnp.float32)
        summed = summed + tap_matrix[tap_count - 1 - offset][None, :] * shifted * same_seq[:, None]
    return jax.nn.silu(summed)


def scan_block(state_now, decay_matrix, block_data):
    step_sizes, step_inputs, step_b, step_c, step_keep = block_data
    outputs = []
    for step_index in range(step_sizes.shape[0]):
        decay_now = jnp.exp(-step_sizes[step_index][None, :] * decay_matrix)
        state_now = (
            step_keep[step_index] * decay_now * state_now
            + step_b[step_index][:, None]
            * (step_sizes[step_index] * step_inputs[step_index])[None, :]
        )
        outputs.append(jnp.sum(step_c[step_index][:, None] * state_now, axis=0))
    return (state_now, jnp.stack(outputs))


def selective_scan(step_sizes, step_inputs, b_rows, c_rows, keep_rows, decay_matrix):
    block_len = 16

    def advance(state_now, block_data):
        return jax.checkpoint(scan_block)(state_now, decay_matrix, block_data)

    blocks = tuple(
        (
            piece_array.reshape((-1, block_len) + piece_array.shape[1:])
            for piece_array in (step_sizes, step_inputs, b_rows, c_rows, keep_rows)
        )
    )
    start_state = jnp.zeros((b_rows.shape[1], step_inputs.shape[1]), jnp.float32)
    final_state, outputs = lax.scan(advance, start_state, blocks)
    return outputs.reshape(step_inputs.shape)


def mamba_core(
    conv_act, select_rows, step_pre, gate_in, step_shift, decay_matrix, skip_row, keep_rows
):
    step_sizes = jax.nn.softplus(step_pre + step_shift)
    scanned = selective_scan(
        step_sizes,
        conv_act,
        select_rows[:, :STATE],
        select_rows[:, STATE:],
        keep_rows,
        decay_matrix,
    )
    return (scanned + skip_row * conv_act) * jax.nn.silu(gate_in)


def join_branches(attn_rows, mamba_rows, attn_gain, mamba_gain):
    return 0.5 * (rms_scale(attn_rows, attn_gain) + rms_scale(mamba_rows, mamba_gain))


def swiglu(gate_rows, up_rows):
    return jax.nn.silu(gate_rows) * up_rows


def block_scores(query_block, start, key_rows, segments):
    block_rows = query_block.shape[0]
    places = jnp.arange(segments.shape[0], dtype=jnp.int32)
    query_places = start + jnp.arange(block_rows, dtype=jnp.int32)
    allowed = (segments[:, None] == segments[None, :]) & (places[None, :] <= query_places[:, None])
    scores = jnp.einsum(
        "tgrd,ugd->grtu", query_block, key_rows, preferred_element_type=jnp.float32
    ) * HEAD ** (-0.5)
    return jnp.where(allowed[None, None], scores, -1e30)


def attention_forward(queries, key_rows, value_rows, segments):
    row_count = queries.shape[0]
    block_rows = min(row_count, 512)
    query_blocks = queries.reshape((row_count // block_rows, block_rows) + queries.shape[1:])
    starts = jnp.arange(row_count // block_rows, dtype=jnp.int32) * block_rows

    def one_block(block_item):
        scores = block_scores(block_item[0], block_item[1], key_rows, segments)
        top_score = jnp.max(scores, axis=-1, keepdims=True)
        raised = jnp.exp(scores - top_score)
        exp_sum = jnp.sum(raised, axis=-1, keepdims=True)
        weights = (raised / exp_sum).astype(jnp.bfloat16)
        outputs = jnp.einsum(
            "grtu,ugd->tgrd", weights, value_rows, preferred_element_type=jnp.float32
        )
        return (outputs, top_score, exp_sum)

    outputs, top_scores, exp_sums = lax.map(one_block, (query_blocks, starts))
    return (outputs.reshape(row_count, -1), top_scores, exp_sums, query_blocks, starts)


def attention_backward(
    query_blocks, starts, key_rows, value_rows, segments, top_scores, exp_sums, out_grad
):
    row_count = key_rows.shape[0]
    grad_blocks = out_grad.reshape(query_blocks.shape)

    def one_block(carry_sums, block_item):
        key_acc, value_acc = carry_sums
        query_block, start, top_score, exp_sum, grad_block = block_item
        scores = block_scores(query_block, start, key_rows, segments)
        weights = jnp.exp(scores - top_score) / exp_sum
        weight_grad = jnp.einsum(
            "tgrd,ugd->grtu", grad_block, value_rows, preferred_element_type=jnp.float32
        )
        score_grad = (
            weights * (weight_grad - jnp.sum(weights * weight_grad, axis=-1, keepdims=True))
        ).astype(jnp.bfloat16)
        query_grad = jnp.einsum(
            "grtu,ugd->tgrd", score_grad, key_rows, preferred_element_type=jnp.float32
        ) * HEAD ** (-0.5)
        key_acc = key_acc + jnp.einsum(
            "grtu,tgrd->ugd", score_grad, query_block, preferred_element_type=jnp.float32
        ) * HEAD ** (-0.5)
        value_acc = value_acc + jnp.einsum(
            "grtu,tgrd->ugd",
            weights.astype(jnp.bfloat16),
            grad_block,
            preferred_element_type=jnp.float32,
        )
        return ((key_acc, value_acc), query_grad)

    zero_rows = jnp.zeros(key_rows.shape, jnp.float32)
    (key_grad, value_grad), query_grads = lax.scan(
        one_block, (zero_rows, zero_rows), (query_blocks, starts, top_scores, exp_sums, grad_blocks)
    )
    return (
        query_grads.reshape(row_count, -1),
        key_grad.reshape(row_count, -1),
        value_grad.reshape(row_count, -1),
    )


def shape_mixer(flat_list):
    return (
        flat_list[0].reshape(D, QKV),
        flat_list[1].reshape(D, 2 * INNER),
        flat_list[2].reshape(INNER, XPROJ),
        flat_list[3].reshape(RANK, INNER),
        flat_list[4].reshape(INNER, D),
        flat_list[5].reshape(D, D),
    )


def small_mixer(flat_list):
    return (
        flat_list[6].astype(jnp.float32).reshape(CONV, INNER),
        flat_list[7].astype(jnp.float32),
        flat_list[8].astype(jnp.float32),
        flat_list[9].astype(jnp.float32).reshape(STATE, INNER),
        flat_list[10].astype(jnp.float32),
        flat_list[11].astype(jnp.float32).reshape(4, D),
    )


def shape_ffn(flat_list):
    return (flat_list[0].reshape(D, FF), flat_list[1].reshape(D, FF), flat_list[2].reshape(FF, D))


def on_device(
    tokens,
    cotangent,
    seq_lengths,
    qkv_proj,
    mamba_in,
    select_proj,
    step_proj,
    mamba_out,
    join_out,
    conv_taps,
    conv_bias,
    step_bias,
    decay_rates,
    skip_gain,
    norm_gains,
    ffn_gate,
    ffn_up,
    ffn_down,
):
    mixer_flat = (
        lax.all_gather(qkv_proj, "fsdp", axis=0, tiled=True),
        lax.all_gather(mamba_in, "fsdp", axis=0, tiled=True),
        lax.all_gather(select_proj, "fsdp", axis=0, tiled=True),
        lax.all_gather(step_proj, "fsdp", axis=0, tiled=True),
        lax.all_gather(mamba_out, "fsdp", axis=0, tiled=True),
        lax.all_gather(join_out, "fsdp", axis=0, tiled=True),
        lax.all_gather(conv_taps, "fsdp", axis=0, tiled=True),
        lax.all_gather(conv_bias, "fsdp", axis=0, tiled=True),
        lax.all_gather(step_bias, "fsdp", axis=0, tiled=True),
        lax.all_gather(decay_rates, "fsdp", axis=0, tiled=True),
        lax.all_gather(skip_gain, "fsdp", axis=0, tiled=True),
        lax.all_gather(norm_gains, "fsdp", axis=0, tiled=True),
    )
    ffn_flat = (
        lax.all_gather(ffn_gate, "fsdp", axis=0, tiled=True),
        lax.all_gather(ffn_up, "fsdp", axis=0, tiled=True),
        lax.all_gather(ffn_down, "fsdp", axis=0, tiled=True),
    )
    qkv_matrix, mamba_in_matrix, select_matrix, step_matrix, mamba_out_matrix, join_matrix = (
        shape_mixer(mixer_flat)
    )
    tap_matrix, conv_shift, step_shift, decay_matrix, skip_row, gain_rows = small_mixer(mixer_flat)
    gate_matrix, up_matrix, down_matrix = shape_ffn(ffn_flat)
    row_count = tokens.shape[0]
    segments = segment_ids(seq_lengths, row_count)
    live_rows = (segments < seq_lengths.shape[0]).astype(jnp.float32)
    keep_rows = keep_flags(segments)
    inputs = tokens.astype(jnp.float32)
    normed_full, norm_pull = jax.vjp(rms_scale, inputs, gain_rows[0])
    normed = normed_full.astype(jnp.bfloat16)
    qkv_rows = flat_product(normed, qkv_matrix).astype(jnp.bfloat16)
    queries = qkv_rows[:, :D].reshape(row_count, KV_HEADS, HEADS // KV_HEADS, HEAD)
    key_rows = qkv_rows[:, D : D + KV_HEADS * HEAD].reshape(row_count, KV_HEADS, HEAD)
    value_rows = qkv_rows[:, D + KV_HEADS * HEAD :].reshape(row_count, KV_HEADS, HEAD)
    attn_rows, top_scores, exp_sums, query_blocks, starts = attention_forward(
        queries, key_rows, value_rows, segments
    )
    mixed_in = flat_product(normed, mamba_in_matrix)

    def conv_piece(inner_rows, tap_values, shift_values):
        return conv_silu(inner_rows, tap_values, shift_values, segments)

    conv_act, conv_pull = jax.vjp(conv_piece, mixed_in[:, :INNER], tap_matrix, conv_shift)
    conv_low = conv_act.astype(jnp.bfloat16)
    selected = flat_product(conv_low, select_matrix)
    step_low = selected[:, :RANK].astype(jnp.bfloat16)
    step_pre = flat_product(step_low, step_matrix)

    def core_piece(
        conv_values,
        select_values,
        step_values,
        gate_values,
        shift_values,
        decay_values,
        skip_values,
    ):
        return mamba_core(
            conv_values,
            select_values,
            step_values,
            gate_values,
            shift_values,
            decay_values,
            skip_values,
            keep_rows,
        )

    gated_full, core_pull = jax.vjp(
        core_piece,
        conv_act,
        selected[:, RANK:],
        step_pre,
        mixed_in[:, INNER:],
        step_shift,
        decay_matrix,
        skip_row,
    )
    gated = gated_full.astype(jnp.bfloat16)
    mamba_rows = flat_product(gated, mamba_out_matrix)
    joined_full, join_pull = jax.vjp(
        join_branches, attn_rows, mamba_rows, gain_rows[1], gain_rows[2]
    )
    joined = joined_full.astype(jnp.bfloat16)
    middle = inputs + flat_product(joined, join_matrix)
    normed_two_full, norm_two_pull = jax.vjp(rms_scale, middle, gain_rows[3])
    normed_two = normed_two_full.astype(jnp.bfloat16)
    gate_rows = flat_product(normed_two, gate_matrix)
    up_rows = flat_product(normed_two, up_matrix)
    act_full, act_pull = jax.vjp(swiglu, gate_rows, up_rows)
    activated = act_full.astype(jnp.bfloat16)
    result_rows = middle + flat_product(activated, down_matrix)
    block_out = (result_rows * live_rows[:, None]).astype(jnp.bfloat16)
    ffn_flat = (
        lax.all_gather(ffn_gate, "fsdp", axis=0, tiled=True),
        lax.all_gather(ffn_up, "fsdp", axis=0, tiled=True),
        lax.all_gather(ffn_down, "fsdp", axis=0, tiled=True),
    )
    gate_matrix, up_matrix, down_matrix = shape_ffn(ffn_flat)
    out_grad = cotangent.astype(jnp.float32) * live_rows[:, None]
    down_low = out_grad.astype(jnp.bfloat16)
    down_weight_grad = outer_sum(activated, down_low)
    gate_grad, up_grad = act_pull(back_product(down_low, down_matrix))
    gate_low = gate_grad.astype(jnp.bfloat16)
    up_low = up_grad.astype(jnp.bfloat16)
    gate_weight_grad = outer_sum(normed_two, gate_low)
    up_weight_grad = outer_sum(normed_two, up_low)
    middle_norm_grad, ffn_gain_grad = norm_two_pull(
        back_product(gate_low, gate_matrix) + back_product(up_low, up_matrix)
    )
    middle_grad = out_grad + middle_norm_grad
    ffn_sums = (
        lax.psum_scatter(gate_weight_grad.reshape(-1), "fsdp", scatter_dimension=0, tiled=True),
        lax.psum_scatter(up_weight_grad.reshape(-1), "fsdp", scatter_dimension=0, tiled=True),
        lax.psum_scatter(down_weight_grad.reshape(-1), "fsdp", scatter_dimension=0, tiled=True),
    )
    mixer_flat = (
        lax.all_gather(qkv_proj, "fsdp", axis=0, tiled=True),
        lax.all_gather(mamba_in, "fsdp", axis=0, tiled=True),
        lax.all_gather(select_proj, "fsdp", axis=0, tiled=True),
        lax.all_gather(step_proj, "fsdp", axis=0, tiled=True),
        lax.all_gather(mamba_out, "fsdp", axis=0, tiled=True),
        lax.all_gather(join_out, "fsdp", axis=0, tiled=True),
        lax.all_gather(conv_taps, "fsdp", axis=0, tiled=True),
        lax.all_gather(conv_bias, "fsdp", axis=0, tiled=True),
        lax.all_gather(step_bias, "fsdp", axis=0, tiled=True),
        lax.all_gather(decay_rates, "fsdp", axis=0, tiled=True),
        lax.all_gather(skip_gain, "fsdp", axis=0, tiled=True),
        lax.all_gather(norm_gains, "fsdp", axis=0, tiled=True),
    )
    qkv_matrix, mamba_in_matrix, select_matrix, step_matrix, mamba_out_matrix, join_matrix = (
        shape_mixer(mixer_flat)
    )
    join_low = middle_grad.astype(jnp.bfloat16)
    join_weight_grad = outer_sum(joined, join_low)
    attn_grad, mamba_grad, attn_gain_grad, mamba_gain_grad = join_pull(
        back_product(join_low, join_matrix)
    )
    mamba_low = mamba_grad.astype(jnp.bfloat16)
    mamba_out_weight_grad = outer_sum(gated, mamba_low)
    (
        conv_core_grad,
        select_part_grad,
        step_pre_grad,
        gate_in_grad,
        step_shift_grad,
        decay_grad,
        skip_grad,
    ) = core_pull(back_product(mamba_low, mamba_out_matrix))
    step_low_grad = step_pre_grad.astype(jnp.bfloat16)
    step_weight_grad = outer_sum(step_low, step_low_grad)
    select_low = jnp.concatenate(
        [back_product(step_low_grad, step_matrix), select_part_grad], axis=1
    ).astype(jnp.bfloat16)
    select_weight_grad = outer_sum(conv_low, select_low)
    conv_grad = conv_core_grad + back_product(select_low, select_matrix)
    conv_in_grad, taps_grad, conv_shift_grad = conv_pull(conv_grad)
    mixed_low = jnp.concatenate([conv_in_grad, gate_in_grad], axis=1).astype(jnp.bfloat16)
    mamba_in_weight_grad = outer_sum(normed, mixed_low)
    query_grad, key_grad, value_grad = attention_backward(
        query_blocks,
        starts,
        key_rows,
        value_rows,
        segments,
        top_scores,
        exp_sums,
        attn_grad.astype(jnp.bfloat16),
    )
    qkv_low = jnp.concatenate([query_grad, key_grad, value_grad], axis=1).astype(jnp.bfloat16)
    qkv_weight_grad = outer_sum(normed, qkv_low)
    normed_grad = back_product(qkv_low, qkv_matrix) + back_product(mixed_low, mamba_in_matrix)
    input_norm_grad, input_gain_grad = norm_pull(normed_grad)
    input_grad = middle_grad + input_norm_grad
    gain_grads = jnp.stack(
        [input_gain_grad, attn_gain_grad, mamba_gain_grad, ffn_gain_grad]
    ).reshape(-1)
    mixer_sums = (
        lax.psum_scatter(qkv_weight_grad.reshape(-1), "fsdp", scatter_dimension=0, tiled=True),
        lax.psum_scatter(mamba_in_weight_grad.reshape(-1), "fsdp", scatter_dimension=0, tiled=True),
        lax.psum_scatter(select_weight_grad.reshape(-1), "fsdp", scatter_dimension=0, tiled=True),
        lax.psum_scatter(step_weight_grad.reshape(-1), "fsdp", scatter_dimension=0, tiled=True),
        lax.psum_scatter(
            mamba_out_weight_grad.reshape(-1), "fsdp", scatter_dimension=0, tiled=True
        ),
        lax.psum_scatter(join_weight_grad.reshape(-1), "fsdp", scatter_dimension=0, tiled=True),
        lax.psum_scatter(taps_grad.reshape(-1), "fsdp", scatter_dimension=0, tiled=True),
        lax.psum_scatter(conv_shift_grad, "fsdp", scatter_dimension=0, tiled=True),
        lax.psum_scatter(step_shift_grad, "fsdp", scatter_dimension=0, tiled=True),
        lax.psum_scatter(decay_grad.reshape(-1), "fsdp", scatter_dimension=0, tiled=True),
        lax.psum_scatter(skip_grad, "fsdp", scatter_dimension=0, tiled=True),
        lax.psum_scatter(gain_grads, "fsdp", scatter_dimension=0, tiled=True),
    )
    return (block_out, input_grad) + tuple(mixer_sums) + tuple(ffn_sums)


PLANES = 4
CHIPS = 4
CORES = 2
PLANE_DEV = CHIPS * CORES
FAST_DEV = PLANES * PLANE_DEV
RING = (0, 1, 3, 2)
MAIN_D = 48
MAIN_I = 96
SLICE_FF = FF // FAST_DEV
HALF_GU = 768
WIDE = 8704
GU = 2 * HALF_GU
REST_ROWS = 224
SMALL_ROWS = 208
LANES = 640
BIG = 1e30
LOG2E = 1.4426950408889634


def ring_place(k):
    return k + k // 2 - 2 * (k // 3)


def chip_pairs(step):
    pairs = []
    for d in range(FAST_DEV):
        z, v, c = d // PLANE_DEV, (d // CORES) % CHIPS, d % CORES
        w = RING[(RING.index(v) + step) % CHIPS]
        pairs.append((d, z * PLANE_DEV + w * CORES + c))
    return pairs


def plane_pairs(step):
    return [
        (d, RING[(RING.index(d // PLANE_DEV) + step) % PLANES] * PLANE_DEV + d % PLANE_DEV)
        for d in range(FAST_DEV)
    ]


CORE_PAIRS = [(d, d ^ 1) for d in range(FAST_DEV)]


def gather_kernel(names, *refs):
    count = len(names)
    ins, outs = refs[:count], refs[count : 2 * count]
    own_sem, z_send, z_recv, p_send, p_recv, c_send, c_recv = refs[2 * count :]
    me = lax.axis_index("fsdp")
    z, v, c = me // PLANE_DEV, (me // CORES) % CHIPS, me % CORES
    zp, vp = ring_place(z), ring_place(v)
    mesh_id = pl.DeviceIdType.MESH
    z_at = [ring_place((zp + k) % PLANES) for k in range(PLANES)]
    v_at = [ring_place((vp + k) % CHIPS) for k in range(CHIPS)]
    z_next = z_at[1] * PLANE_DEV + v * CORES + c
    z_prev = z_at[3] * PLANE_DEV + v * CORES + c
    right = z * PLANE_DEV + v_at[1] * CORES + c
    left = z * PLANE_DEV + v_at[3] * CORES + c
    partner = me + 1 - 2 * c

    barrier = pltpu.get_barrier_semaphore()
    greeted = (right, left, z_next, z_prev, partner)
    for d in greeted:
        pl.semaphore_signal(barrier, inc=1, device_id=(d,), device_id_type=mesh_id)
    pl.semaphore_wait(barrier, len(greeted))

    def block(k, back, chip):
        zz, vv = z_at[(PLANES - back) % PLANES], v_at[chip]
        if names[k] == "mamba_out":
            return outs[k].at[(zz // 2) * 16 + c * 8 + (zz % 2) * 4 + vv]
        if names[k] == "smalls":
            return outs[k].at[zz * PLANE_DEV + vv * CORES + c]
        return outs[k].at[c * 16 + zz * 4 + vv]

    started, z_copies, p_copies, c_copies = [], {}, {}, {}

    def send(src, dst, ss, rs, target):
        copy = pltpu.make_async_remote_copy(
            src_ref=src, dst_ref=dst, send_sem=ss, recv_sem=rs, device_id=(target,), device_id_type=mesh_id
        )
        copy.start()
        started.append(copy)
        return copy

    own = [pltpu.make_async_copy(ins[k], block(k, 0, 0), own_sem.at[k]) for k in range(count)]
    for copy in own:
        copy.start()

    def core_send(k, event, src, dst):
        c_copies[k, event] = send(src, dst, c_send.at[k, event], c_recv.at[k, event], partner)

    def hop(k, s):
        here = block(k, s, 0)
        src = here if s else ins[k]
        if s < PLANES - 1:
            z_copies[k, s] = send(src, here, z_send.at[k, s], z_recv.at[k, s], z_next)
        p_copies[k, s] = send(src, here, p_send.at[k, s], p_recv.at[k, s], right)
        p_copies[k, 4 + s] = send(src, here, p_send.at[k, 4 + s], p_recv.at[k, 4 + s], left)
        core_send(k, s, src, here)

    def near(k, s):
        for from_left, event in ((True, s), (False, 4 + s)):
            p_copies[k, event].wait_recv()
            here = block(k, s, 3 if from_left else 1)
            if from_left == (s < 2):
                p_copies[k, 8 + s] = send(
                    here, here, p_send.at[k, 8 + s], p_recv.at[k, 8 + s], right if from_left else left
                )
            core_send(k, 4 + event, here, here)

    def far(k, s):
        p_copies[k, 8 + s].wait_recv()
        here = block(k, s, 2)
        core_send(k, 12 + s, here, here)

    for k in range(count):
        hop(k, 0)
    for s in range(1, PLANES):
        for k in range(count):
            z_copies[k, s - 1].wait_recv()
            hop(k, s)
        for k in range(count):
            near(k, s - 1)
            if s > 1:
                far(k, s - 2)
    for k in range(count):
        near(k, 3)
    for k in range(count):
        far(k, 2)
        far(k, 3)
    for copy in c_copies.values():
        copy.wait_recv()
    for copy in started:
        copy.wait_send()
    for copy in own:
        copy.wait()


def gather_weights(collective, name, names, blocks):
    count = len(names)
    sem = pltpu.SemaphoreType.DMA
    return pl.pallas_call(
        functools.partial(gather_kernel, names),
        out_shape=[jax.ShapeDtypeStruct((FAST_DEV,) + block.shape, jnp.bfloat16) for block in blocks],
        in_specs=[pl.BlockSpec(memory_space=pl.ANY)] * count,
        out_specs=[pl.BlockSpec(memory_space=pl.ANY)] * count,
        scratch_shapes=[sem((count,))] + [sem((count, k)) for k in (3, 3, 12, 12, 16, 16)],
        compiler_params=pltpu.CompilerParams(collective_id=collective, has_side_effects=True),
        name=name,
    )(*blocks)


REST_COLUMNS = 1152
WIDE_BLOCKS = [(0, 7 * REST_COLUMNS, WIDE - 7 * REST_COLUMNS)] + [(0, k * REST_COLUMNS, REST_COLUMNS) for k in range(7)]
BRANCH_BLOCKS = [(0, 0, 768), (0, 768, 832), (1, 0, 768), (1, 768, 832)]
SUM_LAGS = (2, 3, 4, 5, 6)
GRAD_ROWS = 192
GROUPS = PLANES * CHIPS


def add_rows(target, *others):
    @pl.loop(0, target.shape[0] // 16)
    def _(k):
        rows = pl.ds(pl.multiple_of(k * 16, 16), 16)
        total = target[rows, :].astype(jnp.float32)
        for other in others:
            total = total + other[rows, :].astype(jnp.float32)
        target[rows, :] = total.astype(target.dtype)


def sum_kernel(blocks, rest_rows, has_smalls, *refs):
    pairs = len(rest_rows)
    refs = list(refs)

    def take(k):
        taken = refs[:k]
        del refs[:k]
        return taken

    columns_in, rests_in, lows_in, smalls_in = take(pairs), take(pairs), take(pairs), take(int(has_smalls))
    totals, rest_total, smalls_total = take(pairs), take(1)[0], take(int(has_smalls))
    columns_all, rests_all, lows_all = take(pairs), take(pairs), take(pairs)
    rest_stage, smalls_stage = take(1)[0], take(int(has_smalls))
    count = len(blocks) + 1 + int(has_smalls)
    partial, through, from_left, from_right, along = [take(count) for _ in range(5)]
    t_send, t_recv, s_send, s_recv, z_send, z_recv, c_send, c_recv, local = take(9)
    rest_at, smalls_at = len(blocks), len(blocks) + 1
    group_rows = [p.shape[0] // GROUPS for p in partial]

    me = lax.axis_index("fsdp")
    z, v, c = me // PLANE_DEV, (me // CORES) % CHIPS, me % CORES
    zp, vp = ring_place(z), ring_place(v)
    mesh_id = pl.DeviceIdType.MESH
    z_at = [ring_place((zp + k) % PLANES) for k in range(PLANES)]
    v_at = [ring_place((vp + k) % CHIPS) for k in range(CHIPS)]
    right = z * PLANE_DEV + v_at[1] * CORES + c
    left = z * PLANE_DEV + v_at[3] * CORES + c
    z_next = z_at[1] * PLANE_DEV + v * CORES + c
    z_prev = z_at[3] * PLANE_DEV + v * CORES + c
    partner = me + 1 - 2 * c

    barrier = pltpu.get_barrier_semaphore()
    greeted = (right, left, z_next, z_prev, partner)
    for d in greeted:
        pl.semaphore_signal(barrier, inc=1, device_id=(d,), device_id_type=mesh_id)
    pl.semaphore_wait(barrier, len(greeted))

    sent, own = [], []
    arriving = {}

    def send(key, src, dst, ss, rs, target):
        copy = pltpu.make_async_remote_copy(
            src_ref=src, dst_ref=dst, send_sem=ss, recv_sem=rs, device_id=(target,), device_id_type=mesh_id
        )
        copy.start()
        sent.append(copy)
        arriving[key] = copy

    def stay(src, dst, sem):
        copy = pltpu.make_async_copy(src, dst, sem)
        copy.start()
        own.append(copy)

    for k in range(pairs):
        rows = lows_in[k].shape[0]
        halves, gathered = columns_in[k].shape[0], columns_in[k].shape[1]
        half = gathered // CORES
        mine, other = pl.ds(0, rows), pl.ds(rows, rows)
        stay(lows_in[k], lows_all[k].at[mine], local.at[k, 0])
        send(("l", k), lows_in[k], lows_all[k].at[other], c_send.at[k, 0], c_recv.at[k, 0], partner)
        stay(rests_in[k].at[c], rests_all[k].at[:, mine], local.at[k, 1])
        send(("r", k), rests_in[k].at[1 - c], rests_all[k].at[:, other], c_send.at[k, 1], c_recv.at[k, 1], partner)
        for h in range(halves):
            place = pl.ds(h * half, half)
            stay(
                columns_in[k].at[h, pl.ds(pl.multiple_of(c * half, half), half)],
                columns_all[k].at[place, mine],
                local.at[k, 2 + h],
            )
            send(
                ("x", k, h),
                columns_in[k].at[h, pl.ds(pl.multiple_of((1 - c) * half, half), half)],
                columns_all[k].at[place, other],
                c_send.at[k, 2 + h],
                c_recv.at[k, 2 + h],
                partner,
            )
    if has_smalls:
        stay(smalls_in[0].at[c], partial[smalls_at], local.at[0, 4])
        send(("m",), smalls_in[0].at[1 - c], smalls_stage[0], c_send.at[0, 4], c_recv.at[0, 4], partner)
    for copy in own:
        copy.wait()
    for k in range(pairs):
        arriving["l", k].wait_recv()
        arriving["r", k].wait_recv()
        for h in range(columns_in[k].shape[0]):
            arriving["x", k, h].wait_recv()

    def rest_block():
        rest_stage[...] = jnp.zeros_like(rest_stage)
        row = 0
        for k in range(pairs):
            r, width = rest_rows[k], rest_stage.shape[1]
            for column in range(0, lows_all[k].shape[1], width):
                columns = min(width, lows_all[k].shape[1] - column)
                product = flat_product(rests_all[k][...], lows_all[k][:, column : column + columns])
                for g in range(GROUPS):
                    at = 16 * g + row
                    rest_stage[at : at + r, :columns] = product[g * r : (g + 1) * r]
                row += r
        partial[rest_at][...] = rest_stage[...].astype(jnp.bfloat16)

    def compute(i):
        if i == rest_at:
            rest_block()
            return
        if i == smalls_at:
            arriving["m",].wait_recv()
            add_rows(partial[i], smalls_stage[0])
            return
        pair, column, columns = blocks[i]

        @pl.loop(0, partial[i].shape[0] // GRAD_ROWS)
        def _(j):
            rows = pl.ds(pl.multiple_of(j * GRAD_ROWS, GRAD_ROWS), GRAD_ROWS)
            partial[i][rows, :] = flat_product(
                columns_all[pair][rows, :], lows_all[pair][:, pl.ds(column, columns)]
            ).astype(jnp.bfloat16)

    def part(i, k, chip):
        rows = group_rows[i]
        return partial[i].at[pl.ds(pl.multiple_of((z_at[k] * CHIPS + v_at[chip]) * rows, rows), rows)]

    def launch(i):
        compute(i)
        for k in (3, 2, 1, 0):
            far, direct = (right, left) if k % 2 else (left, right)
            send((i, "t", k), part(i, k, 2), through[i].at[k], t_send.at[i, k], t_recv.at[i, k], far)
            landing, event = (from_right, 4 + k) if k % 2 else (from_left, k)
            send(
                (i, "s", event), part(i, k, 3 if k % 2 else 1), landing[i].at[k],
                s_send.at[i, event], s_recv.at[i, event], direct,
            )

    def relay(i):
        for k in (3, 2, 1, 0):
            arriving[i, "t", k].wait_recv()
            add_rows(through[i].at[k], part(i, k, 1 if k % 2 else 3))
            far = right if k % 2 else left
            landing, event = (from_left, k) if k % 2 else (from_right, 4 + k)
            send(
                (i, "s", event), through[i].at[k], landing[i].at[k], s_send.at[i, event], s_recv.at[i, event], far
            )

    def pass_on(i, k):
        send((i, "z", 3 - k), part(i, k, 0), along[i].at[3 - k], z_send.at[i, 3 - k], z_recv.at[i, 3 - k], z_next)

    def collect(i):
        for k in (3, 2, 1, 0):
            arriving[i, "s", k].wait_recv()
            arriving[i, "s", 4 + k].wait_recv()
            add_rows(part(i, k, 0), from_left[i].at[k], from_right[i].at[k])
            if k == 3:
                pass_on(i, 3)

    def planes(i, k):
        arriving[i, "z", 2 - k].wait_recv()
        mine = part(i, k, 0)
        if k:
            add_rows(mine, along[i].at[2 - k])
            pass_on(i, k)
            return
        if i == rest_at:
            total, column, columns = rest_total, 0, rest_total.shape[1]
        elif i == smalls_at:
            total, column, columns = smalls_total[0], 0, smalls_total[0].shape[1]
        else:
            pair, column, columns = blocks[i]
            total = totals[pair]

        @pl.loop(0, group_rows[i] // 16)
        def _(j):
            rows = pl.ds(pl.multiple_of(j * 16, 16), 16)
            total[rows, pl.ds(column, columns)] = mine[rows, :].astype(jnp.float32) + along[i][2, rows, :].astype(
                jnp.float32
            )

    stages = (relay, collect, lambda i: planes(i, 2), lambda i: planes(i, 1), lambda i: planes(i, 0))
    order = list(range(len(blocks)))
    order = order[:2] + list(range(len(blocks), count)) + order[2:]
    for step in range(count + SUM_LAGS[-1]):
        if step < count:
            launch(order[step])
        for lag, stage in zip(SUM_LAGS, stages):
            if 0 <= step - lag < count:
                stage(order[step - lag])
    for copy in sent:
        copy.wait_send()


def sum_gradients(collective, name, blocks, shard_rows, rest_rows, rest_columns, columns, rests, lows, smalls=None):
    bf16, f32 = jnp.bfloat16, jnp.float32
    rows, has_smalls = lows[0].shape[0], smalls is not None
    vmem, anywhere = pl.BlockSpec(memory_space=pltpu.VMEM), pl.BlockSpec(memory_space=pl.ANY)
    out_shape = [jax.ShapeDtypeStruct((r, y.shape[1]), f32) for r, y in zip(shard_rows, lows)]
    out_shape.append(jax.ShapeDtypeStruct((16, rest_columns), f32))
    scratch = [pltpu.VMEM((x.shape[0] * x.shape[1] // CORES, CORES * rows), bf16) for x in columns]
    scratch += [pltpu.VMEM((x.shape[1], CORES * rows), bf16) for x in rests]
    scratch += [pltpu.VMEM((CORES * rows, y.shape[1]), bf16) for y in lows]
    scratch.append(pltpu.VMEM((16 * GROUPS, rest_columns), f32))
    shapes = [(shard_rows[pair], n) for pair, _, n in blocks] + [(16, rest_columns)]
    operands = list(columns) + list(rests) + list(lows)
    if has_smalls:
        shapes.append((smalls.shape[1] // GROUPS, smalls.shape[2]))
        scratch.append(pltpu.VMEM(smalls.shape[1:], bf16))
        out_shape.append(jax.ShapeDtypeStruct(shapes[-1], f32))
        operands.append(smalls)
    for copies in (0, 4, 4, 4, 3):
        for r, n in shapes:
            scratch.append(pltpu.VMEM((copies, r, n) if copies else (GROUPS * r, n), bf16))
    sem = pltpu.SemaphoreType.DMA
    count = len(shapes)
    scratch += [sem((count, k)) for k in (4, 4, 8, 8, 3, 3)] + [sem((len(lows), 5))] * 3
    return pl.pallas_call(
        functools.partial(sum_kernel, blocks, rest_rows, has_smalls),
        out_shape=out_shape,
        in_specs=[anywhere] * len(operands),
        out_specs=[vmem] * len(out_shape),
        scratch_shapes=scratch,
        compiler_params=pltpu.CompilerParams(
            collective_id=collective, has_side_effects=True, vmem_limit_bytes=58 * 1024 * 1024
        ),
        name=name,
    )(*operands)


def scan_setup(pre, shift, conv, hold):
    step = jax.nn.softplus(pre + shift)
    return step, step + hold, step * conv


def tiled(block):
    return jnp.concatenate([block] * (LANES // 128), axis=1)


def folded(block):
    total = block[:, :128]
    for k in range(1, LANES // 128):
        total = total + block[:, 128 * k : 128 * (k + 1)]
    return total


GROUP = HEADS // KV_HEADS


def group_scores(qkv_ref, seg_col_ref, seg_row_ref, g):
    rows = qkv_ref.shape[0]
    queries = jnp.concatenate(
        [qkv_ref[:, (g * GROUP + r) * HEAD : (g * GROUP + r + 1) * HEAD] for r in range(GROUP)], axis=0
    )
    keys = qkv_ref[:, D + g * HEAD : D + (g + 1) * HEAD]
    values = qkv_ref[:, D + (KV_HEADS + g) * HEAD : D + (KV_HEADS + g + 1) * HEAD]
    scores = back_product(queries, keys) * HEAD ** (-0.5)
    t = lax.broadcasted_iota(jnp.int32, (rows, rows), 0)
    u = lax.broadcasted_iota(jnp.int32, (rows, rows), 1)
    allowed = (seg_col_ref[...] == seg_row_ref[...]) & (u <= t)
    scores = jnp.where(jnp.concatenate([allowed] * GROUP, axis=0), scores, -1e30)
    raised = jnp.exp(scores - jnp.max(scores, axis=-1, keepdims=True))
    probs = raised / jnp.sum(raised, axis=-1, keepdims=True)
    return queries, keys, values, probs


def attention_forward_kernel(qkv_ref, seg_col_ref, seg_row_ref, out_ref):
    rows = qkv_ref.shape[0]
    for g in range(KV_HEADS):
        _, _, values, probs = group_scores(qkv_ref, seg_col_ref, seg_row_ref, g)
        mixed = flat_product(probs.astype(jnp.bfloat16), values)
        for r in range(GROUP):
            head = g * GROUP + r
            out_ref[:, head * HEAD : (head + 1) * HEAD] = mixed[r * rows : (r + 1) * rows]


def attention_backward_kernel(qkv_ref, seg_col_ref, seg_row_ref, grad_ref, low_ref, first):
    rows = qkv_ref.shape[0]
    bf16 = jnp.bfloat16
    for g in range(KV_HEADS):
        queries, keys, values, probs = group_scores(qkv_ref, seg_col_ref, seg_row_ref, g)
        grads = jnp.concatenate(
            [grad_ref[:, (g * GROUP + r) * HEAD : (g * GROUP + r + 1) * HEAD] for r in range(GROUP)], axis=0
        )
        prob_grad = back_product(grads, values)
        score_low = (
            probs * (prob_grad - jnp.sum(probs * prob_grad, axis=-1, keepdims=True))
        ).astype(bf16)
        query_grad = (flat_product(score_low, keys) * HEAD ** (-0.5)).astype(bf16)
        for r in range(GROUP):
            head = g * GROUP + r
            low_ref[:, first + head * HEAD : first + (head + 1) * HEAD] = query_grad[r * rows : (r + 1) * rows]
        key_grad = outer_sum(score_low, queries) * HEAD ** (-0.5)
        low_ref[:, first + D + g * HEAD : first + D + (g + 1) * HEAD] = key_grad.astype(bf16)
        value_grad = outer_sum(probs.astype(bf16), grads)
        low_ref[:, first + D + (KV_HEADS + g) * HEAD : first + D + (KV_HEADS + g + 1) * HEAD] = value_grad.astype(bf16)


CHUNKS = INNER // LANES
WIDE_CHUNKS = [(k * LANES, LANES) for k in range(WIDE // LANES)] + [(WIDE // LANES * LANES, WIDE % LANES)]
WIDE_BUFFERS = 3
MAIN = FAST_DEV * MAIN_D
LOW_PAD = 128


def lanes_at(k):
    return pl.ds(pl.multiple_of(k * LANES, 128), LANES)


def write_order(table_ref, matrix_ref):
    size, step = matrix_ref.shape[0], 160

    @pl.loop(0, size // step)
    def _(k):
        at = pl.multiple_of(k * step, 16)
        places = lax.broadcasted_iota(jnp.int32, (step, size), 0) + at
        matrix_ref[pl.ds(at, step), :] = jnp.where(places == table_ref[...], 1.0, 0.0).astype(jnp.bfloat16)


def rms_parts(values):
    scale = lax.rsqrt(jnp.mean(values * values, axis=-1, keepdims=True) + epsilon)
    return values * scale, scale


def rms_pull(unit, scale, gain_row, grad):
    inner = grad * gain_row
    back = scale * (inner - unit * jnp.mean(inner * unit, axis=-1, keepdims=True))
    return back, jnp.sum(grad * unit, axis=0, keepdims=True)


def wide_copy(wide_ref, buffer, sem, j):
    column, columns = WIDE_CHUNKS[j]
    slot = j % WIDE_BUFFERS
    return pltpu.make_async_copy(
        wide_ref.at[:, pl.ds(column, columns)], buffer.at[slot, :, pl.ds(0, columns)], sem.at[slot]
    )


def conv_sum(inner, taps, shift, same_ref):
    earlier = [pltpu.roll(inner, k, axis=0) * same_ref[:, k - 1 : k] for k in range(1, CONV)]
    total = shift + taps[CONV - 1 : CONV] * inner
    for k in range(1, CONV):
        total = total + taps[CONV - 1 - k : CONV - k] * earlier[k - 1]
    return total, earlier


def scan_rows(lanes, b_ref, c_ref, y_ref, rates, decay_step, step_input, keep=None):
    rows_all = decay_step.shape[0]

    def eight(k, state):
        base = pl.multiple_of(k * 8, 8)
        steps = decay_step[pl.ds(base, 8), :]
        inputs = step_input[pl.ds(base, 8), :]
        rows = []
        for i in range(8):
            decay = jnp.exp2(steps[i : i + 1] * rates)
            state = decay * state + tiled(b_ref[base + i]) * inputs[i : i + 1]
            if keep is None:
                rows.append(jnp.sum(tiled(c_ref[base + i]) * state, axis=0, keepdims=True))
            else:
                keep(base + i, state)
        if keep is None:
            y_ref[pl.ds(base, 8), lanes] = jnp.concatenate(rows, axis=0)
        return state

    lax.fori_loop(0, rows_all // 8, eight, jnp.zeros((STATE, LANES), jnp.float32))


def spread_lanes(rows_ref, first, out_ref):
    lane = lax.broadcasted_iota(jnp.int32, (STATE, 128), 1)
    place = lax.broadcasted_iota(jnp.int32, (STATE, 128), 0) + first

    @pl.loop(0, rows_ref.shape[0] // 8)
    def _(k):
        base = pl.multiple_of(k * 8, 8)
        rows = rows_ref[pl.ds(base, 8), :]
        for i in range(8):
            picked = jnp.where(lane == place, jnp.broadcast_to(rows[i : i + 1], (STATE, 128)), 0.0)
            out_ref[base + i] = jnp.broadcast_to(jnp.sum(picked, axis=1, keepdims=True), (STATE, 128))


def gather_lanes(b_ref, c_ref, out_ref):
    lane = lax.broadcasted_iota(jnp.int32, (STATE, 128), 1)
    place = lax.broadcasted_iota(jnp.int32, (STATE, 128), 0)

    @pl.loop(0, out_ref.shape[0] // 8)
    def _(k):
        base = pl.multiple_of(k * 8, 8)
        rows = []
        for i in range(8):
            b = jnp.where(lane == place, jnp.sum(b_ref[base + i], axis=1, keepdims=True), 0.0)
            c = jnp.where(lane == place + STATE, jnp.sum(c_ref[base + i], axis=1, keepdims=True), 0.0)
            rows.append(jnp.sum(b + c, axis=0, keepdims=True))
        out_ref[pl.ds(base, 8), :] = jnp.concatenate(rows, axis=0)


def mixer_forward_kernel(
    tokens_ref, gains_ref, seg_col_ref, seg_row_ref, hold_ref, same_ref, table_d_ref, table_i_ref,
    wide_ref, wide_rest_ref, taps_ref, conv_shift_ref, select_ref, step_ref, step_shift_ref, decay_ref, skip_ref,
    out_ref, out_rest_ref, join_ref, join_rest_ref,
    normed_ref, mixed_ref, qkv_ref, conv_ref, step_low_ref, pre_ref, b_ref, c_ref, y_ref, gated_ref, attn_ref,
    mamba_ref, joined_ref, middle_ref, normed_two_ref,
    order, wide_buffer, out_all, join_all, conv_low, gated, decay_step, step_input, select_rows, wide_sem, sem,
):
    bf16, f32 = jnp.bfloat16, jnp.float32
    count = len(WIDE_CHUNKS)
    for j in range(WIDE_BUFFERS):
        wide_copy(wide_ref, wide_buffer, wide_sem, j).start()
    out_copy = pltpu.make_async_copy(out_ref, out_all, sem.at[0])
    join_copy = pltpu.make_async_copy(join_ref, join_all, sem.at[1])
    out_copy.start()
    join_copy.start()
    inputs = tokens_ref[...].astype(f32)
    write_order(table_d_ref, order)
    normed_ref[...] = flat_product((rms_parts(inputs)[0] * gains_ref[0:1]).astype(bf16), order[...]).astype(bf16)
    for j, (column, columns) in enumerate(WIDE_CHUNKS):
        copy = wide_copy(wide_ref, wide_buffer, wide_sem, j)
        copy.wait()
        part = flat_product(normed_ref[:, :MAIN], wide_buffer[j % WIDE_BUFFERS, :, :columns]) + flat_product(
            normed_ref[:, MAIN:], wide_rest_ref[:, column : column + columns]
        )
        if column < 2 * INNER:
            mixed_ref[:, column : column + columns] = part
        else:
            first, last = column - 2 * INNER, min(column - 2 * INNER + columns, QKV)
            qkv_ref[:, first:last] = part[:, : last - first].astype(bf16)
        if j + WIDE_BUFFERS < count:
            wide_copy(wide_ref, wide_buffer, wide_sem, j + WIDE_BUFFERS).start()

    @pl.loop(0, CHUNKS)
    def _(k):
        lanes = lanes_at(k)
        total, _ = conv_sum(mixed_ref[:, lanes], taps_ref[:, lanes], conv_shift_ref[:, lanes], same_ref)
        act = total / (1.0 + jnp.exp(-total))
        conv_ref[:, lanes] = act
        conv_low[:, lanes] = act.astype(bf16)

    selected = flat_product(conv_low[...], select_ref[...])
    step_low_ref[...] = selected[:, :LOW_PAD].astype(bf16)
    select_rows[...] = selected[:, LOW_PAD:]
    spread_lanes(select_rows, 0, b_ref)
    spread_lanes(select_rows, STATE, c_ref)
    attention_forward_kernel(qkv_ref, seg_col_ref, seg_row_ref, attn_ref)
    write_order(table_i_ref, order)

    @pl.loop(0, CHUNKS)
    def _(k):
        lanes = lanes_at(k)
        pre = flat_product(step_low_ref[...], step_ref[:, lanes])
        pre_ref[:, lanes] = pre
        conv = conv_ref[:, lanes]
        _, decay_step[...], step_input[...] = scan_setup(pre, step_shift_ref[:, lanes], conv, hold_ref[...])
        scan_rows(lanes, b_ref, c_ref, y_ref, decay_ref[:, lanes] * (-LOG2E), decay_step, step_input)
        gate = mixed_ref[:, pl.ds(pl.multiple_of(k * LANES + INNER, 128), LANES)]
        gated[:, lanes] = (
            (y_ref[:, lanes] + skip_ref[:, lanes] * conv) * (gate / (1.0 + jnp.exp(-gate)))
        ).astype(bf16)

    half = INNER // 2
    out_copy.wait()
    total = jnp.zeros(mamba_ref.shape, f32)
    for h in range(2):
        moved = flat_product(gated[:, h * half : (h + 1) * half], order[...]).astype(bf16)
        gated_ref[h] = moved
        total = total + flat_product(moved[:, :MAIN], out_all[h * MAIN : (h + 1) * MAIN])
        total = total + flat_product(moved[:, MAIN:], out_rest_ref[h])
    mamba_ref[...] = total
    joined = 0.5 * (rms_parts(attn_ref[...])[0] * gains_ref[1:2] + rms_parts(total)[0] * gains_ref[2:3])
    write_order(table_d_ref, order)
    joined_ref[...] = flat_product(joined.astype(bf16), order[...]).astype(bf16)
    join_copy.wait()
    middle = (
        inputs
        + flat_product(joined_ref[:, :MAIN], join_all[...])
        + flat_product(joined_ref[:, MAIN:], join_rest_ref[...])
    )
    middle_ref[...] = middle
    normed_two_ref[...] = (rms_parts(middle)[0] * gains_ref[3:4]).astype(bf16)


def mixer_forward(*operands):
    rows = operands[0].shape[0]
    bf16, f32 = jnp.bfloat16, jnp.float32
    vmem, anywhere = pl.BlockSpec(memory_space=pltpu.VMEM), pl.BlockSpec(memory_space=pl.ANY)
    in_specs = [vmem] * len(operands)
    for k in (8, 17, 19):
        in_specs[k] = anywhere
    shapes = (
        ((rows, D), bf16), ((rows, 2 * INNER), f32), ((rows, QKV), bf16), ((rows, INNER), f32), ((rows, LOW_PAD), bf16),
        ((rows, INNER), f32), ((rows, STATE, 128), f32), ((rows, STATE, 128), f32), ((rows, INNER), f32),
        ((2, rows, D), bf16), ((rows, D), f32), ((rows, D), f32), ((rows, D), bf16), ((rows, D), f32), ((rows, D), bf16),
    )
    return pl.pallas_call(
        mixer_forward_kernel,
        out_shape=[jax.ShapeDtypeStruct(shape, kind) for shape, kind in shapes],
        in_specs=in_specs,
        out_specs=[vmem] * len(shapes),
        scratch_shapes=[
            pltpu.VMEM((D, D), bf16),
            pltpu.VMEM((WIDE_BUFFERS, MAIN, LANES), bf16),
            pltpu.VMEM((2 * MAIN, D), bf16),
            pltpu.VMEM((MAIN, D), bf16),
            pltpu.VMEM((rows, INNER), bf16),
            pltpu.VMEM((rows, INNER), bf16),
            pltpu.VMEM((rows, LANES), f32),
            pltpu.VMEM((rows, LANES), f32),
            pltpu.VMEM((rows, 128), f32),
            pltpu.SemaphoreType.DMA((WIDE_BUFFERS,)),
            pltpu.SemaphoreType.DMA((2,)),
        ],
        compiler_params=pltpu.CompilerParams(vmem_limit_bytes=60 * 1024 * 1024),
        name="mixer_forward",
    )(*operands)


def mixer_backward_kernel(
    part_grad_ref, out_grad_ref, tokens_ref, gains_ref, seg_col_ref, seg_row_ref, hold_ref, same_ref,
    table_d_ref, table_i_ref,
    wide_ref, wide_rest_ref, taps_ref, conv_shift_ref, select_ref, step_ref, step_shift_ref, decay_ref, skip_ref,
    out_ref, out_rest_ref, join_ref, join_rest_ref,
    mixed_ref, qkv_ref, conv_ref, step_low_ref, pre_ref, b_ref, c_ref, y_ref, attn_ref, mamba_ref, middle_ref,
    input_grad_ref, gains_grad_ref, wide_low_ref, mamba_low_ref, join_low_ref, select_grad_ref, step_grad_ref,
    taps_grad_ref, conv_shift_grad_ref, step_shift_grad_ref, decay_grad_ref, skip_grad_ref,
    order, wide_buffer, row_buffer, wide_sem, sem, attn_low, lane_grad, low_grad,
    step_size, decay_step, step_input, y_grad, input_part, step_part, states, b_grad, c_grad, select_rows, select_low,
):
    bf16, f32 = jnp.bfloat16, jnp.float32
    rows_all = tokens_ref.shape[0]
    count = len(WIDE_CHUNKS)
    half_rows = MAIN // 2
    row_blocks = [(join_ref, k) for k in range(2)] + [(out_ref, k) for k in range(4)]

    def row_copy(i):
        source, k = row_blocks[i]
        return pltpu.make_async_copy(
            source.at[pl.ds(k * half_rows, half_rows)], row_buffer.at[i % 2], sem.at[i % 2]
        )

    def row_products(low, first):
        products = []
        for i in (first, first + 1):
            row_copy(i).wait()
            products.append(back_product(low, row_buffer[i % 2]))
            if i + 2 < len(row_blocks):
                row_copy(i + 2).start()
        return products

    row_copy(0).start()
    row_copy(1).start()
    for j in range(WIDE_BUFFERS):
        wide_copy(wide_ref, wide_buffer, wide_sem, j).start()
    write_order(table_d_ref, order)

    def move_back(rows_wide):
        high = rows_wide.astype(bf16)
        rest = (rows_wide - high.astype(f32)).astype(bf16)
        return back_product(high, order[...]) + back_product(rest, order[...])

    unit, scale = rms_parts(middle_ref[...])
    back, gain_grad = rms_pull(unit, scale, gains_ref[3:4], part_grad_ref[...])
    gains_grad_ref[3:4] = gain_grad
    middle_grad = out_grad_ref[...] + back
    input_grad_ref[...] = middle_grad
    join_low = middle_grad.astype(bf16)
    join_low_ref[...] = join_low
    joined_grad = 0.5 * move_back(
        jnp.concatenate(row_products(join_low, 0) + [back_product(join_low, join_rest_ref[...])], axis=1)
    )
    unit, scale = rms_parts(attn_ref[...])
    back, gain_grad = rms_pull(unit, scale, gains_ref[1:2], joined_grad)
    gains_grad_ref[1:2] = gain_grad
    attn_low[...] = back.astype(bf16)
    unit, scale = rms_parts(mamba_ref[...])
    back, gain_grad = rms_pull(unit, scale, gains_ref[2:3], joined_grad)
    gains_grad_ref[2:3] = gain_grad
    mamba_low = back.astype(bf16)
    mamba_low_ref[...] = mamba_low
    write_order(table_i_ref, order)
    half = INNER // 2
    for h in range(2):
        lane_grad[:, h * half : (h + 1) * half] = move_back(
            jnp.concatenate(row_products(mamba_low, 2 + 2 * h) + [back_product(mamba_low, out_rest_ref[h])], axis=1)
        )
    b_grad[...] = jnp.zeros_like(b_grad)
    c_grad[...] = jnp.zeros_like(c_grad)
    states[0] = jnp.zeros((STATE, LANES), f32)
    zeros = jnp.zeros((STATE, LANES), f32)

    @pl.loop(0, CHUNKS)
    def _(k):
        lanes = lanes_at(k)
        gate_lanes = pl.ds(pl.multiple_of(k * LANES + INNER, 128), LANES)
        conv, shift, skip = conv_ref[:, lanes], step_shift_ref[:, lanes], skip_ref[:, lanes]
        step_size[...], decay_step[...], step_input[...] = scan_setup(pre_ref[:, lanes], shift, conv, hold_ref[...])
        gate, grad = mixed_ref[:, gate_lanes], lane_grad[:, lanes]
        open_gate = 1.0 / (1.0 + jnp.exp(-gate))
        wide_low_ref[:, gate_lanes] = (
            grad * (y_ref[:, lanes] + skip * conv) * open_gate * (1.0 + gate * (1.0 - open_gate))
        ).astype(bf16)
        y_grad[...] = grad * gate * open_gate
        skip_grad_ref[:, lanes] = jnp.sum(y_grad[...] * conv, axis=0, keepdims=True)
        decay_rows = decay_ref[:, lanes]

        rates = decay_rows * (-LOG2E)

        def keep(t, state):
            states[t + 1] = state

        scan_rows(lanes, b_ref, c_ref, None, rates, decay_step, step_input, keep)

        def backward(i, carry):
            state_grad, decay_grad = carry
            base = pl.multiple_of(rows_all - 8 - i * 8, 8)
            inputs = step_input[pl.ds(base, 8), :]
            sizes = step_size[pl.ds(base, 8), :]
            held = decay_step[pl.ds(base, 8), :]
            y_rows = y_grad[pl.ds(base, 8), :]
            input_rows, step_rows = [None] * 8, [None] * 8
            for r in range(7, -1, -1):
                t = base + r
                y_row = y_rows[r : r + 1]
                full = state_grad + tiled(c_ref[t]) * y_row
                c_grad[t] += folded(states[t + 1] * y_row)
                b_grad[t] += folded(full * inputs[r : r + 1])
                input_rows[r] = jnp.sum(tiled(b_ref[t]) * full, axis=0, keepdims=True)
                state_grad = jnp.exp2(held[r : r + 1] * rates) * full
                through = state_grad * states[t]
                step_rows[r] = jnp.sum(decay_rows * through, axis=0, keepdims=True)
                decay_grad = decay_grad - sizes[r : r + 1] * through
            input_part[pl.ds(base, 8), :] = jnp.concatenate(input_rows, axis=0)
            step_part[pl.ds(base, 8), :] = jnp.concatenate(step_rows, axis=0)
            return state_grad, decay_grad

        _, decay_grad = lax.fori_loop(0, rows_all // 8, backward, (zeros, zeros))
        decay_grad_ref[:, lanes] = decay_grad
        lane_grad[:, lanes] = input_part[...] * step_size[...] + skip * y_grad[...]
        pre_grad = (input_part[...] * conv - step_part[...]) / (1.0 + jnp.exp(-(pre_ref[:, lanes] + shift)))
        step_shift_grad_ref[:, lanes] = jnp.sum(pre_grad, axis=0, keepdims=True)
        low_grad[:, lanes] = pre_grad.astype(bf16)

    gather_lanes(b_grad, c_grad, select_rows)
    select_low[:, :LOW_PAD] = back_product(low_grad[...], step_ref[...]).astype(bf16)
    select_low[:, LOW_PAD:] = select_rows[...].astype(bf16)

    @pl.loop(0, CHUNKS)
    def _(k):
        lanes = lanes_at(k)
        step_grad_ref[:, lanes] = outer_sum(step_low_ref[...], low_grad[:, lanes]).astype(bf16)
        conv = conv_ref[:, lanes]
        some = pl.ds(pl.multiple_of(k * LANES, 128), LANES)
        select_grad_ref[some, :] = outer_sum(conv.astype(bf16), select_low[...]).astype(bf16)
        grad = lane_grad[:, lanes] + back_product(select_low[...], select_ref[some, :])
        inner, taps = mixed_ref[:, lanes], taps_ref[:, lanes]
        total, earlier = conv_sum(inner, taps, conv_shift_ref[:, lanes], same_ref)
        opened = 1.0 / (1.0 + jnp.exp(-total))
        grad = grad * opened * (1.0 + total * (1.0 - opened))
        conv_shift_grad_ref[:, lanes] = jnp.sum(grad, axis=0, keepdims=True)
        tap_rows = [jnp.sum(grad * earlier[j - 1], axis=0, keepdims=True) for j in range(CONV - 1, 0, -1)]
        tap_rows.append(jnp.sum(grad * inner, axis=0, keepdims=True))
        taps_grad_ref[:, lanes] = jnp.concatenate(tap_rows, axis=0)
        inner_grad = taps[CONV - 1 : CONV] * grad
        for j in range(1, CONV):
            moved = taps[CONV - 1 - j : CONV - j] * grad * same_ref[:, j - 1 : j]
            inner_grad = inner_grad + pltpu.roll(moved, rows_all - j, axis=0)
        wide_low_ref[:, lanes] = inner_grad.astype(bf16)

    attention_backward_kernel(qkv_ref, seg_col_ref, seg_row_ref, attn_low, wide_low_ref, 2 * INNER)
    wide_low_ref[:, 2 * INNER + QKV :] = jnp.zeros((rows_all, WIDE - 2 * INNER - QKV), bf16)
    write_order(table_d_ref, order)
    total = jnp.zeros((rows_all, MAIN), f32)
    for j, (column, columns) in enumerate(WIDE_CHUNKS):
        wide_copy(wide_ref, wide_buffer, wide_sem, j).wait()
        total = total + back_product(
            wide_low_ref[:, column : column + columns], wide_buffer[j % WIDE_BUFFERS, :, :columns]
        )
        if j + WIDE_BUFFERS < count:
            wide_copy(wide_ref, wide_buffer, wide_sem, j + WIDE_BUFFERS).start()
    normed_grad = move_back(
        jnp.concatenate([total, back_product(wide_low_ref[...], wide_rest_ref[...])], axis=1)
    )
    unit, scale = rms_parts(tokens_ref[...].astype(f32))
    back, gain_grad = rms_pull(unit, scale, gains_ref[0:1], normed_grad)
    gains_grad_ref[0:1] = gain_grad
    input_grad_ref[...] = input_grad_ref[...] + back


def mixer_backward(*operands):
    rows = operands[0].shape[0]
    bf16, f32 = jnp.bfloat16, jnp.float32
    vmem, anywhere = pl.BlockSpec(memory_space=pltpu.VMEM), pl.BlockSpec(memory_space=pl.ANY)
    in_specs = [vmem] * len(operands)
    for k in (10, 19, 21):
        in_specs[k] = anywhere
    shapes = (
        ((rows, D), f32), ((4, D), f32), ((rows, WIDE), bf16), ((rows, D), bf16), ((rows, D), bf16),
        ((INNER, 2 * LOW_PAD), bf16), ((LOW_PAD, INNER), bf16), ((CONV, INNER), f32), ((1, INNER), f32), ((1, INNER), f32),
        ((STATE, INNER), f32), ((1, INNER), f32),
    )
    lane_rows = pltpu.VMEM((rows, LANES), f32)
    return pl.pallas_call(
        mixer_backward_kernel,
        out_shape=[jax.ShapeDtypeStruct(shape, kind) for shape, kind in shapes],
        in_specs=in_specs,
        out_specs=[vmem] * len(shapes),
        scratch_shapes=[
            pltpu.VMEM((D, D), bf16),
            pltpu.VMEM((WIDE_BUFFERS, MAIN, LANES), bf16),
            pltpu.VMEM((2, MAIN // 2, D), bf16),
            pltpu.SemaphoreType.DMA((WIDE_BUFFERS,)),
            pltpu.SemaphoreType.DMA((2,)),
            pltpu.VMEM((rows, D), bf16),
            pltpu.VMEM((rows, INNER), f32),
            pltpu.VMEM((rows, INNER), bf16),
        ]
        + [lane_rows] * 6
        + [
            pltpu.VMEM((rows + 1, STATE, LANES), f32),
            pltpu.VMEM((rows, STATE, 128), f32),
            pltpu.VMEM((rows, STATE, 128), f32),
            pltpu.VMEM((rows, 128), f32),
            pltpu.VMEM((rows, 2 * LOW_PAD), bf16),
        ],
        compiler_params=pltpu.CompilerParams(vmem_limit_bytes=62 * 1024 * 1024),
        name="mixer_backward",
    )(*operands)


def spread_table(shard_rows, main_rows, shards):
    half = shards // CORES
    order = [k * CORES + c for c in range(CORES) for k in range(half)]
    main = [d * shard_rows + r for d in order for r in range(main_rows)]
    rest = [d * shard_rows + r for d in order for r in range(main_rows, shard_rows)]
    return np.asarray(main + rest, np.int32)


def pick(array, index, axis):
    return lax.dynamic_index_in_dim(array, index, axis, keepdims=False)


def plus(left, right):
    return (left.astype(jnp.float32) + right.astype(jnp.float32)).astype(jnp.bfloat16)


def shift_chip(rows, step):
    return lax.ppermute(rows, "fsdp", chip_pairs(step))


def shift_plane(rows, step):
    return lax.ppermute(rows, "fsdp", plane_pairs(step))


def swap_core(rows):
    return lax.ppermute(rows, "fsdp", CORE_PAIRS)


def tie(*values):
    return lax.optimization_barrier(values)


class PlaneGather:
    def __init__(self, block, place):
        self.parts, self.place = [block], place

    def step(self):
        self.parts.append(shift_plane(self.parts[-1], 1))
        return self.parts[-1]

    def whole(self):
        stacked = jnp.stack(self.parts)
        order = [(self.place + PLANES - RING.index(z)) % PLANES for z in range(PLANES)]
        return jnp.concatenate([pick(stacked, k, 0) for k in order], axis=0)


class PlaneSum:
    def __init__(self, parts, place):
        self.parts, self.place, self.hops, self.came = parts, place, 0, None

    def here(self):
        return pick(self.parts, ring_place((self.place + PLANES - 1 - self.hops) % PLANES), 0)

    def step(self):
        moving = self.here() if self.came is None else plus(self.here(), self.came)
        self.came = shift_plane(moving, 1)
        self.hops += 1

    def total(self):
        return self.here().astype(jnp.float32) + self.came.astype(jnp.float32)


def gather_plane(rows):
    half = rows.shape[0] // 2
    right, left = shift_chip(rows, 3), shift_chip(rows, 1)
    far = [shift_chip(right[:half], 3), shift_chip(left[half:], 1)]
    chips = jnp.concatenate([rows, right] + far + [left], axis=0)
    return jnp.concatenate([chips, swap_core(chips)], axis=0)


def scatter_plane(parts):
    rows = parts.shape[0] // PLANE_DEV
    half = rows // 2
    chips = plus(parts[: CHIPS * rows], swap_core(parts[CHIPS * rows :]))
    own, right, far, left = [chips[k * rows : (k + 1) * rows] for k in range(CHIPS)]
    from_left = shift_chip(far[:half], 1)
    from_right = shift_chip(far[half:], 3)
    right = jnp.concatenate([plus(right[:half], from_left), right[half:]], axis=0)
    left = jnp.concatenate([left[:half], plus(left[half:], from_right)], axis=0)
    came_left, came_right = shift_chip(right, 1), shift_chip(left, 3)
    return own.astype(jnp.float32) + came_left.astype(jnp.float32) + came_right.astype(jnp.float32)


def as_rows(flats, rows):
    flat = jnp.concatenate(flats)
    return jnp.pad(flat, (0, rows * 128 - flat.size)).reshape(rows, 128)


def split_flat(block, sizes):
    pieces, at = [], 0
    for size in sizes:
        pieces.append(block[..., at : at + size])
        at += size
    return pieces


def on_fast_device(
    tokens, cotangent, seq_lengths, qkv_proj, mamba_in, select_proj, step_proj, mamba_out, join_out,
    conv_taps, conv_bias, step_bias, decay_rates, skip_gain, norm_gains, ffn_gate, ffn_up, ffn_down,
):
    bf16, f32 = jnp.bfloat16, jnp.float32
    n = FAST_DEV
    zp = ring_place(lax.axis_index("fsdp") // PLANE_DEV)
    row_count = tokens.shape[0]
    d_rows, i_rows = D // n, INNER // n
    d_rest, i_rest = d_rows - MAIN_D, i_rows - MAIN_I

    own_ff = PLANES * SLICE_FF

    def ff_columns(flat):
        block = flat.reshape(d_rows, PLANES, PLANE_DEV, SLICE_FF).transpose(2, 0, 1, 3)
        return jnp.pad(block.reshape(PLANE_DEV, d_rows, own_ff), ((0, 0), (0, 0), (0, HALF_GU - own_ff)))

    planes = [[z * PLANE_DEV + p for p in range(PLANE_DEV)] for z in range(PLANES)]
    gu = jnp.concatenate([ff_columns(ffn_gate), ff_columns(ffn_up)], axis=2)
    gu = lax.all_to_all(gu, "fsdp", 0, 0, axis_index_groups=planes, tiled=True).reshape(PLANE_DEV * d_rows, GU)
    plane_down = PlaneGather(ffn_down.reshape(SLICE_FF, D), zp)

    wide = jnp.concatenate([mamba_in.reshape(d_rows, 2 * INNER), qkv_proj.reshape(d_rows, QKV)], axis=1)
    wide = jnp.pad(wide, ((0, 0), (0, WIDE - wide.shape[1])))
    out_block = mamba_out.reshape(i_rows, D)
    join_block = join_out.reshape(d_rows, D)
    rest_sizes = [d_rest * WIDE, d_rest * D, i_rest * D]
    rest = as_rows(
        [wide[MAIN_D:].reshape(-1), join_block[MAIN_D:].reshape(-1), out_block[MAIN_I:].reshape(-1)], REST_ROWS
    )
    smalls = [select_proj, step_proj, conv_taps, conv_bias, step_bias, decay_rates, skip_gain, norm_gains]
    small_sizes = [s.size for s in smalls]
    smalls = as_rows(smalls, SMALL_ROWS)
    gu, wide_block = tie(gu, wide[:MAIN_D])
    plane_gu = PlaneGather(gu, zp)
    plane_gu.step()
    plane_down.step()
    wide_all, rest_all, smalls_all = gather_weights(
        0, "gather_first", ("wide", "rest", "smalls"), (wide_block, rest, smalls)
    )
    out_block, join_block, _, _ = tie(out_block[:MAIN_I], join_block[:MAIN_D], plane_gu.step(), plane_down.step())
    plane_gu.parts[1], plane_down.parts[1], wide_all, out_block = tie(
        plane_gu.parts[1], plane_down.parts[1], wide_all, out_block
    )
    out_all, join_all = gather_weights(1, "gather_second", ("mamba_out", "join"), (out_block, join_block))
    wide_all = wide_all.reshape(MAIN, WIDE)
    out_all, join_all = out_all.reshape(2 * MAIN, D), join_all.reshape(MAIN, D)
    pieces = split_flat(rest_all.reshape(n, REST_ROWS * 128), rest_sizes)
    wide_rest = pieces[0].reshape(n * d_rest, WIDE)
    join_rest = pieces[1].reshape(n * d_rest, D)
    out_rest = pieces[2].reshape(CORES, 2, -1, D).transpose(1, 0, 2, 3).reshape(2, -1, D)
    pieces = split_flat(smalls_all.reshape(n, SMALL_ROWS * 128), small_sizes)
    select = pieces[0].reshape(INNER, XPROJ)
    select = jnp.concatenate(
        [
            jnp.pad(select[:, :RANK], ((0, 0), (0, LOW_PAD - RANK))),
            jnp.pad(select[:, RANK:], ((0, 0), (0, LOW_PAD - 2 * STATE))),
        ],
        axis=1,
    )
    step_matrix = jnp.pad(pieces[1].reshape(RANK, INNER), ((0, LOW_PAD - RANK), (0, 0)))
    taps = pieces[2].reshape(CONV, INNER).astype(f32)
    conv_shift = pieces[3].reshape(1, INNER).astype(f32)
    step_shift = pieces[4].reshape(1, INNER).astype(f32)
    decay = pieces[5].reshape(STATE, INNER).astype(f32)
    skip = pieces[6].reshape(1, INNER).astype(f32)
    gains = pieces[7].reshape(4, D).astype(f32)

    table_d = jnp.asarray(spread_table(d_rows, MAIN_D, n))[None]
    table_i = jnp.asarray(spread_table(i_rows, MAIN_I, n // 2))[None]
    segments = segment_ids(seq_lengths, row_count)
    live_rows = (segments < seq_lengths.shape[0]).astype(f32)[:, None]
    hold = ((1.0 - keep_flags(segments)) * BIG)[:, None]
    same = jnp.stack(
        [
            (jnp.concatenate([jnp.full((k,), -1, jnp.int32), segments[:-k]]) == segments).astype(f32)
            for k in range(1, CONV)
        ],
        axis=1,
    )
    places = (segments[:, None], segments[None, :], hold, same, table_d, table_i)
    out_grad = cotangent.astype(f32) * live_rows
    out_low = gather_plane(out_grad.astype(bf16))
    matrices = (
        wide_all, wide_rest, taps, conv_shift, select, step_matrix, step_shift, decay, skip,
        out_all, out_rest, join_all, join_rest,
    )
    plane_gu.parts[2], plane_down.parts[2], gains, out_low = tie(
        plane_gu.parts[2], plane_down.parts[2], gains, out_low
    )
    plane_gu.step()
    plane_down.step()
    (
        normed, mixed, qkv_rows, conv_act, step_low, step_pre, b_wide, c_wide, scanned, gated, attn_rows, mamba_rows,
        joined, middle, normed_two,
    ) = mixer_forward(tokens, gains, *places, *matrices)

    normed_two, plane_gu.parts[3], plane_down.parts[3] = tie(normed_two, plane_gu.parts[3], plane_down.parts[3])
    gu_matrix = plane_gu.whole()
    down_matrix = jnp.pad(plane_down.whole(), ((0, HALF_GU - own_ff), (0, 0)))
    normed_two = gather_plane(normed_two)
    gu_rows = flat_product(normed_two, gu_matrix)
    act_full, act_pull = jax.vjp(swiglu, gu_rows[:, :HALF_GU], gu_rows[:, HALF_GU:])
    activated = act_full.astype(bf16)
    act_grad = back_product(out_low, down_matrix)
    gu_low = jnp.concatenate(act_pull(act_grad), axis=1).astype(bf16)
    part_grad = scatter_plane(back_product(gu_low, gu_matrix).astype(bf16))
    down_sum = PlaneSum(outer_sum(activated, out_low)[:own_ff].astype(bf16).reshape(PLANES, SLICE_FF, D), zp)
    gu_sum = PlaneSum(outer_sum(normed_two, gu_low).astype(bf16).reshape(PLANES, PLANE_DEV * d_rows, GU), zp)
    ffn_part = flat_product(activated, down_matrix).astype(bf16)
    block_out = ((middle + scatter_plane(ffn_part)) * live_rows).astype(bf16)

    gu_sum.step()
    down_sum.step()
    (
        input_grad, gains_grad, wide_low, mamba_low, join_low, select_grad, step_grad, taps_grad, conv_shift_grad,
        step_shift_grad, decay_grad, skip_grad,
    ) = mixer_backward(
        part_grad, out_grad, tokens, gains, *places, *matrices,
        mixed, qkv_rows, conv_act, step_low, step_pre, b_wide, c_wide, scanned, attn_rows, mamba_rows, middle,
    )
    mamba_low, gu_sum.came, down_sum.came = tie(mamba_low, gu_sum.came, down_sum.came)
    gu_sum.step()
    down_sum.step()

    gated_columns = gated.transpose(0, 2, 1)
    gated_rest = gated_columns[:, MAIN:].reshape(2, CORES, -1, row_count).transpose(1, 0, 2, 3)
    joined_columns, normed_columns = joined.T, normed.T
    out_sum, join_sum, branch_rest = sum_gradients(
        2, "sum_first", BRANCH_BLOCKS, (MAIN_I, MAIN_D), (i_rest, d_rest), D,
        (gated_columns[:, :MAIN], joined_columns[None, :MAIN]),
        (gated_rest.reshape(CORES, -1, row_count), joined_columns[MAIN:].reshape(CORES, -1, row_count)),
        (mamba_low, join_low),
    )
    select_grad = jnp.concatenate([select_grad[:, :RANK], select_grad[:, LOW_PAD : LOW_PAD + 2 * STATE]], axis=1)
    small_grads = [
        select_grad, step_grad[:RANK], taps_grad, conv_shift_grad, step_shift_grad, decay_grad, skip_grad, gains_grad,
    ]
    small_grads = jnp.concatenate([g.astype(bf16).reshape(n, -1) for g in small_grads], axis=1)
    small_grads = jnp.pad(small_grads, ((0, 0), (0, SMALL_ROWS * 128 - small_grads.shape[1])))
    small_grads = small_grads.reshape(GROUPS, CORES, SMALL_ROWS, 128).transpose(1, 0, 2, 3)
    out_sum, small_grads, gu_sum.came, down_sum.came = tie(out_sum, small_grads, gu_sum.came, down_sum.came)
    gu_sum.step()
    down_sum.step()
    wide_sum, wide_left, small_sum = sum_gradients(
        3, "sum_second", WIDE_BLOCKS, (MAIN_D,), (d_rest,), REST_COLUMNS,
        (normed_columns[None, :MAIN],),
        (normed_columns[MAIN:].reshape(CORES, -1, row_count),),
        (wide_low,),
        small_grads.reshape(CORES, GROUPS * SMALL_ROWS, 128),
    )
    gu_blocks = gu_sum.total().astype(bf16).reshape(PLANE_DEV, d_rows, GU)
    gu_blocks = lax.all_to_all(gu_blocks, "fsdp", 0, 0, axis_index_groups=planes, tiled=True)
    gu_blocks = gu_blocks.reshape(PLANE_DEV, d_rows, 2, HALF_GU)[..., :own_ff].transpose(2, 1, 0, 3)
    gu_blocks = gu_blocks.reshape(2, d_rows, PLANE_DEV, PLANES, SLICE_FF).transpose(0, 1, 3, 2, 4)
    gate_grad, up_grad = [block.astype(f32).reshape(-1) for block in gu_blocks]
    wide_left = wide_left.reshape(-1, d_rest, REST_COLUMNS).transpose(1, 0, 2).reshape(d_rest, -1)[:, :WIDE]
    wide_sum = jnp.concatenate([wide_sum, wide_left], axis=0)
    out_sum = jnp.concatenate([out_sum, branch_rest[:i_rest]], axis=0)
    join_sum = jnp.concatenate([join_sum, branch_rest[i_rest : i_rest + d_rest]], axis=0)
    smalls = split_flat(small_sum.reshape(-1), small_sizes)
    return (
        block_out,
        input_grad,
        wide_sum[:, 2 * INNER : 2 * INNER + QKV].reshape(-1),
        wide_sum[:, : 2 * INNER].reshape(-1),
        smalls[0],
        smalls[1],
        out_sum.reshape(-1),
        join_sum.reshape(-1),
        *smalls[2:],
        gate_grad,
        up_grad,
        down_sum.total().reshape(-1),
    )


def fits_fast_plan(mesh):
    return mesh.shape["fsdp"] == FAST_DEV


def solution(mesh):
    rows, flat = P("fsdp", None), P("fsdp")
    return jax.shard_map(
        on_fast_device if fits_fast_plan(mesh) else on_device,
        mesh=mesh,
        in_specs=(rows, rows) + (flat,) * 16,
        out_specs=(rows, rows) + (flat,) * 15,
        check_vma=False,
    )
```

```python
import functools

import jax
import jax.numpy as jnp
import numpy as np
from jax import lax
from jax.experimental import pallas as pl
from jax.experimental.pallas import tpu as pltpu
from jax.sharding import PartitionSpec as P

D = 1600
HEADS = 25
KV_HEADS = 5
HEAD = 64
INNER = 3200
STATE = 16
CONV = 4
RANK = 100
FF = 5504
QKV = 2240
XPROJ = 132


epsilon = 1e-06


def flat_product(left, right):
    return jnp.dot(left, right, preferred_element_type=jnp.float32)


def outer_sum(left, right):
    return lax.dot_general(
        left, right, (((0,), (0,)), ((), ())), preferred_element_type=jnp.float32
    )


def back_product(grad_rows, matrix):
    return lax.dot_general(
        grad_rows, matrix, (((1,), (1,)), ((), ())), preferred_element_type=jnp.float32
    )


def rms_scale(values, scale_row):
    return (
        values * lax.rsqrt(jnp.mean(values * values, axis=-1, keepdims=True) + epsilon) * scale_row
    )


def segment_ids(lengths, row_count):
    seq_ends = jnp.cumsum(lengths)
    places = jnp.arange(row_count, dtype=jnp.int32)
    return jnp.sum((places[:, None] >= seq_ends[None, :]).astype(jnp.int32), axis=1)


def keep_flags(segments):
    same_seq = (segments[1:] == segments[:-1]).astype(jnp.float32)
    return jnp.concatenate([jnp.zeros((1,), jnp.float32), same_seq])


def conv_silu(inner_rows, tap_matrix, conv_shift, segments):
    tap_count = tap_matrix.shape[0]
    summed = conv_shift[None, :] + tap_matrix[tap_count - 1][None, :] * inner_rows
    for offset in range(1, tap_count):
        shifted = jnp.concatenate(
            [jnp.zeros((offset, inner_rows.shape[1]), jnp.float32), inner_rows[:-offset]], axis=0
        )
        earlier = jnp.concatenate([jnp.full((offset,), -1, jnp.int32), segments[:-offset]])
        same_seq = (earlier == segments).astype(jnp.float32)
        summed = summed + tap_matrix[tap_count - 1 - offset][None, :] * shifted * same_seq[:, None]
    return jax.nn.silu(summed)


def scan_block(state_now, decay_matrix, block_data):
    step_sizes, step_inputs, step_b, step_c, step_keep = block_data
    outputs = []
    for step_index in range(step_sizes.shape[0]):
        decay_now = jnp.exp(-step_sizes[step_index][None, :] * decay_matrix)
        state_now = (
            step_keep[step_index] * decay_now * state_now
            + step_b[step_index][:, None]
            * (step_sizes[step_index] * step_inputs[step_index])[None, :]
        )
        outputs.append(jnp.sum(step_c[step_index][:, None] * state_now, axis=0))
    return (state_now, jnp.stack(outputs))


def selective_scan(step_sizes, step_inputs, b_rows, c_rows, keep_rows, decay_matrix):
    block_len = 16

    def advance(state_now, block_data):
        return jax.checkpoint(scan_block)(state_now, decay_matrix, block_data)

    blocks = tuple(
        (
            piece_array.reshape((-1, block_len) + piece_array.shape[1:])
            for piece_array in (step_sizes, step_inputs, b_rows, c_rows, keep_rows)
        )
    )
    start_state = jnp.zeros((b_rows.shape[1], step_inputs.shape[1]), jnp.float32)
    final_state, outputs = lax.scan(advance, start_state, blocks)
    return outputs.reshape(step_inputs.shape)


def mamba_core(
    conv_act, select_rows, step_pre, gate_in, step_shift, decay_matrix, skip_row, keep_rows
):
    step_sizes = jax.nn.softplus(step_pre + step_shift)
    scanned = selective_scan(
        step_sizes,
        conv_act,
        select_rows[:, :STATE],
        select_rows[:, STATE:],
        keep_rows,
        decay_matrix,
    )
    return (scanned + skip_row * conv_act) * jax.nn.silu(gate_in)


def join_branches(attn_rows, mamba_rows, attn_gain, mamba_gain):
    return 0.5 * (rms_scale(attn_rows, attn_gain) + rms_scale(mamba_rows, mamba_gain))


def swiglu(gate_rows, up_rows):
    return jax.nn.silu(gate_rows) * up_rows


def block_scores(query_block, start, key_rows, segments):
    block_rows = query_block.shape[0]
    places = jnp.arange(segments.shape[0], dtype=jnp.int32)
    query_places = start + jnp.arange(block_rows, dtype=jnp.int32)
    allowed = (segments[:, None] == segments[None, :]) & (places[None, :] <= query_places[:, None])
    scores = jnp.einsum(
        "tgrd,ugd->grtu", query_block, key_rows, preferred_element_type=jnp.float32
    ) * HEAD ** (-0.5)
    return jnp.where(allowed[None, None], scores, -1e30)


def attention_forward(queries, key_rows, value_rows, segments):
    row_count = queries.shape[0]
    block_rows = min(row_count, 512)
    query_blocks = queries.reshape((row_count // block_rows, block_rows) + queries.shape[1:])
    starts = jnp.arange(row_count // block_rows, dtype=jnp.int32) * block_rows

    def one_block(block_item):
        scores = block_scores(block_item[0], block_item[1], key_rows, segments)
        top_score = jnp.max(scores, axis=-1, keepdims=True)
        raised = jnp.exp(scores - top_score)
        exp_sum = jnp.sum(raised, axis=-1, keepdims=True)
        weights = (raised / exp_sum).astype(jnp.bfloat16)
        outputs = jnp.einsum(
            "grtu,ugd->tgrd", weights, value_rows, preferred_element_type=jnp.float32
        )
        return (outputs, top_score, exp_sum)

    outputs, top_scores, exp_sums = lax.map(one_block, (query_blocks, starts))
    return (outputs.reshape(row_count, -1), top_scores, exp_sums, query_blocks, starts)


def attention_backward(
    query_blocks, starts, key_rows, value_rows, segments, top_scores, exp_sums, out_grad
):
    row_count = key_rows.shape[0]
    grad_blocks = out_grad.reshape(query_blocks.shape)

    def one_block(carry_sums, block_item):
        key_acc, value_acc = carry_sums
        query_block, start, top_score, exp_sum, grad_block = block_item
        scores = block_scores(query_block, start, key_rows, segments)
        weights = jnp.exp(scores - top_score) / exp_sum
        weight_grad = jnp.einsum(
            "tgrd,ugd->grtu", grad_block, value_rows, preferred_element_type=jnp.float32
        )
        score_grad = (
            weights * (weight_grad - jnp.sum(weights * weight_grad, axis=-1, keepdims=True))
        ).astype(jnp.bfloat16)
        query_grad = jnp.einsum(
            "grtu,ugd->tgrd", score_grad, key_rows, preferred_element_type=jnp.float32
        ) * HEAD ** (-0.5)
        key_acc = key_acc + jnp.einsum(
            "grtu,tgrd->ugd", score_grad, query_block, preferred_element_type=jnp.float32
        ) * HEAD ** (-0.5)
        value_acc = value_acc + jnp.einsum(
            "grtu,tgrd->ugd",
            weights.astype(jnp.bfloat16),
            grad_block,
            preferred_element_type=jnp.float32,
        )
        return ((key_acc, value_acc), query_grad)

    zero_rows = jnp.zeros(key_rows.shape, jnp.float32)
    (key_grad, value_grad), query_grads = lax.scan(
        one_block, (zero_rows, zero_rows), (query_blocks, starts, top_scores, exp_sums, grad_blocks)
    )
    return (
        query_grads.reshape(row_count, -1),
        key_grad.reshape(row_count, -1),
        value_grad.reshape(row_count, -1),
    )


def shape_mixer(flat_list):
    return (
        flat_list[0].reshape(D, QKV),
        flat_list[1].reshape(D, 2 * INNER),
        flat_list[2].reshape(INNER, XPROJ),
        flat_list[3].reshape(RANK, INNER),
        flat_list[4].reshape(INNER, D),
        flat_list[5].reshape(D, D),
    )


def small_mixer(flat_list):
    return (
        flat_list[6].astype(jnp.float32).reshape(CONV, INNER),
        flat_list[7].astype(jnp.float32),
        flat_list[8].astype(jnp.float32),
        flat_list[9].astype(jnp.float32).reshape(STATE, INNER),
        flat_list[10].astype(jnp.float32),
        flat_list[11].astype(jnp.float32).reshape(4, D),
    )


def shape_ffn(flat_list):
    return (flat_list[0].reshape(D, FF), flat_list[1].reshape(D, FF), flat_list[2].reshape(FF, D))


def on_device(
    tokens,
    cotangent,
    seq_lengths,
    qkv_proj,
    mamba_in,
    select_proj,
    step_proj,
    mamba_out,
    join_out,
    conv_taps,
    conv_bias,
    step_bias,
    decay_rates,
    skip_gain,
    norm_gains,
    ffn_gate,
    ffn_up,
    ffn_down,
):
    mixer_flat = (
        lax.all_gather(qkv_proj, "fsdp", axis=0, tiled=True),
        lax.all_gather(mamba_in, "fsdp", axis=0, tiled=True),
        lax.all_gather(select_proj, "fsdp", axis=0, tiled=True),
        lax.all_gather(step_proj, "fsdp", axis=0, tiled=True),
        lax.all_gather(mamba_out, "fsdp", axis=0, tiled=True),
        lax.all_gather(join_out, "fsdp", axis=0, tiled=True),
        lax.all_gather(conv_taps, "fsdp", axis=0, tiled=True),
        lax.all_gather(conv_bias, "fsdp", axis=0, tiled=True),
        lax.all_gather(step_bias, "fsdp", axis=0, tiled=True),
        lax.all_gather(decay_rates, "fsdp", axis=0, tiled=True),
        lax.all_gather(skip_gain, "fsdp", axis=0, tiled=True),
        lax.all_gather(norm_gains, "fsdp", axis=0, tiled=True),
    )
    ffn_flat = (
        lax.all_gather(ffn_gate, "fsdp", axis=0, tiled=True),
        lax.all_gather(ffn_up, "fsdp", axis=0, tiled=True),
        lax.all_gather(ffn_down, "fsdp", axis=0, tiled=True),
    )
    qkv_matrix, mamba_in_matrix, select_matrix, step_matrix, mamba_out_matrix, join_matrix = (
        shape_mixer(mixer_flat)
    )
    tap_matrix, conv_shift, step_shift, decay_matrix, skip_row, gain_rows = small_mixer(mixer_flat)
    gate_matrix, up_matrix, down_matrix = shape_ffn(ffn_flat)
    row_count = tokens.shape[0]
    segments = segment_ids(seq_lengths, row_count)
    live_rows = (segments < seq_lengths.shape[0]).astype(jnp.float32)
    keep_rows = keep_flags(segments)
    inputs = tokens.astype(jnp.float32)
    normed_full, norm_pull = jax.vjp(rms_scale, inputs, gain_rows[0])
    normed = normed_full.astype(jnp.bfloat16)
    qkv_rows = flat_product(normed, qkv_matrix).astype(jnp.bfloat16)
    queries = qkv_rows[:, :D].reshape(row_count, KV_HEADS, HEADS // KV_HEADS, HEAD)
    key_rows = qkv_rows[:, D : D + KV_HEADS * HEAD].reshape(row_count, KV_HEADS, HEAD)
    value_rows = qkv_rows[:, D + KV_HEADS * HEAD :].reshape(row_count, KV_HEADS, HEAD)
    attn_rows, top_scores, exp_sums, query_blocks, starts = attention_forward(
        queries, key_rows, value_rows, segments
    )
    mixed_in = flat_product(normed, mamba_in_matrix)

    def conv_piece(inner_rows, tap_values, shift_values):
        return conv_silu(inner_rows, tap_values, shift_values, segments)

    conv_act, conv_pull = jax.vjp(conv_piece, mixed_in[:, :INNER], tap_matrix, conv_shift)
    conv_low = conv_act.astype(jnp.bfloat16)
    selected = flat_product(conv_low, select_matrix)
    step_low = selected[:, :RANK].astype(jnp.bfloat16)
    step_pre = flat_product(step_low, step_matrix)

    def core_piece(
        conv_values,
        select_values,
        step_values,
        gate_values,
        shift_values,
        decay_values,
        skip_values,
    ):
        return mamba_core(
            conv_values,
            select_values,
            step_values,
            gate_values,
            shift_values,
            decay_values,
            skip_values,
            keep_rows,
        )

    gated_full, core_pull = jax.vjp(
        core_piece,
        conv_act,
        selected[:, RANK:],
        step_pre,
        mixed_in[:, INNER:],
        step_shift,
        decay_matrix,
        skip_row,
    )
    gated = gated_full.astype(jnp.bfloat16)
    mamba_rows = flat_product(gated, mamba_out_matrix)
    joined_full, join_pull = jax.vjp(
        join_branches, attn_rows, mamba_rows, gain_rows[1], gain_rows[2]
    )
    joined = joined_full.astype(jnp.bfloat16)
    middle = inputs + flat_product(joined, join_matrix)
    normed_two_full, norm_two_pull = jax.vjp(rms_scale, middle, gain_rows[3])
    normed_two = normed_two_full.astype(jnp.bfloat16)
    gate_rows = flat_product(normed_two, gate_matrix)
    up_rows = flat_product(normed_two, up_matrix)
    act_full, act_pull = jax.vjp(swiglu, gate_rows, up_rows)
    activated = act_full.astype(jnp.bfloat16)
    result_rows = middle + flat_product(activated, down_matrix)
    block_out = (result_rows * live_rows[:, None]).astype(jnp.bfloat16)
    ffn_flat = (
        lax.all_gather(ffn_gate, "fsdp", axis=0, tiled=True),
        lax.all_gather(ffn_up, "fsdp", axis=0, tiled=True),
        lax.all_gather(ffn_down, "fsdp", axis=0, tiled=True),
    )
    gate_matrix, up_matrix, down_matrix = shape_ffn(ffn_flat)
    out_grad = cotangent.astype(jnp.float32) * live_rows[:, None]
    down_low = out_grad.astype(jnp.bfloat16)
    down_weight_grad = outer_sum(activated, down_low)
    gate_grad, up_grad = act_pull(back_product(down_low, down_matrix))
    gate_low = gate_grad.astype(jnp.bfloat16)
    up_low = up_grad.astype(jnp.bfloat16)
    gate_weight_grad = outer_sum(normed_two, gate_low)
    up_weight_grad = outer_sum(normed_two, up_low)
    middle_norm_grad, ffn_gain_grad = norm_two_pull(
        back_product(gate_low, gate_matrix) + back_product(up_low, up_matrix)
    )
    middle_grad = out_grad + middle_norm_grad
    ffn_sums = (
        lax.psum_scatter(gate_weight_grad.reshape(-1), "fsdp", scatter_dimension=0, tiled=True),
        lax.psum_scatter(up_weight_grad.reshape(-1), "fsdp", scatter_dimension=0, tiled=True),
        lax.psum_scatter(down_weight_grad.reshape(-1), "fsdp", scatter_dimension=0, tiled=True),
    )
    mixer_flat = (
        lax.all_gather(qkv_proj, "fsdp", axis=0, tiled=True),
        lax.all_gather(mamba_in, "fsdp", axis=0, tiled=True),
        lax.all_gather(select_proj, "fsdp", axis=0, tiled=True),
        lax.all_gather(step_proj, "fsdp", axis=0, tiled=True),
        lax.all_gather(mamba_out, "fsdp", axis=0, tiled=True),
        lax.all_gather(join_out, "fsdp", axis=0, tiled=True),
        lax.all_gather(conv_taps, "fsdp", axis=0, tiled=True),
        lax.all_gather(conv_bias, "fsdp", axis=0, tiled=True),
        lax.all_gather(step_bias, "fsdp", axis=0, tiled=True),
        lax.all_gather(decay_rates, "fsdp", axis=0, tiled=True),
        lax.all_gather(skip_gain, "fsdp", axis=0, tiled=True),
        lax.all_gather(norm_gains, "fsdp", axis=0, tiled=True),
    )
    qkv_matrix, mamba_in_matrix, select_matrix, step_matrix, mamba_out_matrix, join_matrix = (
        shape_mixer(mixer_flat)
    )
    join_low = middle_grad.astype(jnp.bfloat16)
    join_weight_grad = outer_sum(joined, join_low)
    attn_grad, mamba_grad, attn_gain_grad, mamba_gain_grad = join_pull(
        back_product(join_low, join_matrix)
    )
    mamba_low = mamba_grad.astype(jnp.bfloat16)
    mamba_out_weight_grad = outer_sum(gated, mamba_low)
    (
        conv_core_grad,
        select_part_grad,
        step_pre_grad,
        gate_in_grad,
        step_shift_grad,
        decay_grad,
        skip_grad,
    ) = core_pull(back_product(mamba_low, mamba_out_matrix))
    step_low_grad = step_pre_grad.astype(jnp.bfloat16)
    step_weight_grad = outer_sum(step_low, step_low_grad)
    select_low = jnp.concatenate(
        [back_product(step_low_grad, step_matrix), select_part_grad], axis=1
    ).astype(jnp.bfloat16)
    select_weight_grad = outer_sum(conv_low, select_low)
    conv_grad = conv_core_grad + back_product(select_low, select_matrix)
    conv_in_grad, taps_grad, conv_shift_grad = conv_pull(conv_grad)
    mixed_low = jnp.concatenate([conv_in_grad, gate_in_grad], axis=1).astype(jnp.bfloat16)
    mamba_in_weight_grad = outer_sum(normed, mixed_low)
    query_grad, key_grad, value_grad = attention_backward(
        query_blocks,
        starts,
        key_rows,
        value_rows,
        segments,
        top_scores,
        exp_sums,
        attn_grad.astype(jnp.bfloat16),
    )
    qkv_low = jnp.concatenate([query_grad, key_grad, value_grad], axis=1).astype(jnp.bfloat16)
    qkv_weight_grad = outer_sum(normed, qkv_low)
    normed_grad = back_product(qkv_low, qkv_matrix) + back_product(mixed_low, mamba_in_matrix)
    input_norm_grad, input_gain_grad = norm_pull(normed_grad)
    input_grad = middle_grad + input_norm_grad
    gain_grads = jnp.stack(
        [input_gain_grad, attn_gain_grad, mamba_gain_grad, ffn_gain_grad]
    ).reshape(-1)
    mixer_sums = (
        lax.psum_scatter(qkv_weight_grad.reshape(-1), "fsdp", scatter_dimension=0, tiled=True),
        lax.psum_scatter(mamba_in_weight_grad.reshape(-1), "fsdp", scatter_dimension=0, tiled=True),
        lax.psum_scatter(select_weight_grad.reshape(-1), "fsdp", scatter_dimension=0, tiled=True),
        lax.psum_scatter(step_weight_grad.reshape(-1), "fsdp", scatter_dimension=0, tiled=True),
        lax.psum_scatter(
            mamba_out_weight_grad.reshape(-1), "fsdp", scatter_dimension=0, tiled=True
        ),
        lax.psum_scatter(join_weight_grad.reshape(-1), "fsdp", scatter_dimension=0, tiled=True),
        lax.psum_scatter(taps_grad.reshape(-1), "fsdp", scatter_dimension=0, tiled=True),
        lax.psum_scatter(conv_shift_grad, "fsdp", scatter_dimension=0, tiled=True),
        lax.psum_scatter(step_shift_grad, "fsdp", scatter_dimension=0, tiled=True),
        lax.psum_scatter(decay_grad.reshape(-1), "fsdp", scatter_dimension=0, tiled=True),
        lax.psum_scatter(skip_grad, "fsdp", scatter_dimension=0, tiled=True),
        lax.psum_scatter(gain_grads, "fsdp", scatter_dimension=0, tiled=True),
    )
    return (block_out, input_grad) + tuple(mixer_sums) + tuple(ffn_sums)


PLANES = 4
CHIPS = 4
CORES = 2
PLANE_DEV = CHIPS * CORES
FAST_DEV = PLANES * PLANE_DEV
RING = (0, 1, 3, 2)
MAIN_D = 48
MAIN_I = 96
SLICE_FF = FF // FAST_DEV
PAD_FF = 176
HALF_GU = 768
WIDE = 8704
GU = 2 * HALF_GU
REST_ROWS = 224
SMALL_ROWS = 208
LANES = 640
BIG = 1e30
LOG2E = 1.4426950408889634


def ring_place(k):
    return k + k // 2 - 2 * (k // 3)


class Links:
    def __init__(self, send_sems, recv_sems):
        me = lax.axis_index("fsdp")
        self.z, self.v, self.c = me // PLANE_DEV, (me // CORES) % CHIPS, me % CORES
        zp, vp = ring_place(self.z), ring_place(self.v)
        self.z_at = [ring_place((zp + k) % PLANES) for k in range(PLANES)]
        self.v_at = [ring_place((vp + k) % CHIPS) for k in range(CHIPS)]
        z, v, c = self.z, self.v, self.c
        self.z_next = self.z_at[1] * PLANE_DEV + v * CORES + c
        self.z_prev = self.z_at[3] * PLANE_DEV + v * CORES + c
        self.right = z * PLANE_DEV + self.v_at[1] * CORES + c
        self.left = z * PLANE_DEV + self.v_at[3] * CORES + c
        self.partner = me + 1 - 2 * c
        self.sems = send_sems, recv_sems
        self.copies = []

    def greet(self):
        barrier = pltpu.get_barrier_semaphore()
        greeted = (self.right, self.left, self.z_next, self.z_prev, self.partner)
        for d in greeted:
            pl.semaphore_signal(barrier, inc=1, device_id=(d,), device_id_type=pl.DeviceIdType.MESH)
        pl.semaphore_wait(barrier, len(greeted))

    def send(self, src, dst, target):
        k = len(self.copies)
        copy = pltpu.make_async_remote_copy(
            src_ref=src, dst_ref=dst, send_sem=self.sems[0].at[k], recv_sem=self.sems[1].at[k],
            device_id=(target,), device_id_type=pl.DeviceIdType.MESH,
        )
        copy.start()
        self.copies.append(copy)
        return copy

    def finish(self):
        for copy in self.copies:
            copy.wait_send()


class Gather:
    def __init__(self, links, source, place, local_sem):
        self.links, self.source, self.place = links, source, place
        self.along, self.near_in, self.far_in, self.core_in = {}, {}, {}, []
        self.own = pltpu.make_async_copy(source, self.block(0, OWN), local_sem)
        self.own.start()

    def block(self, back, chip):
        links = self.links
        return self.place(links.z_at[(PLANES - back) % PLANES], links.v_at[chip], links.c)

    def to_core(self, src, dst):
        self.core_in.append(self.links.send(src, dst, self.links.partner))

    def hop(self, s):
        links, here = self.links, self.block(s, OWN)
        if s:
            self.along[s - 1].wait_recv()
        src = here if s else self.source
        if s < PLANES - 1:
            self.along[s] = links.send(src, here, links.z_next)
        self.near_in[s, LEFT] = links.send(src, here, links.right)
        self.near_in[s, RIGHT] = links.send(src, here, links.left)
        self.to_core(src, here)

    def near(self, s):
        links = self.links
        for chip in (LEFT, RIGHT):
            self.near_in[s, chip].wait_recv()
            here = self.block(s, chip)
            if (chip == LEFT) == (s < 2):
                self.far_in[s] = links.send(here, here, links.right if chip == LEFT else links.left)
            self.to_core(here, here)

    def far(self, s):
        self.far_in[s].wait_recv()
        here = self.block(s, FAR)
        self.to_core(here, here)

    def wait(self):
        self.own.wait()
        for copy in self.core_in:
            copy.wait_recv()


GATHER_SENDS = 31
OWN, RIGHT, FAR, LEFT = range(CHIPS)


def shard_place(name, out):
    if name == "mamba_out":
        return lambda z, v, c: out.at[(z // 2) * 16 + c * 8 + (z % 2) * 4 + v]
    if name == "smalls":
        return lambda z, v, c: out.at[z * PLANE_DEV + v * CORES + c]
    return lambda z, v, c: out.at[c * 16 + z * 4 + v]


def gather_first_kernel(names, *refs):
    count = len(names)
    ins, units, outs, moved = refs[:count], refs[count : count + 2], refs[count + 2 : 2 * count + 2], refs[2 * count + 2 :]
    moved, (send_sems, recv_sems, local) = moved[:4], moved[4:]
    links = Links(send_sems, recv_sems)
    links.greet()
    gathers = [Gather(links, ins[k], shard_place(names[k], outs[k]), local.at[k]) for k in range(count)]
    for s in range(PLANES):
        for g in gathers:
            g.hop(s)
    hops = [links.send(units[k], moved[2 * k], links.z_next) for k in range(2)]
    for s in range(PLANES):
        for g in gathers:
            g.near(s)
    for s in range(PLANES):
        for g in gathers:
            g.far(s)
        if s == 1:
            for k in range(2):
                hops[k].wait_recv()
                hops.append(links.send(moved[2 * k], moved[2 * k + 1], links.z_next))
    for g in gathers:
        g.wait()
    for copy in hops[2:]:
        copy.wait_recv()
    links.finish()


def gather_first(names, blocks, units):
    count, sends = len(names), GATHER_SENDS * len(names) + 4
    sem, anywhere = pltpu.SemaphoreType.DMA, pl.BlockSpec(memory_space=pl.ANY)
    shapes = [(FAST_DEV,) + block.shape for block in blocks] + [u.shape for u in units for _ in range(2)]
    return pl.pallas_call(
        functools.partial(gather_first_kernel, names),
        out_shape=[jax.ShapeDtypeStruct(shape, jnp.bfloat16) for shape in shapes],
        in_specs=[anywhere] * (count + 2),
        out_specs=[anywhere] * (count + 4),
        scratch_shapes=[sem((sends,))] * 2 + [sem((count,))],
        compiler_params=pltpu.CompilerParams(collective_id=0, has_side_effects=True),
        name="gather_first",
    )(*blocks, *units)


REST_COLUMNS = 1152
WIDE_BLOCKS = [(0, 7 * REST_COLUMNS, WIDE - 7 * REST_COLUMNS)] + [(0, k * REST_COLUMNS, REST_COLUMNS) for k in range(7)]
BRANCH_BLOCKS = [(0, 0, 768), (0, 768, 832), (1, 0, 768), (1, 768, 832)]
SUM_LAGS = (2, 3, 4, 5, 6)
GRAD_ROWS = 192
GROUPS = PLANES * CHIPS
GAIN_LANES = 256


def add_rows(target, *others):
    @pl.loop(0, target.shape[0] // 16)
    def _(k):
        rows = pl.ds(pl.multiple_of(k * 16, 16), 16)
        total = target[rows, :].astype(jnp.float32)
        for other in others:
            total = total + other[rows, :].astype(jnp.float32)
        target[rows, :] = total.astype(target.dtype)


class Taker:
    def __init__(self, refs):
        self.refs = list(refs)

    def __call__(self, count):
        taken, self.refs = self.refs[:count], self.refs[count:]
        return taken


class SumPlan:
    def __init__(self, blocks, shard_rows, rest_rows, rest_columns, columns, rests, lows, smalls=None):
        self.blocks, self.rest_rows, self.has_smalls = blocks, rest_rows, smalls is not None
        self.operands = list(columns) + list(rests) + list(lows) + ([smalls] if self.has_smalls else [])
        f32, bf16 = jnp.float32, jnp.bfloat16
        self.pairs, rows = len(lows), lows[0].shape[0]
        self.out_shape = [jax.ShapeDtypeStruct((r, y.shape[1]), f32) for r, y in zip(shard_rows, lows)]
        self.out_shape.append(jax.ShapeDtypeStruct((16, rest_columns), f32))
        scratch = [pltpu.VMEM((x.shape[0] * x.shape[1] // CORES, CORES * rows), bf16) for x in columns]
        scratch += [pltpu.VMEM((x.shape[1], CORES * rows), bf16) for x in rests]
        scratch += [pltpu.VMEM((CORES * rows, y.shape[1]), bf16) for y in lows]
        scratch.append(pltpu.VMEM((16 * GROUPS, rest_columns), f32))
        shapes = [(shard_rows[pair], n) for pair, _, n in blocks] + [(16, rest_columns)]
        if self.has_smalls:
            shapes.append((smalls.shape[1] // GROUPS, smalls.shape[2]))
            scratch.append(pltpu.VMEM(smalls.shape[1:], bf16))
            self.out_shape.append(jax.ShapeDtypeStruct(shapes[-1], f32))
        for copies in (0, 4, 4, 4, 3):
            scratch += [pltpu.VMEM((copies, r, n) if copies else (GROUPS * r, n), bf16) for r, n in shapes]
        sem = pltpu.SemaphoreType.DMA
        self.count = len(shapes)
        scratch += [sem((self.count, k)) for k in (4, 4, 8, 8, 3, 3)] + [sem((self.pairs, 5))] * 3
        self.scratch = scratch


class Summing:
    def __init__(self, plan, links, ins, totals, scratch):
        self.blocks, self.rest_rows, self.has_smalls = plan.blocks, plan.rest_rows, plan.has_smalls
        self.pairs, self.count = plan.pairs, plan.count
        self.links = links
        take = Taker(ins)
        self.columns_in, self.rests_in, self.lows_in = take(self.pairs), take(self.pairs), take(self.pairs)
        self.smalls_in = take(int(self.has_smalls))
        take = Taker(totals)
        self.totals, self.rest_total = take(self.pairs), take(1)[0]
        self.smalls_total = take(int(self.has_smalls))
        take = Taker(scratch)
        self.columns_all, self.rests_all, self.lows_all = take(self.pairs), take(self.pairs), take(self.pairs)
        self.rest_stage, self.smalls_stage = take(1)[0], take(int(self.has_smalls))
        self.partial, self.through, self.from_left, self.from_right, self.along = [take(self.count) for _ in range(5)]
        self.t_send, self.t_recv, self.s_send, self.s_recv, self.z_send, self.z_recv = take(6)
        self.c_send, self.c_recv, self.local = take(3)
        self.rest_at, self.smalls_at = len(self.blocks), len(self.blocks) + 1
        self.group_rows = [p.shape[0] // GROUPS for p in self.partial]
        self.sent, self.own, self.arriving = [], [], {}
        self.extra_rest = None
        self.order = list(range(len(self.blocks)))
        if self.has_smalls:
            self.order.insert(2, self.smalls_at)
        self.order.append(self.rest_at)
        self.step_now = 0

    def send(self, key, src, dst, ss, rs, target):
        copy = pltpu.make_async_remote_copy(
            src_ref=src, dst_ref=dst, send_sem=ss, recv_sem=rs, device_id=(target,),
            device_id_type=pl.DeviceIdType.MESH,
        )
        copy.start()
        self.sent.append(copy)
        self.arriving[key] = copy

    def stay(self, src, dst, sem):
        copy = pltpu.make_async_copy(src, dst, sem)
        copy.start()
        self.own.append(copy)

    def exchange(self):
        c, partner = self.links.c, self.links.partner
        c_send, c_recv, local = self.c_send, self.c_recv, self.local
        for k in range(self.pairs):
            columns_in, columns_all = self.columns_in[k], self.columns_all[k]
            lows_in, rests_in = self.lows_in[k], self.rests_in[k]
            rows = lows_in.shape[0]
            half = columns_in.shape[1] // CORES
            mine, other = pl.ds(0, rows), pl.ds(rows, rows)
            self.stay(lows_in, self.lows_all[k].at[mine], local.at[k, 0])
            self.send(("l", k), lows_in, self.lows_all[k].at[other], c_send.at[k, 0], c_recv.at[k, 0], partner)
            self.stay(rests_in.at[c], self.rests_all[k].at[:, mine], local.at[k, 1])
            self.send(
                ("r", k), rests_in.at[1 - c], self.rests_all[k].at[:, other], c_send.at[k, 1], c_recv.at[k, 1], partner
            )
            for h in range(columns_in.shape[0]):
                place = pl.ds(h * half, half)
                self.stay(
                    columns_in.at[h, pl.ds(pl.multiple_of(c * half, half), half)],
                    columns_all.at[place, mine],
                    local.at[k, 2 + h],
                )
                self.send(
                    ("x", k, h),
                    columns_in.at[h, pl.ds(pl.multiple_of((1 - c) * half, half), half)],
                    columns_all.at[place, other],
                    c_send.at[k, 2 + h],
                    c_recv.at[k, 2 + h],
                    partner,
                )
        if self.has_smalls:
            smalls = self.smalls_in[0]
            self.stay(smalls.at[c], self.partial[self.smalls_at], local.at[0, 4])
            self.send(("m",), smalls.at[1 - c], self.smalls_stage[0], c_send.at[0, 4], c_recv.at[0, 4], partner)

    def exchanged(self):
        for copy in self.own:
            copy.wait()
        for k in range(self.pairs):
            self.arriving["l", k].wait_recv()
            self.arriving["r", k].wait_recv()
            for h in range(self.columns_in[k].shape[0]):
                self.arriving["x", k, h].wait_recv()

    def rest_block(self):
        stage = self.rest_stage
        stage[...] = jnp.zeros_like(stage)
        row, width = 0, stage.shape[1]
        for k in range(self.pairs):
            r, lows = self.rest_rows[k], self.lows_all[k]
            for column in range(0, lows.shape[1], width):
                columns = min(width, lows.shape[1] - column)
                product = flat_product(self.rests_all[k][...], lows[:, column : column + columns])
                for g in range(GROUPS):
                    at = 16 * g + row
                    stage[at : at + r, :columns] = product[g * r : (g + 1) * r]
                row += r
        if self.extra_rest is not None:
            self.extra_rest(stage)
        self.partial[self.rest_at][...] = stage[...].astype(jnp.bfloat16)

    def compute(self, i):
        partial = self.partial[i]
        if i == self.rest_at:
            self.rest_block()
            return
        if i == self.smalls_at:
            self.arriving["m",].wait_recv()
            add_rows(partial, self.smalls_stage[0])
            return
        pair, column, columns = self.blocks[i]

        @pl.loop(0, partial.shape[0] // GRAD_ROWS)
        def _(j):
            rows = pl.ds(pl.multiple_of(j * GRAD_ROWS, GRAD_ROWS), GRAD_ROWS)
            partial[rows, :] = flat_product(
                self.columns_all[pair][rows, :], self.lows_all[pair][:, pl.ds(column, columns)]
            ).astype(jnp.bfloat16)

    def part(self, i, k, chip):
        rows = self.group_rows[i]
        at = (self.links.z_at[k] * CHIPS + self.links.v_at[chip]) * rows
        return self.partial[i].at[pl.ds(pl.multiple_of(at, rows), rows)]

    def launch(self, i):
        right, left = self.links.right, self.links.left
        self.compute(i)
        for k in (3, 2, 1, 0):
            far, direct = (right, left) if k % 2 else (left, right)
            self.send(
                (i, "t", k), self.part(i, k, FAR), self.through[i].at[k], self.t_send.at[i, k], self.t_recv.at[i, k], far
            )
            landing, event = (self.from_right, 4 + k) if k % 2 else (self.from_left, k)
            self.send(
                (i, "s", event), self.part(i, k, LEFT if k % 2 else RIGHT), landing[i].at[k],
                self.s_send.at[i, event], self.s_recv.at[i, event], direct,
            )

    def relay(self, i):
        for k in (3, 2, 1, 0):
            self.arriving[i, "t", k].wait_recv()
            add_rows(self.through[i].at[k], self.part(i, k, RIGHT if k % 2 else LEFT))
            landing, event = (self.from_left, k) if k % 2 else (self.from_right, 4 + k)
            self.send(
                (i, "s", event), self.through[i].at[k], landing[i].at[k], self.s_send.at[i, event],
                self.s_recv.at[i, event], self.links.right if k % 2 else self.links.left,
            )

    def pass_on(self, i, k):
        self.send(
            (i, "z", 3 - k), self.part(i, k, OWN), self.along[i].at[3 - k], self.z_send.at[i, 3 - k],
            self.z_recv.at[i, 3 - k], self.links.z_next,
        )

    def collect(self, i):
        for k in (3, 2, 1, 0):
            self.arriving[i, "s", k].wait_recv()
            self.arriving[i, "s", 4 + k].wait_recv()
            add_rows(self.part(i, k, OWN), self.from_left[i].at[k], self.from_right[i].at[k])
            if k == 3:
                self.pass_on(i, 3)

    def planes(self, i, k):
        self.arriving[i, "z", 2 - k].wait_recv()
        mine, along = self.part(i, k, OWN), self.along[i]
        if k:
            add_rows(mine, along.at[2 - k])
            self.pass_on(i, k)
            return
        if i == self.rest_at:
            total, column, columns = self.rest_total, 0, self.rest_total.shape[1]
        elif i == self.smalls_at:
            total, column, columns = self.smalls_total[0], 0, self.smalls_total[0].shape[1]
        else:
            pair, column, columns = self.blocks[i]
            total = self.totals[pair]

        @pl.loop(0, self.group_rows[i] // 16)
        def _(j):
            rows = pl.ds(pl.multiple_of(j * 16, 16), 16)
            total[rows, pl.ds(column, columns)] = mine[rows, :].astype(jnp.float32) + along[2, rows, :].astype(
                jnp.float32
            )

    def step(self):
        stages = (
            self.relay, self.collect, lambda i: self.planes(i, 2), lambda i: self.planes(i, 1), lambda i: self.planes(i, 0),
        )
        now, self.step_now = self.step_now, self.step_now + 1
        if now < self.count:
            self.launch(self.order[now])
        for lag, stage in zip(SUM_LAGS, stages):
            if 0 <= now - lag < self.count:
                stage(self.order[now - lag])

    def finish(self):
        while self.step_now < self.count + SUM_LAGS[-1]:
            self.step()
        for copy in self.sent:
            copy.wait_send()


UNIT_PAD = 64
BACK_LANES = 512


def last_kernel(plan, *refs):
    bf16, f32 = jnp.bfloat16, jnp.float32
    take = Taker(refs)
    ins = take(len(plan.operands))
    middle_grad_ref, tokens_ref, gains_ref, table_d_ref, wide_ref, wide_rest_ref = take(6)
    gu_grad_ref, down_grad_ref, gu_came_ref, down_came_ref = take(4)
    totals = take(len(plan.out_shape))
    input_grad_ref, gu_out_ref, down_out_ref = take(3)
    scratch = take(len(plan.scratch))
    order, wide_buffer, total, gain, gain_other = take(5)
    gu_own, gu_sum, gu_next, down_own, down_sum, down_next, gu_rows, gu_send = take(8)
    wide_sem, unit_sem, send_sems, recv_sems = take(4)
    count = WIDE // BACK_LANES
    links = Links(send_sems, recv_sems)
    me = lax.axis_index("fsdp")
    first = me // PLANE_DEV * PLANE_DEV
    others = [first + (me % PLANE_DEV + k) % PLANE_DEV for k in range(1, PLANE_DEV)]
    barrier = pltpu.get_barrier_semaphore()
    for d in others + [links.z_next, links.z_prev]:
        pl.semaphore_signal(barrier, inc=1, device_id=(d,), device_id_type=pl.DeviceIdType.MESH)
    pl.semaphore_wait(barrier, len(others) + 2)

    summing = Summing(plan, links, ins, totals, scratch)
    summing.exchange()
    gu_height, down_height = gu_own.shape[0], down_own.shape[0]
    wide_low = summing.lows_all[0].at[pl.ds(0, tokens_ref.shape[0])]

    def piece(ref, height, k):
        return ref.at[pl.ds(pl.multiple_of(links.z_at[k] * height, 16), height)]

    middle_copy = pltpu.make_async_copy(middle_grad_ref, input_grad_ref, unit_sem.at[4])
    middle_copy.start()
    loads = [
        pltpu.make_async_copy(gu_came_ref, gu_sum, unit_sem.at[0]),
        pltpu.make_async_copy(down_came_ref, down_sum, unit_sem.at[1]),
    ]
    def load_own(k):
        copies = [
            pltpu.make_async_copy(piece(gu_grad_ref, gu_height, k), gu_own, unit_sem.at[2]),
            pltpu.make_async_copy(piece(down_grad_ref, down_height, k), down_own, unit_sem.at[3]),
        ]
        for copy in copies:
            copy.start()
        return copies

    loads += load_own(1)
    for copy in loads[:2]:
        copy.start()
    def column_copy(j):
        return pltpu.make_async_copy(
            wide_ref.at[:, pl.ds(j * BACK_LANES, BACK_LANES)], wide_buffer.at[j % 2], wide_sem.at[j % 2]
        )

    column_copy(0).start()
    column_copy(1).start()
    summing.exchanged()
    summing.step()
    summing.step()
    for copy in loads:
        copy.wait()
    add_rows(gu_sum, gu_own)
    add_rows(down_sum, down_own)
    loads = load_own(0)
    hops = [links.send(gu_sum, gu_next, links.z_next), links.send(down_sum, down_next, links.z_next)]

    write_order(table_d_ref, order)
    total[...] = jnp.zeros_like(total)
    for j in range(count):
        column_copy(j).wait()
        total[...] += back_product(wide_low[:, j * BACK_LANES : (j + 1) * BACK_LANES], wide_buffer[j % 2])
        if j + 2 < count:
            column_copy(j + 2).start()
        if j % 6 == 5:
            summing.step()
    normed_grad = move_back(
        order, jnp.concatenate([total[...], back_product(wide_low[...], wide_rest_ref[...])], axis=1)
    )
    unit, scale = rms_parts(tokens_ref[...].astype(f32))
    back, gain_grad = rms_pull(unit, scale, gains_ref[0:1], normed_grad)
    middle_copy.wait()
    input_grad_ref[...] += back
    gain[...] = jnp.broadcast_to(gain_grad, gain.shape)
    gain_copy = links.send(gain, gain_other, links.partner)
    summing.step()

    def gain_rows(stage):
        gain_copy.wait_recv()
        size = 4 * D // FAST_DEV
        lane = lax.broadcasted_iota(jnp.int32, (D, CHIPS * GAIN_LANES), 1)
        source = (lane // GAIN_LANES) * (CORES * size) + links.c * size + lane % GAIN_LANES
        place = lax.broadcasted_iota(jnp.int32, (D, CHIPS * GAIN_LANES), 0)
        picks = (place == source) & (lane % GAIN_LANES < size)
        select = order.at[:, pl.ds(0, CHIPS * GAIN_LANES)]
        select[...] = jnp.where(picks, 1.0, 0.0).astype(bf16)
        both = gain[0:1] + gain_other[0:1]
        both = jnp.broadcast_to(both, (16, D))
        high = both.astype(bf16)
        rest = (both - high.astype(f32)).astype(bf16)
        moved = flat_product(high, select[...]) + flat_product(rest, select[...])
        width, last = stage.shape[1], WIDE % REST_COLUMNS
        for v in range(CHIPS):
            stage[16 * v + 14 : 16 * v + 15, last : last + GAIN_LANES] = moved[
                0:1, v * GAIN_LANES : (v + 1) * GAIN_LANES
            ]

    summing.extra_rest = gain_rows
    summing.step()
    for copy in hops:
        copy.wait_recv()
    for copy in loads:
        copy.wait()
    rows = D // FAST_DEV

    for quarter in range(4):
        lanes = pl.ds(quarter * (GU // 4), GU // 4)

        @pl.loop(0, gu_height // 16)
        def _(k):
            some = pl.ds(pl.multiple_of(k * 16, 16), 16)
            gu_rows[some, :] = gu_own[some, lanes].astype(f32) + gu_next[some, lanes].astype(f32)

        for p in range(PLANE_DEV):
            gu_send[p, :, lanes] = gu_rows[p * rows : p * rows + UNIT_PAD, :].astype(bf16)

    @pl.loop(0, down_height // 16)
    def _(k):
        some = pl.ds(pl.multiple_of(k * 16, 16), 16)
        down_out_ref[some, :] = down_own[some, :].astype(f32) + down_next[some, :].astype(f32)

    keep = pltpu.make_async_copy(gu_send.at[me % PLANE_DEV], gu_out_ref.at[me % PLANE_DEV], unit_sem.at[6])
    keep.start()
    given = [links.send(gu_send.at[d % PLANE_DEV], gu_out_ref.at[me % PLANE_DEV], d) for d in others]
    summing.finish()
    for copy in given:
        copy.wait_recv()
    keep.wait()
    links.finish()


def last_sums(plan, *operands):
    bf16, f32 = jnp.bfloat16, jnp.float32
    rows, gu_came, down_came = operands[0].shape[0], operands[8], operands[9]
    vmem, anywhere = pl.BlockSpec(memory_space=pltpu.VMEM), pl.BlockSpec(memory_space=pl.ANY)
    in_specs = [anywhere] * len(plan.operands) + [anywhere] + [vmem] * 3 + [anywhere, vmem] + [anywhere] * 4
    out_shape = plan.out_shape + [
        jax.ShapeDtypeStruct((rows, D), f32),
        jax.ShapeDtypeStruct((PLANE_DEV, UNIT_PAD, GU), bf16),
        jax.ShapeDtypeStruct(down_came.shape, f32),
    ]
    unit, downs = gu_came.shape, down_came.shape
    pad = (unit[0] + UNIT_PAD, unit[1] // 4)
    sem = pltpu.SemaphoreType.DMA
    return pl.pallas_call(
        functools.partial(last_kernel, plan),
        out_shape=out_shape,
        in_specs=in_specs,
        out_specs=[vmem] * (len(plan.out_shape) + 1) + [anywhere, vmem],
        scratch_shapes=plan.scratch
        + [
            pltpu.VMEM((D, D), bf16),
            pltpu.VMEM((2, MAIN, BACK_LANES), bf16),
            pltpu.VMEM((rows, MAIN), f32),
            pltpu.VMEM((8, D), f32),
            pltpu.VMEM((8, D), f32),
            pltpu.VMEM(unit, bf16),
            pltpu.VMEM(unit, bf16),
            pltpu.VMEM(unit, bf16),
            pltpu.VMEM(downs, bf16),
            pltpu.VMEM(downs, bf16),
            pltpu.VMEM(downs, bf16),
            pltpu.VMEM(pad, f32),
            pltpu.VMEM((PLANE_DEV, UNIT_PAD, GU), bf16),
            sem((2,)),
            sem((7,)),
            sem((10,)),
            sem((10,)),
        ],
        compiler_params=pltpu.CompilerParams(
            collective_id=3, has_side_effects=True, vmem_limit_bytes=63 * 1024 * 1024
        ),
        name="last_sums",
    )(*plan.operands, *operands)


def scan_setup(pre, shift, conv, hold):
    step = jax.nn.softplus(pre + shift)
    return step, step + hold, step * conv


def tiled(block):
    return jnp.concatenate([block] * (LANES // 128), axis=1)


def folded(block):
    total = block[:, :128]
    for k in range(1, LANES // 128):
        total = total + block[:, 128 * k : 128 * (k + 1)]
    return total


GROUP = HEADS // KV_HEADS


def group_scores(qkv_ref, seg_col_ref, seg_row_ref, g):
    rows = qkv_ref.shape[0]
    queries = jnp.concatenate(
        [qkv_ref[:, (g * GROUP + r) * HEAD : (g * GROUP + r + 1) * HEAD] for r in range(GROUP)], axis=0
    )
    keys = qkv_ref[:, D + g * HEAD : D + (g + 1) * HEAD]
    values = qkv_ref[:, D + (KV_HEADS + g) * HEAD : D + (KV_HEADS + g + 1) * HEAD]
    scores = back_product(queries, keys) * HEAD ** (-0.5)
    t = lax.broadcasted_iota(jnp.int32, (rows, rows), 0)
    u = lax.broadcasted_iota(jnp.int32, (rows, rows), 1)
    allowed = (seg_col_ref[...] == seg_row_ref[...]) & (u <= t)
    scores = jnp.where(jnp.concatenate([allowed] * GROUP, axis=0), scores, -1e30)
    raised = jnp.exp(scores - jnp.max(scores, axis=-1, keepdims=True))
    probs = raised / jnp.sum(raised, axis=-1, keepdims=True)
    return queries, keys, values, probs


def attention_forward_kernel(qkv_ref, seg_col_ref, seg_row_ref, out_ref):
    rows = qkv_ref.shape[0]
    for g in range(KV_HEADS):
        _, _, values, probs = group_scores(qkv_ref, seg_col_ref, seg_row_ref, g)
        mixed = flat_product(probs.astype(jnp.bfloat16), values)
        for r in range(GROUP):
            head = g * GROUP + r
            out_ref[:, head * HEAD : (head + 1) * HEAD] = mixed[r * rows : (r + 1) * rows]


def attention_backward_kernel(qkv_ref, seg_col_ref, seg_row_ref, grad_ref, low_ref, first):
    rows = qkv_ref.shape[0]
    bf16 = jnp.bfloat16
    for g in range(KV_HEADS):
        queries, keys, values, probs = group_scores(qkv_ref, seg_col_ref, seg_row_ref, g)
        grads = jnp.concatenate(
            [grad_ref[:, (g * GROUP + r) * HEAD : (g * GROUP + r + 1) * HEAD] for r in range(GROUP)], axis=0
        )
        prob_grad = back_product(grads, values)
        score_low = (
            probs * (prob_grad - jnp.sum(probs * prob_grad, axis=-1, keepdims=True))
        ).astype(bf16)
        query_grad = (flat_product(score_low, keys) * HEAD ** (-0.5)).astype(bf16)
        for r in range(GROUP):
            head = g * GROUP + r
            low_ref[:, first + head * HEAD : first + (head + 1) * HEAD] = query_grad[r * rows : (r + 1) * rows]
        key_grad = outer_sum(score_low, queries) * HEAD ** (-0.5)
        low_ref[:, first + D + g * HEAD : first + D + (g + 1) * HEAD] = key_grad.astype(bf16)
        value_grad = outer_sum(probs.astype(bf16), grads)
        low_ref[:, first + D + (KV_HEADS + g) * HEAD : first + D + (KV_HEADS + g + 1) * HEAD] = value_grad.astype(bf16)


GRAD_LANES = 256


class PlaneTotal:
    def __init__(self, links, parts, core_in, far_in, near_in):
        self.links, self.parts, self.core_in, self.far_in, self.near_in = links, parts, core_in, far_in, near_in
        self.top = pl.ds(0, parts.shape[1] // 2)
        self.low = pl.ds(parts.shape[1] // 2, parts.shape[1] // 2)
        self.core = {}

    def give(self, chip):
        self.core[chip] = self.links.send(self.parts.at[CHIPS + chip], self.core_in.at[chip], self.links.partner)

    def join(self, chip):
        self.core[chip].wait_recv()
        add_rows(self.parts.at[chip], self.core_in.at[chip])

    def start(self):
        links, parts = self.links, self.parts
        self.join(FAR)
        self.far = [
            links.send(parts.at[FAR, self.top], self.far_in.at[0], links.right),
            links.send(parts.at[FAR, self.low], self.far_in.at[1], links.left),
        ]
        self.join(RIGHT)
        self.near = [links.send(parts.at[RIGHT, self.low], self.near_in.at[0, self.low], links.right)]
        self.join(LEFT)
        self.near.append(links.send(parts.at[LEFT, self.top], self.near_in.at[1, self.top], links.left))
        self.join(OWN)

    def relay(self):
        links, parts = self.links, self.parts
        self.far[0].wait_recv()
        add_rows(parts.at[RIGHT, self.top], self.far_in.at[0])
        self.near.append(links.send(parts.at[RIGHT, self.top], self.near_in.at[0, self.top], links.right))
        self.far[1].wait_recv()
        add_rows(parts.at[LEFT, self.low], self.far_in.at[1])
        self.near.append(links.send(parts.at[LEFT, self.low], self.near_in.at[1, self.low], links.left))

    def total(self, out_ref):
        for copy in self.near:
            copy.wait_recv()

        @pl.loop(0, out_ref.shape[0] // 16)
        def _(k):
            rows = pl.ds(pl.multiple_of(k * 16, 16), 16)
            total = self.parts[OWN, rows, :].astype(jnp.float32) + self.near_in[0, rows, :].astype(jnp.float32)
            out_ref[rows, :] = total + self.near_in[1, rows, :].astype(jnp.float32)


def feed_forward_kernel(
    rows_ref, out_low_ref, gu_0_ref, gu_1_ref, gu_2_ref, gu_3_ref, down_0_ref, down_1_ref, down_2_ref, down_3_ref,
    back_ref, ffn_ref, gu_grad_ref, down_grad_ref,
    gu_ref, down_ref, rows_all, act, gu_low, back, ffn, back_core, back_far, back_near, ffn_core, ffn_far, ffn_near,
    send_sems, recv_sems, own_sem,
):
    bf16, f32 = jnp.bfloat16, jnp.float32
    rows = rows_ref.shape[0]
    links = Links(send_sems, recv_sems)
    links.greet()
    own = pltpu.make_async_copy(rows_ref, rows_all.at[OWN], own_sem.at[0])
    own.start()
    copies = []
    for matrix, parts in (
        (gu_ref, (gu_0_ref, gu_1_ref, gu_2_ref, gu_3_ref)),
        (down_ref, (down_0_ref, down_1_ref, down_2_ref, down_3_ref)),
    ):
        height = parts[0].shape[0]
        for hops, part in enumerate(parts):
            place = pl.multiple_of(links.z_at[(PLANES - hops) % PLANES] * height, 16)
            copies.append(
                pltpu.make_async_copy(part, matrix.at[pl.ds(place, height)], own_sem.at[1 + len(copies)])
            )
            copies[-1].start()
    used = PLANES * PAD_FF
    down_ref[used:, :] = jnp.zeros((HALF_GU - used, D), bf16)
    to_right = links.send(rows_ref, rows_all.at[LEFT], links.right)
    to_left = links.send(rows_ref, rows_all.at[RIGHT], links.left)
    cores = {OWN: links.send(rows_ref, rows_all.at[CHIPS + OWN], links.partner)}
    back_sum = PlaneTotal(links, back, back_core, back_far, back_near)
    ffn_sum = PlaneTotal(links, ffn, ffn_core, ffn_far, ffn_near)
    top, low = pl.ds(0, rows // 2), pl.ds(rows // 2, rows // 2)

    def compute(slot):
        here = pl.ds(slot * rows, rows)
        x = rows_all[slot]
        gu = flat_product(x, gu_ref[...])
        gate, up = gu[:, :HALF_GU], gu[:, HALF_GU:]
        opened = 1.0 / (1.0 + jnp.exp(-gate))
        act[here, :] = (gate * opened * up).astype(bf16)
        grad = back_product(out_low_ref[here, :], down_ref[...])
        gu_low[here, :HALF_GU] = (grad * up * opened * (1.0 + gate * (1.0 - opened))).astype(bf16)
        gu_low[here, HALF_GU:] = (grad * gate * opened).astype(bf16)
        back[slot] = back_product(gu_low[here, :], gu_ref[...]).astype(bf16)
        if slot >= CHIPS:
            back_sum.give(slot - CHIPS)

    own.wait()
    for copy in copies:
        copy.wait()
    compute(OWN)
    cores[OWN].wait_recv()
    compute(CHIPS + OWN)
    to_right.wait_recv()
    far = [links.send(rows_all.at[LEFT, top], rows_all.at[FAR, top], links.right)]
    cores[LEFT] = links.send(rows_all.at[LEFT], rows_all.at[CHIPS + LEFT], links.partner)
    to_left.wait_recv()
    far.append(links.send(rows_all.at[RIGHT, low], rows_all.at[FAR, low], links.left))
    cores[RIGHT] = links.send(rows_all.at[RIGHT], rows_all.at[CHIPS + RIGHT], links.partner)
    compute(LEFT)
    compute(RIGHT)
    for copy in far:
        copy.wait_recv()
    cores[FAR] = links.send(rows_all.at[FAR], rows_all.at[CHIPS + FAR], links.partner)
    compute(FAR)
    for chip in (FAR, RIGHT, LEFT):
        cores[chip].wait_recv()
        compute(CHIPS + chip)
    back_sum.start()

    def ffn_rows(slot):
        ffn[slot] = flat_product(act[slot * rows : (slot + 1) * rows], down_ref[...]).astype(bf16)
        if slot >= CHIPS:
            ffn_sum.give(slot - CHIPS)

    for chip in (FAR, RIGHT, LEFT, OWN):
        ffn_rows(CHIPS + chip)
    back_sum.relay()
    for chip in (FAR, RIGHT, LEFT, OWN):
        ffn_rows(chip)
    ffn_sum.start()

    def gu_grad(column, columns):
        left = jnp.concatenate([rows_all[slot, :, column : column + columns] for slot in range(PLANE_DEV)], axis=0)
        gu_grad_ref[column : column + columns, :] = outer_sum(left, gu_low[...]).astype(bf16)

    for column in range(0, 2 * GRAD_LANES, GRAD_LANES):
        gu_grad(column, GRAD_LANES)
    back_sum.total(back_ref)
    ffn_sum.relay()
    for column in range(2 * GRAD_LANES, D, GRAD_LANES):
        gu_grad(column, min(GRAD_LANES, D - column))
    for column in range(0, HALF_GU, GRAD_LANES):
        down_grad_ref[column : column + GRAD_LANES, :] = outer_sum(
            act[:, column : column + GRAD_LANES], out_low_ref[...]
        ).astype(bf16)
    ffn_sum.total(ffn_ref)
    links.finish()


def feed_forward(rows_low, out_low, *units):
    bf16, f32 = jnp.bfloat16, jnp.float32
    rows = rows_low.shape[0]
    vmem, anywhere = pl.BlockSpec(memory_space=pltpu.VMEM), pl.BlockSpec(memory_space=pl.ANY)

    def slots(count, height=rows):
        return pltpu.VMEM((count, height, D), bf16)

    sums = [slots(CHIPS), slots(2, rows // 2), slots(2)]
    return pl.pallas_call(
        feed_forward_kernel,
        out_shape=[
            jax.ShapeDtypeStruct((rows, D), f32),
            jax.ShapeDtypeStruct((rows, D), f32),
            jax.ShapeDtypeStruct((D, GU), bf16),
            jax.ShapeDtypeStruct((HALF_GU, D), bf16),
        ],
        in_specs=[anywhere, vmem] + [anywhere] * len(units),
        out_specs=[vmem] * 4,
        scratch_shapes=[
            pltpu.VMEM((D, GU), bf16),
            pltpu.VMEM((HALF_GU, D), bf16),
            slots(PLANE_DEV),
            pltpu.VMEM((PLANE_DEV * rows, HALF_GU), bf16),
            pltpu.VMEM((PLANE_DEV * rows, GU), bf16),
            slots(PLANE_DEV),
            slots(PLANE_DEV),
        ]
        + sums
        + sums
        + [pltpu.SemaphoreType.DMA((32,))] * 2
        + [pltpu.SemaphoreType.DMA((9,))],
        compiler_params=pltpu.CompilerParams(
            collective_id=4, has_side_effects=True, vmem_limit_bytes=60 * 1024 * 1024
        ),
        name="feed_forward",
    )(rows_low, out_low, *units)


CHUNKS = INNER // LANES
WIDE_CHUNKS = [(k * LANES, LANES) for k in range(WIDE // LANES)] + [(WIDE // LANES * LANES, WIDE % LANES)]
WIDE_BUFFERS = 3
MAIN = FAST_DEV * MAIN_D
LOW_PAD = 128


def lanes_at(k):
    return pl.ds(pl.multiple_of(k * LANES, 128), LANES)


def write_order(table_ref, matrix_ref):
    size, step = matrix_ref.shape[0], 160

    @pl.loop(0, size // step)
    def _(k):
        at = pl.multiple_of(k * step, 16)
        places = lax.broadcasted_iota(jnp.int32, (step, size), 0) + at
        matrix_ref[pl.ds(at, step), :] = jnp.where(places == table_ref[...], 1.0, 0.0).astype(jnp.bfloat16)


def rms_parts(values):
    scale = lax.rsqrt(jnp.mean(values * values, axis=-1, keepdims=True) + epsilon)
    return values * scale, scale


def rms_pull(unit, scale, gain_row, grad):
    inner = grad * gain_row
    back = scale * (inner - unit * jnp.mean(inner * unit, axis=-1, keepdims=True))
    return back, jnp.sum(grad * unit, axis=0, keepdims=True)


def move_back(order, rows_wide):
    high = rows_wide.astype(jnp.bfloat16)
    rest = (rows_wide - high.astype(jnp.float32)).astype(jnp.bfloat16)
    return back_product(high, order[...]) + back_product(rest, order[...])


def wide_copy(wide_ref, buffer, sem, j, buffers=WIDE_BUFFERS):
    column, columns = WIDE_CHUNKS[j]
    slot = j % buffers
    return pltpu.make_async_copy(
        wide_ref.at[:, pl.ds(column, columns)], buffer.at[slot, :, pl.ds(0, columns)], sem.at[slot]
    )


def conv_sum(inner, taps, shift, same_ref):
    earlier = [pltpu.roll(inner, k, axis=0) * same_ref[:, k - 1 : k] for k in range(1, CONV)]
    total = shift + taps[CONV - 1 : CONV] * inner
    for k in range(1, CONV):
        total = total + taps[CONV - 1 - k : CONV - k] * earlier[k - 1]
    return total, earlier


def scan_rows(lanes, b_ref, c_ref, y_ref, rates, decay_step, step_input, keep=None):
    rows_all = decay_step.shape[0]

    def eight(k, state):
        base = pl.multiple_of(k * 8, 8)
        steps = decay_step[pl.ds(base, 8), :]
        inputs = step_input[pl.ds(base, 8), :]
        rows = []
        for i in range(8):
            decay = jnp.exp2(steps[i : i + 1] * rates)
            state = decay * state + tiled(b_ref[base + i]) * inputs[i : i + 1]
            if keep is None:
                rows.append(jnp.sum(tiled(c_ref[base + i]) * state, axis=0, keepdims=True))
            else:
                keep(base + i, state)
        if keep is None:
            y_ref[pl.ds(base, 8), lanes] = jnp.concatenate(rows, axis=0)
        return state

    lax.fori_loop(0, rows_all // 8, eight, jnp.zeros((STATE, LANES), jnp.float32))


def spread_lanes(rows_ref, first, out_ref):
    lane = lax.broadcasted_iota(jnp.int32, (STATE, 128), 1)
    place = lax.broadcasted_iota(jnp.int32, (STATE, 128), 0) + first

    @pl.loop(0, rows_ref.shape[0] // 8)
    def _(k):
        base = pl.multiple_of(k * 8, 8)
        rows = rows_ref[pl.ds(base, 8), :]
        for i in range(8):
            picked = jnp.where(lane == place, jnp.broadcast_to(rows[i : i + 1], (STATE, 128)), 0.0)
            out_ref[base + i] = jnp.broadcast_to(jnp.sum(picked, axis=1, keepdims=True), (STATE, 128))


def gather_lanes(b_ref, c_ref, out_ref):
    lane = lax.broadcasted_iota(jnp.int32, (STATE, 128), 1)
    place = lax.broadcasted_iota(jnp.int32, (STATE, 128), 0)

    @pl.loop(0, out_ref.shape[0] // 8)
    def _(k):
        base = pl.multiple_of(k * 8, 8)
        rows = []
        for i in range(8):
            b = jnp.where(lane == place, jnp.sum(b_ref[base + i], axis=1, keepdims=True), 0.0)
            c = jnp.where(lane == place + STATE, jnp.sum(c_ref[base + i], axis=1, keepdims=True), 0.0)
            rows.append(jnp.sum(b + c, axis=0, keepdims=True))
        out_ref[pl.ds(base, 8), :] = jnp.concatenate(rows, axis=0)


def mixer_forward_kernel(
    tokens_ref, gains_ref, seg_col_ref, seg_row_ref, hold_ref, same_ref, table_d_ref, table_i_ref,
    wide_ref, wide_rest_ref, taps_ref, conv_shift_ref, select_ref, step_ref, step_shift_ref, decay_ref, skip_ref,
    out_block_ref, out_rest_ref, join_block_ref, join_rest_ref,
    out_low_ref, gu_prev_ref, down_prev_ref,
    normed_ref, mixed_ref, qkv_ref, conv_ref, step_low_ref, pre_ref, b_ref, c_ref, y_ref, gated_ref, attn_ref,
    mamba_ref, joined_ref, middle_ref, normed_two_ref,
    out_ref, join_ref, out_low_all_ref, gu_ref, down_ref,
    order, wide_buffer, out_all, join_all, conv_low, gated, decay_step, step_input, select_rows, wide_sem, sem,
    send_sems, recv_sems, local,
):
    bf16, f32 = jnp.bfloat16, jnp.float32
    links = Links(send_sems, recv_sems)
    links.greet()
    branches = [
        Gather(links, out_block_ref, shard_place("mamba_out", out_ref), local.at[0]),
        Gather(links, join_block_ref, shard_place("join", join_ref), local.at[1]),
    ]
    for g in branches:
        g.hop(0)
    low_copy = pltpu.make_async_copy(out_low_ref, out_low_all_ref.at[OWN], local.at[2])
    low_copy.start()
    low_near = [
        links.send(out_low_ref, out_low_all_ref.at[LEFT], links.right),
        links.send(out_low_ref, out_low_all_ref.at[RIGHT], links.left),
    ]
    low_core = [links.send(out_low_ref, out_low_all_ref.at[CHIPS + OWN], links.partner)]
    unit_hops = [
        links.send(prev, last, links.z_next) for prev, last in ((gu_prev_ref, gu_ref), (down_prev_ref, down_ref))
    ]

    def low_service():
        top, low = pl.ds(0, out_low_ref.shape[0] // 2), pl.ds(out_low_ref.shape[0] // 2, out_low_ref.shape[0] // 2)
        for copy in low_near:
            copy.wait_recv()
        far = [
            links.send(out_low_all_ref.at[LEFT, top], out_low_all_ref.at[FAR, top], links.right),
            links.send(out_low_all_ref.at[RIGHT, low], out_low_all_ref.at[FAR, low], links.left),
        ]
        for chip in (LEFT, RIGHT):
            low_core.append(links.send(out_low_all_ref.at[chip], out_low_all_ref.at[CHIPS + chip], links.partner))
        return far

    count = len(WIDE_CHUNKS)
    for j in range(WIDE_BUFFERS):
        wide_copy(wide_ref, wide_buffer, wide_sem, j).start()
    inputs = tokens_ref[...].astype(f32)
    write_order(table_d_ref, order)
    normed_ref[...] = flat_product((rms_parts(inputs)[0] * gains_ref[0:1]).astype(bf16), order[...]).astype(bf16)
    for j, (column, columns) in enumerate(WIDE_CHUNKS):
        copy = wide_copy(wide_ref, wide_buffer, wide_sem, j)
        copy.wait()
        part = flat_product(normed_ref[:, :MAIN], wide_buffer[j % WIDE_BUFFERS, :, :columns]) + flat_product(
            normed_ref[:, MAIN:], wide_rest_ref[:, column : column + columns]
        )
        if column < 2 * INNER:
            mixed_ref[:, column : column + columns] = part
        else:
            first, last = column - 2 * INNER, min(column - 2 * INNER + columns, QKV)
            qkv_ref[:, first:last] = part[:, : last - first].astype(bf16)
        if j + WIDE_BUFFERS < count:
            wide_copy(wide_ref, wide_buffer, wide_sem, j + WIDE_BUFFERS).start()
        if j in (5, 10):
            for g in branches:
                g.hop(j // 5)
    low_far = low_service()

    @pl.loop(0, CHUNKS)
    def _(k):
        lanes = lanes_at(k)
        total, _ = conv_sum(mixed_ref[:, lanes], taps_ref[:, lanes], conv_shift_ref[:, lanes], same_ref)
        act = total / (1.0 + jnp.exp(-total))
        conv_ref[:, lanes] = act
        conv_low[:, lanes] = act.astype(bf16)

    for g in branches:
        g.hop(3)
    selected = flat_product(conv_low[...], select_ref[...])
    step_low_ref[...] = selected[:, :LOW_PAD].astype(bf16)
    select_rows[...] = selected[:, LOW_PAD:]
    spread_lanes(select_rows, 0, b_ref)
    spread_lanes(select_rows, STATE, c_ref)
    attention_forward_kernel(qkv_ref, seg_col_ref, seg_row_ref, attn_ref)
    write_order(table_i_ref, order)
    for copy in low_far:
        copy.wait_recv()
    low_core.append(links.send(out_low_all_ref.at[FAR], out_low_all_ref.at[CHIPS + FAR], links.partner))
    for s in range(PLANES):
        for g in branches:
            g.near(s)

    def scan_chunk(k):
        lanes = lanes_at(k)
        pre = flat_product(step_low_ref[...], step_ref[:, lanes])
        pre_ref[:, lanes] = pre
        conv = conv_ref[:, lanes]
        _, decay_step[...], step_input[...] = scan_setup(pre, step_shift_ref[:, lanes], conv, hold_ref[...])
        scan_rows(lanes, b_ref, c_ref, y_ref, decay_ref[:, lanes] * (-LOG2E), decay_step, step_input)
        gate = mixed_ref[:, pl.ds(pl.multiple_of(k * LANES + INNER, 128), LANES)]
        gated[:, lanes] = (
            (y_ref[:, lanes] + skip_ref[:, lanes] * conv) * (gate / (1.0 + jnp.exp(-gate)))
        ).astype(bf16)

    pl.loop(0, CHUNKS // 2)(scan_chunk)
    for s in range(2):
        for g in branches:
            g.far(s)
    pl.loop(CHUNKS // 2, CHUNKS)(scan_chunk)
    half = INNER // 2
    moved = []
    for h in range(2):
        moved.append(flat_product(gated[:, h * half : (h + 1) * half], order[...]).astype(bf16))
        gated_ref[h] = moved[h]
    write_order(table_d_ref, order)
    for s in range(2, PLANES):
        for g in branches:
            g.far(s)
    branches[0].wait()
    out_copies = [
        pltpu.make_async_copy(out_ref.at[j], out_all.at[pl.ds(j * MAIN_I, MAIN_I)], sem.at[j]) for j in range(FAST_DEV)
    ]
    for copy in out_copies:
        copy.start()
    branches[1].wait()
    join_copies = [
        pltpu.make_async_copy(join_ref.at[j], join_all.at[pl.ds(j * MAIN_D, MAIN_D)], sem.at[FAST_DEV + j])
        for j in range(FAST_DEV)
    ]
    for copy in join_copies:
        copy.start()
    for copy in out_copies:
        copy.wait()
    total = jnp.zeros(mamba_ref.shape, f32)
    for h in range(2):
        total = total + flat_product(moved[h][:, :MAIN], out_all[h * MAIN : (h + 1) * MAIN])
        total = total + flat_product(moved[h][:, MAIN:], out_rest_ref[h])
    mamba_ref[...] = total
    joined = 0.5 * (rms_parts(attn_ref[...])[0] * gains_ref[1:2] + rms_parts(total)[0] * gains_ref[2:3])
    joined_ref[...] = flat_product(joined.astype(bf16), order[...]).astype(bf16)
    for copy in join_copies:
        copy.wait()
    middle = (
        inputs
        + flat_product(joined_ref[:, :MAIN], join_all[...])
        + flat_product(joined_ref[:, MAIN:], join_rest_ref[...])
    )
    middle_ref[...] = middle
    normed_two_ref[...] = (rms_parts(middle)[0] * gains_ref[3:4]).astype(bf16)
    for copy in low_core + unit_hops:
        copy.wait_recv()
    low_copy.wait()
    links.finish()


def mixer_forward(*operands):
    rows = operands[0].shape[0]
    bf16, f32 = jnp.bfloat16, jnp.float32
    vmem, anywhere = pl.BlockSpec(memory_space=pltpu.VMEM), pl.BlockSpec(memory_space=pl.ANY)
    in_specs = [vmem] * len(operands)
    for k in (8, 17, 19, 21, 22, 23):
        in_specs[k] = anywhere
    out_block, join_block, out_low, gu, down = [operands[k] for k in (17, 19, 21, 22, 23)]
    shapes = (
        ((rows, D), bf16), ((rows, 2 * INNER), f32), ((rows, QKV), bf16), ((rows, INNER), f32), ((rows, LOW_PAD), bf16),
        ((rows, INNER), f32), ((rows, STATE, 128), f32), ((rows, STATE, 128), f32), ((rows, INNER), f32),
        ((2, rows, D), bf16), ((rows, D), f32), ((rows, D), f32), ((rows, D), bf16), ((rows, D), f32), ((rows, D), bf16),
    )
    gathered = [
        (FAST_DEV,) + out_block.shape, (FAST_DEV,) + join_block.shape, (PLANE_DEV,) + out_low.shape,
        gu.shape, down.shape,
    ]
    sends = 2 * GATHER_SENDS + 12
    return pl.pallas_call(
        mixer_forward_kernel,
        out_shape=[jax.ShapeDtypeStruct(shape, kind) for shape, kind in shapes]
        + [jax.ShapeDtypeStruct(shape, bf16) for shape in gathered],
        in_specs=in_specs,
        out_specs=[vmem] * len(shapes) + [anywhere] * len(gathered),
        scratch_shapes=[
            pltpu.VMEM((D, D), bf16),
            pltpu.VMEM((WIDE_BUFFERS, MAIN, LANES), bf16),
            pltpu.VMEM((2 * MAIN, D), bf16),
            pltpu.VMEM((MAIN, D), bf16),
            pltpu.VMEM((rows, INNER), bf16),
            pltpu.VMEM((rows, INNER), bf16),
            pltpu.VMEM((rows, LANES), f32),
            pltpu.VMEM((rows, LANES), f32),
            pltpu.VMEM((rows, 128), f32),
            pltpu.SemaphoreType.DMA((WIDE_BUFFERS,)),
            pltpu.SemaphoreType.DMA((2 * FAST_DEV,)),
            pltpu.SemaphoreType.DMA((sends,)),
            pltpu.SemaphoreType.DMA((sends,)),
            pltpu.SemaphoreType.DMA((3,)),
        ],
        compiler_params=pltpu.CompilerParams(
            collective_id=1, has_side_effects=True, vmem_limit_bytes=60 * 1024 * 1024
        ),
        name="mixer_forward",
    )(*operands)


def branch_backward_kernel(
    part_grad_ref, out_grad_ref, gains_ref, table_d_ref, table_i_ref, out_ref, out_rest_ref, join_ref, join_rest_ref,
    attn_ref, mamba_ref, middle_ref,
    middle_grad_ref, gains_grad_ref, join_low_ref, mamba_low_ref, attn_low_ref, gated_grad_ref,
    order, row_buffer, sem,
):
    bf16 = jnp.bfloat16
    half_rows = MAIN // 2
    row_blocks = [(join_ref, k) for k in range(2)] + [(out_ref, k) for k in range(4)]

    def row_copy(i):
        source, k = row_blocks[i]
        return pltpu.make_async_copy(source.at[pl.ds(k * half_rows, half_rows)], row_buffer.at[i], sem.at[i])

    def row_products(low, first):
        products = []
        for i in (first, first + 1):
            row_copy(i).wait()
            products.append(back_product(low, row_buffer[i]))
        return products

    for i in range(len(row_blocks)):
        row_copy(i).start()
    write_order(table_d_ref, order)
    unit, scale = rms_parts(middle_ref[...])
    back, gain_grad = rms_pull(unit, scale, gains_ref[3:4], part_grad_ref[...])
    gains_grad_ref[0:1] = jnp.zeros_like(gain_grad)
    gains_grad_ref[3:4] = gain_grad
    middle_grad = out_grad_ref[...] + back
    middle_grad_ref[...] = middle_grad
    join_low = middle_grad.astype(bf16)
    join_low_ref[...] = join_low
    joined_grad = 0.5 * move_back(
        order, jnp.concatenate(row_products(join_low, 0) + [back_product(join_low, join_rest_ref[...])], axis=1)
    )
    unit, scale = rms_parts(attn_ref[...])
    back, gain_grad = rms_pull(unit, scale, gains_ref[1:2], joined_grad)
    gains_grad_ref[1:2] = gain_grad
    attn_low_ref[...] = back.astype(bf16)
    unit, scale = rms_parts(mamba_ref[...])
    back, gain_grad = rms_pull(unit, scale, gains_ref[2:3], joined_grad)
    gains_grad_ref[2:3] = gain_grad
    mamba_low = back.astype(bf16)
    mamba_low_ref[...] = mamba_low
    write_order(table_i_ref, order)
    half = INNER // 2
    for h in range(2):
        gated_grad_ref[:, h * half : (h + 1) * half] = move_back(
            order,
            jnp.concatenate(row_products(mamba_low, 2 + 2 * h) + [back_product(mamba_low, out_rest_ref[h])], axis=1),
        )


def branch_backward(*operands):
    rows = operands[0].shape[0]
    bf16, f32 = jnp.bfloat16, jnp.float32
    vmem, anywhere = pl.BlockSpec(memory_space=pltpu.VMEM), pl.BlockSpec(memory_space=pl.ANY)
    in_specs = [vmem] * len(operands)
    for k in (5, 7):
        in_specs[k] = anywhere
    shapes = (
        ((rows, D), f32), ((4, D), f32), ((rows, D), bf16), ((rows, D), bf16), ((rows, D), bf16), ((rows, INNER), f32),
    )
    return pl.pallas_call(
        branch_backward_kernel,
        out_shape=[jax.ShapeDtypeStruct(shape, kind) for shape, kind in shapes],
        in_specs=in_specs,
        out_specs=[vmem] * len(shapes),
        scratch_shapes=[
            pltpu.VMEM((D, D), bf16),
            pltpu.VMEM((6, MAIN // 2, D), bf16),
            pltpu.SemaphoreType.DMA((6,)),
        ],
        compiler_params=pltpu.CompilerParams(vmem_limit_bytes=56 * 1024 * 1024),
        name="branch_backward",
    )(*operands)


def mixer_backward_kernel(plan, *refs):
    bf16, f32 = jnp.bfloat16, jnp.float32
    take = Taker(refs)
    ins = take(len(plan.operands))
    gu_grad_ref, down_grad_ref, seg_col_ref, seg_row_ref, hold_ref, same_ref = take(6)
    taps_ref, conv_shift_ref, select_ref, step_ref, step_shift_ref, decay_ref, skip_ref = take(7)
    mixed_ref, qkv_ref, conv_ref, step_low_ref, pre_ref, b_ref, c_ref, y_ref, attn_low_ref, gated_grad_ref = take(10)
    totals = take(len(plan.out_shape))
    wide_low_ref, select_grad_ref, step_grad_ref, taps_grad_ref, conv_shift_grad_ref = take(5)
    step_shift_grad_ref, decay_grad_ref, skip_grad_ref, gu_came_ref, down_came_ref = take(5)
    scratch = take(len(plan.scratch))
    conv_grad, low_grad, step_size, decay_step, step_input, y_grad, input_part, step_part = take(8)
    states, b_grad, c_grad, select_rows, select_low = take(5)
    gu_own, gu_next, down_own, down_next, unit_sem, send_sems, recv_sems = take(7)
    rows_all = conv_ref.shape[0]
    links = Links(send_sems, recv_sems)
    links.greet()
    summing = Summing(plan, links, ins, totals, scratch)
    summing.exchange()
    gu_height, down_height = gu_own.shape[0], down_own.shape[0]

    def piece(ref, height, k):
        return ref.at[pl.ds(pl.multiple_of(links.z_at[k] * height, 16), height)]

    hops = [
        links.send(piece(gu_grad_ref, gu_height, 3), gu_next, links.z_next),
        links.send(piece(down_grad_ref, down_height, 3), down_next, links.z_next),
    ]
    loads = [
        pltpu.make_async_copy(piece(gu_grad_ref, gu_height, 2), gu_own, unit_sem.at[0]),
        pltpu.make_async_copy(piece(down_grad_ref, down_height, 2), down_own, unit_sem.at[1]),
    ]
    for copy in loads:
        copy.start()
    b_grad[...] = jnp.zeros_like(b_grad)
    c_grad[...] = jnp.zeros_like(c_grad)
    states[0] = jnp.zeros((STATE, LANES), f32)
    zeros = jnp.zeros((STATE, LANES), f32)
    summing.exchanged()
    summing.step()
    summing.step()

    def scan_chunk(k):
        lanes = lanes_at(k)
        gate_lanes = pl.ds(pl.multiple_of(k * LANES + INNER, 128), LANES)
        conv, shift, skip = conv_ref[:, lanes], step_shift_ref[:, lanes], skip_ref[:, lanes]
        step_size[...], decay_step[...], step_input[...] = scan_setup(pre_ref[:, lanes], shift, conv, hold_ref[...])
        gate, grad = mixed_ref[:, gate_lanes], gated_grad_ref[:, lanes]
        open_gate = 1.0 / (1.0 + jnp.exp(-gate))
        wide_low_ref[:, gate_lanes] = (
            grad * (y_ref[:, lanes] + skip * conv) * open_gate * (1.0 + gate * (1.0 - open_gate))
        ).astype(bf16)
        y_grad[...] = grad * gate * open_gate
        skip_grad_ref[:, lanes] = jnp.sum(y_grad[...] * conv, axis=0, keepdims=True)
        decay_rows = decay_ref[:, lanes]
        rates = decay_rows * (-LOG2E)

        def keep(t, state):
            states[t + 1] = state

        scan_rows(lanes, b_ref, c_ref, None, rates, decay_step, step_input, keep)

        def backward(i, carry):
            state_grad, decay_grad = carry
            base = pl.multiple_of(rows_all - 8 - i * 8, 8)
            inputs = step_input[pl.ds(base, 8), :]
            sizes = step_size[pl.ds(base, 8), :]
            held = decay_step[pl.ds(base, 8), :]
            y_rows = y_grad[pl.ds(base, 8), :]
            input_rows, step_rows = [None] * 8, [None] * 8
            for r in range(7, -1, -1):
                t = base + r
                y_row = y_rows[r : r + 1]
                full = state_grad + tiled(c_ref[t]) * y_row
                c_grad[t] += folded(states[t + 1] * y_row)
                b_grad[t] += folded(full * inputs[r : r + 1])
                input_rows[r] = jnp.sum(tiled(b_ref[t]) * full, axis=0, keepdims=True)
                state_grad = jnp.exp2(held[r : r + 1] * rates) * full
                through = state_grad * states[t]
                step_rows[r] = jnp.sum(decay_rows * through, axis=0, keepdims=True)
                decay_grad = decay_grad - sizes[r : r + 1] * through
            input_part[pl.ds(base, 8), :] = jnp.concatenate(input_rows, axis=0)
            step_part[pl.ds(base, 8), :] = jnp.concatenate(step_rows, axis=0)
            return state_grad, decay_grad

        _, decay_grad = lax.fori_loop(0, rows_all // 8, backward, (zeros, zeros))
        decay_grad_ref[:, lanes] = decay_grad
        conv_grad[:, lanes] = input_part[...] * step_size[...] + skip * y_grad[...]
        pre_grad = (input_part[...] * conv - step_part[...]) / (1.0 + jnp.exp(-(pre_ref[:, lanes] + shift)))
        step_shift_grad_ref[:, lanes] = jnp.sum(pre_grad, axis=0, keepdims=True)
        low_grad[:, lanes] = pre_grad.astype(bf16)

    for k in range(CHUNKS):
        pl.loop(k, k + 1)(scan_chunk)
        summing.step()
    for copy in loads:
        copy.wait()
    for copy in hops:
        copy.wait_recv()
    add_rows(gu_own, gu_next)
    add_rows(down_own, down_next)
    hops = [links.send(gu_own, gu_came_ref, links.z_next), links.send(down_own, down_came_ref, links.z_next)]

    gather_lanes(b_grad, c_grad, select_rows)
    select_low[:, :LOW_PAD] = back_product(low_grad[...], step_ref[...]).astype(bf16)
    select_low[:, LOW_PAD:] = select_rows[...].astype(bf16)
    summing.step()

    @pl.loop(0, CHUNKS)
    def _(k):
        lanes = lanes_at(k)
        step_grad_ref[:, lanes] = outer_sum(step_low_ref[...], low_grad[:, lanes]).astype(bf16)
        conv = conv_ref[:, lanes]
        some = pl.ds(pl.multiple_of(k * LANES, 128), LANES)
        select_grad_ref[some, :] = outer_sum(conv.astype(bf16), select_low[...]).astype(bf16)
        grad = conv_grad[:, lanes] + back_product(select_low[...], select_ref[some, :])
        inner, taps = mixed_ref[:, lanes], taps_ref[:, lanes]
        total, earlier = conv_sum(inner, taps, conv_shift_ref[:, lanes], same_ref)
        opened = 1.0 / (1.0 + jnp.exp(-total))
        grad = grad * opened * (1.0 + total * (1.0 - opened))
        conv_shift_grad_ref[:, lanes] = jnp.sum(grad, axis=0, keepdims=True)
        tap_rows = [jnp.sum(grad * earlier[j - 1], axis=0, keepdims=True) for j in range(CONV - 1, 0, -1)]
        tap_rows.append(jnp.sum(grad * inner, axis=0, keepdims=True))
        taps_grad_ref[:, lanes] = jnp.concatenate(tap_rows, axis=0)
        inner_grad = taps[CONV - 1 : CONV] * grad
        for j in range(1, CONV):
            moved = taps[CONV - 1 - j : CONV - j] * grad * same_ref[:, j - 1 : j]
            inner_grad = inner_grad + pltpu.roll(moved, rows_all - j, axis=0)
        wide_low_ref[:, lanes] = inner_grad.astype(bf16)

    summing.step()
    attention_backward_kernel(qkv_ref, seg_col_ref, seg_row_ref, attn_low_ref, wide_low_ref, 2 * INNER)
    wide_low_ref[:, 2 * INNER + QKV :] = jnp.zeros((rows_all, WIDE - 2 * INNER - QKV), bf16)
    summing.finish()
    for copy in hops:
        copy.wait_recv()
    links.finish()


def mixer_backward(plan, *operands):
    rows = operands[-1].shape[0]
    bf16, f32 = jnp.bfloat16, jnp.float32
    vmem, anywhere = pl.BlockSpec(memory_space=pltpu.VMEM), pl.BlockSpec(memory_space=pl.ANY)
    in_specs = [anywhere] * (len(plan.operands) + 2) + [vmem] * (len(operands) - 2)
    shapes = (
        ((rows, WIDE), bf16), ((INNER, 2 * LOW_PAD), bf16), ((LOW_PAD, INNER), bf16), ((CONV, INNER), f32),
        ((1, INNER), f32), ((1, INNER), f32), ((STATE, INNER), f32), ((1, INNER), f32),
        ((PLANE_DEV * D // FAST_DEV, GU), bf16), ((PAD_FF, D), bf16),
    )
    lane_rows = pltpu.VMEM((rows, LANES), f32)
    sem = pltpu.SemaphoreType.DMA
    return pl.pallas_call(
        functools.partial(mixer_backward_kernel, plan),
        out_shape=plan.out_shape + [jax.ShapeDtypeStruct(shape, kind) for shape, kind in shapes],
        in_specs=in_specs,
        out_specs=[vmem] * (len(plan.out_shape) + len(shapes) - 2) + [anywhere] * 2,
        scratch_shapes=plan.scratch
        + [pltpu.VMEM((rows, INNER), f32), pltpu.VMEM((rows, INNER), bf16)]
        + [lane_rows] * 6
        + [
            pltpu.VMEM((rows + 1, STATE, LANES), f32),
            pltpu.VMEM((rows, STATE, 128), f32),
            pltpu.VMEM((rows, STATE, 128), f32),
            pltpu.VMEM((rows, 128), f32),
            pltpu.VMEM((rows, 2 * LOW_PAD), bf16),
            pltpu.VMEM(shapes[-2][0], bf16),
            pltpu.VMEM(shapes[-2][0], bf16),
            pltpu.VMEM(shapes[-1][0], bf16),
            pltpu.VMEM(shapes[-1][0], bf16),
            sem((2,)),
            sem((4,)),
            sem((4,)),
        ],
        compiler_params=pltpu.CompilerParams(
            collective_id=2, has_side_effects=True, vmem_limit_bytes=62 * 1024 * 1024
        ),
        name="mixer_backward",
    )(*plan.operands, *operands)


def spread_table(shard_rows, main_rows, shards):
    half = shards // CORES
    order = [k * CORES + c for c in range(CORES) for k in range(half)]
    main = [d * shard_rows + r for d in order for r in range(main_rows)]
    rest = [d * shard_rows + r for d in order for r in range(main_rows, shard_rows)]
    return np.asarray(main + rest, np.int32)


def tie(*values):
    return lax.optimization_barrier(values)


def as_rows(flats, rows):
    flat = jnp.concatenate(flats)
    return jnp.pad(flat, (0, rows * 128 - flat.size)).reshape(rows, 128)


def split_flat(block, sizes):
    pieces, at = [], 0
    for size in sizes:
        pieces.append(block[..., at : at + size])
        at += size
    return pieces


def on_fast_device(
    tokens, cotangent, seq_lengths, qkv_proj, mamba_in, select_proj, step_proj, mamba_out, join_out,
    conv_taps, conv_bias, step_bias, decay_rates, skip_gain, norm_gains, ffn_gate, ffn_up, ffn_down,
):
    bf16, f32 = jnp.bfloat16, jnp.float32
    n = FAST_DEV
    row_count = tokens.shape[0]
    d_rows, i_rows = D // n, INNER // n
    d_rest, i_rest = d_rows - MAIN_D, i_rows - MAIN_I

    own_ff = PLANES * PAD_FF

    def ff_columns(flat):
        block = flat.reshape(d_rows, PLANES, PLANE_DEV, SLICE_FF).transpose(2, 0, 1, 3)
        block = jnp.pad(block, ((0, 0), (0, 0), (0, 0), (0, PAD_FF - SLICE_FF)))
        return jnp.pad(block.reshape(PLANE_DEV, d_rows, own_ff), ((0, 0), (0, 0), (0, HALF_GU - own_ff)))

    planes = [[z * PLANE_DEV + p for p in range(PLANE_DEV)] for z in range(PLANES)]
    gu = jnp.concatenate([ff_columns(ffn_gate), ff_columns(ffn_up)], axis=2)
    gu = lax.all_to_all(gu, "fsdp", 0, 0, axis_index_groups=planes, tiled=True).reshape(PLANE_DEV * d_rows, GU)
    down = jnp.pad(ffn_down.reshape(SLICE_FF, D), ((0, PAD_FF - SLICE_FF), (0, 0)))

    wide = jnp.concatenate([mamba_in.reshape(d_rows, 2 * INNER), qkv_proj.reshape(d_rows, QKV)], axis=1)
    wide = jnp.pad(wide, ((0, 0), (0, WIDE - wide.shape[1])))
    out_block = mamba_out.reshape(i_rows, D)
    join_block = join_out.reshape(d_rows, D)
    rest_sizes = [d_rest * WIDE, d_rest * D, i_rest * D]
    rest = as_rows(
        [wide[MAIN_D:].reshape(-1), join_block[MAIN_D:].reshape(-1), out_block[MAIN_I:].reshape(-1)], REST_ROWS
    )
    smalls = [select_proj, step_proj, conv_taps, conv_bias, step_bias, decay_rates, skip_gain, norm_gains]
    small_sizes = [s.size for s in smalls]
    smalls = as_rows(smalls, SMALL_ROWS)
    segments = segment_ids(seq_lengths, row_count)
    live_rows = (segments < seq_lengths.shape[0]).astype(f32)[:, None]
    out_grad = cotangent.astype(f32) * live_rows
    gu, down, wide_block, rest, smalls, out_grad = tie(gu, down, wide[:MAIN_D], rest, smalls, out_grad)
    wide_all, rest_all, smalls_all, gu_1, gu_2, down_1, down_2 = gather_first(
        ("wide", "rest", "smalls"), (wide_block, rest, smalls), (gu, down)
    )
    wide_all = wide_all.reshape(MAIN, WIDE)
    pieces = split_flat(rest_all.reshape(n, REST_ROWS * 128), rest_sizes)
    wide_rest = pieces[0].reshape(n * d_rest, WIDE)
    join_rest = pieces[1].reshape(n * d_rest, D)
    out_rest = pieces[2].reshape(CORES, 2, -1, D).transpose(1, 0, 2, 3).reshape(2, -1, D)
    pieces = split_flat(smalls_all.reshape(n, SMALL_ROWS * 128), small_sizes)
    select = pieces[0].reshape(INNER, XPROJ)
    select = jnp.concatenate(
        [
            jnp.pad(select[:, :RANK], ((0, 0), (0, LOW_PAD - RANK))),
            jnp.pad(select[:, RANK:], ((0, 0), (0, LOW_PAD - 2 * STATE))),
        ],
        axis=1,
    )
    step_matrix = jnp.pad(pieces[1].reshape(RANK, INNER), ((0, LOW_PAD - RANK), (0, 0)))
    taps = pieces[2].reshape(CONV, INNER).astype(f32)
    conv_shift = pieces[3].reshape(1, INNER).astype(f32)
    step_shift = pieces[4].reshape(1, INNER).astype(f32)
    decay = pieces[5].reshape(STATE, INNER).astype(f32)
    skip = pieces[6].reshape(1, INNER).astype(f32)
    gains = pieces[7].reshape(4, D).astype(f32)

    table_d = jnp.asarray(spread_table(d_rows, MAIN_D, n))[None]
    table_i = jnp.asarray(spread_table(i_rows, MAIN_I, n // 2))[None]
    hold = ((1.0 - keep_flags(segments)) * BIG)[:, None]
    same = jnp.stack(
        [
            (jnp.concatenate([jnp.full((k,), -1, jnp.int32), segments[:-k]]) == segments).astype(f32)
            for k in range(1, CONV)
        ],
        axis=1,
    )
    places = (segments[:, None], segments[None, :], hold, same, table_d, table_i)
    matrices = (
        wide_all, wide_rest, taps, conv_shift, select, step_matrix, step_shift, decay, skip,
    )
    (
        normed, mixed, qkv_rows, conv_act, step_low, step_pre, b_wide, c_wide, scanned, gated, attn_rows, mamba_rows,
        joined, middle, normed_two, out_all, join_all, out_low, gu_3, down_3,
    ) = mixer_forward(
        tokens, gains, *places, *matrices, out_block[:MAIN_I], out_rest, join_block[:MAIN_D], join_rest,
        out_grad.astype(bf16), gu_2, down_2,
    )
    out_all, join_all = out_all.reshape(2 * MAIN, D), join_all.reshape(MAIN, D)

    part_grad, ffn_rows, gu_grad, down_grad = feed_forward(
        normed_two, out_low.reshape(-1, D), gu, gu_1, gu_2, gu_3, down, down_1, down_2, down_3
    )
    block_out = ((middle + ffn_rows) * live_rows).astype(bf16)

    middle_grad, gains_grad, join_low, mamba_low, attn_low, gated_grad = branch_backward(
        part_grad, out_grad, gains, table_d, table_i, out_all, out_rest, join_all, join_rest,
        attn_rows, mamba_rows, middle,
    )
    gated_columns = gated.transpose(0, 2, 1)
    gated_rest = gated_columns[:, MAIN:].reshape(2, CORES, -1, row_count).transpose(1, 0, 2, 3)
    joined_columns, normed_columns = joined.T, normed.T
    branch_plan = SumPlan(
        BRANCH_BLOCKS, (MAIN_I, MAIN_D), (i_rest, d_rest), D,
        (gated_columns[:, :MAIN], joined_columns[None, :MAIN]),
        (gated_rest.reshape(CORES, -1, row_count), joined_columns[MAIN:].reshape(CORES, -1, row_count)),
        (mamba_low, join_low),
    )
    (
        out_sum, join_sum, branch_rest, wide_low, select_grad, step_grad, taps_grad, conv_shift_grad,
        step_shift_grad, decay_grad, skip_grad, gu_came, down_came,
    ) = mixer_backward(
        branch_plan, gu_grad, down_grad, *places[:4], taps, conv_shift, select, step_matrix, step_shift, decay, skip,
        mixed, qkv_rows, conv_act, step_low, step_pre, b_wide, c_wide, scanned, attn_low, gated_grad,
    )
    select_grad = jnp.concatenate([select_grad[:, :RANK], select_grad[:, LOW_PAD : LOW_PAD + 2 * STATE]], axis=1)
    small_grads = [
        select_grad, step_grad[:RANK], taps_grad, conv_shift_grad, step_shift_grad, decay_grad, skip_grad, gains_grad,
    ]
    small_grads = jnp.concatenate([g.astype(bf16).reshape(n, -1) for g in small_grads], axis=1)
    small_grads = jnp.pad(small_grads, ((0, 0), (0, SMALL_ROWS * 128 - small_grads.shape[1])))
    small_grads = small_grads.reshape(GROUPS, CORES, SMALL_ROWS, 128).transpose(1, 0, 2, 3)
    wide_plan = SumPlan(
        WIDE_BLOCKS, (MAIN_D,), (d_rest,), REST_COLUMNS,
        (normed_columns[None, :MAIN],),
        (normed_columns[MAIN:].reshape(CORES, -1, row_count),),
        (wide_low,),
        small_grads.reshape(CORES, GROUPS * SMALL_ROWS, 128),
    )
    wide_sum, wide_left, small_sum, input_grad, gu_blocks, down_sum = last_sums(
        wide_plan, middle_grad, tokens, gains, table_d, wide_all, wide_rest, gu_grad, down_grad, gu_came, down_came
    )
    gu_blocks = gu_blocks[:, :d_rows].reshape(PLANE_DEV, d_rows, 2, HALF_GU)[..., :own_ff].transpose(2, 1, 0, 3)
    gu_blocks = gu_blocks.reshape(2, d_rows, PLANE_DEV, PLANES, PAD_FF)[..., :SLICE_FF].transpose(0, 1, 3, 2, 4)
    gate_grad, up_grad = [block.astype(f32).reshape(-1) for block in gu_blocks]
    first_gain = wide_left[14, WIDE % REST_COLUMNS : WIDE % REST_COLUMNS + norm_gains.size]
    wide_left = wide_left.reshape(-1, d_rest, REST_COLUMNS).transpose(1, 0, 2).reshape(d_rest, -1)[:, :WIDE]
    wide_sum = jnp.concatenate([wide_sum, wide_left], axis=0)
    out_sum = jnp.concatenate([out_sum, branch_rest[:i_rest]], axis=0)
    join_sum = jnp.concatenate([join_sum, branch_rest[i_rest : i_rest + d_rest]], axis=0)
    smalls = split_flat(small_sum.reshape(-1), small_sizes)
    return (
        block_out,
        input_grad,
        wide_sum[:, 2 * INNER : 2 * INNER + QKV].reshape(-1),
        wide_sum[:, : 2 * INNER].reshape(-1),
        smalls[0],
        smalls[1],
        out_sum.reshape(-1),
        join_sum.reshape(-1),
        *smalls[2:-1],
        smalls[-1] + first_gain,
        gate_grad,
        up_grad,
        down_sum[:SLICE_FF].reshape(-1),
    )


def fits_fast_plan(mesh):
    return mesh.shape["fsdp"] == FAST_DEV


def solution(mesh):
    rows, flat = P("fsdp", None), P("fsdp")
    return jax.shard_map(
        on_fast_device if fits_fast_plan(mesh) else on_device,
        mesh=mesh,
        in_specs=(rows, rows) + (flat,) * 16,
        out_specs=(rows, rows) + (flat,) * 15,
        check_vma=False,
    )
```

```python
import functools

import jax
import jax.numpy as jnp
import numpy as np
from jax import lax
from jax.experimental import pallas as pl
from jax.experimental.pallas import tpu as pltpu
from jax.sharding import PartitionSpec as P

D = 1600
HEADS = 25
KV_HEADS = 5
HEAD = 64
INNER = 3200
STATE = 16
CONV = 4
RANK = 100
FF = 5504
QKV = 2240
XPROJ = 132


epsilon = 1e-06


def flat_product(left, right):
    return jnp.dot(left, right, preferred_element_type=jnp.float32)


def outer_sum(left, right):
    return lax.dot_general(
        left, right, (((0,), (0,)), ((), ())), preferred_element_type=jnp.float32
    )


def back_product(grad_rows, matrix):
    return lax.dot_general(
        grad_rows, matrix, (((1,), (1,)), ((), ())), preferred_element_type=jnp.float32
    )


def rms_scale(values, scale_row):
    return (
        values * lax.rsqrt(jnp.mean(values * values, axis=-1, keepdims=True) + epsilon) * scale_row
    )


def segment_ids(lengths, row_count):
    seq_ends = jnp.cumsum(lengths)
    places = jnp.arange(row_count, dtype=jnp.int32)
    return jnp.sum((places[:, None] >= seq_ends[None, :]).astype(jnp.int32), axis=1)


def keep_flags(segments):
    same_seq = (segments[1:] == segments[:-1]).astype(jnp.float32)
    return jnp.concatenate([jnp.zeros((1,), jnp.float32), same_seq])


def conv_silu(inner_rows, tap_matrix, conv_shift, segments):
    tap_count = tap_matrix.shape[0]
    summed = conv_shift[None, :] + tap_matrix[tap_count - 1][None, :] * inner_rows
    for offset in range(1, tap_count):
        shifted = jnp.concatenate(
            [jnp.zeros((offset, inner_rows.shape[1]), jnp.float32), inner_rows[:-offset]], axis=0
        )
        earlier = jnp.concatenate([jnp.full((offset,), -1, jnp.int32), segments[:-offset]])
        same_seq = (earlier == segments).astype(jnp.float32)
        summed = summed + tap_matrix[tap_count - 1 - offset][None, :] * shifted * same_seq[:, None]
    return jax.nn.silu(summed)


def scan_block(state_now, decay_matrix, block_data):
    step_sizes, step_inputs, step_b, step_c, step_keep = block_data
    outputs = []
    for step_index in range(step_sizes.shape[0]):
        decay_now = jnp.exp(-step_sizes[step_index][None, :] * decay_matrix)
        state_now = (
            step_keep[step_index] * decay_now * state_now
            + step_b[step_index][:, None]
            * (step_sizes[step_index] * step_inputs[step_index])[None, :]
        )
        outputs.append(jnp.sum(step_c[step_index][:, None] * state_now, axis=0))
    return (state_now, jnp.stack(outputs))


def selective_scan(step_sizes, step_inputs, b_rows, c_rows, keep_rows, decay_matrix):
    block_len = 16

    def advance(state_now, block_data):
        return jax.checkpoint(scan_block)(state_now, decay_matrix, block_data)

    blocks = tuple(
        (
            piece_array.reshape((-1, block_len) + piece_array.shape[1:])
            for piece_array in (step_sizes, step_inputs, b_rows, c_rows, keep_rows)
        )
    )
    start_state = jnp.zeros((b_rows.shape[1], step_inputs.shape[1]), jnp.float32)
    final_state, outputs = lax.scan(advance, start_state, blocks)
    return outputs.reshape(step_inputs.shape)


def mamba_core(
    conv_act, select_rows, step_pre, gate_in, step_shift, decay_matrix, skip_row, keep_rows
):
    step_sizes = jax.nn.softplus(step_pre + step_shift)
    scanned = selective_scan(
        step_sizes,
        conv_act,
        select_rows[:, :STATE],
        select_rows[:, STATE:],
        keep_rows,
        decay_matrix,
    )
    return (scanned + skip_row * conv_act) * jax.nn.silu(gate_in)


def join_branches(attn_rows, mamba_rows, attn_gain, mamba_gain):
    return 0.5 * (rms_scale(attn_rows, attn_gain) + rms_scale(mamba_rows, mamba_gain))


def swiglu(gate_rows, up_rows):
    return jax.nn.silu(gate_rows) * up_rows


def block_scores(query_block, start, key_rows, segments):
    block_rows = query_block.shape[0]
    places = jnp.arange(segments.shape[0], dtype=jnp.int32)
    query_places = start + jnp.arange(block_rows, dtype=jnp.int32)
    allowed = (segments[:, None] == segments[None, :]) & (places[None, :] <= query_places[:, None])
    scores = jnp.einsum(
        "tgrd,ugd->grtu", query_block, key_rows, preferred_element_type=jnp.float32
    ) * HEAD ** (-0.5)
    return jnp.where(allowed[None, None], scores, -1e30)


def attention_forward(queries, key_rows, value_rows, segments):
    row_count = queries.shape[0]
    block_rows = min(row_count, 512)
    query_blocks = queries.reshape((row_count // block_rows, block_rows) + queries.shape[1:])
    starts = jnp.arange(row_count // block_rows, dtype=jnp.int32) * block_rows

    def one_block(block_item):
        scores = block_scores(block_item[0], block_item[1], key_rows, segments)
        top_score = jnp.max(scores, axis=-1, keepdims=True)
        raised = jnp.exp(scores - top_score)
        exp_sum = jnp.sum(raised, axis=-1, keepdims=True)
        weights = (raised / exp_sum).astype(jnp.bfloat16)
        outputs = jnp.einsum(
            "grtu,ugd->tgrd", weights, value_rows, preferred_element_type=jnp.float32
        )
        return (outputs, top_score, exp_sum)

    outputs, top_scores, exp_sums = lax.map(one_block, (query_blocks, starts))
    return (outputs.reshape(row_count, -1), top_scores, exp_sums, query_blocks, starts)


def attention_backward(
    query_blocks, starts, key_rows, value_rows, segments, top_scores, exp_sums, out_grad
):
    row_count = key_rows.shape[0]
    grad_blocks = out_grad.reshape(query_blocks.shape)

    def one_block(carry_sums, block_item):
        key_acc, value_acc = carry_sums
        query_block, start, top_score, exp_sum, grad_block = block_item
        scores = block_scores(query_block, start, key_rows, segments)
        weights = jnp.exp(scores - top_score) / exp_sum
        weight_grad = jnp.einsum(
            "tgrd,ugd->grtu", grad_block, value_rows, preferred_element_type=jnp.float32
        )
        score_grad = (
            weights * (weight_grad - jnp.sum(weights * weight_grad, axis=-1, keepdims=True))
        ).astype(jnp.bfloat16)
        query_grad = jnp.einsum(
            "grtu,ugd->tgrd", score_grad, key_rows, preferred_element_type=jnp.float32
        ) * HEAD ** (-0.5)
        key_acc = key_acc + jnp.einsum(
            "grtu,tgrd->ugd", score_grad, query_block, preferred_element_type=jnp.float32
        ) * HEAD ** (-0.5)
        value_acc = value_acc + jnp.einsum(
            "grtu,tgrd->ugd",
            weights.astype(jnp.bfloat16),
            grad_block,
            preferred_element_type=jnp.float32,
        )
        return ((key_acc, value_acc), query_grad)

    zero_rows = jnp.zeros(key_rows.shape, jnp.float32)
    (key_grad, value_grad), query_grads = lax.scan(
        one_block, (zero_rows, zero_rows), (query_blocks, starts, top_scores, exp_sums, grad_blocks)
    )
    return (
        query_grads.reshape(row_count, -1),
        key_grad.reshape(row_count, -1),
        value_grad.reshape(row_count, -1),
    )


def shape_mixer(flat_list):
    return (
        flat_list[0].reshape(D, QKV),
        flat_list[1].reshape(D, 2 * INNER),
        flat_list[2].reshape(INNER, XPROJ),
        flat_list[3].reshape(RANK, INNER),
        flat_list[4].reshape(INNER, D),
        flat_list[5].reshape(D, D),
    )


def small_mixer(flat_list):
    return (
        flat_list[6].astype(jnp.float32).reshape(CONV, INNER),
        flat_list[7].astype(jnp.float32),
        flat_list[8].astype(jnp.float32),
        flat_list[9].astype(jnp.float32).reshape(STATE, INNER),
        flat_list[10].astype(jnp.float32),
        flat_list[11].astype(jnp.float32).reshape(4, D),
    )


def shape_ffn(flat_list):
    return (flat_list[0].reshape(D, FF), flat_list[1].reshape(D, FF), flat_list[2].reshape(FF, D))


def on_device(
    tokens,
    cotangent,
    seq_lengths,
    qkv_proj,
    mamba_in,
    select_proj,
    step_proj,
    mamba_out,
    join_out,
    conv_taps,
    conv_bias,
    step_bias,
    decay_rates,
    skip_gain,
    norm_gains,
    ffn_gate,
    ffn_up,
    ffn_down,
):
    mixer_flat = (
        lax.all_gather(qkv_proj, "fsdp", axis=0, tiled=True),
        lax.all_gather(mamba_in, "fsdp", axis=0, tiled=True),
        lax.all_gather(select_proj, "fsdp", axis=0, tiled=True),
        lax.all_gather(step_proj, "fsdp", axis=0, tiled=True),
        lax.all_gather(mamba_out, "fsdp", axis=0, tiled=True),
        lax.all_gather(join_out, "fsdp", axis=0, tiled=True),
        lax.all_gather(conv_taps, "fsdp", axis=0, tiled=True),
        lax.all_gather(conv_bias, "fsdp", axis=0, tiled=True),
        lax.all_gather(step_bias, "fsdp", axis=0, tiled=True),
        lax.all_gather(decay_rates, "fsdp", axis=0, tiled=True),
        lax.all_gather(skip_gain, "fsdp", axis=0, tiled=True),
        lax.all_gather(norm_gains, "fsdp", axis=0, tiled=True),
    )
    ffn_flat = (
        lax.all_gather(ffn_gate, "fsdp", axis=0, tiled=True),
        lax.all_gather(ffn_up, "fsdp", axis=0, tiled=True),
        lax.all_gather(ffn_down, "fsdp", axis=0, tiled=True),
    )
    qkv_matrix, mamba_in_matrix, select_matrix, step_matrix, mamba_out_matrix, join_matrix = (
        shape_mixer(mixer_flat)
    )
    tap_matrix, conv_shift, step_shift, decay_matrix, skip_row, gain_rows = small_mixer(mixer_flat)
    gate_matrix, up_matrix, down_matrix = shape_ffn(ffn_flat)
    row_count = tokens.shape[0]
    segments = segment_ids(seq_lengths, row_count)
    live_rows = (segments < seq_lengths.shape[0]).astype(jnp.float32)
    keep_rows = keep_flags(segments)
    inputs = tokens.astype(jnp.float32)
    normed_full, norm_pull = jax.vjp(rms_scale, inputs, gain_rows[0])
    normed = normed_full.astype(jnp.bfloat16)
    qkv_rows = flat_product(normed, qkv_matrix).astype(jnp.bfloat16)
    queries = qkv_rows[:, :D].reshape(row_count, KV_HEADS, HEADS // KV_HEADS, HEAD)
    key_rows = qkv_rows[:, D : D + KV_HEADS * HEAD].reshape(row_count, KV_HEADS, HEAD)
    value_rows = qkv_rows[:, D + KV_HEADS * HEAD :].reshape(row_count, KV_HEADS, HEAD)
    attn_rows, top_scores, exp_sums, query_blocks, starts = attention_forward(
        queries, key_rows, value_rows, segments
    )
    mixed_in = flat_product(normed, mamba_in_matrix)

    def conv_piece(inner_rows, tap_values, shift_values):
        return conv_silu(inner_rows, tap_values, shift_values, segments)

    conv_act, conv_pull = jax.vjp(conv_piece, mixed_in[:, :INNER], tap_matrix, conv_shift)
    conv_low = conv_act.astype(jnp.bfloat16)
    selected = flat_product(conv_low, select_matrix)
    step_low = selected[:, :RANK].astype(jnp.bfloat16)
    step_pre = flat_product(step_low, step_matrix)

    def core_piece(
        conv_values,
        select_values,
        step_values,
        gate_values,
        shift_values,
        decay_values,
        skip_values,
    ):
        return mamba_core(
            conv_values,
            select_values,
            step_values,
            gate_values,
            shift_values,
            decay_values,
            skip_values,
            keep_rows,
        )

    gated_full, core_pull = jax.vjp(
        core_piece,
        conv_act,
        selected[:, RANK:],
        step_pre,
        mixed_in[:, INNER:],
        step_shift,
        decay_matrix,
        skip_row,
    )
    gated = gated_full.astype(jnp.bfloat16)
    mamba_rows = flat_product(gated, mamba_out_matrix)
    joined_full, join_pull = jax.vjp(
        join_branches, attn_rows, mamba_rows, gain_rows[1], gain_rows[2]
    )
    joined = joined_full.astype(jnp.bfloat16)
    middle = inputs + flat_product(joined, join_matrix)
    normed_two_full, norm_two_pull = jax.vjp(rms_scale, middle, gain_rows[3])
    normed_two = normed_two_full.astype(jnp.bfloat16)
    gate_rows = flat_product(normed_two, gate_matrix)
    up_rows = flat_product(normed_two, up_matrix)
    act_full, act_pull = jax.vjp(swiglu, gate_rows, up_rows)
    activated = act_full.astype(jnp.bfloat16)
    result_rows = middle + flat_product(activated, down_matrix)
    block_out = (result_rows * live_rows[:, None]).astype(jnp.bfloat16)
    ffn_flat = (
        lax.all_gather(ffn_gate, "fsdp", axis=0, tiled=True),
        lax.all_gather(ffn_up, "fsdp", axis=0, tiled=True),
        lax.all_gather(ffn_down, "fsdp", axis=0, tiled=True),
    )
    gate_matrix, up_matrix, down_matrix = shape_ffn(ffn_flat)
    out_grad = cotangent.astype(jnp.float32) * live_rows[:, None]
    down_low = out_grad.astype(jnp.bfloat16)
    down_weight_grad = outer_sum(activated, down_low)
    gate_grad, up_grad = act_pull(back_product(down_low, down_matrix))
    gate_low = gate_grad.astype(jnp.bfloat16)
    up_low = up_grad.astype(jnp.bfloat16)
    gate_weight_grad = outer_sum(normed_two, gate_low)
    up_weight_grad = outer_sum(normed_two, up_low)
    middle_norm_grad, ffn_gain_grad = norm_two_pull(
        back_product(gate_low, gate_matrix) + back_product(up_low, up_matrix)
    )
    middle_grad = out_grad + middle_norm_grad
    ffn_sums = (
        lax.psum_scatter(gate_weight_grad.reshape(-1), "fsdp", scatter_dimension=0, tiled=True),
        lax.psum_scatter(up_weight_grad.reshape(-1), "fsdp", scatter_dimension=0, tiled=True),
        lax.psum_scatter(down_weight_grad.reshape(-1), "fsdp", scatter_dimension=0, tiled=True),
    )
    mixer_flat = (
        lax.all_gather(qkv_proj, "fsdp", axis=0, tiled=True),
        lax.all_gather(mamba_in, "fsdp", axis=0, tiled=True),
        lax.all_gather(select_proj, "fsdp", axis=0, tiled=True),
        lax.all_gather(step_proj, "fsdp", axis=0, tiled=True),
        lax.all_gather(mamba_out, "fsdp", axis=0, tiled=True),
        lax.all_gather(join_out, "fsdp", axis=0, tiled=True),
        lax.all_gather(conv_taps, "fsdp", axis=0, tiled=True),
        lax.all_gather(conv_bias, "fsdp", axis=0, tiled=True),
        lax.all_gather(step_bias, "fsdp", axis=0, tiled=True),
        lax.all_gather(decay_rates, "fsdp", axis=0, tiled=True),
        lax.all_gather(skip_gain, "fsdp", axis=0, tiled=True),
        lax.all_gather(norm_gains, "fsdp", axis=0, tiled=True),
    )
    qkv_matrix, mamba_in_matrix, select_matrix, step_matrix, mamba_out_matrix, join_matrix = (
        shape_mixer(mixer_flat)
    )
    join_low = middle_grad.astype(jnp.bfloat16)
    join_weight_grad = outer_sum(joined, join_low)
    attn_grad, mamba_grad, attn_gain_grad, mamba_gain_grad = join_pull(
        back_product(join_low, join_matrix)
    )
    mamba_low = mamba_grad.astype(jnp.bfloat16)
    mamba_out_weight_grad = outer_sum(gated, mamba_low)
    (
        conv_core_grad,
        select_part_grad,
        step_pre_grad,
        gate_in_grad,
        step_shift_grad,
        decay_grad,
        skip_grad,
    ) = core_pull(back_product(mamba_low, mamba_out_matrix))
    step_low_grad = step_pre_grad.astype(jnp.bfloat16)
    step_weight_grad = outer_sum(step_low, step_low_grad)
    select_low = jnp.concatenate(
        [back_product(step_low_grad, step_matrix), select_part_grad], axis=1
    ).astype(jnp.bfloat16)
    select_weight_grad = outer_sum(conv_low, select_low)
    conv_grad = conv_core_grad + back_product(select_low, select_matrix)
    conv_in_grad, taps_grad, conv_shift_grad = conv_pull(conv_grad)
    mixed_low = jnp.concatenate([conv_in_grad, gate_in_grad], axis=1).astype(jnp.bfloat16)
    mamba_in_weight_grad = outer_sum(normed, mixed_low)
    query_grad, key_grad, value_grad = attention_backward(
        query_blocks,
        starts,
        key_rows,
        value_rows,
        segments,
        top_scores,
        exp_sums,
        attn_grad.astype(jnp.bfloat16),
    )
    qkv_low = jnp.concatenate([query_grad, key_grad, value_grad], axis=1).astype(jnp.bfloat16)
    qkv_weight_grad = outer_sum(normed, qkv_low)
    normed_grad = back_product(qkv_low, qkv_matrix) + back_product(mixed_low, mamba_in_matrix)
    input_norm_grad, input_gain_grad = norm_pull(normed_grad)
    input_grad = middle_grad + input_norm_grad
    gain_grads = jnp.stack(
        [input_gain_grad, attn_gain_grad, mamba_gain_grad, ffn_gain_grad]
    ).reshape(-1)
    mixer_sums = (
        lax.psum_scatter(qkv_weight_grad.reshape(-1), "fsdp", scatter_dimension=0, tiled=True),
        lax.psum_scatter(mamba_in_weight_grad.reshape(-1), "fsdp", scatter_dimension=0, tiled=True),
        lax.psum_scatter(select_weight_grad.reshape(-1), "fsdp", scatter_dimension=0, tiled=True),
        lax.psum_scatter(step_weight_grad.reshape(-1), "fsdp", scatter_dimension=0, tiled=True),
        lax.psum_scatter(
            mamba_out_weight_grad.reshape(-1), "fsdp", scatter_dimension=0, tiled=True
        ),
        lax.psum_scatter(join_weight_grad.reshape(-1), "fsdp", scatter_dimension=0, tiled=True),
        lax.psum_scatter(taps_grad.reshape(-1), "fsdp", scatter_dimension=0, tiled=True),
        lax.psum_scatter(conv_shift_grad, "fsdp", scatter_dimension=0, tiled=True),
        lax.psum_scatter(step_shift_grad, "fsdp", scatter_dimension=0, tiled=True),
        lax.psum_scatter(decay_grad.reshape(-1), "fsdp", scatter_dimension=0, tiled=True),
        lax.psum_scatter(skip_grad, "fsdp", scatter_dimension=0, tiled=True),
        lax.psum_scatter(gain_grads, "fsdp", scatter_dimension=0, tiled=True),
    )
    return (block_out, input_grad) + tuple(mixer_sums) + tuple(ffn_sums)


PLANES = 4
CHIPS = 4
CORES = 2
PLANE_DEV = CHIPS * CORES
FAST_DEV = PLANES * PLANE_DEV
RING = (0, 1, 3, 2)
MAIN_D = 48
MAIN_I = 96
SLICE_FF = FF // FAST_DEV
PAD_FF = 176
HALF_GU = 768
WIDE = 8704
GU = 2 * HALF_GU
REST_ROWS = 224
SMALL_ROWS = 208
LANES = 640
BIG = 1e30
LOG2E = 1.4426950408889634


def ring_place(k):
    return k + k // 2 - 2 * (k // 3)


class Links:
    def __init__(self, send_sems, recv_sems):
        me = lax.axis_index("fsdp")
        self.z, self.v, self.c = me // PLANE_DEV, (me // CORES) % CHIPS, me % CORES
        zp, vp = ring_place(self.z), ring_place(self.v)
        self.z_at = [ring_place((zp + k) % PLANES) for k in range(PLANES)]
        self.v_at = [ring_place((vp + k) % CHIPS) for k in range(CHIPS)]
        z, v, c = self.z, self.v, self.c
        self.z_next = self.z_at[1] * PLANE_DEV + v * CORES + c
        self.z_prev = self.z_at[3] * PLANE_DEV + v * CORES + c
        self.right = z * PLANE_DEV + self.v_at[1] * CORES + c
        self.left = z * PLANE_DEV + self.v_at[3] * CORES + c
        self.partner = me + 1 - 2 * c
        self.sems = send_sems, recv_sems
        self.copies, self.used = [], 0

    def greet(self):
        barrier = pltpu.get_barrier_semaphore()
        greeted = (self.right, self.left, self.z_next, self.z_prev, self.partner)
        for d in greeted:
            pl.semaphore_signal(barrier, inc=1, device_id=(d,), device_id_type=pl.DeviceIdType.MESH)
        pl.semaphore_wait(barrier, len(greeted))

    def send(self, src, dst, target):
        k, self.used = self.used, self.used + 1
        copy = pltpu.make_async_remote_copy(
            src_ref=src, dst_ref=dst, send_sem=self.sems[0].at[k], recv_sem=self.sems[1].at[k],
            device_id=(target,), device_id_type=pl.DeviceIdType.MESH,
        )
        copy.start()
        self.copies.append(copy)
        return copy

    def finish(self):
        for copy in self.copies:
            copy.wait_send()


class Gather:
    def __init__(self, links, source, place, local_sem):
        self.links, self.source, self.place = links, source, place
        self.along, self.near_in, self.far_in, self.core_in = {}, {}, {}, []
        self.own = pltpu.make_async_copy(source, self.block(0, OWN), local_sem)
        self.own.start()

    def block(self, back, chip):
        links = self.links
        return self.place(links.z_at[(PLANES - back) % PLANES], links.v_at[chip], links.c)

    def to_core(self, src, dst):
        self.core_in.append(self.links.send(src, dst, self.links.partner))

    def hop(self, s):
        links, here = self.links, self.block(s, OWN)
        if s:
            self.along[s - 1].wait_recv()
        src = here if s else self.source
        if s < PLANES - 1:
            self.along[s] = links.send(src, here, links.z_next)
        self.near_in[s, LEFT] = links.send(src, here, links.right)
        self.near_in[s, RIGHT] = links.send(src, here, links.left)
        self.to_core(src, here)

    def near(self, s):
        links = self.links
        for chip in (LEFT, RIGHT):
            self.near_in[s, chip].wait_recv()
            here = self.block(s, chip)
            if (chip == LEFT) == (s < 2):
                self.far_in[s] = links.send(here, here, links.right if chip == LEFT else links.left)
            self.to_core(here, here)

    def far(self, s):
        self.far_in[s].wait_recv()
        here = self.block(s, FAR)
        self.to_core(here, here)

    def wait(self):
        self.own.wait()
        for copy in self.core_in:
            copy.wait_recv()


GATHER_SENDS = 31
OWN, RIGHT, FAR, LEFT = range(CHIPS)


def shard_place(name, out):
    if name == "mamba_out":
        return lambda z, v, c: out.at[(z // 2) * 16 + c * 8 + (z % 2) * 4 + v]
    if name == "smalls":
        return lambda z, v, c: out.at[z * PLANE_DEV + v * CORES + c]
    return lambda z, v, c: out.at[c * 16 + z * 4 + v]


def gather_first_kernel(names, *refs):
    count = len(names)
    ins, units, outs, moved = refs[:count], refs[count : count + 2], refs[count + 2 : 2 * count + 2], refs[2 * count + 2 :]
    (gu_1, down_1, down_2), (send_sems, recv_sems, local) = moved[:3], moved[3:]
    links = Links(send_sems, recv_sems)
    links.greet()
    gathers = []
    for k, name in enumerate(names):
        parts = 2 if name == "wide" else 1
        width = ins[k].shape[1] // parts
        for part in range(parts):
            columns = pl.ds(part * width, width)
            place = shard_place(name, outs[k])

            def part_place(z, v, c, place=place, columns=columns):
                return place(z, v, c).at[:, columns]

            gathers.append(Gather(links, ins[k].at[:, columns], part_place, local.at[len(gathers)]))
    for s in range(PLANES):
        for g in gathers:
            g.hop(s)
    hops = [links.send(units[0], gu_1, links.z_next), links.send(units[1], down_1, links.z_next)]
    for s in range(PLANES):
        for g in gathers:
            g.near(s)
    for s in range(PLANES):
        for g in gathers:
            g.far(s)
        if s == 0:
            hops[1].wait_recv()
            hops.append(links.send(down_1, down_2, links.z_next))
    for g in gathers:
        g.wait()
    hops[0].wait_recv()
    hops[2].wait_recv()
    links.finish()


def gather_first(names, blocks, units):
    count, sends = len(names), GATHER_SENDS * (len(names) + 1) + 3
    sem, anywhere = pltpu.SemaphoreType.DMA, pl.BlockSpec(memory_space=pl.ANY)
    shapes = [(FAST_DEV,) + block.shape for block in blocks] + [units[0].shape] + [units[1].shape] * 2
    return pl.pallas_call(
        functools.partial(gather_first_kernel, names),
        out_shape=[jax.ShapeDtypeStruct(shape, jnp.bfloat16) for shape in shapes],
        in_specs=[anywhere] * (count + 2),
        out_specs=[anywhere] * (count + 3),
        scratch_shapes=[sem((sends,))] * 2 + [sem((count + 1,))],
        compiler_params=pltpu.CompilerParams(collective_id=0, has_side_effects=True),
        name="gather_first",
    )(*blocks, *units)


REST_COLUMNS = 1152
WIDE_BLOCKS = [(0, 7 * REST_COLUMNS, WIDE - 7 * REST_COLUMNS)] + [(0, k * REST_COLUMNS, REST_COLUMNS) for k in range(7)]
BRANCH_BLOCKS = [(0, 0, 768), (0, 768, 832), (1, 0, 768), (1, 768, 832)]
GRAD_ROWS = 192
GROUPS = PLANES * CHIPS
GAIN_LANES = 256


def add_rows(target, *others):
    @pl.loop(0, target.shape[0] // 16)
    def _(k):
        rows = pl.ds(pl.multiple_of(k * 16, 16), 16)
        total = target[rows, :].astype(jnp.float32)
        for other in others:
            total = total + other[rows, :].astype(jnp.float32)
        target[rows, :] = total.astype(target.dtype)


class Taker:
    def __init__(self, refs):
        self.refs = list(refs)

    def __call__(self, count):
        taken, self.refs = self.refs[:count], self.refs[count:]
        return taken


class SumPlan:
    def __init__(self, blocks, shard_rows, rest_rows, rest_columns, columns, rests, lows, smalls=None):
        self.blocks, self.rest_rows, self.has_smalls = blocks, rest_rows, smalls is not None
        self.operands = list(columns) + list(rests) + list(lows) + ([smalls] if self.has_smalls else [])
        f32, bf16 = jnp.float32, jnp.bfloat16
        self.pairs, rows = len(lows), lows[0].shape[0]
        self.out_shape = [jax.ShapeDtypeStruct((r, y.shape[1]), f32) for r, y in zip(shard_rows, lows)]
        self.out_shape.append(jax.ShapeDtypeStruct((16, rest_columns), f32))
        scratch = [pltpu.VMEM((x.shape[0] * x.shape[1] // CORES, CORES * rows), bf16) for x in columns]
        scratch += [pltpu.VMEM((x.shape[1], CORES * rows), bf16) for x in rests]
        scratch += [pltpu.VMEM((CORES * rows, y.shape[1]), bf16) for y in lows]
        scratch.append(pltpu.VMEM((16 * GROUPS, rest_columns), f32))
        shapes = [(shard_rows[pair], n) for pair, _, n in blocks] + [(16, rest_columns)]
        if self.has_smalls:
            shapes.append((smalls.shape[1] // GROUPS, smalls.shape[2]))
            scratch.append(pltpu.VMEM(smalls.shape[1:], bf16))
            self.out_shape.append(jax.ShapeDtypeStruct(shapes[-1], f32))
        for copies in (0, 4, 4, 4, 3):
            scratch += [pltpu.VMEM((copies, r, n) if copies else (GROUPS * r, n), bf16) for r, n in shapes]
        sem = pltpu.SemaphoreType.DMA
        self.count = len(shapes)
        scratch += [sem((self.count, k)) for k in (4, 4, 8, 8, 3, 3)] + [sem((self.pairs, 5))] * 3
        self.scratch = scratch


class Summing:
    def __init__(self, plan, links, ins, totals, scratch, early=2):
        self.blocks, self.rest_rows, self.has_smalls = plan.blocks, plan.rest_rows, plan.has_smalls
        self.pairs, self.count = plan.pairs, plan.count
        self.links = links
        take = Taker(ins)
        self.columns_in, self.rests_in, self.lows_in = take(self.pairs), take(self.pairs), take(self.pairs)
        self.smalls_in = take(int(self.has_smalls))
        take = Taker(totals)
        self.totals, self.rest_total = take(self.pairs), take(1)[0]
        self.smalls_total = take(int(self.has_smalls))
        take = Taker(scratch)
        self.columns_all, self.rests_all, self.lows_all = take(self.pairs), take(self.pairs), take(self.pairs)
        self.rest_stage, self.smalls_stage = take(1)[0], take(int(self.has_smalls))
        self.partial, self.through, self.from_left, self.from_right, self.along = [take(self.count) for _ in range(5)]
        self.t_send, self.t_recv, self.s_send, self.s_recv, self.z_send, self.z_recv = take(6)
        self.c_send, self.c_recv, self.local = take(3)
        self.rest_at, self.smalls_at = len(self.blocks), len(self.blocks) + 1
        self.group_rows = [p.shape[0] // GROUPS for p in self.partial]
        self.sent, self.own, self.arriving = [], [], {}
        self.extra_rest = None
        self.order = list(range(len(self.blocks)))
        if self.has_smalls:
            self.order.insert(2, self.smalls_at)
        self.order.append(self.rest_at)
        events = []
        for p, i in enumerate(self.order):
            events += [
                (p - early, self.launch_far, i), (p, self.launch_near, i), (p + 1.5, self.relay, i),
                (p + 2.5, self.collect, i), (p + 3.5, self.planes, i, 2), (p + 4.5, self.planes, i, 1),
                (p + 5.5, self.planes, i, 0),
            ]
        self.events = sorted(events, key=lambda event: event[0])

    def send(self, key, src, dst, ss, rs, target):
        copy = pltpu.make_async_remote_copy(
            src_ref=src, dst_ref=dst, send_sem=ss, recv_sem=rs, device_id=(target,),
            device_id_type=pl.DeviceIdType.MESH,
        )
        copy.start()
        self.sent.append(copy)
        self.arriving[key] = copy

    def stay(self, src, dst, sem):
        copy = pltpu.make_async_copy(src, dst, sem)
        copy.start()
        self.own.append(copy)

    def exchange(self):
        c, partner = self.links.c, self.links.partner
        c_send, c_recv, local = self.c_send, self.c_recv, self.local
        for k in range(self.pairs):
            columns_in, columns_all = self.columns_in[k], self.columns_all[k]
            lows_in, rests_in = self.lows_in[k], self.rests_in[k]
            rows = lows_in.shape[0]
            half = columns_in.shape[1] // CORES
            mine, other = pl.ds(0, rows), pl.ds(rows, rows)
            self.stay(lows_in, self.lows_all[k].at[mine], local.at[k, 0])
            self.send(("l", k), lows_in, self.lows_all[k].at[other], c_send.at[k, 0], c_recv.at[k, 0], partner)
            self.stay(rests_in.at[c], self.rests_all[k].at[:, mine], local.at[k, 1])
            self.send(
                ("r", k), rests_in.at[1 - c], self.rests_all[k].at[:, other], c_send.at[k, 1], c_recv.at[k, 1], partner
            )
            for h in range(columns_in.shape[0]):
                place = pl.ds(h * half, half)
                self.stay(
                    columns_in.at[h, pl.ds(pl.multiple_of(c * half, half), half)],
                    columns_all.at[place, mine],
                    local.at[k, 2 + h],
                )
                self.send(
                    ("x", k, h),
                    columns_in.at[h, pl.ds(pl.multiple_of((1 - c) * half, half), half)],
                    columns_all.at[place, other],
                    c_send.at[k, 2 + h],
                    c_recv.at[k, 2 + h],
                    partner,
                )
        if self.has_smalls:
            smalls = self.smalls_in[0]
            self.stay(smalls.at[c], self.partial[self.smalls_at], local.at[0, 4])
            self.send(("m",), smalls.at[1 - c], self.smalls_stage[0], c_send.at[0, 4], c_recv.at[0, 4], partner)

    def exchanged(self):
        for copy in self.own:
            copy.wait()
        for k in range(self.pairs):
            self.arriving["l", k].wait_recv()
            self.arriving["r", k].wait_recv()
            for h in range(self.columns_in[k].shape[0]):
                self.arriving["x", k, h].wait_recv()

    def rest_block(self):
        stage = self.rest_stage
        stage[...] = jnp.zeros_like(stage)
        row, width = 0, stage.shape[1]
        for k in range(self.pairs):
            r, lows = self.rest_rows[k], self.lows_all[k]
            for column in range(0, lows.shape[1], width):
                columns = min(width, lows.shape[1] - column)
                product = flat_product(self.rests_all[k][...], lows[:, column : column + columns])
                for g in range(GROUPS):
                    at = 16 * g + row
                    stage[at : at + r, :columns] = product[g * r : (g + 1) * r]
                row += r
        if self.extra_rest is not None:
            self.extra_rest(stage)
        self.partial[self.rest_at][...] = stage[...].astype(jnp.bfloat16)

    def compute(self, i):
        partial = self.partial[i]
        if i == self.rest_at:
            self.rest_block()
            return
        if i == self.smalls_at:
            self.arriving["m",].wait_recv()
            add_rows(partial, self.smalls_stage[0])
            return
        pair, column, columns = self.blocks[i]

        @pl.loop(0, partial.shape[0] // GRAD_ROWS)
        def _(j):
            rows = pl.ds(pl.multiple_of(j * GRAD_ROWS, GRAD_ROWS), GRAD_ROWS)
            partial[rows, :] = flat_product(
                self.columns_all[pair][rows, :], self.lows_all[pair][:, pl.ds(column, columns)]
            ).astype(jnp.bfloat16)

    def part(self, i, k, chip):
        rows = self.group_rows[i]
        at = (self.links.z_at[k] * CHIPS + self.links.v_at[chip]) * rows
        return self.partial[i].at[pl.ds(pl.multiple_of(at, rows), rows)]

    def launch_far(self, i):
        self.compute(i)
        for k in (3, 2, 1, 0):
            self.send(
                (i, "t", k), self.part(i, k, FAR), self.through[i].at[k], self.t_send.at[i, k], self.t_recv.at[i, k],
                self.links.right if k % 2 else self.links.left,
            )

    def launch_near(self, i):
        for k in (3, 2, 1, 0):
            landing, event = (self.from_right, 4 + k) if k % 2 else (self.from_left, k)
            self.send(
                (i, "s", event), self.part(i, k, LEFT if k % 2 else RIGHT), landing[i].at[k],
                self.s_send.at[i, event], self.s_recv.at[i, event], self.links.left if k % 2 else self.links.right,
            )

    def relay(self, i):
        for k in (3, 2, 1, 0):
            self.arriving[i, "t", k].wait_recv()
            add_rows(self.through[i].at[k], self.part(i, k, RIGHT if k % 2 else LEFT))
            landing, event = (self.from_left, k) if k % 2 else (self.from_right, 4 + k)
            self.send(
                (i, "s", event), self.through[i].at[k], landing[i].at[k], self.s_send.at[i, event],
                self.s_recv.at[i, event], self.links.right if k % 2 else self.links.left,
            )

    def pass_on(self, i, k):
        self.send(
            (i, "z", 3 - k), self.part(i, k, OWN), self.along[i].at[3 - k], self.z_send.at[i, 3 - k],
            self.z_recv.at[i, 3 - k], self.links.z_next,
        )

    def collect(self, i):
        for k in (3, 2, 1, 0):
            self.arriving[i, "s", k].wait_recv()
            self.arriving[i, "s", 4 + k].wait_recv()
            add_rows(self.part(i, k, OWN), self.from_left[i].at[k], self.from_right[i].at[k])
            if k == 3:
                self.pass_on(i, 3)

    def planes(self, i, k):
        self.arriving[i, "z", 2 - k].wait_recv()
        mine, along = self.part(i, k, OWN), self.along[i]
        if k:
            add_rows(mine, along.at[2 - k])
            self.pass_on(i, k)
            return
        if i == self.rest_at:
            total, column, columns = self.rest_total, 0, self.rest_total.shape[1]
        elif i == self.smalls_at:
            total, column, columns = self.smalls_total[0], 0, self.smalls_total[0].shape[1]
        else:
            pair, column, columns = self.blocks[i]
            total = self.totals[pair]

        @pl.loop(0, self.group_rows[i] // 16)
        def _(j):
            rows = pl.ds(pl.multiple_of(j * 16, 16), 16)
            total[rows, pl.ds(column, columns)] = mine[rows, :].astype(jnp.float32) + along[2, rows, :].astype(
                jnp.float32
            )

    def advance(self, until):
        while self.events and self.events[0][0] < until:
            _, stage, *which = self.events.pop(0)
            stage(*which)

    def finish(self):
        self.advance(1e9)
        for copy in self.sent:
            copy.wait_send()


UNIT_PAD = 64
BACK_LANES = 512


def last_kernel(plan, *refs):
    bf16, f32 = jnp.bfloat16, jnp.float32
    take = Taker(refs)
    ins = take(len(plan.operands))
    middle_grad_ref, tokens_ref, gains_ref, table_d_ref, wide_ref, wide_rest_ref = take(6)
    gu_grad_ref, down_grad_ref, gu_came_ref, down_came_ref = take(4)
    totals = take(len(plan.out_shape))
    input_grad_ref, gate_out_ref, up_out_ref, down_out_ref = take(4)
    scratch = take(len(plan.scratch))
    order, wide_buffer, total, gain, gain_other = take(5)
    gu_own, gu_sum, gu_next, down_own, down_sum, down_next, gu_rows, gu_in = take(8)
    wide_sem, unit_sem, send_sems, recv_sems = take(4)
    count = WIDE // BACK_LANES
    links = Links(send_sems, recv_sems)
    me = lax.axis_index("fsdp")
    first = me // PLANE_DEV * PLANE_DEV
    others = [first + (me % PLANE_DEV + k) % PLANE_DEV for k in range(1, PLANE_DEV)]
    barrier = pltpu.get_barrier_semaphore()
    for d in others + [links.z_next, links.z_prev]:
        pl.semaphore_signal(barrier, inc=1, device_id=(d,), device_id_type=pl.DeviceIdType.MESH)
    pl.semaphore_wait(barrier, len(others) + 2)

    summing = Summing(plan, links, ins, totals, scratch)
    summing.exchange()
    gu_height, down_height = gu_own.shape[0], down_own.shape[0]
    wide_low = summing.lows_all[0].at[pl.ds(0, tokens_ref.shape[0])]

    def piece(ref, height, k):
        return ref.at[pl.ds(pl.multiple_of(links.z_at[k] * height, 16), height)]

    middle_copy = pltpu.make_async_copy(middle_grad_ref, input_grad_ref, unit_sem.at[4])
    middle_copy.start()
    moving = gu_sum.at[pl.ds(0, gu_height)]
    loads = [
        pltpu.make_async_copy(gu_came_ref, moving, unit_sem.at[0]),
        pltpu.make_async_copy(down_came_ref, down_sum, unit_sem.at[1]),
    ]
    def load_own(k):
        copies = [
            pltpu.make_async_copy(piece(gu_grad_ref, gu_height, k), gu_own, unit_sem.at[2]),
            pltpu.make_async_copy(piece(down_grad_ref, down_height, k), down_own, unit_sem.at[3]),
        ]
        for copy in copies:
            copy.start()
        return copies

    loads += load_own(1)
    for copy in loads[:2]:
        copy.start()
    def column_copy(j):
        return pltpu.make_async_copy(
            wide_ref.at[:, pl.ds(j * BACK_LANES, BACK_LANES)], wide_buffer.at[j % 2], wide_sem.at[j % 2]
        )

    column_copy(0).start()
    column_copy(1).start()
    summing.exchanged()
    summing.advance(1.2)
    for copy in loads:
        copy.wait()
    add_rows(moving, gu_own)
    add_rows(down_sum, down_own)
    loads = load_own(0)
    hops = [links.send(moving, gu_next, links.z_next), links.send(down_sum, down_next, links.z_next)]

    write_order(table_d_ref, order)
    total[...] = jnp.zeros_like(total)
    for j in range(count):
        column_copy(j).wait()
        total[...] += back_product(wide_low[:, j * BACK_LANES : (j + 1) * BACK_LANES], wide_buffer[j % 2])
        if j + 2 < count:
            column_copy(j + 2).start()
        if j % 4 == 3:
            summing.advance(1.2 + (j + 1) // 4)
    normed_grad = move_back(
        order, jnp.concatenate([total[...], back_product(wide_low[...], wide_rest_ref[...])], axis=1)
    )
    unit, scale = rms_parts(tokens_ref[...].astype(f32))
    back, gain_grad = rms_pull(unit, scale, gains_ref[0:1], normed_grad)
    middle_copy.wait()
    input_grad_ref[...] += back
    gain[...] = jnp.broadcast_to(gain_grad, gain.shape)
    gain_copy = links.send(gain, gain_other, links.partner)
    summing.advance(6.2)

    def gain_rows(stage):
        gain_copy.wait_recv()
        size = 4 * D // FAST_DEV
        lane = lax.broadcasted_iota(jnp.int32, (D, CHIPS * GAIN_LANES), 1)
        source = (lane // GAIN_LANES) * (CORES * size) + links.c * size + lane % GAIN_LANES
        place = lax.broadcasted_iota(jnp.int32, (D, CHIPS * GAIN_LANES), 0)
        picks = (place == source) & (lane % GAIN_LANES < size)
        select = order.at[:, pl.ds(0, CHIPS * GAIN_LANES)]
        select[...] = jnp.where(picks, 1.0, 0.0).astype(bf16)
        both = gain[0:1] + gain_other[0:1]
        both = jnp.broadcast_to(both, (16, D))
        high = both.astype(bf16)
        rest = (both - high.astype(f32)).astype(bf16)
        moved = flat_product(high, select[...]) + flat_product(rest, select[...])
        width, last = stage.shape[1], WIDE % REST_COLUMNS
        for v in range(CHIPS):
            stage[16 * v + 14 : 16 * v + 15, last : last + GAIN_LANES] = moved[
                0:1, v * GAIN_LANES : (v + 1) * GAIN_LANES
            ]

    summing.extra_rest = gain_rows
    summing.advance(7.2)
    for copy in hops:
        copy.wait()
        links.copies.remove(copy)
    for copy in loads:
        copy.wait()
    rows = D // FAST_DEV

    for piece_at in range(0, GU, GAIN_LANES):
        lanes = pl.ds(piece_at, GAIN_LANES)

        @pl.loop(0, gu_height // 16)
        def _(k):
            some = pl.ds(pl.multiple_of(k * 16, 16), 16)
            gu_rows[some, :] = gu_own[some, lanes].astype(f32) + gu_next[some, lanes].astype(f32)

        for p in range(PLANE_DEV):
            gu_sum[p * UNIT_PAD : (p + 1) * UNIT_PAD, lanes] = gu_rows[p * rows : p * rows + UNIT_PAD, :].astype(bf16)

    @pl.loop(0, down_height // 16)
    def _(k):
        some = pl.ds(pl.multiple_of(k * 16, 16), 16)
        down_out_ref[some, :] = down_own[some, :].astype(f32) + down_next[some, :].astype(f32)


    def unit_block(d):
        return gu_sum.at[pl.ds(pl.multiple_of(d % PLANE_DEV * UNIT_PAD, UNIT_PAD), UNIT_PAD)]

    keep = pltpu.make_async_copy(unit_block(me), gu_in.at[me % PLANE_DEV], unit_sem.at[5])
    keep.start()
    given = [links.send(unit_block(d), gu_in.at[me % PLANE_DEV], d) for d in others]
    summing.advance(12.2)
    for copy in given:
        copy.wait_recv()
    keep.wait()
    for half, out_ref in enumerate((gate_out_ref, up_out_ref)):
        for p in range(PLANE_DEV):
            for k in range(PLANES):
                column = half * HALF_GU + k * PAD_FF
                place = (k * PLANE_DEV + p) * SLICE_FF
                out_ref[:, place : place + SLICE_FF] = gu_in[p, :rows, column : column + SLICE_FF]
    summing.finish()
    links.finish()


def last_sums(plan, *operands):
    bf16, f32 = jnp.bfloat16, jnp.float32
    rows, gu_came, down_came = operands[0].shape[0], operands[8], operands[9]
    vmem, anywhere = pl.BlockSpec(memory_space=pltpu.VMEM), pl.BlockSpec(memory_space=pl.ANY)
    in_specs = [anywhere] * len(plan.operands) + [anywhere] + [vmem] * 3 + [anywhere, vmem] + [anywhere] * 4
    out_shape = plan.out_shape + [
        jax.ShapeDtypeStruct((rows, D), f32),
        jax.ShapeDtypeStruct((D // FAST_DEV, FF), bf16),
        jax.ShapeDtypeStruct((D // FAST_DEV, FF), bf16),
        jax.ShapeDtypeStruct(down_came.shape, f32),
    ]
    unit, downs = gu_came.shape, down_came.shape
    pad = (unit[0] + UNIT_PAD, GAIN_LANES)
    sem = pltpu.SemaphoreType.DMA
    return pl.pallas_call(
        functools.partial(last_kernel, plan),
        out_shape=out_shape,
        in_specs=in_specs,
        out_specs=[vmem] * len(out_shape),
        scratch_shapes=plan.scratch
        + [
            pltpu.VMEM((D, D), bf16),
            pltpu.VMEM((2, MAIN, BACK_LANES), bf16),
            pltpu.VMEM((rows, MAIN), f32),
            pltpu.VMEM((8, D), f32),
            pltpu.VMEM((8, D), f32),
            pltpu.VMEM(unit, bf16),
            pltpu.VMEM((PLANE_DEV * UNIT_PAD, GU), bf16),
            pltpu.VMEM(unit, bf16),
            pltpu.VMEM(downs, bf16),
            pltpu.VMEM(downs, bf16),
            pltpu.VMEM(downs, bf16),
            pltpu.VMEM(pad, f32),
            pltpu.VMEM((PLANE_DEV, UNIT_PAD, GU), bf16),
            sem((2,)),
            sem((7,)),
            sem((10,)),
            sem((10,)),
        ],
        compiler_params=pltpu.CompilerParams(
            collective_id=3, has_side_effects=True, vmem_limit_bytes=63 * 1024 * 1024
        ),
        name="last_sums",
    )(*plan.operands, *operands)


def scan_setup(pre, shift, conv, hold):
    step = jax.nn.softplus(pre + shift)
    return step, step + hold, step * conv


def tiled(block):
    return jnp.concatenate([block] * (LANES // 128), axis=1)


def folded(block):
    total = block[:, :128]
    for k in range(1, LANES // 128):
        total = total + block[:, 128 * k : 128 * (k + 1)]
    return total


GROUP = HEADS // KV_HEADS


def group_scores(qkv_ref, seg_col_ref, seg_row_ref, g):
    rows = qkv_ref.shape[0]
    queries = jnp.concatenate(
        [qkv_ref[:, (g * GROUP + r) * HEAD : (g * GROUP + r + 1) * HEAD] for r in range(GROUP)], axis=0
    )
    keys = qkv_ref[:, D + g * HEAD : D + (g + 1) * HEAD]
    values = qkv_ref[:, D + (KV_HEADS + g) * HEAD : D + (KV_HEADS + g + 1) * HEAD]
    scores = back_product(queries, keys) * HEAD ** (-0.5)
    t = lax.broadcasted_iota(jnp.int32, (rows, rows), 0)
    u = lax.broadcasted_iota(jnp.int32, (rows, rows), 1)
    allowed = (seg_col_ref[...] == seg_row_ref[...]) & (u <= t)
    scores = jnp.where(jnp.concatenate([allowed] * GROUP, axis=0), scores, -1e30)
    raised = jnp.exp(scores - jnp.max(scores, axis=-1, keepdims=True))
    probs = raised / jnp.sum(raised, axis=-1, keepdims=True)
    return queries, keys, values, probs


def attention_forward_kernel(qkv_ref, seg_col_ref, seg_row_ref, out_ref):
    rows = qkv_ref.shape[0]
    for g in range(KV_HEADS):
        _, _, values, probs = group_scores(qkv_ref, seg_col_ref, seg_row_ref, g)
        mixed = flat_product(probs.astype(jnp.bfloat16), values)
        for r in range(GROUP):
            head = g * GROUP + r
            out_ref[:, head * HEAD : (head + 1) * HEAD] = mixed[r * rows : (r + 1) * rows]


def attention_backward_kernel(qkv_ref, seg_col_ref, seg_row_ref, grad_ref, low_ref, first):
    rows = qkv_ref.shape[0]
    bf16 = jnp.bfloat16
    for g in range(KV_HEADS):
        queries, keys, values, probs = group_scores(qkv_ref, seg_col_ref, seg_row_ref, g)
        grads = jnp.concatenate(
            [grad_ref[:, (g * GROUP + r) * HEAD : (g * GROUP + r + 1) * HEAD] for r in range(GROUP)], axis=0
        )
        prob_grad = back_product(grads, values)
        score_low = (
            probs * (prob_grad - jnp.sum(probs * prob_grad, axis=-1, keepdims=True))
        ).astype(bf16)
        query_grad = (flat_product(score_low, keys) * HEAD ** (-0.5)).astype(bf16)
        for r in range(GROUP):
            head = g * GROUP + r
            low_ref[:, first + head * HEAD : first + (head + 1) * HEAD] = query_grad[r * rows : (r + 1) * rows]
        key_grad = outer_sum(score_low, queries) * HEAD ** (-0.5)
        low_ref[:, first + D + g * HEAD : first + D + (g + 1) * HEAD] = key_grad.astype(bf16)
        value_grad = outer_sum(probs.astype(bf16), grads)
        low_ref[:, first + D + (KV_HEADS + g) * HEAD : first + D + (KV_HEADS + g + 1) * HEAD] = value_grad.astype(bf16)


GRAD_LANES = 256


class PlaneTotal:
    def __init__(self, links, parts, core_in, far_in, near_in):
        self.links, self.parts, self.core_in, self.far_in, self.near_in = links, parts, core_in, far_in, near_in
        self.top = pl.ds(0, parts.shape[1] // 2)
        self.low = pl.ds(parts.shape[1] // 2, parts.shape[1] // 2)
        self.core = {}

    def give(self, chip):
        self.core[chip] = self.links.send(self.parts.at[CHIPS + chip], self.core_in.at[chip], self.links.partner)

    def join(self, chip):
        self.core[chip].wait_recv()
        add_rows(self.parts.at[chip], self.core_in.at[chip])

    def start(self):
        links, parts = self.links, self.parts
        self.join(FAR)
        self.far = [
            links.send(parts.at[FAR, self.top], self.far_in.at[0], links.right),
            links.send(parts.at[FAR, self.low], self.far_in.at[1], links.left),
        ]
        self.join(RIGHT)
        self.near = [links.send(parts.at[RIGHT, self.low], self.near_in.at[0, self.low], links.right)]
        self.join(LEFT)
        self.near.append(links.send(parts.at[LEFT, self.top], self.near_in.at[1, self.top], links.left))
        self.join(OWN)

    def relay(self):
        links, parts = self.links, self.parts
        self.far[0].wait_recv()
        add_rows(parts.at[RIGHT, self.top], self.far_in.at[0])
        self.near.append(links.send(parts.at[RIGHT, self.top], self.near_in.at[0, self.top], links.right))
        self.far[1].wait_recv()
        add_rows(parts.at[LEFT, self.low], self.far_in.at[1])
        self.near.append(links.send(parts.at[LEFT, self.low], self.near_in.at[1, self.low], links.left))

    def total(self, out_ref):
        for copy in self.near:
            copy.wait_recv()

        @pl.loop(0, out_ref.shape[0] // 16)
        def _(k):
            rows = pl.ds(pl.multiple_of(k * 16, 16), 16)
            total = self.parts[OWN, rows, :].astype(jnp.float32) + self.near_in[0, rows, :].astype(jnp.float32)
            out_ref[rows, :] = total + self.near_in[1, rows, :].astype(jnp.float32)


def feed_forward_kernel(
    rows_ref, out_low_ref, gu_0_ref, gu_1_ref, gu_2_ref, gu_3_ref, down_0_ref, down_1_ref, down_2_ref, down_3_ref,
    back_ref, ffn_ref, gu_grad_ref, down_grad_ref,
    gu_ref, down_ref, rows_all, act, gu_low, back, ffn, back_core, back_far, back_near, ffn_core, ffn_far, ffn_near,
    send_sems, recv_sems, own_sem,
):
    bf16, f32 = jnp.bfloat16, jnp.float32
    rows = rows_ref.shape[0]
    links = Links(send_sems, recv_sems)
    links.greet()
    own = pltpu.make_async_copy(rows_ref, rows_all.at[OWN], own_sem.at[0])
    own.start()
    copies = []
    for matrix, parts in (
        (gu_ref, (gu_0_ref, gu_1_ref, gu_2_ref, gu_3_ref)),
        (down_ref, (down_0_ref, down_1_ref, down_2_ref, down_3_ref)),
    ):
        height = parts[0].shape[0]
        for hops, part in enumerate(parts):
            place = pl.multiple_of(links.z_at[(PLANES - hops) % PLANES] * height, 16)
            copies.append(
                pltpu.make_async_copy(part, matrix.at[pl.ds(place, height)], own_sem.at[1 + len(copies)])
            )
            copies[-1].start()
    used = PLANES * PAD_FF
    down_ref[used:, :] = jnp.zeros((HALF_GU - used, D), bf16)
    to_right = links.send(rows_ref, rows_all.at[LEFT], links.right)
    to_left = links.send(rows_ref, rows_all.at[RIGHT], links.left)
    cores = {OWN: links.send(rows_ref, rows_all.at[CHIPS + OWN], links.partner)}
    back_sum = PlaneTotal(links, back, back_core, back_far, back_near)
    ffn_sum = PlaneTotal(links, ffn, ffn_core, ffn_far, ffn_near)
    top, low = pl.ds(0, rows // 2), pl.ds(rows // 2, rows // 2)

    def compute(slot):
        here = pl.ds(slot * rows, rows)
        x = rows_all[slot]
        gu = flat_product(x, gu_ref[...])
        gate, up = gu[:, :HALF_GU], gu[:, HALF_GU:]
        opened = 1.0 / (1.0 + jnp.exp(-gate))
        act[here, :] = (gate * opened * up).astype(bf16)
        grad = back_product(out_low_ref[here, :], down_ref[...])
        gu_low[here, :HALF_GU] = (grad * up * opened * (1.0 + gate * (1.0 - opened))).astype(bf16)
        gu_low[here, HALF_GU:] = (grad * gate * opened).astype(bf16)
        back[slot] = back_product(gu_low[here, :], gu_ref[...]).astype(bf16)
        if slot >= CHIPS:
            back_sum.give(slot - CHIPS)

    own.wait()
    for copy in copies:
        copy.wait()
    compute(OWN)
    cores[OWN].wait_recv()
    compute(CHIPS + OWN)
    to_right.wait_recv()
    far = [links.send(rows_all.at[LEFT, top], rows_all.at[FAR, top], links.right)]
    cores[LEFT] = links.send(rows_all.at[LEFT], rows_all.at[CHIPS + LEFT], links.partner)
    to_left.wait_recv()
    far.append(links.send(rows_all.at[RIGHT, low], rows_all.at[FAR, low], links.left))
    cores[RIGHT] = links.send(rows_all.at[RIGHT], rows_all.at[CHIPS + RIGHT], links.partner)
    compute(LEFT)
    compute(RIGHT)
    for copy in far:
        copy.wait_recv()
    cores[FAR] = links.send(rows_all.at[FAR], rows_all.at[CHIPS + FAR], links.partner)
    compute(FAR)
    for chip in (FAR, RIGHT, LEFT):
        cores[chip].wait_recv()
        compute(CHIPS + chip)
    back_sum.start()

    def ffn_rows(slot):
        ffn[slot] = flat_product(act[slot * rows : (slot + 1) * rows], down_ref[...]).astype(bf16)
        if slot >= CHIPS:
            ffn_sum.give(slot - CHIPS)

    for chip in (FAR, RIGHT, LEFT, OWN):
        ffn_rows(CHIPS + chip)
    back_sum.relay()
    for chip in (FAR, RIGHT, LEFT, OWN):
        ffn_rows(chip)
    ffn_sum.start()

    def gu_grad(column, columns):
        left = jnp.concatenate([rows_all[slot, :, column : column + columns] for slot in range(PLANE_DEV)], axis=0)
        gu_grad_ref[column : column + columns, :] = outer_sum(left, gu_low[...]).astype(bf16)

    for column in range(0, 2 * GRAD_LANES, GRAD_LANES):
        gu_grad(column, GRAD_LANES)
    back_sum.total(back_ref)
    ffn_sum.relay()
    for column in range(2 * GRAD_LANES, D, GRAD_LANES):
        gu_grad(column, min(GRAD_LANES, D - column))
    for column in range(0, HALF_GU, GRAD_LANES):
        down_grad_ref[column : column + GRAD_LANES, :] = outer_sum(
            act[:, column : column + GRAD_LANES], out_low_ref[...]
        ).astype(bf16)
    ffn_sum.total(ffn_ref)
    links.finish()


def feed_forward(rows_low, out_low, *units):
    bf16, f32 = jnp.bfloat16, jnp.float32
    rows = rows_low.shape[0]
    vmem, anywhere = pl.BlockSpec(memory_space=pltpu.VMEM), pl.BlockSpec(memory_space=pl.ANY)

    def slots(count, height=rows):
        return pltpu.VMEM((count, height, D), bf16)

    sums = [slots(CHIPS), slots(2, rows // 2), slots(2)]
    return pl.pallas_call(
        feed_forward_kernel,
        out_shape=[
            jax.ShapeDtypeStruct((rows, D), f32),
            jax.ShapeDtypeStruct((rows, D), f32),
            jax.ShapeDtypeStruct((D, GU), bf16),
            jax.ShapeDtypeStruct((HALF_GU, D), bf16),
        ],
        in_specs=[anywhere, vmem] + [anywhere] * len(units),
        out_specs=[vmem] * 4,
        scratch_shapes=[
            pltpu.VMEM((D, GU), bf16),
            pltpu.VMEM((HALF_GU, D), bf16),
            slots(PLANE_DEV),
            pltpu.VMEM((PLANE_DEV * rows, HALF_GU), bf16),
            pltpu.VMEM((PLANE_DEV * rows, GU), bf16),
            slots(PLANE_DEV),
            slots(PLANE_DEV),
        ]
        + sums
        + sums
        + [pltpu.SemaphoreType.DMA((32,))] * 2
        + [pltpu.SemaphoreType.DMA((9,))],
        compiler_params=pltpu.CompilerParams(
            collective_id=4, has_side_effects=True, vmem_limit_bytes=60 * 1024 * 1024
        ),
        name="feed_forward",
    )(rows_low, out_low, *units)


CHUNKS = INNER // LANES
WIDE_CHUNKS = [(k * LANES, LANES) for k in range(WIDE // LANES)] + [(WIDE // LANES * LANES, WIDE % LANES)]
WIDE_BUFFERS = 3
MAIN = FAST_DEV * MAIN_D
LOW_PAD = 128


def lanes_at(k):
    return pl.ds(pl.multiple_of(k * LANES, 128), LANES)


def write_order(table_ref, matrix_ref):
    size, step = matrix_ref.shape[0], 160

    @pl.loop(0, size // step)
    def _(k):
        at = pl.multiple_of(k * step, 16)
        places = lax.broadcasted_iota(jnp.int32, (step, size), 0) + at
        matrix_ref[pl.ds(at, step), :] = jnp.where(places == table_ref[...], 1.0, 0.0).astype(jnp.bfloat16)


def rms_parts(values):
    scale = lax.rsqrt(jnp.mean(values * values, axis=-1, keepdims=True) + epsilon)
    return values * scale, scale


def rms_pull(unit, scale, gain_row, grad):
    inner = grad * gain_row
    back = scale * (inner - unit * jnp.mean(inner * unit, axis=-1, keepdims=True))
    return back, jnp.sum(grad * unit, axis=0, keepdims=True)


def move_back(order, rows_wide):
    high = rows_wide.astype(jnp.bfloat16)
    rest = (rows_wide - high.astype(jnp.float32)).astype(jnp.bfloat16)
    return back_product(high, order[...]) + back_product(rest, order[...])


def wide_copy(wide_ref, buffer, sem, j, buffers=WIDE_BUFFERS):
    column, columns = WIDE_CHUNKS[j]
    slot = j % buffers
    return pltpu.make_async_copy(
        wide_ref.at[:, pl.ds(column, columns)], buffer.at[slot, :, pl.ds(0, columns)], sem.at[slot]
    )


def conv_sum(inner, taps, shift, same_ref):
    earlier = [pltpu.roll(inner, k, axis=0) * same_ref[:, k - 1 : k] for k in range(1, CONV)]
    total = shift + taps[CONV - 1 : CONV] * inner
    for k in range(1, CONV):
        total = total + taps[CONV - 1 - k : CONV - k] * earlier[k - 1]
    return total, earlier


def scan_rows(lanes, b_ref, c_ref, y_ref, rates, decay_step, step_input, keep=None):
    rows_all = decay_step.shape[0]

    def eight(k, state):
        base = pl.multiple_of(k * 8, 8)
        steps = decay_step[pl.ds(base, 8), :]
        inputs = step_input[pl.ds(base, 8), :]
        rows = []
        for i in range(8):
            decay = jnp.exp2(steps[i : i + 1] * rates)
            state = decay * state + tiled(b_ref[base + i]) * inputs[i : i + 1]
            if keep is None:
                rows.append(jnp.sum(tiled(c_ref[base + i]) * state, axis=0, keepdims=True))
            else:
                keep(base + i, state)
        if keep is None:
            y_ref[pl.ds(base, 8), lanes] = jnp.concatenate(rows, axis=0)
        return state

    lax.fori_loop(0, rows_all // 8, eight, jnp.zeros((STATE, LANES), jnp.float32))


def spread_lanes(rows_ref, first, out_ref):
    lane = lax.broadcasted_iota(jnp.int32, (STATE, 128), 1)
    place = lax.broadcasted_iota(jnp.int32, (STATE, 128), 0) + first

    @pl.loop(0, rows_ref.shape[0] // 8)
    def _(k):
        base = pl.multiple_of(k * 8, 8)
        rows = rows_ref[pl.ds(base, 8), :]
        for i in range(8):
            picked = jnp.where(lane == place, jnp.broadcast_to(rows[i : i + 1], (STATE, 128)), 0.0)
            out_ref[base + i] = jnp.broadcast_to(jnp.sum(picked, axis=1, keepdims=True), (STATE, 128))


def gather_lanes(b_ref, c_ref, out_ref):
    lane = lax.broadcasted_iota(jnp.int32, (STATE, 128), 1)
    place = lax.broadcasted_iota(jnp.int32, (STATE, 128), 0)

    @pl.loop(0, out_ref.shape[0] // 8)
    def _(k):
        base = pl.multiple_of(k * 8, 8)
        rows = []
        for i in range(8):
            b = jnp.where(lane == place, jnp.sum(b_ref[base + i], axis=1, keepdims=True), 0.0)
            c = jnp.where(lane == place + STATE, jnp.sum(c_ref[base + i], axis=1, keepdims=True), 0.0)
            rows.append(jnp.sum(b + c, axis=0, keepdims=True))
        out_ref[pl.ds(base, 8), :] = jnp.concatenate(rows, axis=0)


def mixer_forward_kernel(
    tokens_ref, gains_ref, seg_col_ref, seg_row_ref, hold_ref, same_ref, table_d_ref, table_i_ref,
    wide_ref, wide_rest_ref, taps_ref, conv_shift_ref, select_ref, step_ref, step_shift_ref, decay_ref, skip_ref,
    out_block_ref, out_rest_ref, join_block_ref, join_rest_ref,
    out_low_ref, gu_1_ref, down_2_ref,
    normed_ref, mixed_ref, qkv_ref, conv_ref, step_low_ref, pre_ref, b_ref, c_ref, y_ref, gated_ref, attn_ref,
    mamba_ref, joined_ref, middle_ref, normed_two_ref,
    out_ref, join_ref, out_low_all_ref, gu_2_ref, gu_3_ref, down_3_ref,
    order, wide_buffer, out_all, join_all, conv_low, gated, decay_step, step_input, select_rows, wide_sem, sem,
    send_sems, recv_sems, local,
):
    bf16, f32 = jnp.bfloat16, jnp.float32
    links = Links(send_sems, recv_sems)
    links.greet()
    branches = [
        Gather(links, out_block_ref, shard_place("mamba_out", out_ref), local.at[0]),
        Gather(links, join_block_ref, shard_place("join", join_ref), local.at[1]),
    ]
    for g in branches:
        g.hop(0)
    low_copy = pltpu.make_async_copy(out_low_ref, out_low_all_ref.at[OWN], local.at[2])
    low_copy.start()
    low_near = [
        links.send(out_low_ref, out_low_all_ref.at[LEFT], links.right),
        links.send(out_low_ref, out_low_all_ref.at[RIGHT], links.left),
    ]
    low_core = [links.send(out_low_ref, out_low_all_ref.at[CHIPS + OWN], links.partner)]
    def low_service():
        top, low = pl.ds(0, out_low_ref.shape[0] // 2), pl.ds(out_low_ref.shape[0] // 2, out_low_ref.shape[0] // 2)
        for copy in low_near:
            copy.wait_recv()
        far = [
            links.send(out_low_all_ref.at[LEFT, top], out_low_all_ref.at[FAR, top], links.right),
            links.send(out_low_all_ref.at[RIGHT, low], out_low_all_ref.at[FAR, low], links.left),
        ]
        for chip in (LEFT, RIGHT):
            low_core.append(links.send(out_low_all_ref.at[chip], out_low_all_ref.at[CHIPS + chip], links.partner))
        return far

    count = len(WIDE_CHUNKS)
    for j in range(WIDE_BUFFERS):
        wide_copy(wide_ref, wide_buffer, wide_sem, j).start()
    inputs = tokens_ref[...].astype(f32)
    write_order(table_d_ref, order)
    normed_ref[...] = flat_product((rms_parts(inputs)[0] * gains_ref[0:1]).astype(bf16), order[...]).astype(bf16)
    for j, (column, columns) in enumerate(WIDE_CHUNKS):
        copy = wide_copy(wide_ref, wide_buffer, wide_sem, j)
        copy.wait()
        part = flat_product(normed_ref[:, :MAIN], wide_buffer[j % WIDE_BUFFERS, :, :columns]) + flat_product(
            normed_ref[:, MAIN:], wide_rest_ref[:, column : column + columns]
        )
        if column < 2 * INNER:
            mixed_ref[:, column : column + columns] = part
        else:
            first, last = column - 2 * INNER, min(column - 2 * INNER + columns, QKV)
            qkv_ref[:, first:last] = part[:, : last - first].astype(bf16)
        if j + WIDE_BUFFERS < count:
            wide_copy(wide_ref, wide_buffer, wide_sem, j + WIDE_BUFFERS).start()
        if j in (4, 8):
            for g in branches:
                g.hop(j // 4)
    low_far = low_service()
    for g in branches:
        g.near(0)

    @pl.loop(0, CHUNKS)
    def _(k):
        lanes = lanes_at(k)
        total, _ = conv_sum(mixed_ref[:, lanes], taps_ref[:, lanes], conv_shift_ref[:, lanes], same_ref)
        act = total / (1.0 + jnp.exp(-total))
        conv_ref[:, lanes] = act
        conv_low[:, lanes] = act.astype(bf16)

    for g in branches:
        g.hop(3)
    unit_hops = [links.send(gu_1_ref, gu_2_ref, links.z_next), links.send(down_2_ref, down_3_ref, links.z_next)]
    for g in branches:
        g.near(1)
    selected = flat_product(conv_low[...], select_ref[...])
    step_low_ref[...] = selected[:, :LOW_PAD].astype(bf16)
    select_rows[...] = selected[:, LOW_PAD:]
    spread_lanes(select_rows, 0, b_ref)
    spread_lanes(select_rows, STATE, c_ref)
    attention_forward_kernel(qkv_ref, seg_col_ref, seg_row_ref, attn_ref)
    write_order(table_i_ref, order)
    for copy in low_far:
        copy.wait_recv()
    low_core.append(links.send(out_low_all_ref.at[FAR], out_low_all_ref.at[CHIPS + FAR], links.partner))
    for g in branches:
        g.near(2)
        g.far(0)

    def scan_chunk(k):
        lanes = lanes_at(k)
        pre = flat_product(step_low_ref[...], step_ref[:, lanes])
        pre_ref[:, lanes] = pre
        conv = conv_ref[:, lanes]
        _, decay_step[...], step_input[...] = scan_setup(pre, step_shift_ref[:, lanes], conv, hold_ref[...])
        scan_rows(lanes, b_ref, c_ref, y_ref, decay_ref[:, lanes] * (-LOG2E), decay_step, step_input)
        gate = mixed_ref[:, pl.ds(pl.multiple_of(k * LANES + INNER, 128), LANES)]
        gated[:, lanes] = (
            (y_ref[:, lanes] + skip_ref[:, lanes] * conv) * (gate / (1.0 + jnp.exp(-gate)))
        ).astype(bf16)

    pl.loop(0, 1)(scan_chunk)
    for g in branches:
        g.near(3)
        g.far(1)
    pl.loop(1, 3)(scan_chunk)
    unit_hops[0].wait_recv()
    unit_hops.append(links.send(gu_2_ref, gu_3_ref, links.z_next))
    for g in branches:
        g.far(2)
    pl.loop(3, CHUNKS)(scan_chunk)
    half = INNER // 2
    moved = []
    for h in range(2):
        moved.append(flat_product(gated[:, h * half : (h + 1) * half], order[...]).astype(bf16))
        gated_ref[h] = moved[h]
    write_order(table_d_ref, order)
    for g in branches:
        g.far(3)
    branches[0].wait()
    out_copies = [
        pltpu.make_async_copy(out_ref.at[j], out_all.at[pl.ds(j * MAIN_I, MAIN_I)], sem.at[j]) for j in range(FAST_DEV)
    ]
    for copy in out_copies:
        copy.start()
    branches[1].wait()
    join_copies = [
        pltpu.make_async_copy(join_ref.at[j], join_all.at[pl.ds(j * MAIN_D, MAIN_D)], sem.at[FAST_DEV + j])
        for j in range(FAST_DEV)
    ]
    for copy in join_copies:
        copy.start()
    for copy in out_copies:
        copy.wait()
    total = jnp.zeros(mamba_ref.shape, f32)
    for h in range(2):
        total = total + flat_product(moved[h][:, :MAIN], out_all[h * MAIN : (h + 1) * MAIN])
        total = total + flat_product(moved[h][:, MAIN:], out_rest_ref[h])
    mamba_ref[...] = total
    joined = 0.5 * (rms_parts(attn_ref[...])[0] * gains_ref[1:2] + rms_parts(total)[0] * gains_ref[2:3])
    joined_ref[...] = flat_product(joined.astype(bf16), order[...]).astype(bf16)
    for copy in join_copies:
        copy.wait()
    middle = (
        inputs
        + flat_product(joined_ref[:, :MAIN], join_all[...])
        + flat_product(joined_ref[:, MAIN:], join_rest_ref[...])
    )
    middle_ref[...] = middle
    normed_two_ref[...] = (rms_parts(middle)[0] * gains_ref[3:4]).astype(bf16)
    for copy in low_core + unit_hops[1:]:
        copy.wait_recv()
    low_copy.wait()
    links.finish()


def mixer_forward(*operands):
    rows = operands[0].shape[0]
    bf16, f32 = jnp.bfloat16, jnp.float32
    vmem, anywhere = pl.BlockSpec(memory_space=pltpu.VMEM), pl.BlockSpec(memory_space=pl.ANY)
    in_specs = [vmem] * len(operands)
    for k in (8, 17, 19, 21, 22, 23):
        in_specs[k] = anywhere
    out_block, join_block, out_low, gu, down = [operands[k] for k in (17, 19, 21, 22, 23)]
    shapes = (
        ((rows, D), bf16), ((rows, 2 * INNER), f32), ((rows, QKV), bf16), ((rows, INNER), f32), ((rows, LOW_PAD), bf16),
        ((rows, INNER), f32), ((rows, STATE, 128), f32), ((rows, STATE, 128), f32), ((rows, INNER), f32),
        ((2, rows, D), bf16), ((rows, D), f32), ((rows, D), f32), ((rows, D), bf16), ((rows, D), f32), ((rows, D), bf16),
    )
    gathered = [
        (FAST_DEV,) + out_block.shape, (FAST_DEV,) + join_block.shape, (PLANE_DEV,) + out_low.shape,
        gu.shape, gu.shape, down.shape,
    ]
    sends = 2 * GATHER_SENDS + 12
    return pl.pallas_call(
        mixer_forward_kernel,
        out_shape=[jax.ShapeDtypeStruct(shape, kind) for shape, kind in shapes]
        + [jax.ShapeDtypeStruct(shape, bf16) for shape in gathered],
        in_specs=in_specs,
        out_specs=[vmem] * len(shapes) + [anywhere] * len(gathered),
        scratch_shapes=[
            pltpu.VMEM((D, D), bf16),
            pltpu.VMEM((WIDE_BUFFERS, MAIN, LANES), bf16),
            pltpu.VMEM((2 * MAIN, D), bf16),
            pltpu.VMEM((MAIN, D), bf16),
            pltpu.VMEM((rows, INNER), bf16),
            pltpu.VMEM((rows, INNER), bf16),
            pltpu.VMEM((rows, LANES), f32),
            pltpu.VMEM((rows, LANES), f32),
            pltpu.VMEM((rows, 128), f32),
            pltpu.SemaphoreType.DMA((WIDE_BUFFERS,)),
            pltpu.SemaphoreType.DMA((2 * FAST_DEV,)),
            pltpu.SemaphoreType.DMA((sends,)),
            pltpu.SemaphoreType.DMA((sends,)),
            pltpu.SemaphoreType.DMA((3,)),
        ],
        compiler_params=pltpu.CompilerParams(
            collective_id=1, has_side_effects=True, vmem_limit_bytes=60 * 1024 * 1024
        ),
        name="mixer_forward",
    )(*operands)


def branch_backward_kernel(
    part_grad_ref, out_grad_ref, gains_ref, table_d_ref, table_i_ref, out_ref, out_rest_ref, join_ref, join_rest_ref,
    attn_ref, mamba_ref, middle_ref, gu_grad_ref,
    middle_grad_ref, gains_grad_ref, join_low_ref, mamba_low_ref, attn_low_ref, gated_grad_ref, gu_came_ref,
    order, row_buffer, sem, send_sems, recv_sems,
):
    bf16 = jnp.bfloat16
    links = Links(send_sems, recv_sems)
    links.greet()
    height = gu_came_ref.shape[0]
    far_rows = pl.ds(pl.multiple_of(links.z_at[3] * height, 16), height)
    hop = links.send(gu_grad_ref.at[far_rows], gu_came_ref, links.z_next)
    half_rows = MAIN // 2
    row_blocks = [(join_ref, k) for k in range(2)] + [(out_ref, k) for k in range(4)]

    def row_copy(i):
        source, k = row_blocks[i]
        return pltpu.make_async_copy(source.at[pl.ds(k * half_rows, half_rows)], row_buffer.at[i], sem.at[i])

    def row_products(low, first):
        products = []
        for i in (first, first + 1):
            row_copy(i).wait()
            products.append(back_product(low, row_buffer[i]))
        return products

    for i in range(len(row_blocks)):
        row_copy(i).start()
    write_order(table_d_ref, order)
    unit, scale = rms_parts(middle_ref[...])
    back, gain_grad = rms_pull(unit, scale, gains_ref[3:4], part_grad_ref[...])
    gains_grad_ref[0:1] = jnp.zeros_like(gain_grad)
    gains_grad_ref[3:4] = gain_grad
    middle_grad = out_grad_ref[...] + back
    middle_grad_ref[...] = middle_grad
    join_low = middle_grad.astype(bf16)
    join_low_ref[...] = join_low
    joined_grad = 0.5 * move_back(
        order, jnp.concatenate(row_products(join_low, 0) + [back_product(join_low, join_rest_ref[...])], axis=1)
    )
    unit, scale = rms_parts(attn_ref[...])
    back, gain_grad = rms_pull(unit, scale, gains_ref[1:2], joined_grad)
    gains_grad_ref[1:2] = gain_grad
    attn_low_ref[...] = back.astype(bf16)
    unit, scale = rms_parts(mamba_ref[...])
    back, gain_grad = rms_pull(unit, scale, gains_ref[2:3], joined_grad)
    gains_grad_ref[2:3] = gain_grad
    mamba_low = back.astype(bf16)
    mamba_low_ref[...] = mamba_low
    write_order(table_i_ref, order)
    half = INNER // 2
    for h in range(2):
        gated_grad_ref[:, h * half : (h + 1) * half] = move_back(
            order,
            jnp.concatenate(row_products(mamba_low, 2 + 2 * h) + [back_product(mamba_low, out_rest_ref[h])], axis=1),
        )
    hop.wait_recv()
    links.finish()


def branch_backward(*operands):
    rows = operands[0].shape[0]
    bf16, f32 = jnp.bfloat16, jnp.float32
    vmem, anywhere = pl.BlockSpec(memory_space=pltpu.VMEM), pl.BlockSpec(memory_space=pl.ANY)
    in_specs = [vmem] * len(operands)
    for k in (5, 7, 12):
        in_specs[k] = anywhere
    shapes = (
        ((rows, D), f32), ((4, D), f32), ((rows, D), bf16), ((rows, D), bf16), ((rows, D), bf16), ((rows, INNER), f32),
        ((PLANE_DEV * D // FAST_DEV, GU), bf16),
    )
    return pl.pallas_call(
        branch_backward_kernel,
        out_shape=[jax.ShapeDtypeStruct(shape, kind) for shape, kind in shapes],
        in_specs=in_specs,
        out_specs=[vmem] * (len(shapes) - 1) + [anywhere],
        scratch_shapes=[
            pltpu.VMEM((D, D), bf16),
            pltpu.VMEM((6, MAIN // 2, D), bf16),
            pltpu.SemaphoreType.DMA((6,)),
            pltpu.SemaphoreType.DMA((1,)),
            pltpu.SemaphoreType.DMA((1,)),
        ],
        compiler_params=pltpu.CompilerParams(
            collective_id=5, has_side_effects=True, vmem_limit_bytes=56 * 1024 * 1024
        ),
        name="branch_backward",
    )(*operands)


def mixer_backward_kernel(plan, *refs):
    bf16, f32 = jnp.bfloat16, jnp.float32
    take = Taker(refs)
    ins = take(len(plan.operands))
    gu_grad_ref, down_grad_ref, gu_first_ref, seg_col_ref, seg_row_ref, hold_ref, same_ref = take(7)
    taps_ref, conv_shift_ref, select_ref, step_ref, step_shift_ref, decay_ref, skip_ref = take(7)
    mixed_ref, qkv_ref, conv_ref, step_low_ref, pre_ref, b_ref, c_ref, y_ref, attn_low_ref, gated_grad_ref = take(10)
    totals = take(len(plan.out_shape))
    wide_low_ref, select_grad_ref, step_grad_ref, taps_grad_ref, conv_shift_grad_ref = take(5)
    step_shift_grad_ref, decay_grad_ref, skip_grad_ref, gu_came_ref, down_came_ref = take(5)
    scratch = take(len(plan.scratch))
    conv_grad, low_grad, step_size, decay_step, step_input, y_grad, input_part, step_part = take(8)
    states, b_grad, c_grad, select_rows, select_low = take(5)
    gu_own, gu_next, down_own, down_next, unit_sem, send_sems, recv_sems = take(7)
    rows_all = conv_ref.shape[0]
    links = Links(send_sems, recv_sems)
    links.greet()
    summing = Summing(plan, links, ins, totals, scratch, early=len(plan.blocks) + 1)
    summing.exchange()
    gu_height, down_height = gu_own.shape[0], down_own.shape[0]

    def piece(ref, height, k):
        return ref.at[pl.ds(pl.multiple_of(links.z_at[k] * height, 16), height)]

    down_hop = links.send(piece(down_grad_ref, down_height, 3), down_next, links.z_next)
    loads = [
        pltpu.make_async_copy(piece(gu_grad_ref, gu_height, 2), gu_own, unit_sem.at[0]),
        pltpu.make_async_copy(piece(down_grad_ref, down_height, 2), down_own, unit_sem.at[1]),
        pltpu.make_async_copy(gu_first_ref, gu_next, unit_sem.at[2]),
    ]
    for copy in loads:
        copy.start()
    for copy in loads:
        copy.wait()
    add_rows(gu_own, gu_next)
    gu_hop = links.send(gu_own, gu_came_ref, links.z_next)
    b_grad[...] = jnp.zeros_like(b_grad)
    c_grad[...] = jnp.zeros_like(c_grad)
    states[0] = jnp.zeros((STATE, LANES), f32)
    zeros = jnp.zeros((STATE, LANES), f32)
    summing.exchanged()
    summing.advance(1.2)

    def scan_chunk(k):
        lanes = lanes_at(k)
        gate_lanes = pl.ds(pl.multiple_of(k * LANES + INNER, 128), LANES)
        conv, shift, skip = conv_ref[:, lanes], step_shift_ref[:, lanes], skip_ref[:, lanes]
        step_size[...], decay_step[...], step_input[...] = scan_setup(pre_ref[:, lanes], shift, conv, hold_ref[...])
        gate, grad = mixed_ref[:, gate_lanes], gated_grad_ref[:, lanes]
        open_gate = 1.0 / (1.0 + jnp.exp(-gate))
        wide_low_ref[:, gate_lanes] = (
            grad * (y_ref[:, lanes] + skip * conv) * open_gate * (1.0 + gate * (1.0 - open_gate))
        ).astype(bf16)
        y_grad[...] = grad * gate * open_gate
        skip_grad_ref[:, lanes] = jnp.sum(y_grad[...] * conv, axis=0, keepdims=True)
        decay_rows = decay_ref[:, lanes]
        rates = decay_rows * (-LOG2E)

        def keep(t, state):
            states[t + 1] = state

        scan_rows(lanes, b_ref, c_ref, None, rates, decay_step, step_input, keep)

        def backward(i, carry):
            state_grad, decay_grad = carry
            base = pl.multiple_of(rows_all - 8 - i * 8, 8)
            inputs = step_input[pl.ds(base, 8), :]
            sizes = step_size[pl.ds(base, 8), :]
            held = decay_step[pl.ds(base, 8), :]
            y_rows = y_grad[pl.ds(base, 8), :]
            input_rows, step_rows = [None] * 8, [None] * 8
            for r in range(7, -1, -1):
                t = base + r
                y_row = y_rows[r : r + 1]
                full = state_grad + tiled(c_ref[t]) * y_row
                c_grad[t] += folded(states[t + 1] * y_row)
                b_grad[t] += folded(full * inputs[r : r + 1])
                input_rows[r] = jnp.sum(tiled(b_ref[t]) * full, axis=0, keepdims=True)
                state_grad = jnp.exp2(held[r : r + 1] * rates) * full
                through = state_grad * states[t]
                step_rows[r] = jnp.sum(decay_rows * through, axis=0, keepdims=True)
                decay_grad = decay_grad - sizes[r : r + 1] * through
            input_part[pl.ds(base, 8), :] = jnp.concatenate(input_rows, axis=0)
            step_part[pl.ds(base, 8), :] = jnp.concatenate(step_rows, axis=0)
            return state_grad, decay_grad

        _, decay_grad = lax.fori_loop(0, rows_all // 8, backward, (zeros, zeros))
        decay_grad_ref[:, lanes] = decay_grad
        conv_grad[:, lanes] = input_part[...] * step_size[...] + skip * y_grad[...]
        pre_grad = (input_part[...] * conv - step_part[...]) / (1.0 + jnp.exp(-(pre_ref[:, lanes] + shift)))
        step_shift_grad_ref[:, lanes] = jnp.sum(pre_grad, axis=0, keepdims=True)
        low_grad[:, lanes] = pre_grad.astype(bf16)

    for first, last, until in ((0, 2, 2.2), (2, 3, 3.2), (3, 4, 4.3)):
        pl.loop(first, last)(scan_chunk)
        summing.advance(until)
    down_hop.wait_recv()
    add_rows(down_own, down_next)
    down_hop = links.send(down_own, down_came_ref, links.z_next)
    pl.loop(4, CHUNKS)(scan_chunk)
    summing.advance(5.3)

    gather_lanes(b_grad, c_grad, select_rows)
    select_low[:, :LOW_PAD] = back_product(low_grad[...], step_ref[...]).astype(bf16)
    select_low[:, LOW_PAD:] = select_rows[...].astype(bf16)
    summing.advance(6.3)

    @pl.loop(0, CHUNKS)
    def _(k):
        lanes = lanes_at(k)
        step_grad_ref[:, lanes] = outer_sum(step_low_ref[...], low_grad[:, lanes]).astype(bf16)
        conv = conv_ref[:, lanes]
        some = pl.ds(pl.multiple_of(k * LANES, 128), LANES)
        select_grad_ref[some, :] = outer_sum(conv.astype(bf16), select_low[...]).astype(bf16)
        grad = conv_grad[:, lanes] + back_product(select_low[...], select_ref[some, :])
        inner, taps = mixed_ref[:, lanes], taps_ref[:, lanes]
        total, earlier = conv_sum(inner, taps, conv_shift_ref[:, lanes], same_ref)
        opened = 1.0 / (1.0 + jnp.exp(-total))
        grad = grad * opened * (1.0 + total * (1.0 - opened))
        conv_shift_grad_ref[:, lanes] = jnp.sum(grad, axis=0, keepdims=True)
        tap_rows = [jnp.sum(grad * earlier[j - 1], axis=0, keepdims=True) for j in range(CONV - 1, 0, -1)]
        tap_rows.append(jnp.sum(grad * inner, axis=0, keepdims=True))
        taps_grad_ref[:, lanes] = jnp.concatenate(tap_rows, axis=0)
        inner_grad = taps[CONV - 1 : CONV] * grad
        for j in range(1, CONV):
            moved = taps[CONV - 1 - j : CONV - j] * grad * same_ref[:, j - 1 : j]
            inner_grad = inner_grad + pltpu.roll(moved, rows_all - j, axis=0)
        wide_low_ref[:, lanes] = inner_grad.astype(bf16)

    summing.advance(7.3)
    attention_backward_kernel(qkv_ref, seg_col_ref, seg_row_ref, attn_low_ref, wide_low_ref, 2 * INNER)
    wide_low_ref[:, 2 * INNER + QKV :] = jnp.zeros((rows_all, WIDE - 2 * INNER - QKV), bf16)
    summing.finish()
    gu_hop.wait_recv()
    down_hop.wait_recv()
    links.finish()


def mixer_backward(plan, *operands):
    rows = operands[-1].shape[0]
    bf16, f32 = jnp.bfloat16, jnp.float32
    vmem, anywhere = pl.BlockSpec(memory_space=pltpu.VMEM), pl.BlockSpec(memory_space=pl.ANY)
    in_specs = [anywhere] * (len(plan.operands) + 3) + [vmem] * (len(operands) - 3)
    shapes = (
        ((rows, WIDE), bf16), ((INNER, 2 * LOW_PAD), bf16), ((LOW_PAD, INNER), bf16), ((CONV, INNER), f32),
        ((1, INNER), f32), ((1, INNER), f32), ((STATE, INNER), f32), ((1, INNER), f32),
        ((PLANE_DEV * D // FAST_DEV, GU), bf16), ((PAD_FF, D), bf16),
    )
    lane_rows = pltpu.VMEM((rows, LANES), f32)
    sem = pltpu.SemaphoreType.DMA
    return pl.pallas_call(
        functools.partial(mixer_backward_kernel, plan),
        out_shape=plan.out_shape + [jax.ShapeDtypeStruct(shape, kind) for shape, kind in shapes],
        in_specs=in_specs,
        out_specs=[vmem] * (len(plan.out_shape) + len(shapes) - 2) + [anywhere] * 2,
        scratch_shapes=plan.scratch
        + [pltpu.VMEM((rows, INNER), f32), pltpu.VMEM((rows, INNER), bf16)]
        + [lane_rows] * 6
        + [
            pltpu.VMEM((rows + 1, STATE, LANES), f32),
            pltpu.VMEM((rows, STATE, 128), f32),
            pltpu.VMEM((rows, STATE, 128), f32),
            pltpu.VMEM((rows, 128), f32),
            pltpu.VMEM((rows, 2 * LOW_PAD), bf16),
            pltpu.VMEM(shapes[-2][0], bf16),
            pltpu.VMEM(shapes[-2][0], bf16),
            pltpu.VMEM(shapes[-1][0], bf16),
            pltpu.VMEM(shapes[-1][0], bf16),
            sem((3,)),
            sem((3,)),
            sem((3,)),
        ],
        compiler_params=pltpu.CompilerParams(
            collective_id=2, has_side_effects=True, vmem_limit_bytes=62 * 1024 * 1024
        ),
        name="mixer_backward",
    )(*plan.operands, *operands)


def spread_table(shard_rows, main_rows, shards):
    half = shards // CORES
    order = [k * CORES + c for c in range(CORES) for k in range(half)]
    main = [d * shard_rows + r for d in order for r in range(main_rows)]
    rest = [d * shard_rows + r for d in order for r in range(main_rows, shard_rows)]
    return np.asarray(main + rest, np.int32)


def tie(*values):
    return lax.optimization_barrier(values)


def as_rows(flats, rows):
    flat = jnp.concatenate(flats)
    return jnp.pad(flat, (0, rows * 128 - flat.size)).reshape(rows, 128)


def split_flat(block, sizes):
    pieces, at = [], 0
    for size in sizes:
        pieces.append(block[..., at : at + size])
        at += size
    return pieces


def on_fast_device(
    tokens, cotangent, seq_lengths, qkv_proj, mamba_in, select_proj, step_proj, mamba_out, join_out,
    conv_taps, conv_bias, step_bias, decay_rates, skip_gain, norm_gains, ffn_gate, ffn_up, ffn_down,
):
    bf16, f32 = jnp.bfloat16, jnp.float32
    n = FAST_DEV
    row_count = tokens.shape[0]
    d_rows, i_rows = D // n, INNER // n
    d_rest, i_rest = d_rows - MAIN_D, i_rows - MAIN_I

    own_ff = PLANES * PAD_FF

    def ff_columns(flat):
        block = flat.reshape(d_rows, PLANES, PLANE_DEV, SLICE_FF).transpose(2, 0, 1, 3)
        block = jnp.pad(block, ((0, 0), (0, 0), (0, 0), (0, PAD_FF - SLICE_FF)))
        return jnp.pad(block.reshape(PLANE_DEV, d_rows, own_ff), ((0, 0), (0, 0), (0, HALF_GU - own_ff)))

    planes = [[z * PLANE_DEV + p for p in range(PLANE_DEV)] for z in range(PLANES)]
    gu = jnp.concatenate([ff_columns(ffn_gate), ff_columns(ffn_up)], axis=2)
    gu = lax.all_to_all(gu, "fsdp", 0, 0, axis_index_groups=planes, tiled=True).reshape(PLANE_DEV * d_rows, GU)
    down = jnp.pad(ffn_down.reshape(SLICE_FF, D), ((0, PAD_FF - SLICE_FF), (0, 0)))

    wide = jnp.concatenate([mamba_in.reshape(d_rows, 2 * INNER), qkv_proj.reshape(d_rows, QKV)], axis=1)
    wide = jnp.pad(wide, ((0, 0), (0, WIDE - wide.shape[1])))
    out_block = mamba_out.reshape(i_rows, D)
    join_block = join_out.reshape(d_rows, D)
    rest_sizes = [d_rest * WIDE, d_rest * D, i_rest * D]
    rest = as_rows(
        [wide[MAIN_D:].reshape(-1), join_block[MAIN_D:].reshape(-1), out_block[MAIN_I:].reshape(-1)], REST_ROWS
    )
    smalls = [select_proj, step_proj, conv_taps, conv_bias, step_bias, decay_rates, skip_gain, norm_gains]
    small_sizes = [s.size for s in smalls]
    smalls = as_rows(smalls, SMALL_ROWS)
    segments = segment_ids(seq_lengths, row_count)
    live_rows = (segments < seq_lengths.shape[0]).astype(f32)[:, None]
    out_grad = cotangent.astype(f32) * live_rows
    gu, down, wide_block, rest, smalls, out_grad = tie(gu, down, wide[:MAIN_D], rest, smalls, out_grad)
    wide_all, rest_all, smalls_all, gu_1, down_1, down_2 = gather_first(
        ("wide", "rest", "smalls"), (wide_block, rest, smalls), (gu, down)
    )
    wide_all = wide_all.reshape(MAIN, WIDE)
    pieces = split_flat(rest_all.reshape(n, REST_ROWS * 128), rest_sizes)
    wide_rest = pieces[0].reshape(n * d_rest, WIDE)
    join_rest = pieces[1].reshape(n * d_rest, D)
    out_rest = pieces[2].reshape(CORES, 2, -1, D).transpose(1, 0, 2, 3).reshape(2, -1, D)
    pieces = split_flat(smalls_all.reshape(n, SMALL_ROWS * 128), small_sizes)
    select = pieces[0].reshape(INNER, XPROJ)
    select = jnp.concatenate(
        [
            jnp.pad(select[:, :RANK], ((0, 0), (0, LOW_PAD - RANK))),
            jnp.pad(select[:, RANK:], ((0, 0), (0, LOW_PAD - 2 * STATE))),
        ],
        axis=1,
    )
    step_matrix = jnp.pad(pieces[1].reshape(RANK, INNER), ((0, LOW_PAD - RANK), (0, 0)))
    taps = pieces[2].reshape(CONV, INNER).astype(f32)
    conv_shift = pieces[3].reshape(1, INNER).astype(f32)
    step_shift = pieces[4].reshape(1, INNER).astype(f32)
    decay = pieces[5].reshape(STATE, INNER).astype(f32)
    skip = pieces[6].reshape(1, INNER).astype(f32)
    gains = pieces[7].reshape(4, D).astype(f32)

    table_d = jnp.asarray(spread_table(d_rows, MAIN_D, n))[None]
    table_i = jnp.asarray(spread_table(i_rows, MAIN_I, n // 2))[None]
    hold = ((1.0 - keep_flags(segments)) * BIG)[:, None]
    same = jnp.stack(
        [
            (jnp.concatenate([jnp.full((k,), -1, jnp.int32), segments[:-k]]) == segments).astype(f32)
            for k in range(1, CONV)
        ],
        axis=1,
    )
    places = (segments[:, None], segments[None, :], hold, same, table_d, table_i)
    matrices = (
        wide_all, wide_rest, taps, conv_shift, select, step_matrix, step_shift, decay, skip,
    )
    (
        normed, mixed, qkv_rows, conv_act, step_low, step_pre, b_wide, c_wide, scanned, gated, attn_rows, mamba_rows,
        joined, middle, normed_two, out_all, join_all, out_low, gu_2, gu_3, down_3,
    ) = mixer_forward(
        tokens, gains, *places, *matrices, out_block[:MAIN_I], out_rest, join_block[:MAIN_D], join_rest,
        out_grad.astype(bf16), gu_1, down_2,
    )
    out_all, join_all = out_all.reshape(2 * MAIN, D), join_all.reshape(MAIN, D)

    part_grad, ffn_rows, gu_grad, down_grad = feed_forward(
        normed_two, out_low.reshape(-1, D), gu, gu_1, gu_2, gu_3, down, down_1, down_2, down_3
    )
    block_out = ((middle + ffn_rows) * live_rows).astype(bf16)

    middle_grad, gains_grad, join_low, mamba_low, attn_low, gated_grad, gu_first = branch_backward(
        part_grad, out_grad, gains, table_d, table_i, out_all, out_rest, join_all, join_rest,
        attn_rows, mamba_rows, middle, gu_grad,
    )
    gated_columns = gated.transpose(0, 2, 1)
    gated_rest = gated_columns[:, MAIN:].reshape(2, CORES, -1, row_count).transpose(1, 0, 2, 3)
    joined_columns, normed_columns = joined.T, normed.T
    branch_plan = SumPlan(
        BRANCH_BLOCKS, (MAIN_I, MAIN_D), (i_rest, d_rest), D,
        (gated_columns[:, :MAIN], joined_columns[None, :MAIN]),
        (gated_rest.reshape(CORES, -1, row_count), joined_columns[MAIN:].reshape(CORES, -1, row_count)),
        (mamba_low, join_low),
    )
    (
        out_sum, join_sum, branch_rest, wide_low, select_grad, step_grad, taps_grad, conv_shift_grad,
        step_shift_grad, decay_grad, skip_grad, gu_came, down_came,
    ) = mixer_backward(
        branch_plan, gu_grad, down_grad, gu_first, *places[:4], taps, conv_shift, select, step_matrix, step_shift, decay, skip,
        mixed, qkv_rows, conv_act, step_low, step_pre, b_wide, c_wide, scanned, attn_low, gated_grad,
    )
    select_grad = jnp.concatenate([select_grad[:, :RANK], select_grad[:, LOW_PAD : LOW_PAD + 2 * STATE]], axis=1)
    small_grads = [
        select_grad, step_grad[:RANK], taps_grad, conv_shift_grad, step_shift_grad, decay_grad, skip_grad, gains_grad,
    ]
    small_grads = jnp.concatenate([g.astype(bf16).reshape(n, -1) for g in small_grads], axis=1)
    small_grads = jnp.pad(small_grads, ((0, 0), (0, SMALL_ROWS * 128 - small_grads.shape[1])))
    small_grads = small_grads.reshape(GROUPS, CORES, SMALL_ROWS, 128).transpose(1, 0, 2, 3)
    wide_plan = SumPlan(
        WIDE_BLOCKS, (MAIN_D,), (d_rest,), REST_COLUMNS,
        (normed_columns[None, :MAIN],),
        (normed_columns[MAIN:].reshape(CORES, -1, row_count),),
        (wide_low,),
        small_grads.reshape(CORES, GROUPS * SMALL_ROWS, 128),
    )
    wide_sum, wide_left, small_sum, input_grad, gate_grad, up_grad, down_sum = last_sums(
        wide_plan, middle_grad, tokens, gains, table_d, wide_all, wide_rest, gu_grad, down_grad, gu_came, down_came
    )
    gate_grad, up_grad = [block.astype(f32).reshape(-1) for block in (gate_grad, up_grad)]
    first_gain = wide_left[14, WIDE % REST_COLUMNS : WIDE % REST_COLUMNS + norm_gains.size]
    wide_left = wide_left.reshape(-1, d_rest, REST_COLUMNS).transpose(1, 0, 2).reshape(d_rest, -1)[:, :WIDE]
    wide_sum = jnp.concatenate([wide_sum, wide_left], axis=0)
    out_sum = jnp.concatenate([out_sum, branch_rest[:i_rest]], axis=0)
    join_sum = jnp.concatenate([join_sum, branch_rest[i_rest : i_rest + d_rest]], axis=0)
    smalls = split_flat(small_sum.reshape(-1), small_sizes)
    return (
        block_out,
        input_grad,
        wide_sum[:, 2 * INNER : 2 * INNER + QKV].reshape(-1),
        wide_sum[:, : 2 * INNER].reshape(-1),
        smalls[0],
        smalls[1],
        out_sum.reshape(-1),
        join_sum.reshape(-1),
        *smalls[2:-1],
        smalls[-1] + first_gain,
        gate_grad,
        up_grad,
        down_sum[:SLICE_FF].reshape(-1),
    )


def fits_fast_plan(mesh):
    return mesh.shape["fsdp"] == FAST_DEV


def solution(mesh):
    rows, flat = P("fsdp", None), P("fsdp")
    return jax.shard_map(
        on_fast_device if fits_fast_plan(mesh) else on_device,
        mesh=mesh,
        in_specs=(rows, rows) + (flat,) * 16,
        out_specs=(rows, rows) + (flat,) * 15,
        check_vma=False,
    )
```

```python
import functools

import jax
import jax.numpy as jnp
import numpy as np
from jax import lax
from jax.experimental import pallas as pl
from jax.experimental.pallas import tpu as pltpu
from jax.sharding import PartitionSpec as P

D = 1600
HEADS = 25
KV_HEADS = 5
HEAD = 64
INNER = 3200
STATE = 16
CONV = 4
RANK = 100
FF = 5504
QKV = 2240
XPROJ = 132


epsilon = 1e-06


def flat_product(left, right):
    return jnp.dot(left, right, preferred_element_type=jnp.float32)


def outer_sum(left, right):
    return lax.dot_general(
        left, right, (((0,), (0,)), ((), ())), preferred_element_type=jnp.float32
    )


def back_product(grad_rows, matrix):
    return lax.dot_general(
        grad_rows, matrix, (((1,), (1,)), ((), ())), preferred_element_type=jnp.float32
    )


def rms_scale(values, scale_row):
    return (
        values * lax.rsqrt(jnp.mean(values * values, axis=-1, keepdims=True) + epsilon) * scale_row
    )


def segment_ids(lengths, row_count):
    seq_ends = jnp.cumsum(lengths)
    places = jnp.arange(row_count, dtype=jnp.int32)
    return jnp.sum((places[:, None] >= seq_ends[None, :]).astype(jnp.int32), axis=1)


def keep_flags(segments):
    same_seq = (segments[1:] == segments[:-1]).astype(jnp.float32)
    return jnp.concatenate([jnp.zeros((1,), jnp.float32), same_seq])


def conv_silu(inner_rows, tap_matrix, conv_shift, segments):
    tap_count = tap_matrix.shape[0]
    summed = conv_shift[None, :] + tap_matrix[tap_count - 1][None, :] * inner_rows
    for offset in range(1, tap_count):
        shifted = jnp.concatenate(
            [jnp.zeros((offset, inner_rows.shape[1]), jnp.float32), inner_rows[:-offset]], axis=0
        )
        earlier = jnp.concatenate([jnp.full((offset,), -1, jnp.int32), segments[:-offset]])
        same_seq = (earlier == segments).astype(jnp.float32)
        summed = summed + tap_matrix[tap_count - 1 - offset][None, :] * shifted * same_seq[:, None]
    return jax.nn.silu(summed)


def scan_block(state_now, decay_matrix, block_data):
    step_sizes, step_inputs, step_b, step_c, step_keep = block_data
    outputs = []
    for step_index in range(step_sizes.shape[0]):
        decay_now = jnp.exp(-step_sizes[step_index][None, :] * decay_matrix)
        state_now = (
            step_keep[step_index] * decay_now * state_now
            + step_b[step_index][:, None]
            * (step_sizes[step_index] * step_inputs[step_index])[None, :]
        )
        outputs.append(jnp.sum(step_c[step_index][:, None] * state_now, axis=0))
    return (state_now, jnp.stack(outputs))


def selective_scan(step_sizes, step_inputs, b_rows, c_rows, keep_rows, decay_matrix):
    block_len = 16

    def advance(state_now, block_data):
        return jax.checkpoint(scan_block)(state_now, decay_matrix, block_data)

    blocks = tuple(
        (
            piece_array.reshape((-1, block_len) + piece_array.shape[1:])
            for piece_array in (step_sizes, step_inputs, b_rows, c_rows, keep_rows)
        )
    )
    start_state = jnp.zeros((b_rows.shape[1], step_inputs.shape[1]), jnp.float32)
    final_state, outputs = lax.scan(advance, start_state, blocks)
    return outputs.reshape(step_inputs.shape)


def mamba_core(
    conv_act, select_rows, step_pre, gate_in, step_shift, decay_matrix, skip_row, keep_rows
):
    step_sizes = jax.nn.softplus(step_pre + step_shift)
    scanned = selective_scan(
        step_sizes,
        conv_act,
        select_rows[:, :STATE],
        select_rows[:, STATE:],
        keep_rows,
        decay_matrix,
    )
    return (scanned + skip_row * conv_act) * jax.nn.silu(gate_in)


def join_branches(attn_rows, mamba_rows, attn_gain, mamba_gain):
    return 0.5 * (rms_scale(attn_rows, attn_gain) + rms_scale(mamba_rows, mamba_gain))


def swiglu(gate_rows, up_rows):
    return jax.nn.silu(gate_rows) * up_rows


def block_scores(query_block, start, key_rows, segments):
    block_rows = query_block.shape[0]
    places = jnp.arange(segments.shape[0], dtype=jnp.int32)
    query_places = start + jnp.arange(block_rows, dtype=jnp.int32)
    allowed = (segments[:, None] == segments[None, :]) & (places[None, :] <= query_places[:, None])
    scores = jnp.einsum(
        "tgrd,ugd->grtu", query_block, key_rows, preferred_element_type=jnp.float32
    ) * HEAD ** (-0.5)
    return jnp.where(allowed[None, None], scores, -1e30)


def attention_forward(queries, key_rows, value_rows, segments):
    row_count = queries.shape[0]
    block_rows = min(row_count, 512)
    query_blocks = queries.reshape((row_count // block_rows, block_rows) + queries.shape[1:])
    starts = jnp.arange(row_count // block_rows, dtype=jnp.int32) * block_rows

    def one_block(block_item):
        scores = block_scores(block_item[0], block_item[1], key_rows, segments)
        top_score = jnp.max(scores, axis=-1, keepdims=True)
        raised = jnp.exp(scores - top_score)
        exp_sum = jnp.sum(raised, axis=-1, keepdims=True)
        weights = (raised / exp_sum).astype(jnp.bfloat16)
        outputs = jnp.einsum(
            "grtu,ugd->tgrd", weights, value_rows, preferred_element_type=jnp.float32
        )
        return (outputs, top_score, exp_sum)

    outputs, top_scores, exp_sums = lax.map(one_block, (query_blocks, starts))
    return (outputs.reshape(row_count, -1), top_scores, exp_sums, query_blocks, starts)


def attention_backward(
    query_blocks, starts, key_rows, value_rows, segments, top_scores, exp_sums, out_grad
):
    row_count = key_rows.shape[0]
    grad_blocks = out_grad.reshape(query_blocks.shape)

    def one_block(carry_sums, block_item):
        key_acc, value_acc = carry_sums
        query_block, start, top_score, exp_sum, grad_block = block_item
        scores = block_scores(query_block, start, key_rows, segments)
        weights = jnp.exp(scores - top_score) / exp_sum
        weight_grad = jnp.einsum(
            "tgrd,ugd->grtu", grad_block, value_rows, preferred_element_type=jnp.float32
        )
        score_grad = (
            weights * (weight_grad - jnp.sum(weights * weight_grad, axis=-1, keepdims=True))
        ).astype(jnp.bfloat16)
        query_grad = jnp.einsum(
            "grtu,ugd->tgrd", score_grad, key_rows, preferred_element_type=jnp.float32
        ) * HEAD ** (-0.5)
        key_acc = key_acc + jnp.einsum(
            "grtu,tgrd->ugd", score_grad, query_block, preferred_element_type=jnp.float32
        ) * HEAD ** (-0.5)
        value_acc = value_acc + jnp.einsum(
            "grtu,tgrd->ugd",
            weights.astype(jnp.bfloat16),
            grad_block,
            preferred_element_type=jnp.float32,
        )
        return ((key_acc, value_acc), query_grad)

    zero_rows = jnp.zeros(key_rows.shape, jnp.float32)
    (key_grad, value_grad), query_grads = lax.scan(
        one_block, (zero_rows, zero_rows), (query_blocks, starts, top_scores, exp_sums, grad_blocks)
    )
    return (
        query_grads.reshape(row_count, -1),
        key_grad.reshape(row_count, -1),
        value_grad.reshape(row_count, -1),
    )


def shape_mixer(flat_list):
    return (
        flat_list[0].reshape(D, QKV),
        flat_list[1].reshape(D, 2 * INNER),
        flat_list[2].reshape(INNER, XPROJ),
        flat_list[3].reshape(RANK, INNER),
        flat_list[4].reshape(INNER, D),
        flat_list[5].reshape(D, D),
    )


def small_mixer(flat_list):
    return (
        flat_list[6].astype(jnp.float32).reshape(CONV, INNER),
        flat_list[7].astype(jnp.float32),
        flat_list[8].astype(jnp.float32),
        flat_list[9].astype(jnp.float32).reshape(STATE, INNER),
        flat_list[10].astype(jnp.float32),
        flat_list[11].astype(jnp.float32).reshape(4, D),
    )


def shape_ffn(flat_list):
    return (flat_list[0].reshape(D, FF), flat_list[1].reshape(D, FF), flat_list[2].reshape(FF, D))


def on_device(
    tokens,
    cotangent,
    seq_lengths,
    qkv_proj,
    mamba_in,
    select_proj,
    step_proj,
    mamba_out,
    join_out,
    conv_taps,
    conv_bias,
    step_bias,
    decay_rates,
    skip_gain,
    norm_gains,
    ffn_gate,
    ffn_up,
    ffn_down,
):
    mixer_flat = (
        lax.all_gather(qkv_proj, "fsdp", axis=0, tiled=True),
        lax.all_gather(mamba_in, "fsdp", axis=0, tiled=True),
        lax.all_gather(select_proj, "fsdp", axis=0, tiled=True),
        lax.all_gather(step_proj, "fsdp", axis=0, tiled=True),
        lax.all_gather(mamba_out, "fsdp", axis=0, tiled=True),
        lax.all_gather(join_out, "fsdp", axis=0, tiled=True),
        lax.all_gather(conv_taps, "fsdp", axis=0, tiled=True),
        lax.all_gather(conv_bias, "fsdp", axis=0, tiled=True),
        lax.all_gather(step_bias, "fsdp", axis=0, tiled=True),
        lax.all_gather(decay_rates, "fsdp", axis=0, tiled=True),
        lax.all_gather(skip_gain, "fsdp", axis=0, tiled=True),
        lax.all_gather(norm_gains, "fsdp", axis=0, tiled=True),
    )
    ffn_flat = (
        lax.all_gather(ffn_gate, "fsdp", axis=0, tiled=True),
        lax.all_gather(ffn_up, "fsdp", axis=0, tiled=True),
        lax.all_gather(ffn_down, "fsdp", axis=0, tiled=True),
    )
    qkv_matrix, mamba_in_matrix, select_matrix, step_matrix, mamba_out_matrix, join_matrix = (
        shape_mixer(mixer_flat)
    )
    tap_matrix, conv_shift, step_shift, decay_matrix, skip_row, gain_rows = small_mixer(mixer_flat)
    gate_matrix, up_matrix, down_matrix = shape_ffn(ffn_flat)
    row_count = tokens.shape[0]
    segments = segment_ids(seq_lengths, row_count)
    live_rows = (segments < seq_lengths.shape[0]).astype(jnp.float32)
    keep_rows = keep_flags(segments)
    inputs = tokens.astype(jnp.float32)
    normed_full, norm_pull = jax.vjp(rms_scale, inputs, gain_rows[0])
    normed = normed_full.astype(jnp.bfloat16)
    qkv_rows = flat_product(normed, qkv_matrix).astype(jnp.bfloat16)
    queries = qkv_rows[:, :D].reshape(row_count, KV_HEADS, HEADS // KV_HEADS, HEAD)
    key_rows = qkv_rows[:, D : D + KV_HEADS * HEAD].reshape(row_count, KV_HEADS, HEAD)
    value_rows = qkv_rows[:, D + KV_HEADS * HEAD :].reshape(row_count, KV_HEADS, HEAD)
    attn_rows, top_scores, exp_sums, query_blocks, starts = attention_forward(
        queries, key_rows, value_rows, segments
    )
    mixed_in = flat_product(normed, mamba_in_matrix)

    def conv_piece(inner_rows, tap_values, shift_values):
        return conv_silu(inner_rows, tap_values, shift_values, segments)

    conv_act, conv_pull = jax.vjp(conv_piece, mixed_in[:, :INNER], tap_matrix, conv_shift)
    conv_low = conv_act.astype(jnp.bfloat16)
    selected = flat_product(conv_low, select_matrix)
    step_low = selected[:, :RANK].astype(jnp.bfloat16)
    step_pre = flat_product(step_low, step_matrix)

    def core_piece(
        conv_values,
        select_values,
        step_values,
        gate_values,
        shift_values,
        decay_values,
        skip_values,
    ):
        return mamba_core(
            conv_values,
            select_values,
            step_values,
            gate_values,
            shift_values,
            decay_values,
            skip_values,
            keep_rows,
        )

    gated_full, core_pull = jax.vjp(
        core_piece,
        conv_act,
        selected[:, RANK:],
        step_pre,
        mixed_in[:, INNER:],
        step_shift,
        decay_matrix,
        skip_row,
    )
    gated = gated_full.astype(jnp.bfloat16)
    mamba_rows = flat_product(gated, mamba_out_matrix)
    joined_full, join_pull = jax.vjp(
        join_branches, attn_rows, mamba_rows, gain_rows[1], gain_rows[2]
    )
    joined = joined_full.astype(jnp.bfloat16)
    middle = inputs + flat_product(joined, join_matrix)
    normed_two_full, norm_two_pull = jax.vjp(rms_scale, middle, gain_rows[3])
    normed_two = normed_two_full.astype(jnp.bfloat16)
    gate_rows = flat_product(normed_two, gate_matrix)
    up_rows = flat_product(normed_two, up_matrix)
    act_full, act_pull = jax.vjp(swiglu, gate_rows, up_rows)
    activated = act_full.astype(jnp.bfloat16)
    result_rows = middle + flat_product(activated, down_matrix)
    block_out = (result_rows * live_rows[:, None]).astype(jnp.bfloat16)
    ffn_flat = (
        lax.all_gather(ffn_gate, "fsdp", axis=0, tiled=True),
        lax.all_gather(ffn_up, "fsdp", axis=0, tiled=True),
        lax.all_gather(ffn_down, "fsdp", axis=0, tiled=True),
    )
    gate_matrix, up_matrix, down_matrix = shape_ffn(ffn_flat)
    out_grad = cotangent.astype(jnp.float32) * live_rows[:, None]
    down_low = out_grad.astype(jnp.bfloat16)
    down_weight_grad = outer_sum(activated, down_low)
    gate_grad, up_grad = act_pull(back_product(down_low, down_matrix))
    gate_low = gate_grad.astype(jnp.bfloat16)
    up_low = up_grad.astype(jnp.bfloat16)
    gate_weight_grad = outer_sum(normed_two, gate_low)
    up_weight_grad = outer_sum(normed_two, up_low)
    middle_norm_grad, ffn_gain_grad = norm_two_pull(
        back_product(gate_low, gate_matrix) + back_product(up_low, up_matrix)
    )
    middle_grad = out_grad + middle_norm_grad
    ffn_sums = (
        lax.psum_scatter(gate_weight_grad.reshape(-1), "fsdp", scatter_dimension=0, tiled=True),
        lax.psum_scatter(up_weight_grad.reshape(-1), "fsdp", scatter_dimension=0, tiled=True),
        lax.psum_scatter(down_weight_grad.reshape(-1), "fsdp", scatter_dimension=0, tiled=True),
    )
    mixer_flat = (
        lax.all_gather(qkv_proj, "fsdp", axis=0, tiled=True),
        lax.all_gather(mamba_in, "fsdp", axis=0, tiled=True),
        lax.all_gather(select_proj, "fsdp", axis=0, tiled=True),
        lax.all_gather(step_proj, "fsdp", axis=0, tiled=True),
        lax.all_gather(mamba_out, "fsdp", axis=0, tiled=True),
        lax.all_gather(join_out, "fsdp", axis=0, tiled=True),
        lax.all_gather(conv_taps, "fsdp", axis=0, tiled=True),
        lax.all_gather(conv_bias, "fsdp", axis=0, tiled=True),
        lax.all_gather(step_bias, "fsdp", axis=0, tiled=True),
        lax.all_gather(decay_rates, "fsdp", axis=0, tiled=True),
        lax.all_gather(skip_gain, "fsdp", axis=0, tiled=True),
        lax.all_gather(norm_gains, "fsdp", axis=0, tiled=True),
    )
    qkv_matrix, mamba_in_matrix, select_matrix, step_matrix, mamba_out_matrix, join_matrix = (
        shape_mixer(mixer_flat)
    )
    join_low = middle_grad.astype(jnp.bfloat16)
    join_weight_grad = outer_sum(joined, join_low)
    attn_grad, mamba_grad, attn_gain_grad, mamba_gain_grad = join_pull(
        back_product(join_low, join_matrix)
    )
    mamba_low = mamba_grad.astype(jnp.bfloat16)
    mamba_out_weight_grad = outer_sum(gated, mamba_low)
    (
        conv_core_grad,
        select_part_grad,
        step_pre_grad,
        gate_in_grad,
        step_shift_grad,
        decay_grad,
        skip_grad,
    ) = core_pull(back_product(mamba_low, mamba_out_matrix))
    step_low_grad = step_pre_grad.astype(jnp.bfloat16)
    step_weight_grad = outer_sum(step_low, step_low_grad)
    select_low = jnp.concatenate(
        [back_product(step_low_grad, step_matrix), select_part_grad], axis=1
    ).astype(jnp.bfloat16)
    select_weight_grad = outer_sum(conv_low, select_low)
    conv_grad = conv_core_grad + back_product(select_low, select_matrix)
    conv_in_grad, taps_grad, conv_shift_grad = conv_pull(conv_grad)
    mixed_low = jnp.concatenate([conv_in_grad, gate_in_grad], axis=1).astype(jnp.bfloat16)
    mamba_in_weight_grad = outer_sum(normed, mixed_low)
    query_grad, key_grad, value_grad = attention_backward(
        query_blocks,
        starts,
        key_rows,
        value_rows,
        segments,
        top_scores,
        exp_sums,
        attn_grad.astype(jnp.bfloat16),
    )
    qkv_low = jnp.concatenate([query_grad, key_grad, value_grad], axis=1).astype(jnp.bfloat16)
    qkv_weight_grad = outer_sum(normed, qkv_low)
    normed_grad = back_product(qkv_low, qkv_matrix) + back_product(mixed_low, mamba_in_matrix)
    input_norm_grad, input_gain_grad = norm_pull(normed_grad)
    input_grad = middle_grad + input_norm_grad
    gain_grads = jnp.stack(
        [input_gain_grad, attn_gain_grad, mamba_gain_grad, ffn_gain_grad]
    ).reshape(-1)
    mixer_sums = (
        lax.psum_scatter(qkv_weight_grad.reshape(-1), "fsdp", scatter_dimension=0, tiled=True),
        lax.psum_scatter(mamba_in_weight_grad.reshape(-1), "fsdp", scatter_dimension=0, tiled=True),
        lax.psum_scatter(select_weight_grad.reshape(-1), "fsdp", scatter_dimension=0, tiled=True),
        lax.psum_scatter(step_weight_grad.reshape(-1), "fsdp", scatter_dimension=0, tiled=True),
        lax.psum_scatter(
            mamba_out_weight_grad.reshape(-1), "fsdp", scatter_dimension=0, tiled=True
        ),
        lax.psum_scatter(join_weight_grad.reshape(-1), "fsdp", scatter_dimension=0, tiled=True),
        lax.psum_scatter(taps_grad.reshape(-1), "fsdp", scatter_dimension=0, tiled=True),
        lax.psum_scatter(conv_shift_grad, "fsdp", scatter_dimension=0, tiled=True),
        lax.psum_scatter(step_shift_grad, "fsdp", scatter_dimension=0, tiled=True),
        lax.psum_scatter(decay_grad.reshape(-1), "fsdp", scatter_dimension=0, tiled=True),
        lax.psum_scatter(skip_grad, "fsdp", scatter_dimension=0, tiled=True),
        lax.psum_scatter(gain_grads, "fsdp", scatter_dimension=0, tiled=True),
    )
    return (block_out, input_grad) + tuple(mixer_sums) + tuple(ffn_sums)


PLANES = 4
CHIPS = 4
CORES = 2
PLANE_DEV = CHIPS * CORES
FAST_DEV = PLANES * PLANE_DEV
RING = (0, 1, 3, 2)
MAIN_D = 48
MAIN_I = 96
SLICE_FF = FF // FAST_DEV
PAD_FF = 176
HALF_GU = 768
WIDE = 8704
GU = 2 * HALF_GU
REST_ROWS = 224
SMALL_ROWS = 208
LANES = 640
BIG = 1e30
LOG2E = 1.4426950408889634


def ring_place(k):
    return k + k // 2 - 2 * (k // 3)


class Links:
    def __init__(self, send_sems, recv_sems):
        me = lax.axis_index("fsdp")
        self.z, self.v, self.c = me // PLANE_DEV, (me // CORES) % CHIPS, me % CORES
        zp, vp = ring_place(self.z), ring_place(self.v)
        self.z_at = [ring_place((zp + k) % PLANES) for k in range(PLANES)]
        self.v_at = [ring_place((vp + k) % CHIPS) for k in range(CHIPS)]
        z, v, c = self.z, self.v, self.c
        self.z_next = self.z_at[1] * PLANE_DEV + v * CORES + c
        self.z_prev = self.z_at[3] * PLANE_DEV + v * CORES + c
        self.right = z * PLANE_DEV + self.v_at[1] * CORES + c
        self.left = z * PLANE_DEV + self.v_at[3] * CORES + c
        self.partner = me + 1 - 2 * c
        self.sems = send_sems, recv_sems
        self.copies, self.used = [], 0

    def greet(self):
        barrier = pltpu.get_barrier_semaphore()
        greeted = (self.right, self.left, self.z_next, self.z_prev, self.partner)
        for d in greeted:
            pl.semaphore_signal(barrier, inc=1, device_id=(d,), device_id_type=pl.DeviceIdType.MESH)
        pl.semaphore_wait(barrier, len(greeted))

    def send(self, src, dst, target):
        k, self.used = self.used, self.used + 1
        copy = pltpu.make_async_remote_copy(
            src_ref=src, dst_ref=dst, send_sem=self.sems[0].at[k], recv_sem=self.sems[1].at[k],
            device_id=(target,), device_id_type=pl.DeviceIdType.MESH,
        )
        copy.start()
        self.copies.append(copy)
        return copy

    def finish(self):
        for copy in self.copies:
            copy.wait_send()


class Gather:
    def __init__(self, links, source, place, local_sem):
        self.links, self.source, self.place = links, source, place
        self.along, self.near_in, self.far_in, self.core_in = {}, {}, {}, []
        self.own = pltpu.make_async_copy(source, self.block(0, OWN), local_sem)
        self.own.start()

    def block(self, back, chip):
        links = self.links
        return self.place(links.z_at[(PLANES - back) % PLANES], links.v_at[chip], links.c)

    def to_core(self, src, dst):
        self.core_in.append(self.links.send(src, dst, self.links.partner))

    def hop(self, s):
        links, here = self.links, self.block(s, OWN)
        if s:
            self.along[s - 1].wait_recv()
        src = here if s else self.source
        if s < PLANES - 1:
            self.along[s] = links.send(src, here, links.z_next)
        self.near_in[s, LEFT] = links.send(src, here, links.right)
        self.near_in[s, RIGHT] = links.send(src, here, links.left)
        self.to_core(src, here)

    def near(self, s):
        links = self.links
        for chip in (LEFT, RIGHT):
            self.near_in[s, chip].wait_recv()
            here = self.block(s, chip)
            if (chip == LEFT) == (s < 2):
                self.far_in[s] = links.send(here, here, links.right if chip == LEFT else links.left)
            self.to_core(here, here)

    def far(self, s):
        self.far_in[s].wait_recv()
        here = self.block(s, FAR)
        self.to_core(here, here)

    def wait(self):
        self.own.wait()
        for copy in self.core_in:
            copy.wait_recv()


GATHER_SENDS = 31
OWN, RIGHT, FAR, LEFT = range(CHIPS)


def shard_place(name, out):
    if name == "mamba_out":
        return lambda z, v, c: out.at[(z // 2) * 16 + c * 8 + (z % 2) * 4 + v]
    if name == "smalls":
        return lambda z, v, c: out.at[z * PLANE_DEV + v * CORES + c]
    return lambda z, v, c: out.at[c * 16 + z * 4 + v]


def gather_first_kernel(names, *refs):
    count = len(names)
    ins, units, outs, moved = refs[:count], refs[count : count + 2], refs[count + 2 : 2 * count + 2], refs[2 * count + 2 :]
    (gu_1, down_1, down_2), (send_sems, recv_sems, local) = moved[:3], moved[3:]
    links = Links(send_sems, recv_sems)
    links.greet()
    gathers = []
    for k, name in enumerate(names):
        parts = 2 if name == "wide" else 1
        width = ins[k].shape[1] // parts
        for part in range(parts):
            columns = pl.ds(part * width, width)
            place = shard_place(name, outs[k])

            def part_place(z, v, c, place=place, columns=columns):
                return place(z, v, c).at[:, columns]

            gathers.append(Gather(links, ins[k].at[:, columns], part_place, local.at[len(gathers)]))
    for s in range(PLANES):
        for g in gathers:
            g.hop(s)
    hops = [links.send(units[0], gu_1, links.z_next), links.send(units[1], down_1, links.z_next)]
    for s in range(PLANES):
        for g in gathers:
            g.near(s)
    for s in range(PLANES):
        for g in gathers:
            g.far(s)
        if s == 0:
            hops[1].wait_recv()
            hops.append(links.send(down_1, down_2, links.z_next))
    for g in gathers:
        g.wait()
    hops[0].wait_recv()
    hops[2].wait_recv()
    links.finish()


def gather_first(names, blocks, units):
    count, sends = len(names), GATHER_SENDS * (len(names) + 1) + 3
    sem, anywhere = pltpu.SemaphoreType.DMA, pl.BlockSpec(memory_space=pl.ANY)
    shapes = [(FAST_DEV,) + block.shape for block in blocks] + [units[0].shape] + [units[1].shape] * 2
    return pl.pallas_call(
        functools.partial(gather_first_kernel, names),
        out_shape=[jax.ShapeDtypeStruct(shape, jnp.bfloat16) for shape in shapes],
        in_specs=[anywhere] * (count + 2),
        out_specs=[anywhere] * (count + 3),
        scratch_shapes=[sem((sends,))] * 2 + [sem((count + 1,))],
        compiler_params=pltpu.CompilerParams(collective_id=0, has_side_effects=True),
        name="gather_first",
    )(*blocks, *units)


REST_COLUMNS = 1152
WIDE_BLOCKS = [(0, 7 * REST_COLUMNS, WIDE - 7 * REST_COLUMNS)] + [(0, k * REST_COLUMNS, REST_COLUMNS) for k in range(7)]
BRANCH_BLOCKS = [(0, 0, 768), (0, 768, 832), (1, 0, D)]
GRAD_ROWS = 192
GROUPS = PLANES * CHIPS
GAIN_LANES = 256


def add_rows(target, *others):
    @pl.loop(0, target.shape[0] // 16)
    def _(k):
        rows = pl.ds(pl.multiple_of(k * 16, 16), 16)
        total = target[rows, :].astype(jnp.float32)
        for other in others:
            total = total + other[rows, :].astype(jnp.float32)
        target[rows, :] = total.astype(target.dtype)


class Taker:
    def __init__(self, refs):
        self.refs = list(refs)

    def __call__(self, count):
        taken, self.refs = self.refs[:count], self.refs[count:]
        return taken


class SumPlan:
    def __init__(self, blocks, shard_rows, rest_rows, rest_columns, widths, columns, lows, smalls=None):
        self.blocks, self.rest_rows, self.has_smalls = blocks, rest_rows, smalls is not None
        self.shard_rows, self.widths = shard_rows, widths
        self.operands = list(columns) + list(lows) + ([smalls] if self.has_smalls else [])
        f32, bf16 = jnp.float32, jnp.bfloat16
        self.pairs, rows = len(lows), lows[0].shape[0]
        self.out_shape = [
            jax.ShapeDtypeStruct((shard_rows[k] + rest_rows[k], width), f32)
            for k in range(self.pairs)
            for width in widths[k]
        ]
        self.out_shape.append(jax.ShapeDtypeStruct((16, rest_columns), f32))
        scratch = [pltpu.VMEM((x.shape[0] * MAIN // CORES, CORES * rows), bf16) for x in columns]
        scratch += [pltpu.VMEM((x.shape[0] * (x.shape[1] - MAIN) // CORES, CORES * rows), bf16) for x in columns]
        scratch += [pltpu.VMEM((CORES * rows, y.shape[1]), bf16) for y in lows]
        scratch.append(pltpu.VMEM((16 * GROUPS, rest_columns), f32))
        shapes = [(shard_rows[pair], n) for pair, _, n in blocks] + [(16, rest_columns)]
        if self.has_smalls:
            shapes.append((smalls.shape[1] // GROUPS, smalls.shape[2]))
            scratch.append(pltpu.VMEM(smalls.shape[1:], bf16))
            self.out_shape.append(jax.ShapeDtypeStruct(shapes[-1], f32))
        for copies in (0, 4, 4, 4, 3):
            scratch += [pltpu.VMEM((copies, r, n) if copies else (GROUPS * r, n), bf16) for r, n in shapes]
        sem = pltpu.SemaphoreType.DMA
        self.count = len(shapes)
        scratch += [sem((self.count, k)) for k in (4, 4, 8, 8, 3, 3)] + [sem((self.pairs, 6))] * 3
        self.scratch = scratch


class Summing:
    def __init__(self, plan, links, ins, totals, scratch, early=2):
        self.blocks, self.rest_rows, self.has_smalls = plan.blocks, plan.rest_rows, plan.has_smalls
        self.pairs, self.count = plan.pairs, plan.count
        self.links = links
        take = Taker(ins)
        self.columns_in, self.lows_in = take(self.pairs), take(self.pairs)
        self.smalls_in = take(int(self.has_smalls))
        take = Taker(totals)
        self.shard_rows, self.totals = plan.shard_rows, []
        for widths in plan.widths:
            starts = [sum(widths[:j]) for j in range(len(widths))]
            self.totals.append([(ref, start, start + width) for ref, start, width in zip(take(len(widths)), starts, widths)])
        self.rest_total = take(1)[0]
        self.smalls_total = take(int(self.has_smalls))
        take = Taker(scratch)
        self.columns_all, self.rests_all, self.lows_all = take(self.pairs), take(self.pairs), take(self.pairs)
        self.rest_stage, self.smalls_stage = take(1)[0], take(int(self.has_smalls))
        self.partial, self.through, self.from_left, self.from_right, self.along = [take(self.count) for _ in range(5)]
        self.t_send, self.t_recv, self.s_send, self.s_recv, self.z_send, self.z_recv = take(6)
        self.c_send, self.c_recv, self.local = take(3)
        self.rest_at, self.smalls_at = len(self.blocks), len(self.blocks) + 1
        self.group_rows = [p.shape[0] // GROUPS for p in self.partial]
        self.sent, self.own, self.arriving = [], [], {}
        self.extra_rest = None
        self.order = list(range(len(self.blocks)))
        if self.has_smalls:
            self.order.insert(2, self.smalls_at)
        self.order.append(self.rest_at)
        events = []
        for p, i in enumerate(self.order):
            events += [
                (p - early, self.launch_far, i), (p, self.launch_near, i), (p + 1.5, self.relay, i),
                (p + 2.5, self.collect, i),
            ]
            events += [(p + 3.5 + j, self.planes, i, 2 - j) for j in range(3)]
        self.events = sorted(events, key=lambda event: event[0])

    def send(self, key, src, dst, ss, rs, target):
        copy = pltpu.make_async_remote_copy(
            src_ref=src, dst_ref=dst, send_sem=ss, recv_sem=rs, device_id=(target,),
            device_id_type=pl.DeviceIdType.MESH,
        )
        copy.start()
        self.sent.append(copy)
        self.arriving[key] = copy

    def stay(self, src, dst, sem):
        copy = pltpu.make_async_copy(src, dst, sem)
        copy.start()
        self.own.append(copy)

    def exchange(self):
        c, partner = self.links.c, self.links.partner
        c_send, c_recv, local = self.c_send, self.c_recv, self.local
        for k in range(self.pairs):
            columns_in, lows_in = self.columns_in[k], self.lows_in[k]
            rows, rest = lows_in.shape[0], columns_in.shape[1] - MAIN
            mine, other = pl.ds(0, rows), pl.ds(rows, rows)
            self.stay(lows_in, self.lows_all[k].at[mine], local.at[k, 0])
            self.send(("l", k), lows_in, self.lows_all[k].at[other], c_send.at[k, 0], c_recv.at[k, 0], partner)
            for h in range(columns_in.shape[0]):
                for kind, target, first, half in (
                    (0, self.columns_all[k], 0, MAIN // CORES), (1, self.rests_all[k], MAIN, rest // CORES),
                ):
                    place, at = pl.ds(h * half, half), 1 + 2 * kind + h
                    self.stay(
                        columns_in.at[h, pl.ds(pl.multiple_of(first + c * half, half), half)],
                        target.at[place, mine],
                        local.at[k, at],
                    )
                    self.send(
                        ("x", k, at),
                        columns_in.at[h, pl.ds(pl.multiple_of(first + (1 - c) * half, half), half)],
                        target.at[place, other],
                        c_send.at[k, at],
                        c_recv.at[k, at],
                        partner,
                    )
        if self.has_smalls:
            smalls = self.smalls_in[0]
            self.stay(smalls.at[c], self.partial[self.smalls_at], local.at[0, 5])
            self.send(("m",), smalls.at[1 - c], self.smalls_stage[0], c_send.at[0, 5], c_recv.at[0, 5], partner)

    def exchanged(self):
        for copy in self.own:
            copy.wait()
        for k in range(self.pairs):
            self.arriving["l", k].wait_recv()
            for h in range(self.columns_in[k].shape[0]):
                self.arriving["x", k, 1 + h].wait_recv()
                self.arriving["x", k, 3 + h].wait_recv()

    def rest_block(self):
        stage = self.rest_stage
        stage[...] = jnp.zeros_like(stage)
        row, width = 0, stage.shape[1]
        for k in range(self.pairs):
            r, lows = self.rest_rows[k], self.lows_all[k]
            for column in range(0, lows.shape[1], width):
                columns = min(width, lows.shape[1] - column)
                product = flat_product(self.rests_all[k][...], lows[:, column : column + columns])
                for g in range(GROUPS):
                    at = 16 * g + row
                    stage[at : at + r, :columns] = product[g * r : (g + 1) * r]
                row += r
        if self.extra_rest is not None:
            self.extra_rest(stage)
        self.partial[self.rest_at][...] = stage[...].astype(jnp.bfloat16)

    def compute(self, i):
        partial = self.partial[i]
        if i == self.rest_at:
            self.rest_block()
            return
        if i == self.smalls_at:
            self.arriving["m",].wait_recv()
            add_rows(partial, self.smalls_stage[0])
            return
        pair, column, columns = self.blocks[i]

        @pl.loop(0, partial.shape[0] // GRAD_ROWS)
        def _(j):
            rows = pl.ds(pl.multiple_of(j * GRAD_ROWS, GRAD_ROWS), GRAD_ROWS)
            partial[rows, :] = flat_product(
                self.columns_all[pair][rows, :], self.lows_all[pair][:, pl.ds(column, columns)]
            ).astype(jnp.bfloat16)

    def part(self, i, k, chip):
        rows = self.group_rows[i]
        at = (self.links.z_at[k] * CHIPS + self.links.v_at[chip]) * rows
        return self.partial[i].at[pl.ds(pl.multiple_of(at, rows), rows)]

    def launch_far(self, i):
        self.compute(i)
        for k in (3, 2, 1, 0):
            self.send(
                (i, "t", k), self.part(i, k, FAR), self.through[i].at[k], self.t_send.at[i, k], self.t_recv.at[i, k],
                self.links.right if k % 2 else self.links.left,
            )

    def launch_near(self, i):
        for k in (3, 2, 1, 0):
            landing, event = (self.from_right, 4 + k) if k % 2 else (self.from_left, k)
            self.send(
                (i, "s", event), self.part(i, k, LEFT if k % 2 else RIGHT), landing[i].at[k],
                self.s_send.at[i, event], self.s_recv.at[i, event], self.links.left if k % 2 else self.links.right,
            )

    def relay(self, i):
        for k in (3, 2, 1, 0):
            self.arriving[i, "t", k].wait_recv()
            add_rows(self.through[i].at[k], self.part(i, k, RIGHT if k % 2 else LEFT))
            landing, event = (self.from_left, k) if k % 2 else (self.from_right, 4 + k)
            self.send(
                (i, "s", event), self.through[i].at[k], landing[i].at[k], self.s_send.at[i, event],
                self.s_recv.at[i, event], self.links.right if k % 2 else self.links.left,
            )

    def pass_on(self, i, k):
        self.send(
            (i, "z", 3 - k), self.part(i, k, OWN), self.along[i].at[3 - k], self.z_send.at[i, 3 - k],
            self.z_recv.at[i, 3 - k], self.links.z_next,
        )

    def collect(self, i):
        for k in (3, 2, 1, 0):
            self.arriving[i, "s", k].wait_recv()
            self.arriving[i, "s", 4 + k].wait_recv()
            add_rows(self.part(i, k, OWN), self.from_left[i].at[k], self.from_right[i].at[k])
            if k == 3:
                self.pass_on(i, k)

    def planes(self, i, k):
        mine, along = self.part(i, k, OWN), self.along[i]
        self.arriving[i, "z", 2 - k].wait_recv()
        if k:
            add_rows(mine, along.at[2 - k])
            self.pass_on(i, k)
            return
        if i == self.rest_at:
            targets, column, columns = [(self.rest_total, 0, self.rest_total.shape[1])], 0, self.rest_total.shape[1]
        elif i == self.smalls_at:
            targets, column, columns = [(self.smalls_total[0], 0, 128)], 0, 128
        else:
            pair, column, columns = self.blocks[i]
            targets = self.totals[pair]

        @pl.loop(0, self.group_rows[i] // 16)
        def _(j):
            rows = pl.ds(pl.multiple_of(j * 16, 16), 16)
            total = mine[rows, :].astype(jnp.float32) + along[2, rows, :].astype(jnp.float32)
            for ref, start, stop in targets:
                low, high = max(start, column), min(stop, column + columns)
                if low < high:
                    ref[rows, low - start : high - start] = total[:, low - column : high - column]

        if i == self.rest_at:
            self.place_rest()

    def place_rest(self):
        row, width = 0, self.rest_total.shape[1]
        for k in range(self.pairs):
            r, first = self.rest_rows[k], self.shard_rows[k]
            for column in range(0, self.lows_all[k].shape[1], width):
                for ref, start, stop in self.totals[k]:
                    low, high = max(start, column), min(stop, column + width)
                    if low < high:
                        ref[first : first + r, low - start : high - start] = self.rest_total[
                            row : row + r, low - column : high - column
                        ]
                row += r

    def advance(self, until):
        while self.events and self.events[0][0] < until:
            _, stage, *which = self.events.pop(0)
            stage(*which)

    def finish(self):
        self.advance(1e9)
        for copy in self.sent:
            copy.wait_send()


UNIT_PAD = 64
BACK_LANES = 256


def last_kernel(plan, *refs):
    bf16, f32 = jnp.bfloat16, jnp.float32
    take = Taker(refs)
    ins = take(len(plan.operands))
    middle_grad_ref, tokens_ref, gains_ref, table_d_ref, wide_ref, wide_rest_ref = take(6)
    gu_grad_ref, down_grad_ref, gu_came_ref, down_came_ref = take(4)
    totals = take(len(plan.out_shape))
    input_grad_ref, gate_out_ref, up_out_ref, down_out_ref = take(4)
    scratch = take(len(plan.scratch))
    order, wide_buffer, total, gain, gain_other = take(5)
    gu_own, gu_sum, gu_next, down_own, down_sum, down_next, gu_rows, gu_in = take(8)
    wide_sem, unit_sem, send_sems, recv_sems = take(4)
    count = WIDE // BACK_LANES
    links = Links(send_sems, recv_sems)
    me = lax.axis_index("fsdp")
    first = me // PLANE_DEV * PLANE_DEV
    others = [first + (me % PLANE_DEV + k) % PLANE_DEV for k in range(1, PLANE_DEV)]
    barrier = pltpu.get_barrier_semaphore()
    greeted = others + [links.z_next, links.z_prev]
    for d in greeted:
        pl.semaphore_signal(barrier, inc=1, device_id=(d,), device_id_type=pl.DeviceIdType.MESH)
    pl.semaphore_wait(barrier, len(greeted))

    summing = Summing(plan, links, ins, totals, scratch)
    summing.exchange()
    gu_height, down_height = gu_own.shape[0], down_own.shape[0]
    wide_low = summing.lows_all[0].at[pl.ds(0, tokens_ref.shape[0])]

    def piece(ref, height, k):
        return ref.at[pl.ds(pl.multiple_of(links.z_at[k] * height, 16), height)]

    middle_copy = pltpu.make_async_copy(middle_grad_ref, input_grad_ref, unit_sem.at[4])
    middle_copy.start()
    moving = gu_sum.at[pl.ds(0, gu_height)]
    loads = [
        pltpu.make_async_copy(gu_came_ref, moving, unit_sem.at[0]),
        pltpu.make_async_copy(down_came_ref, down_sum, unit_sem.at[1]),
    ]
    def load_own(k):
        copies = [
            pltpu.make_async_copy(piece(gu_grad_ref, gu_height, k), gu_own, unit_sem.at[2]),
            pltpu.make_async_copy(piece(down_grad_ref, down_height, k), down_own, unit_sem.at[3]),
        ]
        for copy in copies:
            copy.start()
        return copies

    loads += load_own(1)
    for copy in loads[:2]:
        copy.start()
    def column_copy(j):
        return pltpu.make_async_copy(
            wide_ref.at[:, pl.ds(j * BACK_LANES, BACK_LANES)], wide_buffer.at[j % 2], wide_sem.at[j % 2]
        )

    column_copy(0).start()
    column_copy(1).start()
    summing.exchanged()
    summing.advance(1.2)
    for copy in loads:
        copy.wait()
    add_rows(moving, gu_own)
    add_rows(down_sum, down_own)
    loads = load_own(0)
    hops = [links.send(moving, gu_next, links.z_next), links.send(down_sum, down_next, links.z_next)]

    write_order(table_d_ref, order)
    total[...] = jnp.zeros_like(total)
    for j in range(count):
        column_copy(j).wait()
        total[...] += back_product(wide_low[:, j * BACK_LANES : (j + 1) * BACK_LANES], wide_buffer[j % 2])
        if j + 2 < count:
            column_copy(j + 2).start()
        if j % 8 == 7:
            summing.advance(1.2 + (j + 1) // 8)
    normed_grad = move_back(
        order, jnp.concatenate([total[...], back_product(wide_low[...], wide_rest_ref[...])], axis=1)
    )
    unit, scale = rms_parts(tokens_ref[...].astype(f32))
    back, gain_grad = rms_pull(unit, scale, gains_ref[0:1], normed_grad)
    middle_copy.wait()
    input_grad_ref[...] += back
    gain[...] = jnp.broadcast_to(gain_grad, gain.shape)
    gain_copy = links.send(gain, gain_other, links.partner)
    summing.advance(6.2)

    def gain_rows(stage):
        gain_copy.wait_recv()
        size = 4 * D // FAST_DEV
        lane = lax.broadcasted_iota(jnp.int32, (D, CHIPS * GAIN_LANES), 1)
        source = (lane // GAIN_LANES) * (CORES * size) + links.c * size + lane % GAIN_LANES
        place = lax.broadcasted_iota(jnp.int32, (D, CHIPS * GAIN_LANES), 0)
        picks = (place == source) & (lane % GAIN_LANES < size)
        select = order.at[:, pl.ds(0, CHIPS * GAIN_LANES)]
        select[...] = jnp.where(picks, 1.0, 0.0).astype(bf16)
        both = gain[0:1] + gain_other[0:1]
        both = jnp.broadcast_to(both, (16, D))
        high = both.astype(bf16)
        rest = (both - high.astype(f32)).astype(bf16)
        moved = flat_product(high, select[...]) + flat_product(rest, select[...])
        width, last = stage.shape[1], WIDE % REST_COLUMNS
        for v in range(CHIPS):
            stage[16 * v + 14 : 16 * v + 15, last : last + GAIN_LANES] = moved[
                0:1, v * GAIN_LANES : (v + 1) * GAIN_LANES
            ]

    summing.extra_rest = gain_rows
    summing.advance(7.2)
    for copy in hops:
        copy.wait()
        links.copies.remove(copy)
    for copy in loads:
        copy.wait()
    rows = D // FAST_DEV

    for piece_at in range(0, GU, GAIN_LANES):
        lanes = pl.ds(piece_at, GAIN_LANES)

        @pl.loop(0, gu_height // 16)
        def _(k):
            some = pl.ds(pl.multiple_of(k * 16, 16), 16)
            gu_rows[some, :] = gu_own[some, lanes].astype(f32) + gu_next[some, lanes].astype(f32)

        for p in range(PLANE_DEV):
            gu_sum[p * UNIT_PAD : (p + 1) * UNIT_PAD, lanes] = gu_rows[p * rows : p * rows + UNIT_PAD, :].astype(bf16)

    @pl.loop(0, down_height // 16)
    def _(k):
        some = pl.ds(pl.multiple_of(k * 16, 16), 16)
        down_out_ref[some, :] = down_own[some, :].astype(f32) + down_next[some, :].astype(f32)


    def unit_block(d):
        return gu_sum.at[pl.ds(pl.multiple_of(d % PLANE_DEV * UNIT_PAD, UNIT_PAD), UNIT_PAD)]

    keep = pltpu.make_async_copy(unit_block(me), gu_in.at[me % PLANE_DEV], unit_sem.at[5])
    keep.start()
    given = [links.send(unit_block(d), gu_in.at[me % PLANE_DEV], d) for d in others]
    summing.advance(12.2)
    for copy in given:
        copy.wait_recv()
    keep.wait()
    for half, out_ref in enumerate((gate_out_ref, up_out_ref)):
        for p in range(PLANE_DEV):
            for k in range(PLANES):
                column = half * HALF_GU + k * PAD_FF
                place = (k * PLANE_DEV + p) * SLICE_FF
                out_ref[:, place : place + SLICE_FF] = gu_in[p, :rows, column : column + SLICE_FF]
    summing.finish()
    links.finish()


def last_sums(plan, *operands):
    bf16, f32 = jnp.bfloat16, jnp.float32
    rows, gu_came, down_came = operands[0].shape[0], operands[8], operands[9]
    vmem, anywhere = pl.BlockSpec(memory_space=pltpu.VMEM), pl.BlockSpec(memory_space=pl.ANY)
    in_specs = [anywhere] * len(plan.operands) + [anywhere] + [vmem] * 3 + [anywhere, vmem] + [anywhere] * 4
    out_shape = plan.out_shape + [
        jax.ShapeDtypeStruct((rows, D), f32),
        jax.ShapeDtypeStruct((D // FAST_DEV, FF), bf16),
        jax.ShapeDtypeStruct((D // FAST_DEV, FF), bf16),
        jax.ShapeDtypeStruct(down_came.shape, f32),
    ]
    unit, downs = gu_came.shape, down_came.shape
    pad = (unit[0] + UNIT_PAD, GAIN_LANES)
    sem = pltpu.SemaphoreType.DMA
    return pl.pallas_call(
        functools.partial(last_kernel, plan),
        out_shape=out_shape,
        in_specs=in_specs,
        out_specs=[vmem] * len(out_shape),
        scratch_shapes=plan.scratch
        + [
            pltpu.VMEM((D, D), bf16),
            pltpu.VMEM((2, MAIN, BACK_LANES), bf16),
            pltpu.VMEM((rows, MAIN), f32),
            pltpu.VMEM((8, D), f32),
            pltpu.VMEM((8, D), f32),
            pltpu.VMEM(unit, bf16),
            pltpu.VMEM((PLANE_DEV * UNIT_PAD, GU), bf16),
            pltpu.VMEM(unit, bf16),
            pltpu.VMEM(downs, bf16),
            pltpu.VMEM(downs, bf16),
            pltpu.VMEM(downs, bf16),
            pltpu.VMEM(pad, f32),
            pltpu.VMEM((PLANE_DEV, UNIT_PAD, GU), bf16),
            sem((2,)),
            sem((7,)),
            sem((10,)),
            sem((10,)),
        ],
        compiler_params=pltpu.CompilerParams(
            collective_id=3, has_side_effects=True, vmem_limit_bytes=63 * 1024 * 1024
        ),
        name="last_sums",
    )(*plan.operands, *operands)


def scan_setup(pre, shift, conv, hold):
    step = jax.nn.softplus(pre + shift)
    return step, step + hold, step * conv


def tiled(block):
    return jnp.concatenate([block] * (LANES // 128), axis=1)


def folded(block):
    total = block[:, :128]
    for k in range(1, LANES // 128):
        total = total + block[:, 128 * k : 128 * (k + 1)]
    return total


GROUP = HEADS // KV_HEADS


def group_scores(qkv_ref, seg_col_ref, seg_row_ref, g):
    rows = qkv_ref.shape[0]
    queries = jnp.concatenate(
        [qkv_ref[:, (g * GROUP + r) * HEAD : (g * GROUP + r + 1) * HEAD] for r in range(GROUP)], axis=0
    )
    keys = qkv_ref[:, D + g * HEAD : D + (g + 1) * HEAD]
    values = qkv_ref[:, D + (KV_HEADS + g) * HEAD : D + (KV_HEADS + g + 1) * HEAD]
    scores = back_product(queries, keys) * HEAD ** (-0.5)
    t = lax.broadcasted_iota(jnp.int32, (rows, rows), 0)
    u = lax.broadcasted_iota(jnp.int32, (rows, rows), 1)
    allowed = (seg_col_ref[...] == seg_row_ref[...]) & (u <= t)
    scores = jnp.where(jnp.concatenate([allowed] * GROUP, axis=0), scores, -1e30)
    raised = jnp.exp(scores - jnp.max(scores, axis=-1, keepdims=True))
    probs = raised / jnp.sum(raised, axis=-1, keepdims=True)
    return queries, keys, values, probs


def attention_forward_kernel(qkv_ref, seg_col_ref, seg_row_ref, out_ref):
    rows = qkv_ref.shape[0]
    for g in range(KV_HEADS):
        _, _, values, probs = group_scores(qkv_ref, seg_col_ref, seg_row_ref, g)
        mixed = flat_product(probs.astype(jnp.bfloat16), values)
        for r in range(GROUP):
            head = g * GROUP + r
            out_ref[:, head * HEAD : (head + 1) * HEAD] = mixed[r * rows : (r + 1) * rows]


def attention_backward_kernel(qkv_ref, seg_col_ref, seg_row_ref, grad_ref, low_ref, first):
    rows = qkv_ref.shape[0]
    bf16 = jnp.bfloat16
    for g in range(KV_HEADS):
        queries, keys, values, probs = group_scores(qkv_ref, seg_col_ref, seg_row_ref, g)
        grads = jnp.concatenate(
            [grad_ref[:, (g * GROUP + r) * HEAD : (g * GROUP + r + 1) * HEAD] for r in range(GROUP)], axis=0
        )
        prob_grad = back_product(grads, values)
        score_low = (
            probs * (prob_grad - jnp.sum(probs * prob_grad, axis=-1, keepdims=True))
        ).astype(bf16)
        query_grad = (flat_product(score_low, keys) * HEAD ** (-0.5)).astype(bf16)
        for r in range(GROUP):
            head = g * GROUP + r
            low_ref[:, first + head * HEAD : first + (head + 1) * HEAD] = query_grad[r * rows : (r + 1) * rows]
        key_grad = outer_sum(score_low, queries) * HEAD ** (-0.5)
        low_ref[:, first + D + g * HEAD : first + D + (g + 1) * HEAD] = key_grad.astype(bf16)
        value_grad = outer_sum(probs.astype(bf16), grads)
        low_ref[:, first + D + (KV_HEADS + g) * HEAD : first + D + (KV_HEADS + g + 1) * HEAD] = value_grad.astype(bf16)


GRAD_LANES = 256


class PlaneTotal:
    def __init__(self, links, parts, core_in, far_in, near_in):
        self.links, self.parts, self.core_in, self.far_in, self.near_in = links, parts, core_in, far_in, near_in
        self.top = pl.ds(0, parts.shape[1] // 2)
        self.low = pl.ds(parts.shape[1] // 2, parts.shape[1] // 2)
        self.core = {}

    def give(self, chip):
        self.core[chip] = self.links.send(self.parts.at[CHIPS + chip], self.core_in.at[chip], self.links.partner)

    def join(self, chip):
        self.core[chip].wait_recv()
        add_rows(self.parts.at[chip], self.core_in.at[chip])

    def start(self):
        links, parts = self.links, self.parts
        self.join(FAR)
        self.far = [
            links.send(parts.at[FAR, self.top], self.far_in.at[0], links.right),
            links.send(parts.at[FAR, self.low], self.far_in.at[1], links.left),
        ]
        self.join(RIGHT)
        self.near = [links.send(parts.at[RIGHT, self.low], self.near_in.at[0, self.low], links.right)]
        self.join(LEFT)
        self.near.append(links.send(parts.at[LEFT, self.top], self.near_in.at[1, self.top], links.left))
        self.join(OWN)

    def relay(self):
        links, parts = self.links, self.parts
        self.far[0].wait_recv()
        add_rows(parts.at[RIGHT, self.top], self.far_in.at[0])
        self.near.append(links.send(parts.at[RIGHT, self.top], self.near_in.at[0, self.top], links.right))
        self.far[1].wait_recv()
        add_rows(parts.at[LEFT, self.low], self.far_in.at[1])
        self.near.append(links.send(parts.at[LEFT, self.low], self.near_in.at[1, self.low], links.left))

    def total(self, out_ref):
        for copy in self.near:
            copy.wait_recv()

        @pl.loop(0, out_ref.shape[0] // 16)
        def _(k):
            rows = pl.ds(pl.multiple_of(k * 16, 16), 16)
            total = self.parts[OWN, rows, :].astype(jnp.float32) + self.near_in[0, rows, :].astype(jnp.float32)
            out_ref[rows, :] = total + self.near_in[1, rows, :].astype(jnp.float32)


def feed_forward_kernel(
    rows_ref, out_low_ref, gu_0_ref, gu_1_ref, gu_2_ref, gu_3_ref, down_0_ref, down_1_ref, down_2_ref, down_3_ref,
    back_ref, ffn_ref, gu_grad_ref, down_grad_ref,
    gu_ref, down_ref, rows_all, act, gu_low, back, ffn, back_core, back_far, back_near, ffn_core, ffn_far, ffn_near,
    send_sems, recv_sems, own_sem,
):
    bf16, f32 = jnp.bfloat16, jnp.float32
    rows = rows_ref.shape[0]
    links = Links(send_sems, recv_sems)
    links.greet()
    own = pltpu.make_async_copy(rows_ref, rows_all.at[OWN], own_sem.at[0])
    own.start()
    copies = []
    for matrix, parts in (
        (gu_ref, (gu_0_ref, gu_1_ref, gu_2_ref, gu_3_ref)),
        (down_ref, (down_0_ref, down_1_ref, down_2_ref, down_3_ref)),
    ):
        height = parts[0].shape[0]
        for hops, part in enumerate(parts):
            place = pl.multiple_of(links.z_at[(PLANES - hops) % PLANES] * height, 16)
            copies.append(
                pltpu.make_async_copy(part, matrix.at[pl.ds(place, height)], own_sem.at[1 + len(copies)])
            )
            copies[-1].start()
    used = PLANES * PAD_FF
    down_ref[used:, :] = jnp.zeros((HALF_GU - used, D), bf16)
    to_right = links.send(rows_ref, rows_all.at[LEFT], links.right)
    to_left = links.send(rows_ref, rows_all.at[RIGHT], links.left)
    cores = {OWN: links.send(rows_ref, rows_all.at[CHIPS + OWN], links.partner)}
    back_sum = PlaneTotal(links, back, back_core, back_far, back_near)
    ffn_sum = PlaneTotal(links, ffn, ffn_core, ffn_far, ffn_near)
    top, low = pl.ds(0, rows // 2), pl.ds(rows // 2, rows // 2)

    def compute(slot):
        here = pl.ds(slot * rows, rows)
        x = rows_all[slot]
        gu = flat_product(x, gu_ref[...])
        gate, up = gu[:, :HALF_GU], gu[:, HALF_GU:]
        opened = 1.0 / (1.0 + jnp.exp(-gate))
        act[here, :] = (gate * opened * up).astype(bf16)
        grad = back_product(out_low_ref[here, :], down_ref[...])
        gu_low[here, :HALF_GU] = (grad * up * opened * (1.0 + gate * (1.0 - opened))).astype(bf16)
        gu_low[here, HALF_GU:] = (grad * gate * opened).astype(bf16)
        back[slot] = back_product(gu_low[here, :], gu_ref[...]).astype(bf16)
        if slot >= CHIPS:
            back_sum.give(slot - CHIPS)

    own.wait()
    for copy in copies:
        copy.wait()
    compute(OWN)
    cores[OWN].wait_recv()
    compute(CHIPS + OWN)
    to_right.wait_recv()
    far = [links.send(rows_all.at[LEFT, top], rows_all.at[FAR, top], links.right)]
    cores[LEFT] = links.send(rows_all.at[LEFT], rows_all.at[CHIPS + LEFT], links.partner)
    to_left.wait_recv()
    far.append(links.send(rows_all.at[RIGHT, low], rows_all.at[FAR, low], links.left))
    cores[RIGHT] = links.send(rows_all.at[RIGHT], rows_all.at[CHIPS + RIGHT], links.partner)
    compute(LEFT)
    compute(RIGHT)
    for copy in far:
        copy.wait_recv()
    cores[FAR] = links.send(rows_all.at[FAR], rows_all.at[CHIPS + FAR], links.partner)
    compute(FAR)
    for chip in (FAR, RIGHT, LEFT):
        cores[chip].wait_recv()
        compute(CHIPS + chip)
    back_sum.start()

    def ffn_rows(slot):
        ffn[slot] = flat_product(act[slot * rows : (slot + 1) * rows], down_ref[...]).astype(bf16)
        if slot >= CHIPS:
            ffn_sum.give(slot - CHIPS)

    for chip in (FAR, RIGHT, LEFT, OWN):
        ffn_rows(CHIPS + chip)
    back_sum.relay()
    for chip in (FAR, RIGHT, LEFT, OWN):
        ffn_rows(chip)
    ffn_sum.start()

    def gu_grad(column, columns):
        left = jnp.concatenate([rows_all[slot, :, column : column + columns] for slot in range(PLANE_DEV)], axis=0)
        gu_grad_ref[column : column + columns, :] = outer_sum(left, gu_low[...]).astype(bf16)

    for column in range(0, 2 * GRAD_LANES, GRAD_LANES):
        gu_grad(column, GRAD_LANES)
    back_sum.total(back_ref)
    ffn_sum.relay()
    for column in range(2 * GRAD_LANES, D, GRAD_LANES):
        gu_grad(column, min(GRAD_LANES, D - column))
    for column in range(0, HALF_GU, GRAD_LANES):
        down_grad_ref[column : column + GRAD_LANES, :] = outer_sum(
            act[:, column : column + GRAD_LANES], out_low_ref[...]
        ).astype(bf16)
    ffn_sum.total(ffn_ref)
    links.finish()


def feed_forward(rows_low, out_low, *units):
    bf16, f32 = jnp.bfloat16, jnp.float32
    rows = rows_low.shape[0]
    vmem, anywhere = pl.BlockSpec(memory_space=pltpu.VMEM), pl.BlockSpec(memory_space=pl.ANY)

    def slots(count, height=rows):
        return pltpu.VMEM((count, height, D), bf16)

    sums = [slots(CHIPS), slots(2, rows // 2), slots(2)]
    return pl.pallas_call(
        feed_forward_kernel,
        out_shape=[
            jax.ShapeDtypeStruct((rows, D), f32),
            jax.ShapeDtypeStruct((rows, D), f32),
            jax.ShapeDtypeStruct((D, GU), bf16),
            jax.ShapeDtypeStruct((HALF_GU, D), bf16),
        ],
        in_specs=[anywhere, vmem] + [anywhere] * len(units),
        out_specs=[vmem] * 4,
        scratch_shapes=[
            pltpu.VMEM((D, GU), bf16),
            pltpu.VMEM((HALF_GU, D), bf16),
            slots(PLANE_DEV),
            pltpu.VMEM((PLANE_DEV * rows, HALF_GU), bf16),
            pltpu.VMEM((PLANE_DEV * rows, GU), bf16),
            slots(PLANE_DEV),
            slots(PLANE_DEV),
        ]
        + sums
        + sums
        + [pltpu.SemaphoreType.DMA((32,))] * 2
        + [pltpu.SemaphoreType.DMA((9,))],
        compiler_params=pltpu.CompilerParams(
            collective_id=4, has_side_effects=True, vmem_limit_bytes=60 * 1024 * 1024
        ),
        name="feed_forward",
    )(rows_low, out_low, *units)


CHUNKS = INNER // LANES
WIDE_CHUNKS = [(k * LANES, LANES) for k in range(WIDE // LANES)] + [(WIDE // LANES * LANES, WIDE % LANES)]
WIDE_BUFFERS = 3
MAIN = FAST_DEV * MAIN_D
LOW_PAD = 128


def lanes_at(k):
    return pl.ds(pl.multiple_of(k * LANES, 128), LANES)


def write_order(table_ref, matrix_ref):
    size, step = matrix_ref.shape[0], 160

    @pl.loop(0, size // step)
    def _(k):
        at = pl.multiple_of(k * step, 16)
        places = lax.broadcasted_iota(jnp.int32, (step, size), 0) + at
        matrix_ref[pl.ds(at, step), :] = jnp.where(places == table_ref[...], 1.0, 0.0).astype(jnp.bfloat16)


def rms_parts(values):
    scale = lax.rsqrt(jnp.mean(values * values, axis=-1, keepdims=True) + epsilon)
    return values * scale, scale


def rms_pull(unit, scale, gain_row, grad):
    inner = grad * gain_row
    back = scale * (inner - unit * jnp.mean(inner * unit, axis=-1, keepdims=True))
    return back, jnp.sum(grad * unit, axis=0, keepdims=True)


def move_back(order, rows_wide):
    high = rows_wide.astype(jnp.bfloat16)
    rest = (rows_wide - high.astype(jnp.float32)).astype(jnp.bfloat16)
    return back_product(high, order[...]) + back_product(rest, order[...])


def wide_copy(wide_ref, buffer, sem, j, buffers=WIDE_BUFFERS):
    column, columns = WIDE_CHUNKS[j]
    slot = j % buffers
    return pltpu.make_async_copy(
        wide_ref.at[:, pl.ds(column, columns)], buffer.at[slot, :, pl.ds(0, columns)], sem.at[slot]
    )


def write_columns(rows, out_ref):
    for column in range(0, rows.shape[1], 128):
        some = rows[:, column : column + 128].astype(jnp.float32)
        out_ref[column : column + some.shape[1], :] = some.T.astype(jnp.bfloat16)


def conv_sum(inner, taps, shift, same_ref):
    earlier = [pltpu.roll(inner, k, axis=0) * same_ref[:, k - 1 : k] for k in range(1, CONV)]
    total = shift + taps[CONV - 1 : CONV] * inner
    for k in range(1, CONV):
        total = total + taps[CONV - 1 - k : CONV - k] * earlier[k - 1]
    return total, earlier


def scan_rows(lanes, b_ref, c_ref, y_ref, rates, decay_step, step_input, keep=None):
    rows_all = decay_step.shape[0]

    def eight(k, state):
        base = pl.multiple_of(k * 8, 8)
        steps = decay_step[pl.ds(base, 8), :]
        inputs = step_input[pl.ds(base, 8), :]
        rows = []
        for i in range(8):
            decay = jnp.exp2(steps[i : i + 1] * rates)
            state = decay * state + tiled(b_ref[base + i]) * inputs[i : i + 1]
            if keep is None:
                rows.append(jnp.sum(tiled(c_ref[base + i]) * state, axis=0, keepdims=True))
            else:
                keep(base + i, state)
        if keep is None:
            y_ref[pl.ds(base, 8), lanes] = jnp.concatenate(rows, axis=0)
        return state

    lax.fori_loop(0, rows_all // 8, eight, jnp.zeros((STATE, LANES), jnp.float32))


def spread_lanes(rows_ref, first, out_ref):
    lane = lax.broadcasted_iota(jnp.int32, (STATE, 128), 1)
    place = lax.broadcasted_iota(jnp.int32, (STATE, 128), 0) + first

    @pl.loop(0, rows_ref.shape[0] // 8)
    def _(k):
        base = pl.multiple_of(k * 8, 8)
        rows = rows_ref[pl.ds(base, 8), :]
        for i in range(8):
            picked = jnp.where(lane == place, jnp.broadcast_to(rows[i : i + 1], (STATE, 128)), 0.0)
            out_ref[base + i] = jnp.broadcast_to(jnp.sum(picked, axis=1, keepdims=True), (STATE, 128))


def gather_lanes(b_ref, c_ref, out_ref):
    lane = lax.broadcasted_iota(jnp.int32, (STATE, 128), 1)
    place = lax.broadcasted_iota(jnp.int32, (STATE, 128), 0)

    @pl.loop(0, out_ref.shape[0] // 8)
    def _(k):
        base = pl.multiple_of(k * 8, 8)
        rows = []
        for i in range(8):
            b = jnp.where(lane == place, jnp.sum(b_ref[base + i], axis=1, keepdims=True), 0.0)
            c = jnp.where(lane == place + STATE, jnp.sum(c_ref[base + i], axis=1, keepdims=True), 0.0)
            rows.append(jnp.sum(b + c, axis=0, keepdims=True))
        out_ref[pl.ds(base, 8), :] = jnp.concatenate(rows, axis=0)


def mixer_forward_kernel(
    tokens_ref, gains_ref, seg_col_ref, seg_row_ref, hold_ref, same_ref, table_d_ref, table_i_ref,
    wide_ref, wide_rest_ref, taps_ref, conv_shift_ref, select_ref, step_ref, step_shift_ref, decay_ref, skip_ref,
    out_block_ref, out_rest_ref, join_block_ref, join_rest_ref,
    out_low_ref, gu_1_ref, down_2_ref,
    normed_columns_ref, mixed_ref, qkv_ref, conv_ref, step_low_ref, pre_ref, b_ref, c_ref, y_ref, gated_columns_ref,
    attn_ref, mamba_ref, joined_columns_ref, middle_ref, normed_two_ref,
    out_ref, join_ref, out_low_all_ref, gu_2_ref, gu_3_ref, down_3_ref,
    order, wide_buffer, out_all, join_all, conv_low, gated, normed_ref, joined_ref, decay_step, step_input, select_rows, wide_sem, sem,
    send_sems, recv_sems, local,
):
    bf16, f32 = jnp.bfloat16, jnp.float32
    links = Links(send_sems, recv_sems)
    links.greet()
    branches = [
        Gather(links, out_block_ref, shard_place("mamba_out", out_ref), local.at[0]),
        Gather(links, join_block_ref, shard_place("join", join_ref), local.at[1]),
    ]
    for g in branches:
        g.hop(0)
    low_copy = pltpu.make_async_copy(out_low_ref, out_low_all_ref.at[OWN], local.at[2])
    low_copy.start()
    low_near = [
        links.send(out_low_ref, out_low_all_ref.at[LEFT], links.right),
        links.send(out_low_ref, out_low_all_ref.at[RIGHT], links.left),
    ]
    low_core = [links.send(out_low_ref, out_low_all_ref.at[CHIPS + OWN], links.partner)]
    def low_service():
        top, low = pl.ds(0, out_low_ref.shape[0] // 2), pl.ds(out_low_ref.shape[0] // 2, out_low_ref.shape[0] // 2)
        for copy in low_near:
            copy.wait_recv()
        far = [
            links.send(out_low_all_ref.at[LEFT, top], out_low_all_ref.at[FAR, top], links.right),
            links.send(out_low_all_ref.at[RIGHT, low], out_low_all_ref.at[FAR, low], links.left),
        ]
        for chip in (LEFT, RIGHT):
            low_core.append(links.send(out_low_all_ref.at[chip], out_low_all_ref.at[CHIPS + chip], links.partner))
        return far

    count = len(WIDE_CHUNKS)
    for j in range(WIDE_BUFFERS):
        wide_copy(wide_ref, wide_buffer, wide_sem, j).start()
    inputs = tokens_ref[...].astype(f32)
    write_order(table_d_ref, order)
    normed_ref[...] = flat_product((rms_parts(inputs)[0] * gains_ref[0:1]).astype(bf16), order[...]).astype(bf16)
    for j, (column, columns) in enumerate(WIDE_CHUNKS):
        copy = wide_copy(wide_ref, wide_buffer, wide_sem, j)
        copy.wait()
        part = flat_product(normed_ref[:, :MAIN], wide_buffer[j % WIDE_BUFFERS, :, :columns]) + flat_product(
            normed_ref[:, MAIN:], wide_rest_ref[:, column : column + columns]
        )
        if column < 2 * INNER:
            mixed_ref[:, column : column + columns] = part
        else:
            first, last = column - 2 * INNER, min(column - 2 * INNER + columns, QKV)
            qkv_ref[:, first:last] = part[:, : last - first].astype(bf16)
        if j + WIDE_BUFFERS < count:
            wide_copy(wide_ref, wide_buffer, wide_sem, j + WIDE_BUFFERS).start()
        if j in (4, 8):
            for g in branches:
                g.hop(j // 4)
    low_far = low_service()
    for g in branches:
        g.near(0)
    write_columns(normed_ref[...], normed_columns_ref.at[0])

    @pl.loop(0, CHUNKS)
    def _(k):
        lanes = lanes_at(k)
        total, _ = conv_sum(mixed_ref[:, lanes], taps_ref[:, lanes], conv_shift_ref[:, lanes], same_ref)
        act = total / (1.0 + jnp.exp(-total))
        conv_ref[:, lanes] = act
        conv_low[:, lanes] = act.astype(bf16)

    for g in branches:
        g.hop(3)
    unit_hops = [links.send(gu_1_ref, gu_2_ref, links.z_next), links.send(down_2_ref, down_3_ref, links.z_next)]
    for g in branches:
        g.near(1)
    selected = flat_product(conv_low[...], select_ref[...])
    step_low_ref[...] = selected[:, :LOW_PAD].astype(bf16)
    select_rows[...] = selected[:, LOW_PAD:]
    spread_lanes(select_rows, 0, b_ref)
    spread_lanes(select_rows, STATE, c_ref)
    attention_forward_kernel(qkv_ref, seg_col_ref, seg_row_ref, attn_ref)
    write_order(table_i_ref, order)
    for copy in low_far:
        copy.wait_recv()
    low_core.append(links.send(out_low_all_ref.at[FAR], out_low_all_ref.at[CHIPS + FAR], links.partner))
    for g in branches:
        g.near(2)
        g.far(0)

    def scan_chunk(k):
        lanes = lanes_at(k)
        pre = flat_product(step_low_ref[...], step_ref[:, lanes])
        pre_ref[:, lanes] = pre
        conv = conv_ref[:, lanes]
        _, decay_step[...], step_input[...] = scan_setup(pre, step_shift_ref[:, lanes], conv, hold_ref[...])
        scan_rows(lanes, b_ref, c_ref, y_ref, decay_ref[:, lanes] * (-LOG2E), decay_step, step_input)
        gate = mixed_ref[:, pl.ds(pl.multiple_of(k * LANES + INNER, 128), LANES)]
        gated[:, lanes] = (
            (y_ref[:, lanes] + skip_ref[:, lanes] * conv) * (gate / (1.0 + jnp.exp(-gate)))
        ).astype(bf16)

    pl.loop(0, 1)(scan_chunk)
    for g in branches:
        g.near(3)
        g.far(1)
    pl.loop(1, 3)(scan_chunk)
    unit_hops[0].wait_recv()
    unit_hops.append(links.send(gu_2_ref, gu_3_ref, links.z_next))
    for g in branches:
        g.far(2)
    pl.loop(3, CHUNKS)(scan_chunk)
    half = INNER // 2
    moved = []
    for h in range(2):
        moved.append(flat_product(gated[:, h * half : (h + 1) * half], order[...]).astype(bf16))
        write_columns(moved[h], gated_columns_ref.at[h])
    write_order(table_d_ref, order)
    for g in branches:
        g.far(3)
    branches[0].wait()
    out_copies = [
        pltpu.make_async_copy(out_ref.at[j], out_all.at[pl.ds(j * MAIN_I, MAIN_I)], sem.at[j]) for j in range(FAST_DEV)
    ]
    for copy in out_copies:
        copy.start()
    branches[1].wait()
    join_copies = [
        pltpu.make_async_copy(join_ref.at[j], join_all.at[pl.ds(j * MAIN_D, MAIN_D)], sem.at[FAST_DEV + j])
        for j in range(FAST_DEV)
    ]
    for copy in join_copies:
        copy.start()
    for copy in out_copies:
        copy.wait()
    total = jnp.zeros(mamba_ref.shape, f32)
    for h in range(2):
        total = total + flat_product(moved[h][:, :MAIN], out_all[h * MAIN : (h + 1) * MAIN])
        total = total + flat_product(moved[h][:, MAIN:], out_rest_ref[h])
    mamba_ref[...] = total
    joined = 0.5 * (rms_parts(attn_ref[...])[0] * gains_ref[1:2] + rms_parts(total)[0] * gains_ref[2:3])
    joined_ref[...] = flat_product(joined.astype(bf16), order[...]).astype(bf16)
    for copy in join_copies:
        copy.wait()
    middle = (
        inputs
        + flat_product(joined_ref[:, :MAIN], join_all[...])
        + flat_product(joined_ref[:, MAIN:], join_rest_ref[...])
    )
    middle_ref[...] = middle
    normed_two_ref[...] = (rms_parts(middle)[0] * gains_ref[3:4]).astype(bf16)
    write_columns(joined_ref[...], joined_columns_ref.at[0])
    for copy in low_core + unit_hops[1:]:
        copy.wait_recv()
    low_copy.wait()
    links.finish()


def mixer_forward(*operands):
    rows = operands[0].shape[0]
    bf16, f32 = jnp.bfloat16, jnp.float32
    vmem, anywhere = pl.BlockSpec(memory_space=pltpu.VMEM), pl.BlockSpec(memory_space=pl.ANY)
    in_specs = [vmem] * len(operands)
    for k in (8, 17, 19, 21, 22, 23):
        in_specs[k] = anywhere
    out_block, join_block, out_low, gu, down = [operands[k] for k in (17, 19, 21, 22, 23)]
    shapes = (
        ((1, D, rows), bf16), ((rows, 2 * INNER), f32), ((rows, QKV), bf16), ((rows, INNER), f32), ((rows, LOW_PAD), bf16),
        ((rows, INNER), f32), ((rows, STATE, 128), f32), ((rows, STATE, 128), f32), ((rows, INNER), f32),
        ((2, D, rows), bf16), ((rows, D), f32), ((rows, D), f32), ((1, D, rows), bf16), ((rows, D), f32), ((rows, D), bf16),
    )
    gathered = [
        (FAST_DEV,) + out_block.shape, (FAST_DEV,) + join_block.shape, (PLANE_DEV,) + out_low.shape,
        gu.shape, gu.shape, down.shape,
    ]
    sends = 2 * GATHER_SENDS + 12
    return pl.pallas_call(
        mixer_forward_kernel,
        out_shape=[jax.ShapeDtypeStruct(shape, kind) for shape, kind in shapes]
        + [jax.ShapeDtypeStruct(shape, bf16) for shape in gathered],
        in_specs=in_specs,
        out_specs=[vmem] * len(shapes) + [anywhere] * len(gathered),
        scratch_shapes=[
            pltpu.VMEM((D, D), bf16),
            pltpu.VMEM((WIDE_BUFFERS, MAIN, LANES), bf16),
            pltpu.VMEM((2 * MAIN, D), bf16),
            pltpu.VMEM((MAIN, D), bf16),
            pltpu.VMEM((rows, INNER), bf16),
            pltpu.VMEM((rows, INNER), bf16),
            pltpu.VMEM((rows, D), bf16),
            pltpu.VMEM((rows, D), bf16),
            pltpu.VMEM((rows, LANES), f32),
            pltpu.VMEM((rows, LANES), f32),
            pltpu.VMEM((rows, 128), f32),
            pltpu.SemaphoreType.DMA((WIDE_BUFFERS,)),
            pltpu.SemaphoreType.DMA((2 * FAST_DEV,)),
            pltpu.SemaphoreType.DMA((sends,)),
            pltpu.SemaphoreType.DMA((sends,)),
            pltpu.SemaphoreType.DMA((3,)),
        ],
        compiler_params=pltpu.CompilerParams(
            collective_id=1, has_side_effects=True, vmem_limit_bytes=60 * 1024 * 1024
        ),
        name="mixer_forward",
    )(*operands)


def branch_backward_kernel(
    part_grad_ref, out_grad_ref, gains_ref, table_d_ref, table_i_ref, out_ref, out_rest_ref, join_ref, join_rest_ref,
    attn_ref, mamba_ref, middle_ref, gu_grad_ref,
    middle_grad_ref, gains_grad_ref, join_low_ref, mamba_low_ref, attn_low_ref, gated_grad_ref, gu_came_ref,
    order, row_buffer, sem, send_sems, recv_sems,
):
    bf16 = jnp.bfloat16
    links = Links(send_sems, recv_sems)
    links.greet()
    height = gu_came_ref.shape[0]
    far_rows = pl.ds(pl.multiple_of(links.z_at[3] * height, 16), height)
    hop = links.send(gu_grad_ref.at[far_rows], gu_came_ref, links.z_next)
    half_rows = MAIN // 2
    row_blocks = [(join_ref, k) for k in range(2)] + [(out_ref, k) for k in range(4)]

    def row_copy(i):
        source, k = row_blocks[i]
        return pltpu.make_async_copy(source.at[pl.ds(k * half_rows, half_rows)], row_buffer.at[i], sem.at[i])

    def row_products(low, first):
        products = []
        for i in (first, first + 1):
            row_copy(i).wait()
            products.append(back_product(low, row_buffer[i]))
        return products

    for i in range(len(row_blocks)):
        row_copy(i).start()
    write_order(table_d_ref, order)
    unit, scale = rms_parts(middle_ref[...])
    back, gain_grad = rms_pull(unit, scale, gains_ref[3:4], part_grad_ref[...])
    gains_grad_ref[0:1] = jnp.zeros_like(gain_grad)
    gains_grad_ref[3:4] = gain_grad
    middle_grad = out_grad_ref[...] + back
    middle_grad_ref[...] = middle_grad
    join_low = middle_grad.astype(bf16)
    join_low_ref[...] = join_low
    joined_grad = 0.5 * move_back(
        order, jnp.concatenate(row_products(join_low, 0) + [back_product(join_low, join_rest_ref[...])], axis=1)
    )
    unit, scale = rms_parts(attn_ref[...])
    back, gain_grad = rms_pull(unit, scale, gains_ref[1:2], joined_grad)
    gains_grad_ref[1:2] = gain_grad
    attn_low_ref[...] = back.astype(bf16)
    unit, scale = rms_parts(mamba_ref[...])
    back, gain_grad = rms_pull(unit, scale, gains_ref[2:3], joined_grad)
    gains_grad_ref[2:3] = gain_grad
    mamba_low = back.astype(bf16)
    mamba_low_ref[...] = mamba_low
    write_order(table_i_ref, order)
    half = INNER // 2
    for h in range(2):
        gated_grad_ref[:, h * half : (h + 1) * half] = move_back(
            order,
            jnp.concatenate(row_products(mamba_low, 2 + 2 * h) + [back_product(mamba_low, out_rest_ref[h])], axis=1),
        )
    hop.wait_recv()
    links.finish()


def branch_backward(*operands):
    rows = operands[0].shape[0]
    bf16, f32 = jnp.bfloat16, jnp.float32
    vmem, anywhere = pl.BlockSpec(memory_space=pltpu.VMEM), pl.BlockSpec(memory_space=pl.ANY)
    in_specs = [vmem] * len(operands)
    for k in (5, 7, 12):
        in_specs[k] = anywhere
    shapes = (
        ((rows, D), f32), ((4, D), f32), ((rows, D), bf16), ((rows, D), bf16), ((rows, D), bf16), ((rows, INNER), f32),
        ((PLANE_DEV * D // FAST_DEV, GU), bf16),
    )
    return pl.pallas_call(
        branch_backward_kernel,
        out_shape=[jax.ShapeDtypeStruct(shape, kind) for shape, kind in shapes],
        in_specs=in_specs,
        out_specs=[vmem] * (len(shapes) - 1) + [anywhere],
        scratch_shapes=[
            pltpu.VMEM((D, D), bf16),
            pltpu.VMEM((6, MAIN // 2, D), bf16),
            pltpu.SemaphoreType.DMA((6,)),
            pltpu.SemaphoreType.DMA((1,)),
            pltpu.SemaphoreType.DMA((1,)),
        ],
        compiler_params=pltpu.CompilerParams(
            collective_id=5, has_side_effects=True, vmem_limit_bytes=56 * 1024 * 1024
        ),
        name="branch_backward",
    )(*operands)


BACK_STAGED = 9


def mixer_backward_kernel(plan, *refs):
    bf16, f32 = jnp.bfloat16, jnp.float32
    take = Taker(refs)
    ins = take(len(plan.operands))
    gu_grad_ref, down_grad_ref, gu_first_ref, seg_col_ref, seg_row_ref, hold_ref, same_ref = take(7)
    taps_ref, conv_shift_ref, select_ref, step_ref, step_shift_ref, decay_ref, skip_ref = take(7)
    mixed_ref, qkv_ref, conv_ref, step_low_ref, pre_ref, b_ref, c_ref, y_ref, attn_low_ref, gated_grad_ref = take(10)
    totals = take(len(plan.out_shape))
    wide_low_ref, select_grad_ref, step_grad_ref, taps_grad_ref, conv_shift_grad_ref = take(5)
    step_shift_grad_ref, decay_grad_ref, skip_grad_ref, gu_came_ref, down_came_ref = take(5)
    scratch = take(len(plan.scratch))
    conv_grad, low_grad, step_size, decay_step, step_input, y_grad, input_part, step_part = take(8)
    states, b_grad, c_grad, select_rows, select_low = take(5)
    gu_own, gu_next, down_own, down_next, unit_sem, send_sems, recv_sems = take(7)
    staged, stage_sem = take(BACK_STAGED), take(1)[0]
    rows_all = conv_ref.shape[0]
    links = Links(send_sems, recv_sems)
    links.greet()
    summing = Summing(plan, links, ins, totals, scratch, early=len(plan.blocks) + 1)
    summing.exchange()
    rows_in = (mixed_ref, conv_ref, pre_ref, b_ref, c_ref, y_ref, gated_grad_ref, select_ref, qkv_ref)
    stages = [pltpu.make_async_copy(rows_in[k], staged[k], stage_sem.at[k]) for k in range(BACK_STAGED)]
    for copy in stages:
        copy.start()
    mixed_ref, conv_ref, pre_ref, b_ref, c_ref, y_ref, gated_grad_ref, select_ref, qkv_ref = staged
    gu_height, down_height = gu_own.shape[0], down_own.shape[0]

    def piece(ref, height, k):
        return ref.at[pl.ds(pl.multiple_of(links.z_at[k] * height, 16), height)]

    down_hop = links.send(piece(down_grad_ref, down_height, 3), down_next, links.z_next)
    loads = [
        pltpu.make_async_copy(piece(gu_grad_ref, gu_height, 2), gu_own, unit_sem.at[0]),
        pltpu.make_async_copy(piece(down_grad_ref, down_height, 2), down_own, unit_sem.at[1]),
        pltpu.make_async_copy(gu_first_ref, gu_next, unit_sem.at[2]),
    ]
    for copy in loads:
        copy.start()
    for copy in loads:
        copy.wait()
    add_rows(gu_own, gu_next)
    gu_hop = links.send(gu_own, gu_came_ref, links.z_next)
    b_grad[...] = jnp.zeros_like(b_grad)
    c_grad[...] = jnp.zeros_like(c_grad)
    states[0] = jnp.zeros((STATE, LANES), f32)
    zeros = jnp.zeros((STATE, LANES), f32)
    summing.exchanged()
    summing.advance(1.2)
    for copy in stages:
        copy.wait()

    def scan_chunk(k):
        lanes = lanes_at(k)
        gate_lanes = pl.ds(pl.multiple_of(k * LANES + INNER, 128), LANES)
        conv, shift, skip = conv_ref[:, lanes], step_shift_ref[:, lanes], skip_ref[:, lanes]
        step_size[...], decay_step[...], step_input[...] = scan_setup(pre_ref[:, lanes], shift, conv, hold_ref[...])
        gate, grad = mixed_ref[:, gate_lanes], gated_grad_ref[:, lanes]
        open_gate = 1.0 / (1.0 + jnp.exp(-gate))
        wide_low_ref[:, gate_lanes] = (
            grad * (y_ref[:, lanes] + skip * conv) * open_gate * (1.0 + gate * (1.0 - open_gate))
        ).astype(bf16)
        y_grad[...] = grad * gate * open_gate
        skip_grad_ref[:, lanes] = jnp.sum(y_grad[...] * conv, axis=0, keepdims=True)
        decay_rows = decay_ref[:, lanes]
        rates = decay_rows * (-LOG2E)

        def keep(t, state):
            states[t + 1] = state

        scan_rows(lanes, b_ref, c_ref, None, rates, decay_step, step_input, keep)

        def backward(i, carry):
            state_grad, decay_grad = carry
            base = pl.multiple_of(rows_all - 8 - i * 8, 8)
            inputs = step_input[pl.ds(base, 8), :]
            sizes = step_size[pl.ds(base, 8), :]
            held = decay_step[pl.ds(base, 8), :]
            y_rows = y_grad[pl.ds(base, 8), :]
            input_rows, step_rows = [None] * 8, [None] * 8
            for r in range(7, -1, -1):
                t = base + r
                y_row = y_rows[r : r + 1]
                full = state_grad + tiled(c_ref[t]) * y_row
                c_grad[t] += folded(states[t + 1] * y_row)
                b_grad[t] += folded(full * inputs[r : r + 1])
                input_rows[r] = jnp.sum(tiled(b_ref[t]) * full, axis=0, keepdims=True)
                state_grad = jnp.exp2(held[r : r + 1] * rates) * full
                through = state_grad * states[t]
                step_rows[r] = jnp.sum(decay_rows * through, axis=0, keepdims=True)
                decay_grad = decay_grad - sizes[r : r + 1] * through
            input_part[pl.ds(base, 8), :] = jnp.concatenate(input_rows, axis=0)
            step_part[pl.ds(base, 8), :] = jnp.concatenate(step_rows, axis=0)
            return state_grad, decay_grad

        _, decay_grad = lax.fori_loop(0, rows_all // 8, backward, (zeros, zeros))
        decay_grad_ref[:, lanes] = decay_grad
        conv_grad[:, lanes] = input_part[...] * step_size[...] + skip * y_grad[...]
        pre_grad = (input_part[...] * conv - step_part[...]) / (1.0 + jnp.exp(-(pre_ref[:, lanes] + shift)))
        step_shift_grad_ref[:, lanes] = jnp.sum(pre_grad, axis=0, keepdims=True)
        low_grad[:, lanes] = pre_grad.astype(bf16)

    for first, last, until in ((0, 2, 2.2), (2, 3, 3.2), (3, 4, 4.3)):
        pl.loop(first, last)(scan_chunk)
        summing.advance(until)
    down_hop.wait_recv()
    add_rows(down_own, down_next)
    down_hop = links.send(down_own, down_came_ref, links.z_next)
    pl.loop(4, CHUNKS)(scan_chunk)
    summing.advance(5.3)

    gather_lanes(b_grad, c_grad, select_rows)
    select_low[:, :LOW_PAD] = back_product(low_grad[...], step_ref[...]).astype(bf16)
    select_low[:, LOW_PAD:] = select_rows[...].astype(bf16)
    summing.advance(6.3)

    @pl.loop(0, CHUNKS)
    def _(k):
        lanes = lanes_at(k)
        step_grad_ref[:, lanes] = outer_sum(step_low_ref[...], low_grad[:, lanes]).astype(bf16)
        conv = conv_ref[:, lanes]
        some = pl.ds(pl.multiple_of(k * LANES, 128), LANES)
        select_grad_ref[some, :] = outer_sum(conv.astype(bf16), select_low[...]).astype(bf16)
        grad = conv_grad[:, lanes] + back_product(select_low[...], select_ref[some, :])
        inner, taps = mixed_ref[:, lanes], taps_ref[:, lanes]
        total, earlier = conv_sum(inner, taps, conv_shift_ref[:, lanes], same_ref)
        opened = 1.0 / (1.0 + jnp.exp(-total))
        grad = grad * opened * (1.0 + total * (1.0 - opened))
        conv_shift_grad_ref[:, lanes] = jnp.sum(grad, axis=0, keepdims=True)
        tap_rows = [jnp.sum(grad * earlier[j - 1], axis=0, keepdims=True) for j in range(CONV - 1, 0, -1)]
        tap_rows.append(jnp.sum(grad * inner, axis=0, keepdims=True))
        taps_grad_ref[:, lanes] = jnp.concatenate(tap_rows, axis=0)
        inner_grad = taps[CONV - 1 : CONV] * grad
        for j in range(1, CONV):
            moved = taps[CONV - 1 - j : CONV - j] * grad * same_ref[:, j - 1 : j]
            inner_grad = inner_grad + pltpu.roll(moved, rows_all - j, axis=0)
        wide_low_ref[:, lanes] = inner_grad.astype(bf16)

    summing.advance(7.3)
    attention_backward_kernel(qkv_ref, seg_col_ref, seg_row_ref, attn_low_ref, wide_low_ref, 2 * INNER)
    wide_low_ref[:, 2 * INNER + QKV :] = jnp.zeros((rows_all, WIDE - 2 * INNER - QKV), bf16)
    summing.finish()
    gu_hop.wait_recv()
    down_hop.wait_recv()
    links.finish()


def mixer_backward(plan, *operands):
    rows = operands[-1].shape[0]
    rows_in = [operands[k] for k in (14, 16, 18, 19, 20, 21, 23, 9, 15)]
    bf16, f32 = jnp.bfloat16, jnp.float32
    vmem, anywhere = pl.BlockSpec(memory_space=pltpu.VMEM), pl.BlockSpec(memory_space=pl.ANY)
    in_specs = [anywhere] * (len(plan.operands) + 3) + [vmem] * (len(operands) - 3)
    for k in (14, 16, 18, 19, 20, 21, 23, 9, 15):
        in_specs[len(plan.operands) + k] = anywhere
    shapes = (
        ((rows, WIDE), bf16), ((INNER, 2 * LOW_PAD), bf16), ((LOW_PAD, INNER), bf16), ((CONV, INNER), f32),
        ((1, INNER), f32), ((1, INNER), f32), ((STATE, INNER), f32), ((1, INNER), f32),
        ((PLANE_DEV * D // FAST_DEV, GU), bf16), ((PAD_FF, D), bf16),
    )
    lane_rows = pltpu.VMEM((rows, LANES), f32)
    sem = pltpu.SemaphoreType.DMA
    return pl.pallas_call(
        functools.partial(mixer_backward_kernel, plan),
        out_shape=plan.out_shape + [jax.ShapeDtypeStruct(shape, kind) for shape, kind in shapes],
        in_specs=in_specs,
        out_specs=[vmem] * (len(plan.out_shape) + len(shapes) - 2) + [anywhere] * 2,
        scratch_shapes=plan.scratch
        + [pltpu.VMEM((rows, INNER), f32), pltpu.VMEM((rows, INNER), bf16)]
        + [lane_rows] * 6
        + [
            pltpu.VMEM((rows + 1, STATE, LANES), f32),
            pltpu.VMEM((rows, STATE, 128), f32),
            pltpu.VMEM((rows, STATE, 128), f32),
            pltpu.VMEM((rows, 128), f32),
            pltpu.VMEM((rows, 2 * LOW_PAD), bf16),
            pltpu.VMEM(shapes[-2][0], bf16),
            pltpu.VMEM(shapes[-2][0], bf16),
            pltpu.VMEM(shapes[-1][0], bf16),
            pltpu.VMEM(shapes[-1][0], bf16),
            sem((3,)),
            sem((3,)),
            sem((3,)),
        ]
        + [pltpu.VMEM(x.shape, x.dtype) for x in rows_in]
        + [sem((BACK_STAGED,))],
        compiler_params=pltpu.CompilerParams(
            collective_id=2, has_side_effects=True, vmem_limit_bytes=62 * 1024 * 1024
        ),
        name="mixer_backward",
    )(*plan.operands, *operands)


def spread_table(shard_rows, main_rows, shards):
    half = shards // CORES
    order = [k * CORES + c for c in range(CORES) for k in range(half)]
    main = [d * shard_rows + r for d in order for r in range(main_rows)]
    rest = [d * shard_rows + r for d in order for r in range(main_rows, shard_rows)]
    return np.asarray(main + rest, np.int32)


def tie(*values):
    return lax.optimization_barrier(values)


def as_rows(flats, rows):
    flat = jnp.concatenate(flats)
    return jnp.pad(flat, (0, rows * 128 - flat.size)).reshape(rows, 128)


def split_flat(block, sizes):
    pieces, at = [], 0
    for size in sizes:
        pieces.append(block[..., at : at + size])
        at += size
    return pieces


def on_fast_device(
    tokens, cotangent, seq_lengths, qkv_proj, mamba_in, select_proj, step_proj, mamba_out, join_out,
    conv_taps, conv_bias, step_bias, decay_rates, skip_gain, norm_gains, ffn_gate, ffn_up, ffn_down,
):
    bf16, f32 = jnp.bfloat16, jnp.float32
    n = FAST_DEV
    row_count = tokens.shape[0]
    d_rows, i_rows = D // n, INNER // n
    d_rest, i_rest = d_rows - MAIN_D, i_rows - MAIN_I

    own_ff = PLANES * PAD_FF

    def ff_columns(flat):
        block = flat.reshape(d_rows, PLANES, PLANE_DEV, SLICE_FF).transpose(2, 0, 1, 3)
        block = jnp.pad(block, ((0, 0), (0, 0), (0, 0), (0, PAD_FF - SLICE_FF)))
        return jnp.pad(block.reshape(PLANE_DEV, d_rows, own_ff), ((0, 0), (0, 0), (0, HALF_GU - own_ff)))

    planes = [[z * PLANE_DEV + p for p in range(PLANE_DEV)] for z in range(PLANES)]
    gu = jnp.concatenate([ff_columns(ffn_gate), ff_columns(ffn_up)], axis=2)
    gu = lax.all_to_all(gu, "fsdp", 0, 0, axis_index_groups=planes, tiled=True).reshape(PLANE_DEV * d_rows, GU)
    down = jnp.pad(ffn_down.reshape(SLICE_FF, D), ((0, PAD_FF - SLICE_FF), (0, 0)))

    wide = jnp.concatenate([mamba_in.reshape(d_rows, 2 * INNER), qkv_proj.reshape(d_rows, QKV)], axis=1)
    wide = jnp.pad(wide, ((0, 0), (0, WIDE - wide.shape[1])))
    out_block = mamba_out.reshape(i_rows, D)
    join_block = join_out.reshape(d_rows, D)
    rest_sizes = [d_rest * WIDE, d_rest * D, i_rest * D]
    rest = as_rows(
        [wide[MAIN_D:].reshape(-1), join_block[MAIN_D:].reshape(-1), out_block[MAIN_I:].reshape(-1)], REST_ROWS
    )
    smalls = [select_proj, step_proj, conv_taps, conv_bias, step_bias, decay_rates, skip_gain, norm_gains]
    small_sizes = [s.size for s in smalls]
    smalls = as_rows(smalls, SMALL_ROWS)
    segments = segment_ids(seq_lengths, row_count)
    live_rows = (segments < seq_lengths.shape[0]).astype(f32)[:, None]
    out_grad = cotangent.astype(f32) * live_rows
    gu, down, wide_block, rest, smalls, out_grad = tie(gu, down, wide[:MAIN_D], rest, smalls, out_grad)
    wide_all, rest_all, smalls_all, gu_1, down_1, down_2 = gather_first(
        ("wide", "rest", "smalls"), (wide_block, rest, smalls), (gu, down)
    )
    wide_all = wide_all.reshape(MAIN, WIDE)
    pieces = split_flat(rest_all.reshape(n, REST_ROWS * 128), rest_sizes)
    wide_rest = pieces[0].reshape(n * d_rest, WIDE)
    join_rest = pieces[1].reshape(n * d_rest, D)
    out_rest = pieces[2].reshape(CORES, 2, -1, D).transpose(1, 0, 2, 3).reshape(2, -1, D)
    pieces = split_flat(smalls_all.reshape(n, SMALL_ROWS * 128), small_sizes)
    select = pieces[0].reshape(INNER, XPROJ)
    select = jnp.concatenate(
        [
            jnp.pad(select[:, :RANK], ((0, 0), (0, LOW_PAD - RANK))),
            jnp.pad(select[:, RANK:], ((0, 0), (0, LOW_PAD - 2 * STATE))),
        ],
        axis=1,
    )
    step_matrix = jnp.pad(pieces[1].reshape(RANK, INNER), ((0, LOW_PAD - RANK), (0, 0)))
    taps = pieces[2].reshape(CONV, INNER).astype(f32)
    conv_shift = pieces[3].reshape(1, INNER).astype(f32)
    step_shift = pieces[4].reshape(1, INNER).astype(f32)
    decay = pieces[5].reshape(STATE, INNER).astype(f32)
    skip = pieces[6].reshape(1, INNER).astype(f32)
    gains = pieces[7].reshape(4, D).astype(f32)

    table_d = jnp.asarray(spread_table(d_rows, MAIN_D, n))[None]
    table_i = jnp.asarray(spread_table(i_rows, MAIN_I, n // 2))[None]
    hold = ((1.0 - keep_flags(segments)) * BIG)[:, None]
    same = jnp.stack(
        [
            (jnp.concatenate([jnp.full((k,), -1, jnp.int32), segments[:-k]]) == segments).astype(f32)
            for k in range(1, CONV)
        ],
        axis=1,
    )
    places = (segments[:, None], segments[None, :], hold, same, table_d, table_i)
    matrices = (
        wide_all, wide_rest, taps, conv_shift, select, step_matrix, step_shift, decay, skip,
    )
    (
        normed_columns, mixed, qkv_rows, conv_act, step_low, step_pre, b_wide, c_wide, scanned, gated_columns, attn_rows,
        mamba_rows, joined_columns, middle, normed_two, out_all, join_all, out_low, gu_2, gu_3, down_3,
    ) = mixer_forward(
        tokens, gains, *places, *matrices, out_block[:MAIN_I], out_rest, join_block[:MAIN_D], join_rest,
        out_grad.astype(bf16), gu_1, down_2,
    )
    out_all, join_all = out_all.reshape(2 * MAIN, D), join_all.reshape(MAIN, D)

    part_grad, ffn_rows, gu_grad, down_grad = feed_forward(
        normed_two, out_low.reshape(-1, D), gu, gu_1, gu_2, gu_3, down, down_1, down_2, down_3
    )
    block_out = ((middle + ffn_rows) * live_rows).astype(bf16)

    middle_grad, gains_grad, join_low, mamba_low, attn_low, gated_grad, gu_first = branch_backward(
        part_grad, out_grad, gains, table_d, table_i, out_all, out_rest, join_all, join_rest,
        attn_rows, mamba_rows, middle, gu_grad,
    )
    branch_plan = SumPlan(
        BRANCH_BLOCKS, (MAIN_I, MAIN_D), (i_rest, d_rest), D, ((D,), (D,)),
        (gated_columns, joined_columns), (mamba_low, join_low),
    )
    (
        out_sum, join_sum, _, wide_low, select_grad, step_grad, taps_grad, conv_shift_grad,
        step_shift_grad, decay_grad, skip_grad, gu_came, down_came,
    ) = mixer_backward(
        branch_plan, gu_grad, down_grad, gu_first, *places[:4], taps, conv_shift, select, step_matrix, step_shift, decay,
        skip, mixed, qkv_rows, conv_act, step_low, step_pre, b_wide, c_wide, scanned, attn_low, gated_grad,
    )
    select_grad = jnp.concatenate([select_grad[:, :RANK], select_grad[:, LOW_PAD : LOW_PAD + 2 * STATE]], axis=1)
    small_grads = [
        select_grad, step_grad[:RANK], taps_grad, conv_shift_grad, step_shift_grad, decay_grad, skip_grad, gains_grad,
    ]
    small_grads = jnp.concatenate([g.astype(bf16).reshape(n, -1) for g in small_grads], axis=1)
    small_grads = jnp.pad(small_grads, ((0, 0), (0, SMALL_ROWS * 128 - small_grads.shape[1])))
    small_grads = small_grads.reshape(GROUPS, CORES, SMALL_ROWS, 128).transpose(1, 0, 2, 3)
    wide_plan = SumPlan(
        WIDE_BLOCKS, (MAIN_D,), (d_rest,), REST_COLUMNS, ((2 * INNER, QKV),),
        (normed_columns,), (wide_low,), small_grads.reshape(CORES, GROUPS * SMALL_ROWS, 128),
    )
    mamba_sum, qkv_sum, wide_left, small_sum, input_grad, gate_grad, up_grad, down_sum = last_sums(
        wide_plan, middle_grad, tokens, gains, table_d, wide_all, wide_rest, gu_grad, down_grad, gu_came, down_came
    )
    gate_grad, up_grad = [block.astype(f32).reshape(-1) for block in (gate_grad, up_grad)]
    first_gain = wide_left[14, WIDE % REST_COLUMNS : WIDE % REST_COLUMNS + norm_gains.size]
    smalls = split_flat(small_sum.reshape(-1), small_sizes)
    return (
        block_out,
        input_grad,
        qkv_sum.reshape(-1),
        mamba_sum.reshape(-1),
        smalls[0],
        smalls[1],
        out_sum.reshape(-1),
        join_sum.reshape(-1),
        *smalls[2:-1],
        smalls[-1] + first_gain,
        gate_grad,
        up_grad,
        down_sum[:SLICE_FF].reshape(-1),
    )


def fits_fast_plan(mesh):
    return mesh.shape["fsdp"] == FAST_DEV


def solution(mesh):
    rows, flat = P("fsdp", None), P("fsdp")
    return jax.shard_map(
        on_fast_device if fits_fast_plan(mesh) else on_device,
        mesh=mesh,
        in_specs=(rows, rows) + (flat,) * 16,
        out_specs=(rows, rows) + (flat,) * 15,
        check_vma=False,
    )
```

```python
import functools

import jax
import jax.numpy as jnp
import numpy as np
from jax import lax
from jax.experimental import pallas as pl
from jax.experimental.pallas import tpu as pltpu
from jax.sharding import PartitionSpec as P

D = 1600
HEADS = 25
KV_HEADS = 5
HEAD = 64
INNER = 3200
STATE = 16
CONV = 4
RANK = 100
FF = 5504
QKV = 2240
XPROJ = 132


epsilon = 1e-06


def flat_product(left, right):
    return jnp.dot(left, right, preferred_element_type=jnp.float32)


def outer_sum(left, right):
    return lax.dot_general(
        left, right, (((0,), (0,)), ((), ())), preferred_element_type=jnp.float32
    )


def back_product(grad_rows, matrix):
    return lax.dot_general(
        grad_rows, matrix, (((1,), (1,)), ((), ())), preferred_element_type=jnp.float32
    )


def rms_scale(values, scale_row):
    return (
        values * lax.rsqrt(jnp.mean(values * values, axis=-1, keepdims=True) + epsilon) * scale_row
    )


def segment_ids(lengths, row_count):
    seq_ends = jnp.cumsum(lengths)
    places = jnp.arange(row_count, dtype=jnp.int32)
    return jnp.sum((places[:, None] >= seq_ends[None, :]).astype(jnp.int32), axis=1)


def keep_flags(segments):
    same_seq = (segments[1:] == segments[:-1]).astype(jnp.float32)
    return jnp.concatenate([jnp.zeros((1,), jnp.float32), same_seq])


def conv_silu(inner_rows, tap_matrix, conv_shift, segments):
    tap_count = tap_matrix.shape[0]
    summed = conv_shift[None, :] + tap_matrix[tap_count - 1][None, :] * inner_rows
    for offset in range(1, tap_count):
        shifted = jnp.concatenate(
            [jnp.zeros((offset, inner_rows.shape[1]), jnp.float32), inner_rows[:-offset]], axis=0
        )
        earlier = jnp.concatenate([jnp.full((offset,), -1, jnp.int32), segments[:-offset]])
        same_seq = (earlier == segments).astype(jnp.float32)
        summed = summed + tap_matrix[tap_count - 1 - offset][None, :] * shifted * same_seq[:, None]
    return jax.nn.silu(summed)


def scan_block(state_now, decay_matrix, block_data):
    step_sizes, step_inputs, step_b, step_c, step_keep = block_data
    outputs = []
    for step_index in range(step_sizes.shape[0]):
        decay_now = jnp.exp(-step_sizes[step_index][None, :] * decay_matrix)
        state_now = (
            step_keep[step_index] * decay_now * state_now
            + step_b[step_index][:, None]
            * (step_sizes[step_index] * step_inputs[step_index])[None, :]
        )
        outputs.append(jnp.sum(step_c[step_index][:, None] * state_now, axis=0))
    return (state_now, jnp.stack(outputs))


def selective_scan(step_sizes, step_inputs, b_rows, c_rows, keep_rows, decay_matrix):
    block_len = 16

    def advance(state_now, block_data):
        return jax.checkpoint(scan_block)(state_now, decay_matrix, block_data)

    blocks = tuple(
        (
            piece_array.reshape((-1, block_len) + piece_array.shape[1:])
            for piece_array in (step_sizes, step_inputs, b_rows, c_rows, keep_rows)
        )
    )
    start_state = jnp.zeros((b_rows.shape[1], step_inputs.shape[1]), jnp.float32)
    final_state, outputs = lax.scan(advance, start_state, blocks)
    return outputs.reshape(step_inputs.shape)


def mamba_core(
    conv_act, select_rows, step_pre, gate_in, step_shift, decay_matrix, skip_row, keep_rows
):
    step_sizes = jax.nn.softplus(step_pre + step_shift)
    scanned = selective_scan(
        step_sizes,
        conv_act,
        select_rows[:, :STATE],
        select_rows[:, STATE:],
        keep_rows,
        decay_matrix,
    )
    return (scanned + skip_row * conv_act) * jax.nn.silu(gate_in)


def join_branches(attn_rows, mamba_rows, attn_gain, mamba_gain):
    return 0.5 * (rms_scale(attn_rows, attn_gain) + rms_scale(mamba_rows, mamba_gain))


def swiglu(gate_rows, up_rows):
    return jax.nn.silu(gate_rows) * up_rows


def block_scores(query_block, start, key_rows, segments):
    block_rows = query_block.shape[0]
    places = jnp.arange(segments.shape[0], dtype=jnp.int32)
    query_places = start + jnp.arange(block_rows, dtype=jnp.int32)
    allowed = (segments[:, None] == segments[None, :]) & (places[None, :] <= query_places[:, None])
    scores = jnp.einsum(
        "tgrd,ugd->grtu", query_block, key_rows, preferred_element_type=jnp.float32
    ) * HEAD ** (-0.5)
    return jnp.where(allowed[None, None], scores, -1e30)


def attention_forward(queries, key_rows, value_rows, segments):
    row_count = queries.shape[0]
    block_rows = min(row_count, 512)
    query_blocks = queries.reshape((row_count // block_rows, block_rows) + queries.shape[1:])
    starts = jnp.arange(row_count // block_rows, dtype=jnp.int32) * block_rows

    def one_block(block_item):
        scores = block_scores(block_item[0], block_item[1], key_rows, segments)
        top_score = jnp.max(scores, axis=-1, keepdims=True)
        raised = jnp.exp(scores - top_score)
        exp_sum = jnp.sum(raised, axis=-1, keepdims=True)
        weights = (raised / exp_sum).astype(jnp.bfloat16)
        outputs = jnp.einsum(
            "grtu,ugd->tgrd", weights, value_rows, preferred_element_type=jnp.float32
        )
        return (outputs, top_score, exp_sum)

    outputs, top_scores, exp_sums = lax.map(one_block, (query_blocks, starts))
    return (outputs.reshape(row_count, -1), top_scores, exp_sums, query_blocks, starts)


def attention_backward(
    query_blocks, starts, key_rows, value_rows, segments, top_scores, exp_sums, out_grad
):
    row_count = key_rows.shape[0]
    grad_blocks = out_grad.reshape(query_blocks.shape)

    def one_block(carry_sums, block_item):
        key_acc, value_acc = carry_sums
        query_block, start, top_score, exp_sum, grad_block = block_item
        scores = block_scores(query_block, start, key_rows, segments)
        weights = jnp.exp(scores - top_score) / exp_sum
        weight_grad = jnp.einsum(
            "tgrd,ugd->grtu", grad_block, value_rows, preferred_element_type=jnp.float32
        )
        score_grad = (
            weights * (weight_grad - jnp.sum(weights * weight_grad, axis=-1, keepdims=True))
        ).astype(jnp.bfloat16)
        query_grad = jnp.einsum(
            "grtu,ugd->tgrd", score_grad, key_rows, preferred_element_type=jnp.float32
        ) * HEAD ** (-0.5)
        key_acc = key_acc + jnp.einsum(
            "grtu,tgrd->ugd", score_grad, query_block, preferred_element_type=jnp.float32
        ) * HEAD ** (-0.5)
        value_acc = value_acc + jnp.einsum(
            "grtu,tgrd->ugd",
            weights.astype(jnp.bfloat16),
            grad_block,
            preferred_element_type=jnp.float32,
        )
        return ((key_acc, value_acc), query_grad)

    zero_rows = jnp.zeros(key_rows.shape, jnp.float32)
    (key_grad, value_grad), query_grads = lax.scan(
        one_block, (zero_rows, zero_rows), (query_blocks, starts, top_scores, exp_sums, grad_blocks)
    )
    return (
        query_grads.reshape(row_count, -1),
        key_grad.reshape(row_count, -1),
        value_grad.reshape(row_count, -1),
    )


def shape_mixer(flat_list):
    return (
        flat_list[0].reshape(D, QKV),
        flat_list[1].reshape(D, 2 * INNER),
        flat_list[2].reshape(INNER, XPROJ),
        flat_list[3].reshape(RANK, INNER),
        flat_list[4].reshape(INNER, D),
        flat_list[5].reshape(D, D),
    )


def small_mixer(flat_list):
    return (
        flat_list[6].astype(jnp.float32).reshape(CONV, INNER),
        flat_list[7].astype(jnp.float32),
        flat_list[8].astype(jnp.float32),
        flat_list[9].astype(jnp.float32).reshape(STATE, INNER),
        flat_list[10].astype(jnp.float32),
        flat_list[11].astype(jnp.float32).reshape(4, D),
    )


def shape_ffn(flat_list):
    return (flat_list[0].reshape(D, FF), flat_list[1].reshape(D, FF), flat_list[2].reshape(FF, D))


def on_device(
    tokens,
    cotangent,
    seq_lengths,
    qkv_proj,
    mamba_in,
    select_proj,
    step_proj,
    mamba_out,
    join_out,
    conv_taps,
    conv_bias,
    step_bias,
    decay_rates,
    skip_gain,
    norm_gains,
    ffn_gate,
    ffn_up,
    ffn_down,
):
    mixer_flat = (
        lax.all_gather(qkv_proj, "fsdp", axis=0, tiled=True),
        lax.all_gather(mamba_in, "fsdp", axis=0, tiled=True),
        lax.all_gather(select_proj, "fsdp", axis=0, tiled=True),
        lax.all_gather(step_proj, "fsdp", axis=0, tiled=True),
        lax.all_gather(mamba_out, "fsdp", axis=0, tiled=True),
        lax.all_gather(join_out, "fsdp", axis=0, tiled=True),
        lax.all_gather(conv_taps, "fsdp", axis=0, tiled=True),
        lax.all_gather(conv_bias, "fsdp", axis=0, tiled=True),
        lax.all_gather(step_bias, "fsdp", axis=0, tiled=True),
        lax.all_gather(decay_rates, "fsdp", axis=0, tiled=True),
        lax.all_gather(skip_gain, "fsdp", axis=0, tiled=True),
        lax.all_gather(norm_gains, "fsdp", axis=0, tiled=True),
    )
    ffn_flat = (
        lax.all_gather(ffn_gate, "fsdp", axis=0, tiled=True),
        lax.all_gather(ffn_up, "fsdp", axis=0, tiled=True),
        lax.all_gather(ffn_down, "fsdp", axis=0, tiled=True),
    )
    qkv_matrix, mamba_in_matrix, select_matrix, step_matrix, mamba_out_matrix, join_matrix = (
        shape_mixer(mixer_flat)
    )
    tap_matrix, conv_shift, step_shift, decay_matrix, skip_row, gain_rows = small_mixer(mixer_flat)
    gate_matrix, up_matrix, down_matrix = shape_ffn(ffn_flat)
    row_count = tokens.shape[0]
    segments = segment_ids(seq_lengths, row_count)
    live_rows = (segments < seq_lengths.shape[0]).astype(jnp.float32)
    keep_rows = keep_flags(segments)
    inputs = tokens.astype(jnp.float32)
    normed_full, norm_pull = jax.vjp(rms_scale, inputs, gain_rows[0])
    normed = normed_full.astype(jnp.bfloat16)
    qkv_rows = flat_product(normed, qkv_matrix).astype(jnp.bfloat16)
    queries = qkv_rows[:, :D].reshape(row_count, KV_HEADS, HEADS // KV_HEADS, HEAD)
    key_rows = qkv_rows[:, D : D + KV_HEADS * HEAD].reshape(row_count, KV_HEADS, HEAD)
    value_rows = qkv_rows[:, D + KV_HEADS * HEAD :].reshape(row_count, KV_HEADS, HEAD)
    attn_rows, top_scores, exp_sums, query_blocks, starts = attention_forward(
        queries, key_rows, value_rows, segments
    )
    mixed_in = flat_product(normed, mamba_in_matrix)

    def conv_piece(inner_rows, tap_values, shift_values):
        return conv_silu(inner_rows, tap_values, shift_values, segments)

    conv_act, conv_pull = jax.vjp(conv_piece, mixed_in[:, :INNER], tap_matrix, conv_shift)
    conv_low = conv_act.astype(jnp.bfloat16)
    selected = flat_product(conv_low, select_matrix)
    step_low = selected[:, :RANK].astype(jnp.bfloat16)
    step_pre = flat_product(step_low, step_matrix)

    def core_piece(
        conv_values,
        select_values,
        step_values,
        gate_values,
        shift_values,
        decay_values,
        skip_values,
    ):
        return mamba_core(
            conv_values,
            select_values,
            step_values,
            gate_values,
            shift_values,
            decay_values,
            skip_values,
            keep_rows,
        )

    gated_full, core_pull = jax.vjp(
        core_piece,
        conv_act,
        selected[:, RANK:],
        step_pre,
        mixed_in[:, INNER:],
        step_shift,
        decay_matrix,
        skip_row,
    )
    gated = gated_full.astype(jnp.bfloat16)
    mamba_rows = flat_product(gated, mamba_out_matrix)
    joined_full, join_pull = jax.vjp(
        join_branches, attn_rows, mamba_rows, gain_rows[1], gain_rows[2]
    )
    joined = joined_full.astype(jnp.bfloat16)
    middle = inputs + flat_product(joined, join_matrix)
    normed_two_full, norm_two_pull = jax.vjp(rms_scale, middle, gain_rows[3])
    normed_two = normed_two_full.astype(jnp.bfloat16)
    gate_rows = flat_product(normed_two, gate_matrix)
    up_rows = flat_product(normed_two, up_matrix)
    act_full, act_pull = jax.vjp(swiglu, gate_rows, up_rows)
    activated = act_full.astype(jnp.bfloat16)
    result_rows = middle + flat_product(activated, down_matrix)
    block_out = (result_rows * live_rows[:, None]).astype(jnp.bfloat16)
    ffn_flat = (
        lax.all_gather(ffn_gate, "fsdp", axis=0, tiled=True),
        lax.all_gather(ffn_up, "fsdp", axis=0, tiled=True),
        lax.all_gather(ffn_down, "fsdp", axis=0, tiled=True),
    )
    gate_matrix, up_matrix, down_matrix = shape_ffn(ffn_flat)
    out_grad = cotangent.astype(jnp.float32) * live_rows[:, None]
    down_low = out_grad.astype(jnp.bfloat16)
    down_weight_grad = outer_sum(activated, down_low)
    gate_grad, up_grad = act_pull(back_product(down_low, down_matrix))
    gate_low = gate_grad.astype(jnp.bfloat16)
    up_low = up_grad.astype(jnp.bfloat16)
    gate_weight_grad = outer_sum(normed_two, gate_low)
    up_weight_grad = outer_sum(normed_two, up_low)
    middle_norm_grad, ffn_gain_grad = norm_two_pull(
        back_product(gate_low, gate_matrix) + back_product(up_low, up_matrix)
    )
    middle_grad = out_grad + middle_norm_grad
    ffn_sums = (
        lax.psum_scatter(gate_weight_grad.reshape(-1), "fsdp", scatter_dimension=0, tiled=True),
        lax.psum_scatter(up_weight_grad.reshape(-1), "fsdp", scatter_dimension=0, tiled=True),
        lax.psum_scatter(down_weight_grad.reshape(-1), "fsdp", scatter_dimension=0, tiled=True),
    )
    mixer_flat = (
        lax.all_gather(qkv_proj, "fsdp", axis=0, tiled=True),
        lax.all_gather(mamba_in, "fsdp", axis=0, tiled=True),
        lax.all_gather(select_proj, "fsdp", axis=0, tiled=True),
        lax.all_gather(step_proj, "fsdp", axis=0, tiled=True),
        lax.all_gather(mamba_out, "fsdp", axis=0, tiled=True),
        lax.all_gather(join_out, "fsdp", axis=0, tiled=True),
        lax.all_gather(conv_taps, "fsdp", axis=0, tiled=True),
        lax.all_gather(conv_bias, "fsdp", axis=0, tiled=True),
        lax.all_gather(step_bias, "fsdp", axis=0, tiled=True),
        lax.all_gather(decay_rates, "fsdp", axis=0, tiled=True),
        lax.all_gather(skip_gain, "fsdp", axis=0, tiled=True),
        lax.all_gather(norm_gains, "fsdp", axis=0, tiled=True),
    )
    qkv_matrix, mamba_in_matrix, select_matrix, step_matrix, mamba_out_matrix, join_matrix = (
        shape_mixer(mixer_flat)
    )
    join_low = middle_grad.astype(jnp.bfloat16)
    join_weight_grad = outer_sum(joined, join_low)
    attn_grad, mamba_grad, attn_gain_grad, mamba_gain_grad = join_pull(
        back_product(join_low, join_matrix)
    )
    mamba_low = mamba_grad.astype(jnp.bfloat16)
    mamba_out_weight_grad = outer_sum(gated, mamba_low)
    (
        conv_core_grad,
        select_part_grad,
        step_pre_grad,
        gate_in_grad,
        step_shift_grad,
        decay_grad,
        skip_grad,
    ) = core_pull(back_product(mamba_low, mamba_out_matrix))
    step_low_grad = step_pre_grad.astype(jnp.bfloat16)
    step_weight_grad = outer_sum(step_low, step_low_grad)
    select_low = jnp.concatenate(
        [back_product(step_low_grad, step_matrix), select_part_grad], axis=1
    ).astype(jnp.bfloat16)
    select_weight_grad = outer_sum(conv_low, select_low)
    conv_grad = conv_core_grad + back_product(select_low, select_matrix)
    conv_in_grad, taps_grad, conv_shift_grad = conv_pull(conv_grad)
    mixed_low = jnp.concatenate([conv_in_grad, gate_in_grad], axis=1).astype(jnp.bfloat16)
    mamba_in_weight_grad = outer_sum(normed, mixed_low)
    query_grad, key_grad, value_grad = attention_backward(
        query_blocks,
        starts,
        key_rows,
        value_rows,
        segments,
        top_scores,
        exp_sums,
        attn_grad.astype(jnp.bfloat16),
    )
    qkv_low = jnp.concatenate([query_grad, key_grad, value_grad], axis=1).astype(jnp.bfloat16)
    qkv_weight_grad = outer_sum(normed, qkv_low)
    normed_grad = back_product(qkv_low, qkv_matrix) + back_product(mixed_low, mamba_in_matrix)
    input_norm_grad, input_gain_grad = norm_pull(normed_grad)
    input_grad = middle_grad + input_norm_grad
    gain_grads = jnp.stack(
        [input_gain_grad, attn_gain_grad, mamba_gain_grad, ffn_gain_grad]
    ).reshape(-1)
    mixer_sums = (
        lax.psum_scatter(qkv_weight_grad.reshape(-1), "fsdp", scatter_dimension=0, tiled=True),
        lax.psum_scatter(mamba_in_weight_grad.reshape(-1), "fsdp", scatter_dimension=0, tiled=True),
        lax.psum_scatter(select_weight_grad.reshape(-1), "fsdp", scatter_dimension=0, tiled=True),
        lax.psum_scatter(step_weight_grad.reshape(-1), "fsdp", scatter_dimension=0, tiled=True),
        lax.psum_scatter(
            mamba_out_weight_grad.reshape(-1), "fsdp", scatter_dimension=0, tiled=True
        ),
        lax.psum_scatter(join_weight_grad.reshape(-1), "fsdp", scatter_dimension=0, tiled=True),
        lax.psum_scatter(taps_grad.reshape(-1), "fsdp", scatter_dimension=0, tiled=True),
        lax.psum_scatter(conv_shift_grad, "fsdp", scatter_dimension=0, tiled=True),
        lax.psum_scatter(step_shift_grad, "fsdp", scatter_dimension=0, tiled=True),
        lax.psum_scatter(decay_grad.reshape(-1), "fsdp", scatter_dimension=0, tiled=True),
        lax.psum_scatter(skip_grad, "fsdp", scatter_dimension=0, tiled=True),
        lax.psum_scatter(gain_grads, "fsdp", scatter_dimension=0, tiled=True),
    )
    return (block_out, input_grad) + tuple(mixer_sums) + tuple(ffn_sums)


PLANES = 4
CHIPS = 4
CORES = 2
PLANE_DEV = CHIPS * CORES
FAST_DEV = PLANES * PLANE_DEV
RING = (0, 1, 3, 2)
MAIN_D = 48
MAIN_I = 96
SLICE_FF = FF // FAST_DEV
PAD_FF = 176
HALF_GU = 768
WIDE = 8704
GU = 2 * HALF_GU
REST_ROWS = 224
SMALL_ROWS = 208
LANES = 640
BIG = 1e30
LOG2E = 1.4426950408889634


def ring_place(k):
    return k + k // 2 - 2 * (k // 3)


class Links:
    def __init__(self, send_sems, recv_sems):
        me = lax.axis_index("fsdp")
        self.z, self.v, self.c = me // PLANE_DEV, (me // CORES) % CHIPS, me % CORES
        zp, vp = ring_place(self.z), ring_place(self.v)
        self.z_at = [ring_place((zp + k) % PLANES) for k in range(PLANES)]
        self.v_at = [ring_place((vp + k) % CHIPS) for k in range(CHIPS)]
        z, v, c = self.z, self.v, self.c
        self.z_next = self.z_at[1] * PLANE_DEV + v * CORES + c
        self.z_prev = self.z_at[3] * PLANE_DEV + v * CORES + c
        self.right = z * PLANE_DEV + self.v_at[1] * CORES + c
        self.left = z * PLANE_DEV + self.v_at[3] * CORES + c
        self.partner = me + 1 - 2 * c
        self.sems = send_sems, recv_sems
        self.copies, self.used = [], 0

    def greet(self):
        barrier = pltpu.get_barrier_semaphore()
        greeted = (self.right, self.left, self.z_next, self.z_prev, self.partner)
        for d in greeted:
            pl.semaphore_signal(barrier, inc=1, device_id=(d,), device_id_type=pl.DeviceIdType.MESH)
        pl.semaphore_wait(barrier, len(greeted))

    def send(self, src, dst, target):
        k, self.used = self.used, self.used + 1
        copy = pltpu.make_async_remote_copy(
            src_ref=src, dst_ref=dst, send_sem=self.sems[0].at[k], recv_sem=self.sems[1].at[k],
            device_id=(target,), device_id_type=pl.DeviceIdType.MESH,
        )
        copy.start()
        self.copies.append(copy)
        return copy

    def finish(self):
        for copy in self.copies:
            copy.wait_send()


class Gather:
    def __init__(self, links, source, place, local_sem):
        self.links, self.source, self.place = links, source, place
        self.along, self.near_in, self.far_in, self.core_in = {}, {}, {}, []
        self.own = pltpu.make_async_copy(source, self.block(0, OWN), local_sem)
        self.own.start()

    def block(self, back, chip):
        links = self.links
        return self.place(links.z_at[(PLANES - back) % PLANES], links.v_at[chip], links.c)

    def to_core(self, src, dst):
        self.core_in.append(self.links.send(src, dst, self.links.partner))

    def hop(self, s):
        links, here = self.links, self.block(s, OWN)
        if s:
            self.along[s - 1].wait_recv()
        src = here if s else self.source
        if s < PLANES - 1:
            self.along[s] = links.send(src, here, links.z_next)
        self.near_in[s, LEFT] = links.send(src, here, links.right)
        self.near_in[s, RIGHT] = links.send(src, here, links.left)
        self.to_core(src, here)

    def near(self, s):
        links = self.links
        for chip in (LEFT, RIGHT):
            self.near_in[s, chip].wait_recv()
            here = self.block(s, chip)
            if (chip == LEFT) == (s < 2):
                self.far_in[s] = links.send(here, here, links.right if chip == LEFT else links.left)
            self.to_core(here, here)

    def far(self, s):
        self.far_in[s].wait_recv()
        here = self.block(s, FAR)
        self.to_core(here, here)

    def wait(self):
        self.own.wait()
        for copy in self.core_in:
            copy.wait_recv()


GATHER_SENDS = 31
OWN, RIGHT, FAR, LEFT = range(CHIPS)


def shard_place(name, out):
    if name == "mamba_out":
        return lambda z, v, c: out.at[(z // 2) * 16 + c * 8 + (z % 2) * 4 + v]
    if name == "smalls":
        return lambda z, v, c: out.at[z * PLANE_DEV + v * CORES + c]
    return lambda z, v, c: out.at[c * 16 + z * 4 + v]


def gather_first_kernel(names, *refs):
    count = len(names)
    ins, units, outs, moved = refs[:count], refs[count : count + 2], refs[count + 2 : 2 * count + 2], refs[2 * count + 2 :]
    (gu_1, down_1, down_2), (send_sems, recv_sems, local) = moved[:3], moved[3:]
    links = Links(send_sems, recv_sems)
    links.greet()
    gathers = []
    for k, name in enumerate(names):
        parts = 2 if name == "wide" else 1
        width = ins[k].shape[1] // parts
        for part in range(parts):
            columns = pl.ds(part * width, width)
            place = shard_place(name, outs[k])

            def part_place(z, v, c, place=place, columns=columns):
                return place(z, v, c).at[:, columns]

            gathers.append(Gather(links, ins[k].at[:, columns], part_place, local.at[len(gathers)]))
    for s in range(PLANES):
        for g in gathers:
            g.hop(s)
    hops = [links.send(units[0], gu_1, links.z_next), links.send(units[1], down_1, links.z_next)]
    for s in range(PLANES):
        for g in gathers:
            g.near(s)
    for s in range(PLANES):
        for g in gathers:
            g.far(s)
        if s == 0:
            hops[1].wait_recv()
            hops.append(links.send(down_1, down_2, links.z_next))
    for g in gathers:
        g.wait()
    hops[0].wait_recv()
    hops[2].wait_recv()
    links.finish()


def gather_first(names, blocks, units):
    count, sends = len(names), GATHER_SENDS * (len(names) + 1) + 3
    sem, anywhere = pltpu.SemaphoreType.DMA, pl.BlockSpec(memory_space=pl.ANY)
    shapes = [(FAST_DEV,) + block.shape for block in blocks] + [units[0].shape] + [units[1].shape] * 2
    return pl.pallas_call(
        functools.partial(gather_first_kernel, names),
        out_shape=[jax.ShapeDtypeStruct(shape, jnp.bfloat16) for shape in shapes],
        in_specs=[anywhere] * (count + 2),
        out_specs=[anywhere] * (count + 3),
        scratch_shapes=[sem((sends,))] * 2 + [sem((count + 1,))],
        compiler_params=pltpu.CompilerParams(collective_id=0, has_side_effects=True),
        name="gather_first",
    )(*blocks, *units)


REST_COLUMNS = 1152
WIDE_BLOCKS = [(0, 7 * REST_COLUMNS, WIDE - 7 * REST_COLUMNS)] + [(0, k * REST_COLUMNS, REST_COLUMNS) for k in range(7)]
BRANCH_BLOCKS = [(0, 0, 768), (0, 768, 832), (1, 0, D)]
GRAD_ROWS = 192
GROUPS = PLANES * CHIPS
GAIN_LANES = 256


def add_rows(target, *others):
    @pl.loop(0, target.shape[0] // 16)
    def _(k):
        rows = pl.ds(pl.multiple_of(k * 16, 16), 16)
        total = target[rows, :].astype(jnp.float32)
        for other in others:
            total = total + other[rows, :].astype(jnp.float32)
        target[rows, :] = total.astype(target.dtype)


class Taker:
    def __init__(self, refs):
        self.refs = list(refs)

    def __call__(self, count):
        taken, self.refs = self.refs[:count], self.refs[count:]
        return taken


class SumPlan:
    def __init__(self, blocks, shard_rows, rest_rows, rest_columns, widths, columns, lows, smalls=None):
        self.blocks, self.rest_rows, self.has_smalls = blocks, rest_rows, smalls is not None
        self.shard_rows, self.widths = shard_rows, widths
        self.operands = list(columns) + list(lows) + ([smalls] if self.has_smalls else [])
        f32, bf16 = jnp.float32, jnp.bfloat16
        self.pairs, rows = len(lows), lows[0].shape[0]
        self.out_shape = [
            jax.ShapeDtypeStruct((shard_rows[k] + rest_rows[k], width), f32)
            for k in range(self.pairs)
            for width in widths[k]
        ]
        self.out_shape.append(jax.ShapeDtypeStruct((16, rest_columns), f32))
        scratch = [pltpu.VMEM((x.shape[0] * MAIN // CORES, CORES * rows), bf16) for x in columns]
        scratch += [pltpu.VMEM((x.shape[0] * (x.shape[1] - MAIN) // CORES, CORES * rows), bf16) for x in columns]
        scratch += [pltpu.VMEM((CORES * rows, y.shape[1]), bf16) for y in lows]
        scratch.append(pltpu.VMEM((16 * GROUPS, rest_columns), f32))
        shapes = [(shard_rows[pair], n) for pair, _, n in blocks] + [(16, rest_columns)]
        if self.has_smalls:
            shapes.append((smalls.shape[1] // GROUPS, smalls.shape[2]))
            scratch.append(pltpu.VMEM(smalls.shape[1:], bf16))
            self.out_shape.append(jax.ShapeDtypeStruct(shapes[-1], f32))
        for copies in (0, 4, 4, 4, 3):
            scratch += [pltpu.VMEM((copies, r, n) if copies else (GROUPS * r, n), bf16) for r, n in shapes]
        sem = pltpu.SemaphoreType.DMA
        self.count = len(shapes)
        scratch += [sem((self.count, k)) for k in (4, 4, 8, 8, 3, 3)] + [sem((self.pairs, 6))] * 3
        self.scratch = scratch


class Summing:
    def __init__(self, plan, links, ins, totals, scratch, early=2):
        self.blocks, self.rest_rows, self.has_smalls = plan.blocks, plan.rest_rows, plan.has_smalls
        self.pairs, self.count = plan.pairs, plan.count
        self.links = links
        take = Taker(ins)
        self.columns_in, self.lows_in = take(self.pairs), take(self.pairs)
        self.smalls_in = take(int(self.has_smalls))
        take = Taker(totals)
        self.shard_rows, self.totals = plan.shard_rows, []
        for widths in plan.widths:
            starts = [sum(widths[:j]) for j in range(len(widths))]
            self.totals.append([(ref, start, start + width) for ref, start, width in zip(take(len(widths)), starts, widths)])
        self.rest_total = take(1)[0]
        self.smalls_total = take(int(self.has_smalls))
        take = Taker(scratch)
        self.columns_all, self.rests_all, self.lows_all = take(self.pairs), take(self.pairs), take(self.pairs)
        self.rest_stage, self.smalls_stage = take(1)[0], take(int(self.has_smalls))
        self.partial, self.through, self.from_left, self.from_right, self.along = [take(self.count) for _ in range(5)]
        self.t_send, self.t_recv, self.s_send, self.s_recv, self.z_send, self.z_recv = take(6)
        self.c_send, self.c_recv, self.local = take(3)
        self.rest_at, self.smalls_at = len(self.blocks), len(self.blocks) + 1
        self.group_rows = [p.shape[0] // GROUPS for p in self.partial]
        self.sent, self.own, self.arriving = [], [], {}
        self.extra_rest = None
        self.order = list(range(len(self.blocks)))
        if self.has_smalls:
            self.order.insert(2, self.smalls_at)
        self.order.append(self.rest_at)
        events = []
        for p, i in enumerate(self.order):
            events += [
                (p - early, self.launch_far, i), (p, self.launch_near, i), (p + 1.5, self.relay, i),
                (p + 2.5, self.collect, i),
            ]
            events += [(p + 3.5 + j, self.planes, i, 2 - j) for j in range(3)]
        self.events = sorted(events, key=lambda event: event[0])

    def send(self, key, src, dst, ss, rs, target):
        copy = pltpu.make_async_remote_copy(
            src_ref=src, dst_ref=dst, send_sem=ss, recv_sem=rs, device_id=(target,),
            device_id_type=pl.DeviceIdType.MESH,
        )
        copy.start()
        self.sent.append(copy)
        self.arriving[key] = copy

    def stay(self, src, dst, sem):
        copy = pltpu.make_async_copy(src, dst, sem)
        copy.start()
        self.own.append(copy)

    def exchange(self):
        c, partner = self.links.c, self.links.partner
        c_send, c_recv, local = self.c_send, self.c_recv, self.local
        for k in range(self.pairs):
            columns_in, lows_in = self.columns_in[k], self.lows_in[k]
            rows, rest = lows_in.shape[0], columns_in.shape[1] - MAIN
            mine, other = pl.ds(0, rows), pl.ds(rows, rows)
            self.stay(lows_in, self.lows_all[k].at[mine], local.at[k, 0])
            self.send(("l", k), lows_in, self.lows_all[k].at[other], c_send.at[k, 0], c_recv.at[k, 0], partner)
            for h in range(columns_in.shape[0]):
                for kind, target, first, half in (
                    (0, self.columns_all[k], 0, MAIN // CORES), (1, self.rests_all[k], MAIN, rest // CORES),
                ):
                    place, at = pl.ds(h * half, half), 1 + 2 * kind + h
                    self.stay(
                        columns_in.at[h, pl.ds(pl.multiple_of(first + c * half, half), half)],
                        target.at[place, mine],
                        local.at[k, at],
                    )
                    self.send(
                        ("x", k, at),
                        columns_in.at[h, pl.ds(pl.multiple_of(first + (1 - c) * half, half), half)],
                        target.at[place, other],
                        c_send.at[k, at],
                        c_recv.at[k, at],
                        partner,
                    )
        if self.has_smalls:
            smalls = self.smalls_in[0]
            self.stay(smalls.at[c], self.partial[self.smalls_at], local.at[0, 5])
            self.send(("m",), smalls.at[1 - c], self.smalls_stage[0], c_send.at[0, 5], c_recv.at[0, 5], partner)

    def exchanged(self):
        for copy in self.own:
            copy.wait()
        for k in range(self.pairs):
            self.arriving["l", k].wait_recv()
            for h in range(self.columns_in[k].shape[0]):
                self.arriving["x", k, 1 + h].wait_recv()
                self.arriving["x", k, 3 + h].wait_recv()

    def rest_block(self):
        stage = self.rest_stage
        stage[...] = jnp.zeros_like(stage)
        row, width = 0, stage.shape[1]
        for k in range(self.pairs):
            r, lows = self.rest_rows[k], self.lows_all[k]
            for column in range(0, lows.shape[1], width):
                columns = min(width, lows.shape[1] - column)
                product = flat_product(self.rests_all[k][...], lows[:, column : column + columns])
                for g in range(GROUPS):
                    at = 16 * g + row
                    stage[at : at + r, :columns] = product[g * r : (g + 1) * r]
                row += r
        if self.extra_rest is not None:
            self.extra_rest(stage)
        self.partial[self.rest_at][...] = stage[...].astype(jnp.bfloat16)

    def compute(self, i):
        partial = self.partial[i]
        if i == self.rest_at:
            self.rest_block()
            return
        if i == self.smalls_at:
            self.arriving["m",].wait_recv()
            add_rows(partial, self.smalls_stage[0])
            return
        pair, column, columns = self.blocks[i]

        @pl.loop(0, partial.shape[0] // GRAD_ROWS)
        def _(j):
            rows = pl.ds(pl.multiple_of(j * GRAD_ROWS, GRAD_ROWS), GRAD_ROWS)
            partial[rows, :] = flat_product(
                self.columns_all[pair][rows, :], self.lows_all[pair][:, pl.ds(column, columns)]
            ).astype(jnp.bfloat16)

    def part(self, i, k, chip):
        rows = self.group_rows[i]
        at = (self.links.z_at[k] * CHIPS + self.links.v_at[chip]) * rows
        return self.partial[i].at[pl.ds(pl.multiple_of(at, rows), rows)]

    def launch_far(self, i):
        self.compute(i)
        for k in (3, 2, 1, 0):
            self.send(
                (i, "t", k), self.part(i, k, FAR), self.through[i].at[k], self.t_send.at[i, k], self.t_recv.at[i, k],
                self.links.right if k % 2 else self.links.left,
            )

    def launch_near(self, i):
        for k in (3, 2, 1, 0):
            landing, event = (self.from_right, 4 + k) if k % 2 else (self.from_left, k)
            self.send(
                (i, "s", event), self.part(i, k, LEFT if k % 2 else RIGHT), landing[i].at[k],
                self.s_send.at[i, event], self.s_recv.at[i, event], self.links.left if k % 2 else self.links.right,
            )

    def relay(self, i):
        for k in (3, 2, 1, 0):
            self.arriving[i, "t", k].wait_recv()
            add_rows(self.through[i].at[k], self.part(i, k, RIGHT if k % 2 else LEFT))
            landing, event = (self.from_left, k) if k % 2 else (self.from_right, 4 + k)
            self.send(
                (i, "s", event), self.through[i].at[k], landing[i].at[k], self.s_send.at[i, event],
                self.s_recv.at[i, event], self.links.right if k % 2 else self.links.left,
            )

    def pass_on(self, i, k):
        self.send(
            (i, "z", 3 - k), self.part(i, k, OWN), self.along[i].at[3 - k], self.z_send.at[i, 3 - k],
            self.z_recv.at[i, 3 - k], self.links.z_next,
        )

    def collect(self, i):
        for k in (3, 2, 1, 0):
            self.arriving[i, "s", k].wait_recv()
            self.arriving[i, "s", 4 + k].wait_recv()
            add_rows(self.part(i, k, OWN), self.from_left[i].at[k], self.from_right[i].at[k])
            if k == 3:
                self.pass_on(i, k)

    def planes(self, i, k):
        mine, along = self.part(i, k, OWN), self.along[i]
        self.arriving[i, "z", 2 - k].wait_recv()
        if k:
            add_rows(mine, along.at[2 - k])
            self.pass_on(i, k)
            return
        if i == self.rest_at:
            targets, column, columns = [(self.rest_total, 0, self.rest_total.shape[1])], 0, self.rest_total.shape[1]
        elif i == self.smalls_at:
            targets, column, columns = [(self.smalls_total[0], 0, 128)], 0, 128
        else:
            pair, column, columns = self.blocks[i]
            targets = self.totals[pair]

        @pl.loop(0, self.group_rows[i] // 16)
        def _(j):
            rows = pl.ds(pl.multiple_of(j * 16, 16), 16)
            total = mine[rows, :].astype(jnp.float32) + along[2, rows, :].astype(jnp.float32)
            for ref, start, stop in targets:
                low, high = max(start, column), min(stop, column + columns)
                if low < high:
                    ref[rows, low - start : high - start] = total[:, low - column : high - column]

        if i == self.rest_at:
            self.place_rest()

    def place_rest(self):
        row, width = 0, self.rest_total.shape[1]
        for k in range(self.pairs):
            r, first = self.rest_rows[k], self.shard_rows[k]
            for column in range(0, self.lows_all[k].shape[1], width):
                for ref, start, stop in self.totals[k]:
                    low, high = max(start, column), min(stop, column + width)
                    if low < high:
                        ref[first : first + r, low - start : high - start] = self.rest_total[
                            row : row + r, low - column : high - column
                        ]
                row += r

    def advance(self, until):
        while self.events and self.events[0][0] < until:
            _, stage, *which = self.events.pop(0)
            stage(*which)

    def finish(self):
        self.advance(1e9)
        for copy in self.sent:
            copy.wait_send()


UNIT_PAD = 64
BACK_LANES = 256


def last_kernel(plan, *refs):
    bf16, f32 = jnp.bfloat16, jnp.float32
    take = Taker(refs)
    ins = take(len(plan.operands))
    middle_grad_ref, tokens_ref, gains_ref, table_d_ref, wide_ref, wide_rest_ref = take(6)
    gu_grad_ref, down_grad_ref, gu_came_ref, down_came_ref = take(4)
    totals = take(len(plan.out_shape))
    input_grad_ref, gate_out_ref, up_out_ref, down_out_ref = take(4)
    scratch = take(len(plan.scratch))
    order, wide_buffer, total, gain, gain_other = take(5)
    gu_own, gu_sum, gu_next, down_own, down_sum, down_next, gu_rows, gu_in = take(8)
    wide_sem, unit_sem, send_sems, recv_sems = take(4)
    count = WIDE // BACK_LANES
    links = Links(send_sems, recv_sems)
    me = lax.axis_index("fsdp")
    first = me // PLANE_DEV * PLANE_DEV
    others = [first + (me % PLANE_DEV + k) % PLANE_DEV for k in range(1, PLANE_DEV)]
    barrier = pltpu.get_barrier_semaphore()
    greeted = others + [links.z_next, links.z_prev]
    for d in greeted:
        pl.semaphore_signal(barrier, inc=1, device_id=(d,), device_id_type=pl.DeviceIdType.MESH)
    pl.semaphore_wait(barrier, len(greeted))

    summing = Summing(plan, links, ins, totals, scratch)
    summing.exchange()
    gu_height, down_height = gu_own.shape[0], down_own.shape[0]
    wide_low = summing.lows_all[0].at[pl.ds(0, tokens_ref.shape[0])]

    def piece(ref, height, k):
        return ref.at[pl.ds(pl.multiple_of(links.z_at[k] * height, 16), height)]

    middle_copy = pltpu.make_async_copy(middle_grad_ref, input_grad_ref, unit_sem.at[4])
    middle_copy.start()
    moving = gu_sum.at[pl.ds(0, gu_height)]
    loads = [
        pltpu.make_async_copy(gu_came_ref, moving, unit_sem.at[0]),
        pltpu.make_async_copy(down_came_ref, down_sum, unit_sem.at[1]),
    ]
    def load_own(k):
        copies = [
            pltpu.make_async_copy(piece(gu_grad_ref, gu_height, k), gu_own, unit_sem.at[2]),
            pltpu.make_async_copy(piece(down_grad_ref, down_height, k), down_own, unit_sem.at[3]),
        ]
        for copy in copies:
            copy.start()
        return copies

    loads += load_own(1)
    for copy in loads[:2]:
        copy.start()
    def column_copy(j):
        return pltpu.make_async_copy(
            wide_ref.at[:, pl.ds(j * BACK_LANES, BACK_LANES)], wide_buffer.at[j % 2], wide_sem.at[j % 2]
        )

    column_copy(0).start()
    column_copy(1).start()
    summing.exchanged()
    summing.advance(1.2)
    for copy in loads:
        copy.wait()
    add_rows(moving, gu_own)
    add_rows(down_sum, down_own)
    loads = load_own(0)
    hops = [links.send(moving, gu_next, links.z_next), links.send(down_sum, down_next, links.z_next)]

    write_order(table_d_ref, order)
    total[...] = jnp.zeros_like(total)
    for j in range(count):
        column_copy(j).wait()
        total[...] += back_product(wide_low[:, j * BACK_LANES : (j + 1) * BACK_LANES], wide_buffer[j % 2])
        if j + 2 < count:
            column_copy(j + 2).start()
        if j % 8 == 7:
            summing.advance(1.2 + (j + 1) // 8)
    normed_grad = move_back(
        order, jnp.concatenate([total[...], back_product(wide_low[...], wide_rest_ref[...])], axis=1)
    )
    unit, scale = rms_parts(tokens_ref[...].astype(f32))
    back, gain_grad = rms_pull(unit, scale, gains_ref[0:1], normed_grad)
    middle_copy.wait()
    input_grad_ref[...] += back
    gain[...] = jnp.broadcast_to(gain_grad, gain.shape)
    gain_copy = links.send(gain, gain_other, links.partner)
    summing.advance(6.2)

    def gain_rows(stage):
        gain_copy.wait_recv()
        size = 4 * D // FAST_DEV
        lane = lax.broadcasted_iota(jnp.int32, (D, CHIPS * GAIN_LANES), 1)
        source = (lane // GAIN_LANES) * (CORES * size) + links.c * size + lane % GAIN_LANES
        place = lax.broadcasted_iota(jnp.int32, (D, CHIPS * GAIN_LANES), 0)
        picks = (place == source) & (lane % GAIN_LANES < size)
        select = order.at[:, pl.ds(0, CHIPS * GAIN_LANES)]
        select[...] = jnp.where(picks, 1.0, 0.0).astype(bf16)
        both = gain[0:1] + gain_other[0:1]
        both = jnp.broadcast_to(both, (16, D))
        high = both.astype(bf16)
        rest = (both - high.astype(f32)).astype(bf16)
        moved = flat_product(high, select[...]) + flat_product(rest, select[...])
        width, last = stage.shape[1], WIDE % REST_COLUMNS
        for v in range(CHIPS):
            stage[16 * v + 14 : 16 * v + 15, last : last + GAIN_LANES] = moved[
                0:1, v * GAIN_LANES : (v + 1) * GAIN_LANES
            ]

    summing.extra_rest = gain_rows
    summing.advance(7.2)
    for copy in hops:
        copy.wait()
        links.copies.remove(copy)
    for copy in loads:
        copy.wait()
    rows = D // FAST_DEV

    for piece_at in range(0, GU, GAIN_LANES):
        lanes = pl.ds(piece_at, GAIN_LANES)

        @pl.loop(0, gu_height // 16)
        def _(k):
            some = pl.ds(pl.multiple_of(k * 16, 16), 16)
            gu_rows[some, :] = gu_own[some, lanes].astype(f32) + gu_next[some, lanes].astype(f32)

        for p in range(PLANE_DEV):
            gu_sum[p * UNIT_PAD : (p + 1) * UNIT_PAD, lanes] = gu_rows[p * rows : p * rows + UNIT_PAD, :].astype(bf16)

    @pl.loop(0, down_height // 16)
    def _(k):
        some = pl.ds(pl.multiple_of(k * 16, 16), 16)
        down_out_ref[some, :] = down_own[some, :].astype(f32) + down_next[some, :].astype(f32)


    def unit_block(d):
        return gu_sum.at[pl.ds(pl.multiple_of(d % PLANE_DEV * UNIT_PAD, UNIT_PAD), UNIT_PAD)]

    keep = pltpu.make_async_copy(unit_block(me), gu_in.at[me % PLANE_DEV], unit_sem.at[5])
    keep.start()
    given = [links.send(unit_block(d), gu_in.at[me % PLANE_DEV], d) for d in others]
    summing.advance(12.2)
    for copy in given:
        copy.wait_recv()
    keep.wait()
    for half, out_ref in enumerate((gate_out_ref, up_out_ref)):
        for p in range(PLANE_DEV):
            for k in range(PLANES):
                column = half * HALF_GU + k * PAD_FF
                place = (k * PLANE_DEV + p) * SLICE_FF
                out_ref[:, place : place + SLICE_FF] = gu_in[p, :rows, column : column + SLICE_FF]
    summing.finish()
    links.finish()


def last_sums(plan, *operands):
    bf16, f32 = jnp.bfloat16, jnp.float32
    rows, gu_came, down_came = operands[0].shape[0], operands[8], operands[9]
    vmem, anywhere = pl.BlockSpec(memory_space=pltpu.VMEM), pl.BlockSpec(memory_space=pl.ANY)
    in_specs = [anywhere] * len(plan.operands) + [anywhere] + [vmem] * 3 + [anywhere, vmem] + [anywhere] * 4
    out_shape = plan.out_shape + [
        jax.ShapeDtypeStruct((rows, D), f32),
        jax.ShapeDtypeStruct((D // FAST_DEV, FF), bf16),
        jax.ShapeDtypeStruct((D // FAST_DEV, FF), bf16),
        jax.ShapeDtypeStruct(down_came.shape, f32),
    ]
    unit, downs = gu_came.shape, down_came.shape
    pad = (unit[0] + UNIT_PAD, GAIN_LANES)
    sem = pltpu.SemaphoreType.DMA
    return pl.pallas_call(
        functools.partial(last_kernel, plan),
        out_shape=out_shape,
        in_specs=in_specs,
        out_specs=[vmem] * len(out_shape),
        scratch_shapes=plan.scratch
        + [
            pltpu.VMEM((D, D), bf16),
            pltpu.VMEM((2, MAIN, BACK_LANES), bf16),
            pltpu.VMEM((rows, MAIN), f32),
            pltpu.VMEM((8, D), f32),
            pltpu.VMEM((8, D), f32),
            pltpu.VMEM(unit, bf16),
            pltpu.VMEM((PLANE_DEV * UNIT_PAD, GU), bf16),
            pltpu.VMEM(unit, bf16),
            pltpu.VMEM(downs, bf16),
            pltpu.VMEM(downs, bf16),
            pltpu.VMEM(downs, bf16),
            pltpu.VMEM(pad, f32),
            pltpu.VMEM((PLANE_DEV, UNIT_PAD, GU), bf16),
            sem((2,)),
            sem((7,)),
            sem((10,)),
            sem((10,)),
        ],
        compiler_params=pltpu.CompilerParams(
            collective_id=3, has_side_effects=True, vmem_limit_bytes=63 * 1024 * 1024
        ),
        name="last_sums",
    )(*plan.operands, *operands)


def scan_setup(pre, shift, conv, hold):
    step = jax.nn.softplus(pre + shift)
    return step, step + hold, step * conv


def tiled(block):
    return jnp.concatenate([block] * (LANES // 128), axis=1)


def folded(block):
    total = block[:, :128]
    for k in range(1, LANES // 128):
        total = total + block[:, 128 * k : 128 * (k + 1)]
    return total


GROUP = HEADS // KV_HEADS


def group_scores(qkv_ref, seg_col_ref, seg_row_ref, g):
    rows = qkv_ref.shape[0]
    queries = jnp.concatenate(
        [qkv_ref[:, (g * GROUP + r) * HEAD : (g * GROUP + r + 1) * HEAD] for r in range(GROUP)], axis=0
    )
    keys = qkv_ref[:, D + g * HEAD : D + (g + 1) * HEAD]
    values = qkv_ref[:, D + (KV_HEADS + g) * HEAD : D + (KV_HEADS + g + 1) * HEAD]
    scores = back_product(queries, keys) * HEAD ** (-0.5)
    t = lax.broadcasted_iota(jnp.int32, (rows, rows), 0)
    u = lax.broadcasted_iota(jnp.int32, (rows, rows), 1)
    allowed = (seg_col_ref[...] == seg_row_ref[...]) & (u <= t)
    scores = jnp.where(jnp.concatenate([allowed] * GROUP, axis=0), scores, -1e30)
    raised = jnp.exp(scores - jnp.max(scores, axis=-1, keepdims=True))
    probs = raised / jnp.sum(raised, axis=-1, keepdims=True)
    return queries, keys, values, probs


def attention_forward_kernel(qkv_ref, seg_col_ref, seg_row_ref, out_ref):
    rows = qkv_ref.shape[0]
    for g in range(KV_HEADS):
        _, _, values, probs = group_scores(qkv_ref, seg_col_ref, seg_row_ref, g)
        mixed = flat_product(probs.astype(jnp.bfloat16), values)
        for r in range(GROUP):
            head = g * GROUP + r
            out_ref[:, head * HEAD : (head + 1) * HEAD] = mixed[r * rows : (r + 1) * rows]


def attention_backward_kernel(qkv_ref, seg_col_ref, seg_row_ref, grad_ref, low_ref, first):
    rows = qkv_ref.shape[0]
    bf16 = jnp.bfloat16
    for g in range(KV_HEADS):
        queries, keys, values, probs = group_scores(qkv_ref, seg_col_ref, seg_row_ref, g)
        grads = jnp.concatenate(
            [grad_ref[:, (g * GROUP + r) * HEAD : (g * GROUP + r + 1) * HEAD] for r in range(GROUP)], axis=0
        )
        prob_grad = back_product(grads, values)
        score_low = (
            probs * (prob_grad - jnp.sum(probs * prob_grad, axis=-1, keepdims=True))
        ).astype(bf16)
        query_grad = (flat_product(score_low, keys) * HEAD ** (-0.5)).astype(bf16)
        for r in range(GROUP):
            head = g * GROUP + r
            low_ref[:, first + head * HEAD : first + (head + 1) * HEAD] = query_grad[r * rows : (r + 1) * rows]
        key_grad = outer_sum(score_low, queries) * HEAD ** (-0.5)
        low_ref[:, first + D + g * HEAD : first + D + (g + 1) * HEAD] = key_grad.astype(bf16)
        value_grad = outer_sum(probs.astype(bf16), grads)
        low_ref[:, first + D + (KV_HEADS + g) * HEAD : first + D + (KV_HEADS + g + 1) * HEAD] = value_grad.astype(bf16)


GRAD_LANES = 256


class PlaneTotal:
    def __init__(self, links, parts, core_in, far_in, near_in):
        self.links, self.parts, self.core_in, self.far_in, self.near_in = links, parts, core_in, far_in, near_in
        self.top = pl.ds(0, parts.shape[1] // 2)
        self.low = pl.ds(parts.shape[1] // 2, parts.shape[1] // 2)
        self.core = {}

    def give(self, chip):
        self.core[chip] = self.links.send(self.parts.at[CHIPS + chip], self.core_in.at[chip], self.links.partner)

    def join(self, chip):
        self.core[chip].wait_recv()
        add_rows(self.parts.at[chip], self.core_in.at[chip])

    def start(self):
        links, parts = self.links, self.parts
        self.join(FAR)
        self.far = [
            links.send(parts.at[FAR, self.top], self.far_in.at[0], links.right),
            links.send(parts.at[FAR, self.low], self.far_in.at[1], links.left),
        ]
        self.join(RIGHT)
        self.near = [links.send(parts.at[RIGHT, self.low], self.near_in.at[0, self.low], links.right)]
        self.join(LEFT)
        self.near.append(links.send(parts.at[LEFT, self.top], self.near_in.at[1, self.top], links.left))
        self.join(OWN)

    def relay(self):
        links, parts = self.links, self.parts
        self.far[0].wait_recv()
        add_rows(parts.at[RIGHT, self.top], self.far_in.at[0])
        self.near.append(links.send(parts.at[RIGHT, self.top], self.near_in.at[0, self.top], links.right))
        self.far[1].wait_recv()
        add_rows(parts.at[LEFT, self.low], self.far_in.at[1])
        self.near.append(links.send(parts.at[LEFT, self.low], self.near_in.at[1, self.low], links.left))

    def total(self, out_ref):
        for copy in self.near:
            copy.wait_recv()

        @pl.loop(0, out_ref.shape[0] // 16)
        def _(k):
            rows = pl.ds(pl.multiple_of(k * 16, 16), 16)
            total = self.parts[OWN, rows, :].astype(jnp.float32) + self.near_in[0, rows, :].astype(jnp.float32)
            out_ref[rows, :] = total + self.near_in[1, rows, :].astype(jnp.float32)


def feed_forward_kernel(
    rows_ref, out_low_ref, gu_0_ref, gu_1_ref, gu_2_ref, gu_3_ref, down_0_ref, down_1_ref, down_2_ref, down_3_ref,
    back_ref, ffn_ref, gu_grad_ref, down_grad_ref,
    gu_ref, down_ref, rows_all, act, gu_low, back, ffn, back_core, back_far, back_near, ffn_core, ffn_far, ffn_near,
    send_sems, recv_sems, own_sem,
):
    bf16, f32 = jnp.bfloat16, jnp.float32
    rows = rows_ref.shape[0]
    links = Links(send_sems, recv_sems)
    links.greet()
    own = pltpu.make_async_copy(rows_ref, rows_all.at[OWN], own_sem.at[0])
    own.start()
    copies = []
    for matrix, parts in (
        (gu_ref, (gu_0_ref, gu_1_ref, gu_2_ref, gu_3_ref)),
        (down_ref, (down_0_ref, down_1_ref, down_2_ref, down_3_ref)),
    ):
        height = parts[0].shape[0]
        for hops, part in enumerate(parts):
            place = pl.multiple_of(links.z_at[(PLANES - hops) % PLANES] * height, 16)
            copies.append(
                pltpu.make_async_copy(part, matrix.at[pl.ds(place, height)], own_sem.at[1 + len(copies)])
            )
            copies[-1].start()
    used = PLANES * PAD_FF
    down_ref[used:, :] = jnp.zeros((HALF_GU - used, D), bf16)
    to_right = links.send(rows_ref, rows_all.at[LEFT], links.right)
    to_left = links.send(rows_ref, rows_all.at[RIGHT], links.left)
    cores = {OWN: links.send(rows_ref, rows_all.at[CHIPS + OWN], links.partner)}
    back_sum = PlaneTotal(links, back, back_core, back_far, back_near)
    ffn_sum = PlaneTotal(links, ffn, ffn_core, ffn_far, ffn_near)
    top, low = pl.ds(0, rows // 2), pl.ds(rows // 2, rows // 2)

    def compute(slot):
        here = pl.ds(slot * rows, rows)
        x = rows_all[slot]
        gu = flat_product(x, gu_ref[...])
        gate, up = gu[:, :HALF_GU], gu[:, HALF_GU:]
        opened = 1.0 / (1.0 + jnp.exp(-gate))
        act[here, :] = (gate * opened * up).astype(bf16)
        grad = back_product(out_low_ref[here, :], down_ref[...])
        gu_low[here, :HALF_GU] = (grad * up * opened * (1.0 + gate * (1.0 - opened))).astype(bf16)
        gu_low[here, HALF_GU:] = (grad * gate * opened).astype(bf16)
        back[slot] = back_product(gu_low[here, :], gu_ref[...]).astype(bf16)
        if slot >= CHIPS:
            back_sum.give(slot - CHIPS)

    own.wait()
    for copy in copies:
        copy.wait()
    compute(OWN)
    cores[OWN].wait_recv()
    compute(CHIPS + OWN)
    to_right.wait_recv()
    far = [links.send(rows_all.at[LEFT, top], rows_all.at[FAR, top], links.right)]
    cores[LEFT] = links.send(rows_all.at[LEFT], rows_all.at[CHIPS + LEFT], links.partner)
    to_left.wait_recv()
    far.append(links.send(rows_all.at[RIGHT, low], rows_all.at[FAR, low], links.left))
    cores[RIGHT] = links.send(rows_all.at[RIGHT], rows_all.at[CHIPS + RIGHT], links.partner)
    compute(LEFT)
    compute(RIGHT)
    for copy in far:
        copy.wait_recv()
    cores[FAR] = links.send(rows_all.at[FAR], rows_all.at[CHIPS + FAR], links.partner)
    compute(FAR)
    for chip in (FAR, RIGHT, LEFT):
        cores[chip].wait_recv()
        compute(CHIPS + chip)
    back_sum.start()

    def ffn_rows(slot):
        ffn[slot] = flat_product(act[slot * rows : (slot + 1) * rows], down_ref[...]).astype(bf16)
        if slot >= CHIPS:
            ffn_sum.give(slot - CHIPS)

    for chip in (FAR, RIGHT, LEFT, OWN):
        ffn_rows(CHIPS + chip)
    back_sum.relay()
    for chip in (FAR, RIGHT, LEFT, OWN):
        ffn_rows(chip)
    ffn_sum.start()

    def gu_grad(column, columns):
        left = jnp.concatenate([rows_all[slot, :, column : column + columns] for slot in range(PLANE_DEV)], axis=0)
        gu_grad_ref[column : column + columns, :] = outer_sum(left, gu_low[...]).astype(bf16)

    for column in range(0, 2 * GRAD_LANES, GRAD_LANES):
        gu_grad(column, GRAD_LANES)
    back_sum.total(back_ref)
    ffn_sum.relay()
    for column in range(2 * GRAD_LANES, D, GRAD_LANES):
        gu_grad(column, min(GRAD_LANES, D - column))
    for column in range(0, HALF_GU, GRAD_LANES):
        down_grad_ref[column : column + GRAD_LANES, :] = outer_sum(
            act[:, column : column + GRAD_LANES], out_low_ref[...]
        ).astype(bf16)
    ffn_sum.total(ffn_ref)
    links.finish()


def feed_forward(rows_low, out_low, *units):
    bf16, f32 = jnp.bfloat16, jnp.float32
    rows = rows_low.shape[0]
    vmem, anywhere = pl.BlockSpec(memory_space=pltpu.VMEM), pl.BlockSpec(memory_space=pl.ANY)

    def slots(count, height=rows):
        return pltpu.VMEM((count, height, D), bf16)

    sums = [slots(CHIPS), slots(2, rows // 2), slots(2)]
    return pl.pallas_call(
        feed_forward_kernel,
        out_shape=[
            jax.ShapeDtypeStruct((rows, D), f32),
            jax.ShapeDtypeStruct((rows, D), f32),
            jax.ShapeDtypeStruct((D, GU), bf16),
            jax.ShapeDtypeStruct((HALF_GU, D), bf16),
        ],
        in_specs=[anywhere, vmem] + [anywhere] * len(units),
        out_specs=[vmem] * 4,
        scratch_shapes=[
            pltpu.VMEM((D, GU), bf16),
            pltpu.VMEM((HALF_GU, D), bf16),
            slots(PLANE_DEV),
            pltpu.VMEM((PLANE_DEV * rows, HALF_GU), bf16),
            pltpu.VMEM((PLANE_DEV * rows, GU), bf16),
            slots(PLANE_DEV),
            slots(PLANE_DEV),
        ]
        + sums
        + sums
        + [pltpu.SemaphoreType.DMA((32,))] * 2
        + [pltpu.SemaphoreType.DMA((9,))],
        compiler_params=pltpu.CompilerParams(
            collective_id=4, has_side_effects=True, vmem_limit_bytes=60 * 1024 * 1024
        ),
        name="feed_forward",
    )(rows_low, out_low, *units)


CHUNKS = INNER // LANES
WIDE_CHUNKS = [(k * LANES, LANES) for k in range(WIDE // LANES)] + [(WIDE // LANES * LANES, WIDE % LANES)]
WIDE_BUFFERS = 3
MAIN = FAST_DEV * MAIN_D
LOW_PAD = 128


def lanes_at(k):
    return pl.ds(pl.multiple_of(k * LANES, 128), LANES)


def write_order(table_ref, matrix_ref):
    size, step = matrix_ref.shape[0], 160

    @pl.loop(0, size // step)
    def _(k):
        at = pl.multiple_of(k * step, 16)
        places = lax.broadcasted_iota(jnp.int32, (step, size), 0) + at
        matrix_ref[pl.ds(at, step), :] = jnp.where(places == table_ref[...], 1.0, 0.0).astype(jnp.bfloat16)


def rms_parts(values):
    scale = lax.rsqrt(jnp.mean(values * values, axis=-1, keepdims=True) + epsilon)
    return values * scale, scale


def rms_pull(unit, scale, gain_row, grad):
    inner = grad * gain_row
    back = scale * (inner - unit * jnp.mean(inner * unit, axis=-1, keepdims=True))
    return back, jnp.sum(grad * unit, axis=0, keepdims=True)


def move_back(order, rows_wide):
    high = rows_wide.astype(jnp.bfloat16)
    rest = (rows_wide - high.astype(jnp.float32)).astype(jnp.bfloat16)
    return back_product(high, order[...]) + back_product(rest, order[...])


def wide_copy(wide_ref, buffer, sem, j, buffers=WIDE_BUFFERS):
    column, columns = WIDE_CHUNKS[j]
    slot = j % buffers
    return pltpu.make_async_copy(
        wide_ref.at[:, pl.ds(column, columns)], buffer.at[slot, :, pl.ds(0, columns)], sem.at[slot]
    )


def write_columns(rows, out_ref):
    for column in range(0, rows.shape[1], 128):
        some = rows[:, column : column + 128].astype(jnp.float32)
        out_ref[column : column + some.shape[1], :] = some.T.astype(jnp.bfloat16)


def conv_sum(inner, taps, shift, same_ref):
    earlier = [pltpu.roll(inner, k, axis=0) * same_ref[:, k - 1 : k] for k in range(1, CONV)]
    total = shift + taps[CONV - 1 : CONV] * inner
    for k in range(1, CONV):
        total = total + taps[CONV - 1 - k : CONV - k] * earlier[k - 1]
    return total, earlier


def scan_rows(lanes, b_ref, c_ref, y_ref, rates, decay_step, step_input, keep=None):
    rows_all = decay_step.shape[0]

    def eight(k, state):
        base = pl.multiple_of(k * 8, 8)
        steps = decay_step[pl.ds(base, 8), :]
        inputs = step_input[pl.ds(base, 8), :]
        rows = []
        for i in range(8):
            decay = jnp.exp2(steps[i : i + 1] * rates)
            state = decay * state + tiled(b_ref[base + i]) * inputs[i : i + 1]
            if keep is None:
                rows.append(jnp.sum(tiled(c_ref[base + i]) * state, axis=0, keepdims=True))
            else:
                keep(base + i, state)
        if keep is None:
            y_ref[pl.ds(base, 8), lanes] = jnp.concatenate(rows, axis=0)
        return state

    lax.fori_loop(0, rows_all // 8, eight, jnp.zeros((STATE, LANES), jnp.float32))


def spread_lanes(rows_ref, first, out_ref):
    lane = lax.broadcasted_iota(jnp.int32, (STATE, 128), 1)
    place = lax.broadcasted_iota(jnp.int32, (STATE, 128), 0) + first

    @pl.loop(0, rows_ref.shape[0] // 8)
    def _(k):
        base = pl.multiple_of(k * 8, 8)
        rows = rows_ref[pl.ds(base, 8), :]
        for i in range(8):
            picked = jnp.where(lane == place, jnp.broadcast_to(rows[i : i + 1], (STATE, 128)), 0.0)
            out_ref[base + i] = jnp.broadcast_to(jnp.sum(picked, axis=1, keepdims=True), (STATE, 128))


def gather_lanes(b_ref, c_ref, out_ref):
    lane = lax.broadcasted_iota(jnp.int32, (STATE, 128), 1)
    place = lax.broadcasted_iota(jnp.int32, (STATE, 128), 0)

    @pl.loop(0, out_ref.shape[0] // 8)
    def _(k):
        base = pl.multiple_of(k * 8, 8)
        rows = []
        for i in range(8):
            b = jnp.where(lane == place, jnp.sum(b_ref[base + i], axis=1, keepdims=True), 0.0)
            c = jnp.where(lane == place + STATE, jnp.sum(c_ref[base + i], axis=1, keepdims=True), 0.0)
            rows.append(jnp.sum(b + c, axis=0, keepdims=True))
        out_ref[pl.ds(base, 8), :] = jnp.concatenate(rows, axis=0)


def mixer_forward_kernel(
    tokens_ref, gains_ref, seg_col_ref, seg_row_ref, hold_ref, same_ref, table_d_ref, table_i_ref,
    wide_ref, wide_rest_ref, taps_ref, conv_shift_ref, select_ref, step_ref, step_shift_ref, decay_ref, skip_ref,
    out_block_ref, out_rest_ref, join_block_ref, join_rest_ref,
    out_low_ref, gu_1_ref, down_2_ref,
    normed_columns_ref, mixed_ref, qkv_ref, conv_ref, step_low_ref, pre_ref, b_ref, c_ref, y_ref, gated_columns_ref,
    attn_ref, mamba_ref, joined_columns_ref, middle_ref, normed_two_ref,
    out_ref, join_ref, out_low_all_ref, gu_2_ref, gu_3_ref, down_3_ref,
    order, wide_buffer, out_all, join_all, conv_low, gated, normed_ref, joined_ref, decay_step, step_input, select_rows, wide_sem, sem,
    send_sems, recv_sems, local,
):
    bf16, f32 = jnp.bfloat16, jnp.float32
    links = Links(send_sems, recv_sems)
    links.greet()
    branches = [
        Gather(links, out_block_ref, shard_place("mamba_out", out_ref), local.at[0]),
        Gather(links, join_block_ref, shard_place("join", join_ref), local.at[1]),
    ]
    for g in branches:
        g.hop(0)
    low_copy = pltpu.make_async_copy(out_low_ref, out_low_all_ref.at[OWN], local.at[2])
    low_copy.start()
    low_near = [
        links.send(out_low_ref, out_low_all_ref.at[LEFT], links.right),
        links.send(out_low_ref, out_low_all_ref.at[RIGHT], links.left),
    ]
    low_core = [links.send(out_low_ref, out_low_all_ref.at[CHIPS + OWN], links.partner)]
    def low_service():
        top, low = pl.ds(0, out_low_ref.shape[0] // 2), pl.ds(out_low_ref.shape[0] // 2, out_low_ref.shape[0] // 2)
        for copy in low_near:
            copy.wait_recv()
        far = [
            links.send(out_low_all_ref.at[LEFT, top], out_low_all_ref.at[FAR, top], links.right),
            links.send(out_low_all_ref.at[RIGHT, low], out_low_all_ref.at[FAR, low], links.left),
        ]
        for chip in (LEFT, RIGHT):
            low_core.append(links.send(out_low_all_ref.at[chip], out_low_all_ref.at[CHIPS + chip], links.partner))
        return far

    count = len(WIDE_CHUNKS)
    for j in range(WIDE_BUFFERS):
        wide_copy(wide_ref, wide_buffer, wide_sem, j).start()
    inputs = tokens_ref[...].astype(f32)
    write_order(table_d_ref, order)
    normed_ref[...] = flat_product((rms_parts(inputs)[0] * gains_ref[0:1]).astype(bf16), order[...]).astype(bf16)
    for j, (column, columns) in enumerate(WIDE_CHUNKS):
        copy = wide_copy(wide_ref, wide_buffer, wide_sem, j)
        copy.wait()
        part = flat_product(normed_ref[:, :MAIN], wide_buffer[j % WIDE_BUFFERS, :, :columns]) + flat_product(
            normed_ref[:, MAIN:], wide_rest_ref[:, column : column + columns]
        )
        if column < 2 * INNER:
            mixed_ref[:, column : column + columns] = part
        else:
            first, last = column - 2 * INNER, min(column - 2 * INNER + columns, QKV)
            qkv_ref[:, first:last] = part[:, : last - first].astype(bf16)
        if j + WIDE_BUFFERS < count:
            wide_copy(wide_ref, wide_buffer, wide_sem, j + WIDE_BUFFERS).start()
        if j in (4, 8):
            for g in branches:
                g.hop(j // 4)
    low_far = low_service()
    for g in branches:
        g.near(0)
    write_columns(normed_ref[...], normed_columns_ref.at[0])

    @pl.loop(0, CHUNKS)
    def _(k):
        lanes = lanes_at(k)
        total, _ = conv_sum(mixed_ref[:, lanes], taps_ref[:, lanes], conv_shift_ref[:, lanes], same_ref)
        act = total / (1.0 + jnp.exp(-total))
        conv_ref[:, lanes] = act
        conv_low[:, lanes] = act.astype(bf16)

    for g in branches:
        g.hop(3)
    unit_hops = [links.send(gu_1_ref, gu_2_ref, links.z_next)]
    for g in branches:
        g.near(1)
    selected = flat_product(conv_low[...], select_ref[...])
    step_low_ref[...] = selected[:, :LOW_PAD].astype(bf16)
    select_rows[...] = selected[:, LOW_PAD:]
    spread_lanes(select_rows, 0, b_ref)
    spread_lanes(select_rows, STATE, c_ref)
    attention_forward_kernel(qkv_ref, seg_col_ref, seg_row_ref, attn_ref)
    write_order(table_i_ref, order)
    for copy in low_far:
        copy.wait_recv()
    low_core.append(links.send(out_low_all_ref.at[FAR], out_low_all_ref.at[CHIPS + FAR], links.partner))
    for g in branches:
        g.near(2)
        g.far(0)

    def scan_chunk(k):
        lanes = lanes_at(k)
        pre = flat_product(step_low_ref[...], step_ref[:, lanes])
        pre_ref[:, lanes] = pre
        conv = conv_ref[:, lanes]
        _, decay_step[...], step_input[...] = scan_setup(pre, step_shift_ref[:, lanes], conv, hold_ref[...])
        scan_rows(lanes, b_ref, c_ref, y_ref, decay_ref[:, lanes] * (-LOG2E), decay_step, step_input)
        gate = mixed_ref[:, pl.ds(pl.multiple_of(k * LANES + INNER, 128), LANES)]
        gated[:, lanes] = (
            (y_ref[:, lanes] + skip_ref[:, lanes] * conv) * (gate / (1.0 + jnp.exp(-gate)))
        ).astype(bf16)

    pl.loop(0, 1)(scan_chunk)
    for g in branches:
        g.near(3)
        g.far(1)
    pl.loop(1, 3)(scan_chunk)
    unit_hops[0].wait_recv()
    unit_hops.append(links.send(gu_2_ref, gu_3_ref, links.z_next))
    unit_hops.append(links.send(down_2_ref, down_3_ref, links.z_next))
    for g in branches:
        g.far(2)
    pl.loop(3, CHUNKS)(scan_chunk)
    half = INNER // 2
    moved = []
    for h in range(2):
        moved.append(flat_product(gated[:, h * half : (h + 1) * half], order[...]).astype(bf16))
        write_columns(moved[h], gated_columns_ref.at[h])
    write_order(table_d_ref, order)
    for g in branches:
        g.far(3)
    branches[0].wait()
    out_copies = [
        pltpu.make_async_copy(out_ref.at[j], out_all.at[pl.ds(j * MAIN_I, MAIN_I)], sem.at[j]) for j in range(FAST_DEV)
    ]
    for copy in out_copies:
        copy.start()
    branches[1].wait()
    join_copies = [
        pltpu.make_async_copy(join_ref.at[j], join_all.at[pl.ds(j * MAIN_D, MAIN_D)], sem.at[FAST_DEV + j])
        for j in range(FAST_DEV)
    ]
    for copy in join_copies:
        copy.start()
    for copy in out_copies:
        copy.wait()
    total = jnp.zeros(mamba_ref.shape, f32)
    for h in range(2):
        total = total + flat_product(moved[h][:, :MAIN], out_all[h * MAIN : (h + 1) * MAIN])
        total = total + flat_product(moved[h][:, MAIN:], out_rest_ref[h])
    mamba_ref[...] = total
    joined = 0.5 * (rms_parts(attn_ref[...])[0] * gains_ref[1:2] + rms_parts(total)[0] * gains_ref[2:3])
    joined_ref[...] = flat_product(joined.astype(bf16), order[...]).astype(bf16)
    for copy in join_copies:
        copy.wait()
    middle = (
        inputs
        + flat_product(joined_ref[:, :MAIN], join_all[...])
        + flat_product(joined_ref[:, MAIN:], join_rest_ref[...])
    )
    middle_ref[...] = middle
    normed_two_ref[...] = (rms_parts(middle)[0] * gains_ref[3:4]).astype(bf16)
    write_columns(joined_ref[...], joined_columns_ref.at[0])
    for copy in low_core + unit_hops[1:]:
        copy.wait_recv()
    low_copy.wait()
    links.finish()


def mixer_forward(*operands):
    rows = operands[0].shape[0]
    bf16, f32 = jnp.bfloat16, jnp.float32
    vmem, anywhere = pl.BlockSpec(memory_space=pltpu.VMEM), pl.BlockSpec(memory_space=pl.ANY)
    in_specs = [vmem] * len(operands)
    for k in (8, 17, 19, 21, 22, 23):
        in_specs[k] = anywhere
    out_block, join_block, out_low, gu, down = [operands[k] for k in (17, 19, 21, 22, 23)]
    shapes = (
        ((1, D, rows), bf16), ((rows, 2 * INNER), f32), ((rows, QKV), bf16), ((rows, INNER), f32), ((rows, LOW_PAD), bf16),
        ((rows, INNER), f32), ((rows, STATE, 128), f32), ((rows, STATE, 128), f32), ((rows, INNER), f32),
        ((2, D, rows), bf16), ((rows, D), f32), ((rows, D), f32), ((1, D, rows), bf16), ((rows, D), f32), ((rows, D), bf16),
    )
    gathered = [
        (FAST_DEV,) + out_block.shape, (FAST_DEV,) + join_block.shape, (PLANE_DEV,) + out_low.shape,
        gu.shape, gu.shape, down.shape,
    ]
    sends = 2 * GATHER_SENDS + 12
    return pl.pallas_call(
        mixer_forward_kernel,
        out_shape=[jax.ShapeDtypeStruct(shape, kind) for shape, kind in shapes]
        + [jax.ShapeDtypeStruct(shape, bf16) for shape in gathered],
        in_specs=in_specs,
        out_specs=[vmem] * len(shapes) + [anywhere] * len(gathered),
        scratch_shapes=[
            pltpu.VMEM((D, D), bf16),
            pltpu.VMEM((WIDE_BUFFERS, MAIN, LANES), bf16),
            pltpu.VMEM((2 * MAIN, D), bf16),
            pltpu.VMEM((MAIN, D), bf16),
            pltpu.VMEM((rows, INNER), bf16),
            pltpu.VMEM((rows, INNER), bf16),
            pltpu.VMEM((rows, D), bf16),
            pltpu.VMEM((rows, D), bf16),
            pltpu.VMEM((rows, LANES), f32),
            pltpu.VMEM((rows, LANES), f32),
            pltpu.VMEM((rows, 128), f32),
            pltpu.SemaphoreType.DMA((WIDE_BUFFERS,)),
            pltpu.SemaphoreType.DMA((2 * FAST_DEV,)),
            pltpu.SemaphoreType.DMA((sends,)),
            pltpu.SemaphoreType.DMA((sends,)),
            pltpu.SemaphoreType.DMA((3,)),
        ],
        compiler_params=pltpu.CompilerParams(
            collective_id=1, has_side_effects=True, vmem_limit_bytes=60 * 1024 * 1024
        ),
        name="mixer_forward",
    )(*operands)


def branch_backward_kernel(
    part_grad_ref, out_grad_ref, gains_ref, table_d_ref, table_i_ref, out_ref, out_rest_ref, join_ref, join_rest_ref,
    attn_ref, mamba_ref, middle_ref, gu_grad_ref,
    middle_grad_ref, gains_grad_ref, join_low_ref, mamba_low_ref, attn_low_ref, gated_grad_ref, gu_came_ref,
    order, row_buffer, sem, send_sems, recv_sems,
):
    bf16 = jnp.bfloat16
    links = Links(send_sems, recv_sems)
    links.greet()
    height = gu_came_ref.shape[0]
    far_rows = pl.ds(pl.multiple_of(links.z_at[3] * height, 16), height)
    hop = links.send(gu_grad_ref.at[far_rows], gu_came_ref, links.z_next)
    half_rows = MAIN // 2
    row_blocks = [(join_ref, k) for k in range(2)] + [(out_ref, k) for k in range(4)]

    def row_copy(i):
        source, k = row_blocks[i]
        return pltpu.make_async_copy(source.at[pl.ds(k * half_rows, half_rows)], row_buffer.at[i], sem.at[i])

    def row_products(low, first):
        products = []
        for i in (first, first + 1):
            row_copy(i).wait()
            products.append(back_product(low, row_buffer[i]))
        return products

    for i in range(len(row_blocks)):
        row_copy(i).start()
    write_order(table_d_ref, order)
    unit, scale = rms_parts(middle_ref[...])
    back, gain_grad = rms_pull(unit, scale, gains_ref[3:4], part_grad_ref[...])
    gains_grad_ref[0:1] = jnp.zeros_like(gain_grad)
    gains_grad_ref[3:4] = gain_grad
    middle_grad = out_grad_ref[...] + back
    middle_grad_ref[...] = middle_grad
    join_low = middle_grad.astype(bf16)
    join_low_ref[...] = join_low
    joined_grad = 0.5 * move_back(
        order, jnp.concatenate(row_products(join_low, 0) + [back_product(join_low, join_rest_ref[...])], axis=1)
    )
    unit, scale = rms_parts(attn_ref[...])
    back, gain_grad = rms_pull(unit, scale, gains_ref[1:2], joined_grad)
    gains_grad_ref[1:2] = gain_grad
    attn_low_ref[...] = back.astype(bf16)
    unit, scale = rms_parts(mamba_ref[...])
    back, gain_grad = rms_pull(unit, scale, gains_ref[2:3], joined_grad)
    gains_grad_ref[2:3] = gain_grad
    mamba_low = back.astype(bf16)
    mamba_low_ref[...] = mamba_low
    write_order(table_i_ref, order)
    half = INNER // 2
    for h in range(2):
        gated_grad_ref[:, h * half : (h + 1) * half] = move_back(
            order,
            jnp.concatenate(row_products(mamba_low, 2 + 2 * h) + [back_product(mamba_low, out_rest_ref[h])], axis=1),
        )
    hop.wait_recv()
    links.finish()


def branch_backward(*operands):
    rows = operands[0].shape[0]
    bf16, f32 = jnp.bfloat16, jnp.float32
    vmem, anywhere = pl.BlockSpec(memory_space=pltpu.VMEM), pl.BlockSpec(memory_space=pl.ANY)
    in_specs = [vmem] * len(operands)
    for k in (5, 7, 12):
        in_specs[k] = anywhere
    shapes = (
        ((rows, D), f32), ((4, D), f32), ((rows, D), bf16), ((rows, D), bf16), ((rows, D), bf16), ((rows, INNER), f32),
        ((PLANE_DEV * D // FAST_DEV, GU), bf16),
    )
    return pl.pallas_call(
        branch_backward_kernel,
        out_shape=[jax.ShapeDtypeStruct(shape, kind) for shape, kind in shapes],
        in_specs=in_specs,
        out_specs=[vmem] * (len(shapes) - 1) + [anywhere],
        scratch_shapes=[
            pltpu.VMEM((D, D), bf16),
            pltpu.VMEM((6, MAIN // 2, D), bf16),
            pltpu.SemaphoreType.DMA((6,)),
            pltpu.SemaphoreType.DMA((1,)),
            pltpu.SemaphoreType.DMA((1,)),
        ],
        compiler_params=pltpu.CompilerParams(
            collective_id=5, has_side_effects=True, vmem_limit_bytes=56 * 1024 * 1024
        ),
        name="branch_backward",
    )(*operands)


BACK_STAGED = 9


def mixer_backward_kernel(plan, *refs):
    bf16, f32 = jnp.bfloat16, jnp.float32
    take = Taker(refs)
    ins = take(len(plan.operands))
    gu_grad_ref, down_grad_ref, gu_first_ref, seg_col_ref, seg_row_ref, hold_ref, same_ref = take(7)
    taps_ref, conv_shift_ref, select_ref, step_ref, step_shift_ref, decay_ref, skip_ref = take(7)
    mixed_ref, qkv_ref, conv_ref, step_low_ref, pre_ref, b_ref, c_ref, y_ref, attn_low_ref, gated_grad_ref = take(10)
    totals = take(len(plan.out_shape))
    wide_low_ref, select_grad_ref, step_grad_ref, taps_grad_ref, conv_shift_grad_ref = take(5)
    step_shift_grad_ref, decay_grad_ref, skip_grad_ref, gu_came_ref, down_came_ref = take(5)
    scratch = take(len(plan.scratch))
    conv_grad, low_grad, step_size, decay_step, step_input, y_grad, input_part, step_part = take(8)
    states, b_grad, c_grad, select_rows, select_low = take(5)
    gu_own, gu_next, down_own, down_next, unit_sem, send_sems, recv_sems = take(7)
    staged, stage_sem = take(BACK_STAGED), take(1)[0]
    rows_all = conv_ref.shape[0]
    links = Links(send_sems, recv_sems)
    links.greet()
    summing = Summing(plan, links, ins, totals, scratch, early=len(plan.blocks) + 1)
    summing.exchange()
    rows_in = (mixed_ref, conv_ref, pre_ref, b_ref, c_ref, y_ref, gated_grad_ref, select_ref, qkv_ref)
    stages = [pltpu.make_async_copy(rows_in[k], staged[k], stage_sem.at[k]) for k in range(BACK_STAGED)]
    for copy in stages:
        copy.start()
    mixed_ref, conv_ref, pre_ref, b_ref, c_ref, y_ref, gated_grad_ref, select_ref, qkv_ref = staged
    gu_height, down_height = gu_own.shape[0], down_own.shape[0]

    def piece(ref, height, k):
        return ref.at[pl.ds(pl.multiple_of(links.z_at[k] * height, 16), height)]

    down_hop = links.send(piece(down_grad_ref, down_height, 3), down_next, links.z_next)
    loads = [
        pltpu.make_async_copy(piece(gu_grad_ref, gu_height, 2), gu_own, unit_sem.at[0]),
        pltpu.make_async_copy(piece(down_grad_ref, down_height, 2), down_own, unit_sem.at[1]),
        pltpu.make_async_copy(gu_first_ref, gu_next, unit_sem.at[2]),
    ]
    for copy in loads:
        copy.start()
    for copy in loads:
        copy.wait()
    add_rows(gu_own, gu_next)
    gu_hop = links.send(gu_own, gu_came_ref, links.z_next)
    b_grad[...] = jnp.zeros_like(b_grad)
    c_grad[...] = jnp.zeros_like(c_grad)
    states[0] = jnp.zeros((STATE, LANES), f32)
    zeros = jnp.zeros((STATE, LANES), f32)
    summing.exchanged()
    summing.advance(1.2)
    for copy in stages:
        copy.wait()

    def scan_chunk(k):
        lanes = lanes_at(k)
        gate_lanes = pl.ds(pl.multiple_of(k * LANES + INNER, 128), LANES)
        conv, shift, skip = conv_ref[:, lanes], step_shift_ref[:, lanes], skip_ref[:, lanes]
        step_size[...], decay_step[...], step_input[...] = scan_setup(pre_ref[:, lanes], shift, conv, hold_ref[...])
        gate, grad = mixed_ref[:, gate_lanes], gated_grad_ref[:, lanes]
        open_gate = 1.0 / (1.0 + jnp.exp(-gate))
        wide_low_ref[:, gate_lanes] = (
            grad * (y_ref[:, lanes] + skip * conv) * open_gate * (1.0 + gate * (1.0 - open_gate))
        ).astype(bf16)
        y_grad[...] = grad * gate * open_gate
        skip_grad_ref[:, lanes] = jnp.sum(y_grad[...] * conv, axis=0, keepdims=True)
        decay_rows = decay_ref[:, lanes]
        rates = decay_rows * (-LOG2E)

        def keep(t, state):
            states[t + 1] = state

        scan_rows(lanes, b_ref, c_ref, None, rates, decay_step, step_input, keep)

        def backward(i, carry):
            state_grad, decay_grad = carry
            base = pl.multiple_of(rows_all - 8 - i * 8, 8)
            inputs = step_input[pl.ds(base, 8), :]
            sizes = step_size[pl.ds(base, 8), :]
            held = decay_step[pl.ds(base, 8), :]
            y_rows = y_grad[pl.ds(base, 8), :]
            input_rows, step_rows = [None] * 8, [None] * 8
            for r in range(7, -1, -1):
                t = base + r
                y_row = y_rows[r : r + 1]
                full = state_grad + tiled(c_ref[t]) * y_row
                c_grad[t] += folded(states[t + 1] * y_row)
                b_grad[t] += folded(full * inputs[r : r + 1])
                input_rows[r] = jnp.sum(tiled(b_ref[t]) * full, axis=0, keepdims=True)
                state_grad = jnp.exp2(held[r : r + 1] * rates) * full
                through = state_grad * states[t]
                step_rows[r] = jnp.sum(decay_rows * through, axis=0, keepdims=True)
                decay_grad = decay_grad - sizes[r : r + 1] * through
            input_part[pl.ds(base, 8), :] = jnp.concatenate(input_rows, axis=0)
            step_part[pl.ds(base, 8), :] = jnp.concatenate(step_rows, axis=0)
            return state_grad, decay_grad

        _, decay_grad = lax.fori_loop(0, rows_all // 8, backward, (zeros, zeros))
        decay_grad_ref[:, lanes] = decay_grad
        conv_grad[:, lanes] = input_part[...] * step_size[...] + skip * y_grad[...]
        pre_grad = (input_part[...] * conv - step_part[...]) / (1.0 + jnp.exp(-(pre_ref[:, lanes] + shift)))
        step_shift_grad_ref[:, lanes] = jnp.sum(pre_grad, axis=0, keepdims=True)
        low_grad[:, lanes] = pre_grad.astype(bf16)

    for first, last, until in ((0, 2, 2.2), (2, 3, 3.2), (3, 4, 4.3)):
        pl.loop(first, last)(scan_chunk)
        summing.advance(until)
    down_hop.wait_recv()
    add_rows(down_own, down_next)
    down_hop = links.send(down_own, down_came_ref, links.z_next)
    pl.loop(4, CHUNKS)(scan_chunk)
    summing.advance(5.3)

    gather_lanes(b_grad, c_grad, select_rows)
    select_low[:, :LOW_PAD] = back_product(low_grad[...], step_ref[...]).astype(bf16)
    select_low[:, LOW_PAD:] = select_rows[...].astype(bf16)
    summing.advance(6.3)

    @pl.loop(0, CHUNKS)
    def _(k):
        lanes = lanes_at(k)
        step_grad_ref[:, lanes] = outer_sum(step_low_ref[...], low_grad[:, lanes]).astype(bf16)
        conv = conv_ref[:, lanes]
        some = pl.ds(pl.multiple_of(k * LANES, 128), LANES)
        select_grad_ref[some, :] = outer_sum(conv.astype(bf16), select_low[...]).astype(bf16)
        grad = conv_grad[:, lanes] + back_product(select_low[...], select_ref[some, :])
        inner, taps = mixed_ref[:, lanes], taps_ref[:, lanes]
        total, earlier = conv_sum(inner, taps, conv_shift_ref[:, lanes], same_ref)
        opened = 1.0 / (1.0 + jnp.exp(-total))
        grad = grad * opened * (1.0 + total * (1.0 - opened))
        conv_shift_grad_ref[:, lanes] = jnp.sum(grad, axis=0, keepdims=True)
        tap_rows = [jnp.sum(grad * earlier[j - 1], axis=0, keepdims=True) for j in range(CONV - 1, 0, -1)]
        tap_rows.append(jnp.sum(grad * inner, axis=0, keepdims=True))
        taps_grad_ref[:, lanes] = jnp.concatenate(tap_rows, axis=0)
        inner_grad = taps[CONV - 1 : CONV] * grad
        for j in range(1, CONV):
            moved = taps[CONV - 1 - j : CONV - j] * grad * same_ref[:, j - 1 : j]
            inner_grad = inner_grad + pltpu.roll(moved, rows_all - j, axis=0)
        wide_low_ref[:, lanes] = inner_grad.astype(bf16)

    summing.advance(7.3)
    attention_backward_kernel(qkv_ref, seg_col_ref, seg_row_ref, attn_low_ref, wide_low_ref, 2 * INNER)
    wide_low_ref[:, 2 * INNER + QKV :] = jnp.zeros((rows_all, WIDE - 2 * INNER - QKV), bf16)
    summing.finish()
    gu_hop.wait_recv()
    down_hop.wait_recv()
    links.finish()


def mixer_backward(plan, *operands):
    rows = operands[-1].shape[0]
    rows_in = [operands[k] for k in (14, 16, 18, 19, 20, 21, 23, 9, 15)]
    bf16, f32 = jnp.bfloat16, jnp.float32
    vmem, anywhere = pl.BlockSpec(memory_space=pltpu.VMEM), pl.BlockSpec(memory_space=pl.ANY)
    in_specs = [anywhere] * (len(plan.operands) + 3) + [vmem] * (len(operands) - 3)
    for k in (14, 16, 18, 19, 20, 21, 23, 9, 15):
        in_specs[len(plan.operands) + k] = anywhere
    shapes = (
        ((rows, WIDE), bf16), ((INNER, 2 * LOW_PAD), bf16), ((LOW_PAD, INNER), bf16), ((CONV, INNER), f32),
        ((1, INNER), f32), ((1, INNER), f32), ((STATE, INNER), f32), ((1, INNER), f32),
        ((PLANE_DEV * D // FAST_DEV, GU), bf16), ((PAD_FF, D), bf16),
    )
    lane_rows = pltpu.VMEM((rows, LANES), f32)
    sem = pltpu.SemaphoreType.DMA
    return pl.pallas_call(
        functools.partial(mixer_backward_kernel, plan),
        out_shape=plan.out_shape + [jax.ShapeDtypeStruct(shape, kind) for shape, kind in shapes],
        in_specs=in_specs,
        out_specs=[vmem] * (len(plan.out_shape) + len(shapes) - 2) + [anywhere] * 2,
        scratch_shapes=plan.scratch
        + [pltpu.VMEM((rows, INNER), f32), pltpu.VMEM((rows, INNER), bf16)]
        + [lane_rows] * 6
        + [
            pltpu.VMEM((rows + 1, STATE, LANES), f32),
            pltpu.VMEM((rows, STATE, 128), f32),
            pltpu.VMEM((rows, STATE, 128), f32),
            pltpu.VMEM((rows, 128), f32),
            pltpu.VMEM((rows, 2 * LOW_PAD), bf16),
            pltpu.VMEM(shapes[-2][0], bf16),
            pltpu.VMEM(shapes[-2][0], bf16),
            pltpu.VMEM(shapes[-1][0], bf16),
            pltpu.VMEM(shapes[-1][0], bf16),
            sem((3,)),
            sem((3,)),
            sem((3,)),
        ]
        + [pltpu.VMEM(x.shape, x.dtype) for x in rows_in]
        + [sem((BACK_STAGED,))],
        compiler_params=pltpu.CompilerParams(
            collective_id=2, has_side_effects=True, vmem_limit_bytes=62 * 1024 * 1024
        ),
        name="mixer_backward",
    )(*plan.operands, *operands)


def spread_table(shard_rows, main_rows, shards):
    half = shards // CORES
    order = [k * CORES + c for c in range(CORES) for k in range(half)]
    main = [d * shard_rows + r for d in order for r in range(main_rows)]
    rest = [d * shard_rows + r for d in order for r in range(main_rows, shard_rows)]
    return np.asarray(main + rest, np.int32)


def tie(*values):
    return lax.optimization_barrier(values)


def as_rows(flats, rows):
    flat = jnp.concatenate(flats)
    return jnp.pad(flat, (0, rows * 128 - flat.size)).reshape(rows, 128)


def split_flat(block, sizes):
    pieces, at = [], 0
    for size in sizes:
        pieces.append(block[..., at : at + size])
        at += size
    return pieces


def on_fast_device(
    tokens, cotangent, seq_lengths, qkv_proj, mamba_in, select_proj, step_proj, mamba_out, join_out,
    conv_taps, conv_bias, step_bias, decay_rates, skip_gain, norm_gains, ffn_gate, ffn_up, ffn_down,
):
    bf16, f32 = jnp.bfloat16, jnp.float32
    n = FAST_DEV
    row_count = tokens.shape[0]
    d_rows, i_rows = D // n, INNER // n
    d_rest, i_rest = d_rows - MAIN_D, i_rows - MAIN_I

    own_ff = PLANES * PAD_FF

    def ff_columns(flat):
        block = flat.reshape(d_rows, PLANES, PLANE_DEV, SLICE_FF).transpose(2, 0, 1, 3)
        block = jnp.pad(block, ((0, 0), (0, 0), (0, 0), (0, PAD_FF - SLICE_FF)))
        return jnp.pad(block.reshape(PLANE_DEV, d_rows, own_ff), ((0, 0), (0, 0), (0, HALF_GU - own_ff)))

    planes = [[z * PLANE_DEV + p for p in range(PLANE_DEV)] for z in range(PLANES)]
    gu = jnp.concatenate([ff_columns(ffn_gate), ff_columns(ffn_up)], axis=2)
    gu = lax.all_to_all(gu, "fsdp", 0, 0, axis_index_groups=planes, tiled=True).reshape(PLANE_DEV * d_rows, GU)
    down = jnp.pad(ffn_down.reshape(SLICE_FF, D), ((0, PAD_FF - SLICE_FF), (0, 0)))

    wide = jnp.concatenate([mamba_in.reshape(d_rows, 2 * INNER), qkv_proj.reshape(d_rows, QKV)], axis=1)
    wide = jnp.pad(wide, ((0, 0), (0, WIDE - wide.shape[1])))
    out_block = mamba_out.reshape(i_rows, D)
    join_block = join_out.reshape(d_rows, D)
    rest_sizes = [d_rest * WIDE, d_rest * D, i_rest * D]
    rest = as_rows(
        [wide[MAIN_D:].reshape(-1), join_block[MAIN_D:].reshape(-1), out_block[MAIN_I:].reshape(-1)], REST_ROWS
    )
    smalls = [select_proj, step_proj, conv_taps, conv_bias, step_bias, decay_rates, skip_gain, norm_gains]
    small_sizes = [s.size for s in smalls]
    smalls = as_rows(smalls, SMALL_ROWS)
    segments = segment_ids(seq_lengths, row_count)
    live_rows = (segments < seq_lengths.shape[0]).astype(f32)[:, None]
    out_grad = cotangent.astype(f32) * live_rows
    gu, down, wide_block, rest, smalls, out_grad = tie(gu, down, wide[:MAIN_D], rest, smalls, out_grad)
    wide_all, rest_all, smalls_all, gu_1, down_1, down_2 = gather_first(
        ("wide", "rest", "smalls"), (wide_block, rest, smalls), (gu, down)
    )
    wide_all = wide_all.reshape(MAIN, WIDE)
    pieces = split_flat(rest_all.reshape(n, REST_ROWS * 128), rest_sizes)
    wide_rest = pieces[0].reshape(n * d_rest, WIDE)
    join_rest = pieces[1].reshape(n * d_rest, D)
    out_rest = pieces[2].reshape(CORES, 2, -1, D).transpose(1, 0, 2, 3).reshape(2, -1, D)
    pieces = split_flat(smalls_all.reshape(n, SMALL_ROWS * 128), small_sizes)
    select = pieces[0].reshape(INNER, XPROJ)
    select = jnp.concatenate(
        [
            jnp.pad(select[:, :RANK], ((0, 0), (0, LOW_PAD - RANK))),
            jnp.pad(select[:, RANK:], ((0, 0), (0, LOW_PAD - 2 * STATE))),
        ],
        axis=1,
    )
    step_matrix = jnp.pad(pieces[1].reshape(RANK, INNER), ((0, LOW_PAD - RANK), (0, 0)))
    taps = pieces[2].reshape(CONV, INNER).astype(f32)
    conv_shift = pieces[3].reshape(1, INNER).astype(f32)
    step_shift = pieces[4].reshape(1, INNER).astype(f32)
    decay = pieces[5].reshape(STATE, INNER).astype(f32)
    skip = pieces[6].reshape(1, INNER).astype(f32)
    gains = pieces[7].reshape(4, D).astype(f32)

    table_d = jnp.asarray(spread_table(d_rows, MAIN_D, n))[None]
    table_i = jnp.asarray(spread_table(i_rows, MAIN_I, n // 2))[None]
    hold = ((1.0 - keep_flags(segments)) * BIG)[:, None]
    same = jnp.stack(
        [
            (jnp.concatenate([jnp.full((k,), -1, jnp.int32), segments[:-k]]) == segments).astype(f32)
            for k in range(1, CONV)
        ],
        axis=1,
    )
    places = (segments[:, None], segments[None, :], hold, same, table_d, table_i)
    matrices = (
        wide_all, wide_rest, taps, conv_shift, select, step_matrix, step_shift, decay, skip,
    )
    (
        normed_columns, mixed, qkv_rows, conv_act, step_low, step_pre, b_wide, c_wide, scanned, gated_columns, attn_rows,
        mamba_rows, joined_columns, middle, normed_two, out_all, join_all, out_low, gu_2, gu_3, down_3,
    ) = mixer_forward(
        tokens, gains, *places, *matrices, out_block[:MAIN_I], out_rest, join_block[:MAIN_D], join_rest,
        out_grad.astype(bf16), gu_1, down_2,
    )
    out_all, join_all = out_all.reshape(2 * MAIN, D), join_all.reshape(MAIN, D)

    part_grad, ffn_rows, gu_grad, down_grad = feed_forward(
        normed_two, out_low.reshape(-1, D), gu, gu_1, gu_2, gu_3, down, down_1, down_2, down_3
    )
    block_out = ((middle + ffn_rows) * live_rows).astype(bf16)

    middle_grad, gains_grad, join_low, mamba_low, attn_low, gated_grad, gu_first = branch_backward(
        part_grad, out_grad, gains, table_d, table_i, out_all, out_rest, join_all, join_rest,
        attn_rows, mamba_rows, middle, gu_grad,
    )
    branch_plan = SumPlan(
        BRANCH_BLOCKS, (MAIN_I, MAIN_D), (i_rest, d_rest), D, ((D,), (D,)),
        (gated_columns, joined_columns), (mamba_low, join_low),
    )
    (
        out_sum, join_sum, _, wide_low, select_grad, step_grad, taps_grad, conv_shift_grad,
        step_shift_grad, decay_grad, skip_grad, gu_came, down_came,
    ) = mixer_backward(
        branch_plan, gu_grad, down_grad, gu_first, *places[:4], taps, conv_shift, select, step_matrix, step_shift, decay,
        skip, mixed, qkv_rows, conv_act, step_low, step_pre, b_wide, c_wide, scanned, attn_low, gated_grad,
    )
    select_grad = jnp.concatenate([select_grad[:, :RANK], select_grad[:, LOW_PAD : LOW_PAD + 2 * STATE]], axis=1)
    small_grads = [
        select_grad, step_grad[:RANK], taps_grad, conv_shift_grad, step_shift_grad, decay_grad, skip_grad, gains_grad,
    ]
    small_grads = jnp.concatenate([g.astype(bf16).reshape(n, -1) for g in small_grads], axis=1)
    small_grads = jnp.pad(small_grads, ((0, 0), (0, SMALL_ROWS * 128 - small_grads.shape[1])))
    small_grads = small_grads.reshape(GROUPS, CORES, SMALL_ROWS, 128).transpose(1, 0, 2, 3)
    wide_plan = SumPlan(
        WIDE_BLOCKS, (MAIN_D,), (d_rest,), REST_COLUMNS, ((2 * INNER, QKV),),
        (normed_columns,), (wide_low,), small_grads.reshape(CORES, GROUPS * SMALL_ROWS, 128),
    )
    mamba_sum, qkv_sum, wide_left, small_sum, input_grad, gate_grad, up_grad, down_sum = last_sums(
        wide_plan, middle_grad, tokens, gains, table_d, wide_all, wide_rest, gu_grad, down_grad, gu_came, down_came
    )
    gate_grad, up_grad = [block.astype(f32).reshape(-1) for block in (gate_grad, up_grad)]
    first_gain = wide_left[14, WIDE % REST_COLUMNS : WIDE % REST_COLUMNS + norm_gains.size]
    smalls = split_flat(small_sum.reshape(-1), small_sizes)
    return (
        block_out,
        input_grad,
        qkv_sum.reshape(-1),
        mamba_sum.reshape(-1),
        smalls[0],
        smalls[1],
        out_sum.reshape(-1),
        join_sum.reshape(-1),
        *smalls[2:-1],
        smalls[-1] + first_gain,
        gate_grad,
        up_grad,
        down_sum[:SLICE_FF].reshape(-1),
    )


def fits_fast_plan(mesh):
    return mesh.shape["fsdp"] == FAST_DEV


def solution(mesh):
    rows, flat = P("fsdp", None), P("fsdp")
    return jax.shard_map(
        on_fast_device if fits_fast_plan(mesh) else on_device,
        mesh=mesh,
        in_specs=(rows, rows) + (flat,) * 16,
        out_specs=(rows, rows) + (flat,) * 15,
        check_vma=False,
    )
```
